32 devices in a mesh: rep: 2 (over y), fsdp: 4 (over z), own: 2 (over x), tp: 2 (over core).
Axes of the slice: x: 2, y: 2, z: 4, core: 2. Of those that a mesh axis runs over, the one named last changes fastest.
Arguments:
- tokens: bfloat16 [4096, 8192], P(('rep', 'fsdp', 'own'), 'tp'), parts along dimension 0, may hold values from -6 to 6
- cotangent: bfloat16 [4096, 1024], P(('rep', 'fsdp', 'own'), 'tp'), parts along dimension 0, may hold values from -6 to 6
- frozen_value_weight: bfloat16 [8192, 1024], P('tp', 'fsdp'), may hold values from -0.0625 to 0.0625
- adapter_down_weight: bfloat16 [8, 8192, 128], P(('fsdp', 'own'), 'tp'), may hold values from -0.0625 to 0.0625
- adapter_up_weight: bfloat16 [8, 128, 1024], P(('fsdp', 'own'), None, 'tp'), may hold values from -0.5 to 0.5
- token_adapter: int32 [4096, 1], P(('rep', 'fsdp', 'own')), parts along dimension 0, may hold values from 0 to 7; in each aligned block of 256 rows (0 to 255, 256 to 511, ...) at most 48 rows name the same one
- rank_step_count: int32 [8], replicated, may hold values from 1 to 8
Outputs:
- projected: bfloat16 [4096, 1024], P(('rep', 'fsdp', 'own'), 'tp'), parts along dimension 0
- input_grad: bfloat16 [4096, 8192], P(('rep', 'fsdp', 'own'), 'tp'), parts along dimension 0
- down_gradient: bfloat16 [16, 8192, 128], P(('rep', 'fsdp', 'own'), 'tp'), parts along dimension 0
- up_gradient: bfloat16 [16, 128, 1024], P(('rep', 'fsdp', 'own'), None, 'tp'), parts along dimension 0
The draws below stay inside these ranges and needn't reach their ends.
There are 2 independent parts, one for each index of `rep`. The reference program is written for one: setup_inputs(seed, part) draws one part's arguments, and reference() takes and returns one part's arrays. A program takes and returns all parts, laid end to end along the dimension named above; an argument that names none is the same for every part. Nothing has to cross between parts.
Inputs may be any that keep to these rules, and one draw needn't show every extreme that they name: `token_adapter`: among the 256 tokens of each aligned block (the tokens of one index pair of fsdp and own), no adapter is named more than 48 times, a bound that some block reaches.
All inputs are finite; a program needn't handle non-finite values.
Results may differ from the reference program's by a relative error of at most 0.0051.
Values may be sent and summed in bfloat16 or wider, within the bound.
No kernel may reach another device: no remote copies, remote signals or barrier semaphores. Data moves between devices by JAX's collectives and lax.ppermute only.
A program may use at most 128 MiB of HBM per device.

```python
import math
import jax
import jax.numpy as jnp
import numpy as np
from jax import lax

MODEL_WIDTH = 8192
VALUE_FEATURES = 1024
RANK_LIMIT = 128
RSTEP = 16
TOK_DEV = 256
ADAPTER_COUNT = 8
MOST = 48
TOKENS = 2048


def plant(array, own_key, smallest, high):
    longest = array.shape.index(max(array.shape))
    spots = []
    for shift in (0, 1):
        where = [jax.random.randint(jax.random.fold_in(own_key, axis), (), 0, length) for axis, length in enumerate(array.shape)]
        where[longest] = (where[longest] + shift) % array.shape[longest]
        spots.append(tuple(where))
    return array.at[spots[0]].set(smallest).at[spots[1]].set(high)


def level_of(stream_key, dims, pieces, low, high):
    def one(dim, parts):
        steps = jax.random.uniform(jax.random.fold_in(jax.random.fold_in(stream_key, 6), dim), (parts,), jnp.float32, low / len(pieces), high / len(pieces))
        return jnp.repeat(jnp.exp(steps), dims[dim] // parts).reshape((-1,) + (1,) * (len(dims) - dim - 1))

    level = one(*pieces[0])
    for cut in pieces[1:]:
        level = level * one(*cut)
    return level


def routed_block(stream_key, own, number, rows, number_of, top, limit, skew):
    order = jax.random.permutation(stream_key, number_of)
    heavy_load, usual = portions_of(number_of, rows * top, limit, skew, True), portions_of(number_of, rows * top, limit, skew, False)
    places = jnp.arange(number_of)

    def named(tallies, turn):
        used = int((tallies > 0).sum())
        fixed = max(1, used // 4)
        passed = fixed + (places - fixed + turn * (used - fixed)) % max(1, number_of - fixed)
        return jnp.zeros((number_of,), jnp.int32).at[order[jnp.where(places < fixed, places, passed)]].set(jnp.asarray(tallies, jnp.int32))

    tallies = jnp.where(number % 4 == 0, named(heavy_load, number // 4), named(usual, number - number // 4 - 1))
    mixed = jax.random.permutation(jax.random.fold_in(own, 3), number_of)
    giver, taker = mixed[0:number_of // 2 * 2:2], mixed[1:number_of // 2 * 2:2]
    margin = jnp.minimum(tallies[giver] - 1, limit - tallies[taker]) // 2
    margin = jnp.where((giver == order[0]) | (taker == order[0]) | (tallies[taker] == 0), 0, jnp.maximum(margin, 0))
    passed = jax.random.randint(jax.random.fold_in(own, 4), (number_of // 2,), 0, 1 << 20) % (margin + 1)
    tallies = tallies.at[giver].add(-passed).at[taker].add(passed)
    labels = jnp.searchsorted(jnp.cumsum(tallies), jnp.arange(rows * top), side="right").astype(jnp.int32)
    table = labels.reshape(top, rows).T
    table = table[jax.random.permutation(jax.random.fold_in(own, 1), rows)]
    turn = jax.random.randint(jax.random.fold_in(own, 2), (rows, 1), 0, top)
    return jnp.take_along_axis(table, (jnp.arange(top)[None, :] + turn) % top, axis=1)


def portions_of(amount, total, bound, lean, full):
    weights = [(1 << 20) // math.isqrt(grade ** lean) + 1 for grade in range(1, amount + 1)]
    largest = bound if full else min(bound, max(-(-total // amount), total * weights[0] // sum(weights)))
    least = 1 if total - largest >= amount - 1 else 0
    counts, rest = [largest] + [least] * (amount - 1), total - largest - least * (amount - 1)
    while rest > 0:
        movable = [i for i in range(1, amount) if counts[i] < largest] or [i for i in range(1, amount) if counts[i] < bound]
        whole, left = sum([weights[i] for i in movable]), rest
        for i in movable:
            addition = min(bound - counts[i], max(1, left * weights[i] // whole), rest)
            counts[i] = counts[i] + addition
            rest = rest - addition
    return np.array(counts)


def centred(own_key, dims, deviation, reach, split=(), kind=jnp.bfloat16):
    values = jax.random.normal(own_key, dims, jnp.float32) * deviation
    if len(split) > 0:
        values = level_of(own_key, dims, split, -0.22, 0.18) * values
    return jnp.clip(values, min=-reach, max=reach).astype(kind)


def setup_inputs(seed: int = 0, part: int = 0) -> dict:
    splits = jax.random.split(jax.random.key(seed), 8)
    own_keys = jax.random.split(jax.random.fold_in(splits[7], part), 8)
    tokens = centred(own_keys[0], (TOKENS, MODEL_WIDTH), 1.0, 6.0, ((0, 8), (1, 2)))
    cotangent = centred(own_keys[1], (TOKENS, VALUE_FEATURES), 1.0, 6.0, ((0, 8), (1, 2)))
    frozen_value_weight = centred(splits[2], (MODEL_WIDTH, VALUE_FEATURES), MODEL_WIDTH ** -0.5, 0.0625, ((0, 2), (1, 4)))
    adapter_down_weight = centred(splits[3], (ADAPTER_COUNT, MODEL_WIDTH, RANK_LIMIT), MODEL_WIDTH ** -0.5, 0.0625, ((0, 8), (1, 2)))
    adapter_up_weight = centred(splits[4], (ADAPTER_COUNT, RANK_LIMIT, VALUE_FEATURES), RANK_LIMIT ** -0.5, 0.5, ((0, 8), (2, 2)))
    token_adapter_keys = jax.random.split(jax.random.fold_in(own_keys[5], 1), TOKENS // TOK_DEV)
    token_adapter_turns = jax.random.permutation(jax.random.fold_in(own_keys[5], 3), TOKENS // TOK_DEV)
    token_adapter = jax.vmap(lambda own, number: routed_block(jax.random.fold_in(own_keys[5], 2), own, number, TOK_DEV, ADAPTER_COUNT, 1, MOST, 2))(token_adapter_keys, token_adapter_turns).reshape((TOKENS, 1))
    rank_step_count = plant(jax.random.randint(splits[6], (ADAPTER_COUNT,), 1, 9), jax.random.fold_in(splits[6], 1), 1, 8).astype(jnp.int32)
    return {"tokens": tokens, "cotangent": cotangent, "frozen_value_weight": frozen_value_weight, "adapter_down_weight": adapter_down_weight, "adapter_up_weight": adapter_up_weight, "token_adapter": token_adapter, "rank_step_count": rank_step_count}


def contract_first(left, right):
    return lax.dot_general(left, right, (((0,), (0,)), ((), ())), preferred_element_type=jnp.float32)


def contract_final_axis(left, right):
    return lax.dot_general(left, right, (((1,), (1,)), ((), ())), preferred_element_type=jnp.float32)


def reference(tokens, cotangent, frozen_value_weight, adapter_down_weight, adapter_up_weight, token_adapter, rank_step_count):
    blocks = TOKENS // TOK_DEV
    span = blocks * MOST
    ids = token_adapter[:, 0].reshape(blocks, TOK_DEV)
    table = (ids[:, :, None] == jnp.arange(ADAPTER_COUNT, dtype=jnp.int32)[None, None, :]).astype(jnp.float32)
    order = jnp.arange(TOK_DEV, dtype=jnp.int32)
    earlier = (order[:, None] > order[None, :]).astype(jnp.float32)
    before = jnp.einsum("rc,bca->bra", earlier, table, precision=lax.Precision.HIGHEST)
    place = jnp.sum(before * table, axis=2).astype(jnp.int32)
    position = (ids * span + jnp.arange(blocks, dtype=jnp.int32)[:, None] * MOST + place).reshape(-1)
    source_rows = jnp.full((ADAPTER_COUNT * span,), TOKENS, jnp.int32).at[position].set(jnp.arange(TOKENS, dtype=jnp.int32))
    source_rows = source_rows.reshape(ADAPTER_COUNT, span)
    padded_x = jnp.concatenate([tokens, jnp.zeros((1, MODEL_WIDTH), jnp.bfloat16)], axis=0)
    padded_dy = jnp.concatenate([cotangent, jnp.zeros((1, VALUE_FEATURES), jnp.bfloat16)], axis=0)
    adapter_ranks = RSTEP * rank_step_count

    def single_adapter(carry, item):
        adapter_delta_rows, input_gradient_rows = carry
        selected_rows, down_matrix, up_matrix, rank = item
        xr = jnp.take(padded_x, selected_rows, axis=0)
        dyr = jnp.take(padded_dy, selected_rows, axis=0)
        keep = jnp.arange(RANK_LIMIT, dtype=jnp.int32)[None, :] < rank
        scale = 16.0 / rank.astype(jnp.float32)
        low = jnp.where(keep, jnp.dot(xr, down_matrix, preferred_element_type=jnp.float32), 0.0).astype(jnp.bfloat16)
        backward_pass = (scale * jnp.where(keep, contract_final_axis(dyr, up_matrix), 0.0)).astype(jnp.bfloat16)
        delta = (scale * jnp.dot(low, up_matrix, preferred_element_type=jnp.float32)).astype(jnp.bfloat16)
        adapter_input_gradient = contract_final_axis(backward_pass, down_matrix).astype(jnp.bfloat16)
        grad_down = contract_first(xr, backward_pass).astype(jnp.bfloat16)
        grad_up = (scale * contract_first(low, dyr)).astype(jnp.bfloat16)
        adapter_delta_rows = adapter_delta_rows.at[selected_rows].set(delta)
        input_gradient_rows = input_gradient_rows.at[selected_rows].set(adapter_input_gradient)
        return (adapter_delta_rows, input_gradient_rows), (grad_down, grad_up)

    start_offset = (jnp.zeros((TOKENS + 1, VALUE_FEATURES), jnp.bfloat16), jnp.zeros((TOKENS + 1, MODEL_WIDTH), jnp.bfloat16))
    (adapter_delta_rows, input_gradient_rows), (down_gradient, up_gradient) = lax.scan(single_adapter, start_offset, (source_rows, adapter_down_weight, adapter_up_weight, adapter_ranks))
    base = jnp.dot(tokens, frozen_value_weight, preferred_element_type=jnp.float32)
    projected = (base + adapter_delta_rows[:TOKENS].astype(jnp.float32)).astype(jnp.bfloat16)
    base_dx = contract_final_axis(cotangent, frozen_value_weight)
    input_grad = (base_dx + input_gradient_rows[:TOKENS].astype(jnp.float32)).astype(jnp.bfloat16)
    return projected, input_grad, down_gradient, up_gradient
```

```python
import jax
import jax.numpy as jnp
from jax import lax
from jax.sharding import PartitionSpec as P

bf16 = jnp.bfloat16
f32 = jnp.float32


def contract_first(left, right):
    return lax.dot_general(
        left, right, (((0,), (0,)), ((), ())), preferred_element_type=f32
    )


def contract_final_axis(left, right):
    return lax.dot_general(
        left, right, (((1,), (1,)), ((), ())), preferred_element_type=f32
    )


def matmul(left, right):
    return jnp.dot(left, right, preferred_element_type=f32)


PAIR = [(0, 1), (1, 0)]
NEIGHBOURS = [(0, 1), (1, 0), (2, 3), (3, 2)]
MIDDLE = [(1, 2), (2, 1)]
OUTWARD = [(1, 0), (2, 3)]
INWARD = [(0, 1), (3, 2)]


def swap(value, axis):
    return lax.ppermute(value, axis, PAIR)


def along(value, pairs):
    return lax.ppermute(value, "fsdp", pairs)


def body_line(
    tokens,
    cotangent,
    frozen_value_weight,
    adapter_down_weight,
    adapter_up_weight,
    token_adapter,
    rank_step_count,
):
    rows, width = tokens.shape
    kv = cotangent.shape[1]
    cols = frozen_value_weight.shape[1]
    down = adapter_down_weight[0]
    up = adapter_up_weight[0]
    rank_limit = down.shape[1]
    quarter = width // 2
    eighth = quarter // 2
    kvq = kv // 2
    z, x = lax.axis_index("fsdp"), lax.axis_index("own")
    y, c = lax.axis_index("rep"), lax.axis_index("tp")
    first_pair = z < 2
    is_middle = (z == 1) | (z == 2)
    line = [z, z + 1 - 2 * (z % 2), jnp.where(first_pair, 2, 1), jnp.where(first_pair, 3, 0)]
    adapters = [2 * t + o for t in line for o in (x, 1 - x)]

    def cut(value, start, size, axis):
        return lax.dynamic_slice_in_dim(value, start, size, axis)

    def features(value, side, axis):
        return [
            cut(value, side * quarter + half * eighth, eighth, axis) for half in (y, 1 - y)
        ]

    def gather_line(piece):
        near = along(piece, NEIGHBOURS)
        both = jnp.stack([piece, near])
        crossed = along(both, MIDDLE)
        outer = along(crossed, OUTWARD)
        return near, jnp.where(is_middle, crossed, outer)

    ids_row = token_adapter[:, 0].astype(bf16)[None, :]
    up_here, up_there = cut(up, x * kvq, kvq, 1), cut(up, (1 - x) * kvq, kvq, 1)
    packet = jnp.concatenate(
        [
            cotangent,
            jnp.concatenate([up_there, jnp.broadcast_to(ids_row, (rank_limit, rows))], axis=1),
        ],
        axis=0,
    )
    packet = swap(packet, "own")
    dy_half = jnp.concatenate([cotangent, packet[:rows]], axis=0)
    up_piece = jnp.concatenate([up_here, packet[rows:, :kvq]], axis=0)
    ids = jnp.concatenate([token_adapter[:, 0], packet[rows, kvq:].astype(jnp.int32)])[:, None]
    x_here = jnp.concatenate(features(tokens, x, 1), axis=1)
    x_there = swap(jnp.concatenate(features(tokens, 1 - x, 1), axis=1), "own")
    x_both = jnp.concatenate([x_here, x_there], axis=0)
    down_here = features(down, x, 0)
    down_piece = jnp.concatenate(
        [down_here[0], swap(cut(down, (1 - x) * quarter + y * eighth, eighth, 0), "own")], axis=1
    )

    ranks = rank_limit // 8 * rank_step_count
    number = ranks.shape[0]
    onehot = ids == jnp.arange(number, dtype=jnp.int32)[None, :]
    token_rank = jnp.sum(jnp.where(onehot, ranks[None, :], 0), axis=1, keepdims=True)
    token_scale = 16.0 / token_rank.astype(f32)
    keep = jnp.arange(rank_limit, dtype=jnp.int32)[None, :] < token_rank

    def compact(part):
        total = jnp.zeros((2 * rows, rank_limit), f32)
        for i, a in enumerate(adapters):
            total = total + jnp.where(ids == a, part[:, i * rank_limit : (i + 1) * rank_limit], 0.0)
        return total

    def expand(value, order):
        return jnp.concatenate(
            [jnp.where(ids == a, value, jnp.zeros_like(value)) for a in order], axis=1
        )

    def sum_features(part):
        part = compact(part)
        part = part + swap(part, "tp")
        return part + jnp.roll(swap(part, "own"), rows, axis=0)

    up_near, up_far = gather_line(up_piece)
    up_all = jnp.concatenate([up_piece, up_near, up_far[0], up_far[1]], axis=0)
    dy_quarter = cut(dy_half, x * kvq, kvq, 1)
    back = sum_features(contract_final_axis(dy_quarter, up_all))
    back = (token_scale * jnp.where(keep, back, 0.0)).astype(bf16)
    back_wide = expand(back, adapters)

    wide = 2 * rank_limit

    def partial(i):
        return contract_first(x_both, back_wide[:, i * wide : (i + 1) * wide])

    to_end, to_middle, to_pair, to_self = partial(3), partial(2), partial(1), partial(0)
    from_end = along(to_end.astype(bf16), INWARD)
    from_end_too = along(to_middle.astype(bf16), INWARD)
    crossed_end = along((to_end + from_end.astype(f32)).astype(bf16), MIDDLE)
    crossed_middle = along((to_middle + from_end_too.astype(f32)).astype(bf16), MIDDLE)
    from_pair = along((to_pair + crossed_end.astype(f32)).astype(bf16), NEIGHBOURS)
    grad = (to_self + from_pair.astype(f32) + crossed_middle.astype(f32)).astype(bf16)
    grad_here = grad[:, :rank_limit]
    grad_there = swap(grad[:, rank_limit:], "own")

    def in_place(here, there, axis):
        blocks = jnp.concatenate(here + there, axis=axis)
        size = blocks.shape[axis] // 4
        return jnp.concatenate(
            [
                cut(blocks, (2 * ((i + x) % 2) + (j + y) % 2) * size, size, axis)
                for i in (0, 1)
                for j in (0, 1)
            ],
            axis=axis,
        )

    down_gradient = in_place([grad_here], [grad_there], 0)[None]

    down_near, down_far = gather_line(down_piece)
    down_mine = jnp.concatenate([down_piece, down_near, down_far[0], down_far[1]], axis=1)
    down_other = swap(down_mine, "rep")
    low = sum_features(
        matmul(x_both[:, :eighth], down_mine) + matmul(x_both[:, eighth:], down_other)
    )
    low = jnp.where(keep, low, 0.0).astype(bf16)
    delta = (token_scale * matmul(expand(low, adapters), up_all)).astype(bf16)
    natural = [2 * (i // 2) + i % 2 for i in range(number)]
    up_part = contract_first(expand(low, natural), dy_quarter).astype(bf16)
    up_sent = lax.all_to_all(
        up_part.reshape(4, 2, rank_limit, kvq), "fsdp", split_axis=0, concat_axis=0, tiled=True
    )
    up_sum = jnp.sum(up_sent.astype(f32), axis=0)
    own_ranks = cut(ranks, 2 * z, 2, 0).astype(f32)
    up_sum = ((16.0 / own_ranks)[:, None, None] * up_sum).astype(bf16)
    up_mine = cut(up_sum, x, 1, 0)
    up_theirs = swap(cut(up_sum, 1 - x, 1, 0), "own")
    up_gradient = jnp.where(
        x == 0,
        jnp.concatenate([up_mine, up_theirs], axis=2),
        jnp.concatenate([up_theirs, up_mine], axis=2),
    )

    dy_tp = swap(dy_half, "tp")
    dy_full = jnp.where(
        c == 0,
        jnp.concatenate([dy_half, dy_tp], axis=1),
        jnp.concatenate([dy_tp, dy_half], axis=1),
    )
    dy_line = jnp.concatenate([cut(dy_full, t * cols, cols, 1) for t in line], axis=1)

    weight_here = features(frozen_value_weight, x, 0)
    weight_near, weight_far = gather_line(weight_here[0])
    got = jnp.concatenate([weight_near, weight_far[0], weight_far[1]], axis=1)
    weight_mine = jnp.concatenate([weight_here[0], got], axis=1)
    weight_other = jnp.concatenate([weight_here[1], swap(got, "rep")], axis=1)

    def input_grad_of(weight, adapter):
        lora = contract_final_axis(back_wide, adapter).astype(bf16)
        return (contract_final_axis(dy_line, weight) + lora.astype(f32)).astype(bf16)

    dx_mine = input_grad_of(weight_mine, down_mine)
    dx_other = input_grad_of(weight_other, down_other)
    back_mine = swap(dx_mine[rows:], "own")
    back_other = swap(dx_other[rows:], "own")
    input_grad = in_place([dx_mine[:rows], dx_other[:rows]], [back_mine, back_other], 1)

    part = matmul(x_both[:, :eighth], weight_mine) + matmul(x_both[:, eighth:], weight_other)
    first, second = part[:, :kv], part[:, kv:]
    own_first = (c == 0) == first_pair
    half = jnp.where(own_first, first, second) + swap(jnp.where(own_first, second, first), "tp")
    turned = jnp.where(own_first, z % 2 == 1, z >= 2)
    half = jnp.where(turned, jnp.roll(half, cols, axis=1), half)
    blank = jnp.zeros_like(delta)
    half = half + jnp.where(
        x == 0, jnp.concatenate([delta, blank], axis=1), jnp.concatenate([blank, delta], axis=1)
    ).astype(f32)
    projected = (half[:rows] + swap(half[rows:], "own")).astype(bf16)
    return (projected, input_grad, down_gradient, up_gradient)


def body_routed(
    tokens,
    cotangent,
    frozen_value_weight,
    adapter_down_weight,
    adapter_up_weight,
    token_adapter,
    rank_step_count,
):
    rows, width_halved = tokens.shape
    half_kv = cotangent.shape[1]
    owning_adapters = lax.axis_size(("fsdp", "own"))
    greatest_rank = 3 * rows // (2 * owning_adapters)
    ids = token_adapter[:, 0]
    table = (ids[:, None] == jnp.arange(owning_adapters, dtype=jnp.int32)[None, :]).astype(
        f32
    )
    order = jnp.arange(rows, dtype=jnp.int32)
    earlier = (order[:, None] > order[None, :]).astype(f32)
    before = jnp.dot(earlier, table, precision=lax.Precision.HIGHEST)
    place = jnp.sum(before * table, axis=1).astype(jnp.int32)
    slot = ids * greatest_rank + place
    source_rows = jnp.full((owning_adapters * greatest_rank,), rows, jnp.int32).at[slot].set(order)
    padded_x = jnp.concatenate([tokens, jnp.zeros((1, width_halved), bf16)], axis=0)
    padded_dy = jnp.concatenate([cotangent, jnp.zeros((1, half_kv), bf16)], axis=0)
    send_x = jnp.take(padded_x, source_rows, axis=0)
    send_dy = jnp.take(padded_dy, source_rows, axis=0)
    recv_x, recv_dy = (
        lax.all_to_all(
            send_x.reshape(owning_adapters, greatest_rank, width_halved),
            ("fsdp", "own"),
            split_axis=0,
            concat_axis=0,
            tiled=True,
        ),
        lax.all_to_all(
            send_dy.reshape(owning_adapters, greatest_rank, half_kv),
            ("fsdp", "own"),
            split_axis=0,
            concat_axis=0,
            tiled=True,
        ),
    )
    flat_x = recv_x.reshape(owning_adapters * greatest_rank, width_halved)
    flat_dy = recv_dy.reshape(owning_adapters * greatest_rank, half_kv)
    dy_full = lax.all_gather(cotangent, "tp", axis=1, tiled=True)
    whole = lax.all_gather(frozen_value_weight, "fsdp", axis=1, tiled=True)
    partial_y = jnp.dot(tokens, whole, preferred_element_type=f32)
    base_dx = contract_final_axis(dy_full, whole)
    base_y = lax.psum_scatter(partial_y, "tp", scatter_dimension=1, tiled=True)
    down_matrix = adapter_down_weight[0]
    up_matrix = adapter_up_weight[0]
    part_low = jnp.dot(flat_x, down_matrix, preferred_element_type=f32)
    part_back = contract_final_axis(flat_dy, up_matrix)
    low_sum, back_sum = lax.psum((part_low, part_back), "tp")
    width_rank = down_matrix.shape[1]
    rank = width_rank // 8 * rank_step_count[lax.axis_index(("fsdp", "own"))]
    keep = jnp.arange(width_rank, dtype=jnp.int32)[None, :] < rank
    scale = 16.0 / rank.astype(f32)
    low = jnp.where(keep, low_sum, 0.0).astype(bf16)
    backward_pass = (scale * jnp.where(keep, back_sum, 0.0)).astype(bf16)
    delta = (scale * jnp.dot(low, up_matrix, preferred_element_type=f32)).astype(
        bf16
    )
    adapter_input_gradient = contract_final_axis(backward_pass, down_matrix).astype(bf16)
    down_gradient = contract_first(flat_x, backward_pass).astype(bf16)[None]
    up_gradient = (scale * contract_first(low, flat_dy)).astype(bf16)[None]
    home_delta, home_dx = (
        lax.all_to_all(
            delta.reshape(owning_adapters, greatest_rank, half_kv),
            ("fsdp", "own"),
            split_axis=0,
            concat_axis=0,
            tiled=True,
        ),
        lax.all_to_all(
            adapter_input_gradient.reshape(owning_adapters, greatest_rank, width_halved),
            ("fsdp", "own"),
            split_axis=0,
            concat_axis=0,
            tiled=True,
        ),
    )
    adapter_delta_rows = jnp.take(
        home_delta.reshape(owning_adapters * greatest_rank, half_kv), slot, axis=0
    )
    input_gradient_rows = jnp.take(
        home_dx.reshape(owning_adapters * greatest_rank, width_halved), slot, axis=0
    )
    projected = (base_y + adapter_delta_rows.astype(f32)).astype(bf16)
    input_grad = (base_dx + input_gradient_rows.astype(f32)).astype(bf16)
    return (projected, input_grad, down_gradient, up_gradient)


def solution(mesh):
    placed = (
        P(("rep", "fsdp", "own"), "tp"),
        P(("rep", "fsdp", "own"), "tp"),
        P("tp", "fsdp"),
        P(("fsdp", "own"), "tp", None),
        P(("fsdp", "own"), None, "tp"),
        P(("rep", "fsdp", "own"), None),
        P(),
    )
    line = mesh.shape["fsdp"] == 4 and mesh.shape["own"] == 2 and mesh.shape["rep"] == 2
    return jax.shard_map(
        body_line if line else body_routed,
        mesh=mesh,
        in_specs=placed,
        out_specs=(
            P(("rep", "fsdp", "own"), "tp"),
            P(("rep", "fsdp", "own"), "tp"),
            P(("rep", "fsdp", "own"), "tp", None),
            P(("rep", "fsdp", "own"), None, "tp"),
        ),
        check_vma=False,
    )
```

```python
import jax
import jax.numpy as jnp
from jax import lax
from jax.sharding import PartitionSpec as P

bf16 = jnp.bfloat16
f32 = jnp.float32


def contract_first(left, right):
    return lax.dot_general(
        left, right, (((0,), (0,)), ((), ())), preferred_element_type=f32
    )


def contract_final_axis(left, right):
    return lax.dot_general(
        left, right, (((1,), (1,)), ((), ())), preferred_element_type=f32
    )


def matmul(left, right):
    return jnp.dot(left, right, preferred_element_type=f32)


PAIR = [(0, 1), (1, 0)]
NEIGHBOURS = [(0, 1), (1, 0), (2, 3), (3, 2)]
MIDDLE = [(1, 2), (2, 1)]
OUTWARD = [(1, 0), (2, 3)]
INWARD = [(0, 1), (3, 2)]


def swap(value, axis):
    return lax.ppermute(value, axis, PAIR)


def along(value, pairs):
    return lax.ppermute(value, "fsdp", pairs)


def after(value, *earlier):
    return lax.optimization_barrier((value, *earlier))[0]


def body_line(
    tokens,
    cotangent,
    frozen_value_weight,
    adapter_down_weight,
    adapter_up_weight,
    token_adapter,
    rank_step_count,
):
    rows, width = tokens.shape
    kv = cotangent.shape[1]
    cols = frozen_value_weight.shape[1]
    down = adapter_down_weight[0]
    up = adapter_up_weight[0]
    rank_limit = down.shape[1]
    wide = 2 * rank_limit
    quarter = width // 2
    eighth = quarter // 2
    kvq = kv // 2
    z, x = lax.axis_index("fsdp"), lax.axis_index("own")
    y, c = lax.axis_index("rep"), lax.axis_index("tp")
    first_pair = z < 2
    is_middle = (z == 1) | (z == 2)
    line = [z, z + 1 - 2 * (z % 2), jnp.where(first_pair, 2, 1), jnp.where(first_pair, 3, 0)]
    adapters = [2 * t + o for t in line for o in (x, 1 - x)]
    number = len(adapters)

    def cut(value, start, size, axis):
        return lax.dynamic_slice_in_dim(value, start, size, axis)

    def features(value, side, half, axis):
        return cut(value, side * quarter + half * eighth, eighth, axis)

    weight_here = features(frozen_value_weight, x, y, 0)
    weight_near = along(weight_here, NEIGHBOURS)
    up_sent = jnp.broadcast_to(
        up.reshape(rank_limit, 2, kvq).transpose(1, 0, 2)[None], (4, 2, rank_limit, kvq)
    ).reshape(number, rank_limit, kvq)
    up_all = lax.all_to_all(
        up_sent, ("fsdp", "own"), split_axis=0, concat_axis=0, tiled=True
    ).reshape(number * rank_limit, kvq)

    down_got = swap(features(down, 1 - x, y, 0), "own")
    down_piece = jnp.concatenate([features(down, x, y, 0), down_got], axis=1)
    ids_row = token_adapter[:, 0].astype(bf16)[None, :]
    packet = swap(
        jnp.concatenate(
            [cotangent, jnp.broadcast_to(jnp.concatenate([ids_row, ids_row], axis=1), (16, kv))]
        ),
        "own",
    )
    dy_half = jnp.concatenate([cotangent, packet[:rows]], axis=0)
    ids = jnp.concatenate([token_adapter[:, 0], packet[rows, :rows].astype(jnp.int32)])[:, None]
    def spread(ids, value, order):
        place = jnp.repeat(jnp.stack([jnp.asarray(a, jnp.int32) for a in order]), rank_limit)
        tiled = jnp.concatenate([value] * number, axis=1)
        return jnp.where(ids == place[None, :], tiled, jnp.zeros_like(tiled))

    ranks = rank_limit // 8 * rank_step_count
    token_rank = jnp.sum(
        jnp.where(ids == jnp.arange(number, dtype=jnp.int32)[None, :], ranks[None, :], 0),
        axis=1,
        keepdims=True,
    )
    token_scale = 16.0 / token_rank.astype(f32)
    keep = jnp.arange(rank_limit, dtype=jnp.int32)[None, :] < token_rank

    def compact(part, order):
        total = jnp.zeros((2 * rows, rank_limit), f32)
        for i, a in enumerate(order):
            total = total + jnp.where(ids == a, part[:, i * rank_limit : (i + 1) * rank_limit], 0.0)
        return total + swap(total, "tp")

    def sum_own(total):
        return total + jnp.roll(swap(total, "own"), rows, axis=0)

    def share_tokens(half, *earlier):
        sent = after(features(tokens, 1 - x, half, 1), *earlier)
        return jnp.concatenate([features(tokens, x, half, 1), swap(sent, "own")], axis=0)

    dy_quarter = cut(dy_half, x * kvq, kvq, 1)
    back_half = compact(contract_final_axis(dy_quarter, up_all), range(number))
    x_both = [share_tokens(y, up_all), share_tokens(1 - y, back_half)]
    back = sum_own(back_half)
    back = (token_scale * jnp.where(keep, back, 0.0)).astype(bf16)
    back_wide = spread(ids, back, adapters)
    back_in = along(
        jnp.concatenate([back, jnp.broadcast_to(ids.astype(bf16), back.shape)], axis=1), INWARD
    )
    back_in_wide = spread(
        back_in[:, rank_limit : rank_limit + 1].astype(jnp.int32), back_in[:, :rank_limit], adapters
    )

    def far_pair(piece, near):
        crossed = along(jnp.concatenate([piece, near], axis=1), MIDDLE)
        outer = along(crossed, OUTWARD)
        return jnp.where(is_middle, crossed, outer)

    weight_far = far_pair(weight_here, weight_near)
    down_piece = after(down_piece, up_all)
    down_near = along(down_piece, NEIGHBOURS)
    down_far = far_pair(down_piece, down_near)
    grad_here, grad_there = [], []
    for x_half in x_both:
        x_in = along(x_half, INWARD)

        def total(first, last):
            span = slice(first * wide, last * wide)
            return contract_first(x_half, back_wide[:, span])

        def total_in(first, last):
            span = slice(first * wide, last * wide)
            return contract_first(x_in, back_in_wide[:, span])

        crossed = along((total(2, 4) + total_in(2, 4)).astype(bf16), MIDDLE)
        outer = along((total(1, 2) + crossed[:, wide:].astype(f32)).astype(bf16), OUTWARD)
        grad = total(0, 1) + total_in(0, 1) + crossed[:, :wide].astype(f32) + outer.astype(f32)
        grad = grad.astype(bf16)
        grad_here.append(grad[:, :rank_limit])
        grad_there.append(swap(grad[:, rank_limit:], "own"))

    down_mine = jnp.concatenate([down_piece, down_near, down_far], axis=1)
    down_other = jnp.concatenate(
        [swap(jnp.concatenate([down_piece, down_near], axis=1), "rep"), swap(down_far, "rep")],
        axis=1,
    )
    low = sum_own(
        compact(matmul(x_both[0], down_mine) + matmul(x_both[1], down_other), adapters)
    )
    low = jnp.where(keep, low, 0.0).astype(bf16)
    low_wide = spread(ids, low, range(number))
    delta = (token_scale * matmul(low_wide, up_all)).astype(bf16)
    up_part = contract_first(low_wide, dy_quarter).astype(bf16)
    up_got = lax.all_to_all(
        up_part.reshape(4, 2, rank_limit, kvq), "fsdp", split_axis=0, concat_axis=0, tiled=True
    )
    up_sum = jnp.sum(up_got.astype(f32), axis=0)
    own_ranks = cut(ranks, 2 * z, 2, 0).astype(f32)
    up_sum = ((16.0 / own_ranks)[:, None, None] * up_sum).astype(bf16)
    up_mine = cut(up_sum, x, 1, 0)
    up_theirs = swap(cut(up_sum, 1 - x, 1, 0), "own")
    up_gradient = jnp.where(
        x == 0,
        jnp.concatenate([up_mine, up_theirs], axis=2),
        jnp.concatenate([up_theirs, up_mine], axis=2),
    )

    def in_place(here, there, axis):
        blocks = jnp.concatenate(here + there, axis=axis)
        size = blocks.shape[axis] // 4
        return jnp.concatenate(
            [
                cut(blocks, (2 * ((i + x) % 2) + (j + y) % 2) * size, size, axis)
                for i in (0, 1)
                for j in (0, 1)
            ],
            axis=axis,
        )

    down_gradient = in_place(grad_here, grad_there, 0)[None]

    dy_tp = swap(dy_half, "tp")
    dy_full = jnp.where(
        c == 0,
        jnp.concatenate([dy_half, dy_tp], axis=1),
        jnp.concatenate([dy_tp, dy_half], axis=1),
    )
    dy_line = jnp.concatenate([cut(dy_full, t * cols, cols, 1) for t in line], axis=1)

    weight_mine = jnp.concatenate([weight_here, weight_near, weight_far], axis=1)
    weight_other = jnp.concatenate(
        [
            features(frozen_value_weight, x, 1 - y, 0),
            swap(weight_near, "rep"),
            swap(weight_far, "rep"),
        ],
        axis=1,
    )

    def input_grad_of(weight, adapter):
        lora = contract_final_axis(back_wide, adapter).astype(bf16)
        return (contract_final_axis(dy_line, weight) + lora.astype(f32)).astype(bf16)

    dx_mine = input_grad_of(weight_mine, down_mine)
    dx_other = input_grad_of(weight_other, down_other)
    back_mine = swap(dx_mine[rows:], "own")
    back_other = swap(dx_other[rows:], "own")
    input_grad = in_place([dx_mine[:rows], dx_other[:rows]], [back_mine, back_other], 1)

    part = matmul(x_both[0], weight_mine) + matmul(x_both[1], weight_other)
    first, second = part[:, :kv], part[:, kv:]
    own_first = (c == 0) == first_pair
    half = jnp.where(own_first, first, second) + swap(jnp.where(own_first, second, first), "tp")
    turned = jnp.where(own_first, z % 2 == 1, z >= 2)
    half = jnp.where(turned, jnp.roll(half, cols, axis=1), half)
    blank = jnp.zeros_like(delta)
    half = half + jnp.where(
        x == 0, jnp.concatenate([delta, blank], axis=1), jnp.concatenate([blank, delta], axis=1)
    ).astype(f32)
    projected = (half[:rows] + swap(half[rows:], "own")).astype(bf16)
    return (projected, input_grad, down_gradient, up_gradient)


def body_routed(
    tokens,
    cotangent,
    frozen_value_weight,
    adapter_down_weight,
    adapter_up_weight,
    token_adapter,
    rank_step_count,
):
    rows, width_halved = tokens.shape
    half_kv = cotangent.shape[1]
    owning_adapters = lax.axis_size(("fsdp", "own"))
    greatest_rank = 3 * rows // (2 * owning_adapters)
    ids = token_adapter[:, 0]
    table = (ids[:, None] == jnp.arange(owning_adapters, dtype=jnp.int32)[None, :]).astype(
        f32
    )
    order = jnp.arange(rows, dtype=jnp.int32)
    earlier = (order[:, None] > order[None, :]).astype(f32)
    before = jnp.dot(earlier, table, precision=lax.Precision.HIGHEST)
    place = jnp.sum(before * table, axis=1).astype(jnp.int32)
    slot = ids * greatest_rank + place
    source_rows = jnp.full((owning_adapters * greatest_rank,), rows, jnp.int32).at[slot].set(order)
    padded_x = jnp.concatenate([tokens, jnp.zeros((1, width_halved), bf16)], axis=0)
    padded_dy = jnp.concatenate([cotangent, jnp.zeros((1, half_kv), bf16)], axis=0)
    send_x = jnp.take(padded_x, source_rows, axis=0)
    send_dy = jnp.take(padded_dy, source_rows, axis=0)
    recv_x, recv_dy = (
        lax.all_to_all(
            send_x.reshape(owning_adapters, greatest_rank, width_halved),
            ("fsdp", "own"),
            split_axis=0,
            concat_axis=0,
            tiled=True,
        ),
        lax.all_to_all(
            send_dy.reshape(owning_adapters, greatest_rank, half_kv),
            ("fsdp", "own"),
            split_axis=0,
            concat_axis=0,
            tiled=True,
        ),
    )
    flat_x = recv_x.reshape(owning_adapters * greatest_rank, width_halved)
    flat_dy = recv_dy.reshape(owning_adapters * greatest_rank, half_kv)
    dy_full = lax.all_gather(cotangent, "tp", axis=1, tiled=True)
    whole = lax.all_gather(frozen_value_weight, "fsdp", axis=1, tiled=True)
    partial_y = jnp.dot(tokens, whole, preferred_element_type=f32)
    base_dx = contract_final_axis(dy_full, whole)
    base_y = lax.psum_scatter(partial_y, "tp", scatter_dimension=1, tiled=True)
    down_matrix = adapter_down_weight[0]
    up_matrix = adapter_up_weight[0]
    part_low = jnp.dot(flat_x, down_matrix, preferred_element_type=f32)
    part_back = contract_final_axis(flat_dy, up_matrix)
    low_sum, back_sum = lax.psum((part_low, part_back), "tp")
    width_rank = down_matrix.shape[1]
    rank = width_rank // 8 * rank_step_count[lax.axis_index(("fsdp", "own"))]
    keep = jnp.arange(width_rank, dtype=jnp.int32)[None, :] < rank
    scale = 16.0 / rank.astype(f32)
    low = jnp.where(keep, low_sum, 0.0).astype(bf16)
    backward_pass = (scale * jnp.where(keep, back_sum, 0.0)).astype(bf16)
    delta = (scale * jnp.dot(low, up_matrix, preferred_element_type=f32)).astype(
        bf16
    )
    adapter_input_gradient = contract_final_axis(backward_pass, down_matrix).astype(bf16)
    down_gradient = contract_first(flat_x, backward_pass).astype(bf16)[None]
    up_gradient = (scale * contract_first(low, flat_dy)).astype(bf16)[None]
    home_delta, home_dx = (
        lax.all_to_all(
            delta.reshape(owning_adapters, greatest_rank, half_kv),
            ("fsdp", "own"),
            split_axis=0,
            concat_axis=0,
            tiled=True,
        ),
        lax.all_to_all(
            adapter_input_gradient.reshape(owning_adapters, greatest_rank, width_halved),
            ("fsdp", "own"),
            split_axis=0,
            concat_axis=0,
            tiled=True,
        ),
    )
    adapter_delta_rows = jnp.take(
        home_delta.reshape(owning_adapters * greatest_rank, half_kv), slot, axis=0
    )
    input_gradient_rows = jnp.take(
        home_dx.reshape(owning_adapters * greatest_rank, width_halved), slot, axis=0
    )
    projected = (base_y + adapter_delta_rows.astype(f32)).astype(bf16)
    input_grad = (base_dx + input_gradient_rows.astype(f32)).astype(bf16)
    return (projected, input_grad, down_gradient, up_gradient)


def solution(mesh):
    placed = (
        P(("rep", "fsdp", "own"), "tp"),
        P(("rep", "fsdp", "own"), "tp"),
        P("tp", "fsdp"),
        P(("fsdp", "own"), "tp", None),
        P(("fsdp", "own"), None, "tp"),
        P(("rep", "fsdp", "own"), None),
        P(),
    )
    line = mesh.shape["fsdp"] == 4 and mesh.shape["own"] == 2 and mesh.shape["rep"] == 2
    return jax.shard_map(
        body_line if line else body_routed,
        mesh=mesh,
        in_specs=placed,
        out_specs=(
            P(("rep", "fsdp", "own"), "tp"),
            P(("rep", "fsdp", "own"), "tp"),
            P(("rep", "fsdp", "own"), "tp", None),
            P(("rep", "fsdp", "own"), None, "tp"),
        ),
        check_vma=False,
    )
```

```python
import jax
import jax.numpy as jnp
from jax import lax
from jax.experimental import pallas as pl
from jax.experimental.pallas import tpu as pltpu
from jax.sharding import PartitionSpec as P

bf16 = jnp.bfloat16
f32 = jnp.float32


def contract_first(left, right):
    return lax.dot_general(
        left, right, (((0,), (0,)), ((), ())), preferred_element_type=f32
    )


def contract_final_axis(left, right):
    return lax.dot_general(
        left, right, (((1,), (1,)), ((), ())), preferred_element_type=f32
    )


def matmul(left, right):
    return jnp.dot(left, right, preferred_element_type=f32)


PAIR = [(0, 1), (1, 0)]
NEIGHBOURS = [(0, 1), (1, 0), (2, 3), (3, 2)]
MIDDLE = [(1, 2), (2, 1)]
OUTWARD = [(1, 0), (2, 3)]
INWARD = [(0, 1), (3, 2)]


def swap(value, axis):
    return lax.ppermute(value, axis, PAIR)


def along(value, pairs):
    return lax.ppermute(value, "fsdp", pairs)


def kernel_call(body, outs, *operands, scalars=None):
    specs = [pl.BlockSpec(memory_space=pltpu.VMEM)] * len(operands)
    if scalars is not None:
        operands = (scalars, *operands)
        specs = [pl.BlockSpec(memory_space=pltpu.SMEM), *specs]
    return pl.pallas_call(
        body,
        out_shape=list(outs),
        in_specs=specs,
        out_specs=[pl.BlockSpec(memory_space=pltpu.VMEM)] * len(outs),
        compiler_params=pltpu.CompilerParams(vmem_limit_bytes=28 * 2**20),
        cost_estimate=pl.CostEstimate(flops=0, bytes_accessed=0, transcendentals=0),
    )(*operands)


def spread_kernel(order, ids, value, out):
    size = value.shape[1]
    rows = value[...].astype(f32)
    for i in range(out.shape[1] // size):
        out[:, i * size : (i + 1) * size] = jnp.where(ids[...] == order[i], rows, 0.0).astype(bf16)


def back_kernel(ids, dy, up, out):
    size = out.shape[1]
    for i in range(0, up.shape[0] // size, 2):
        both = contract_final_axis(dy[...], up[i * size : (i + 2) * size, :])
        for j in (0, 1):
            part = jnp.where(ids[...] == i + j, both[:, j * size : (j + 1) * size], 0.0)
            out[...] = part if i + j == 0 else out[...] + part


def low_kernel(order, ids, x_mine, x_other, own, near, far, own_near_other, far_other, out):
    size = out.shape[1]
    wide = 2 * size
    mine = [own[...], near[...], far[:, :wide], far[:, wide:]]
    other = [
        own_near_other[:, :wide],
        own_near_other[:, wide:],
        far_other[:, :wide],
        far_other[:, wide:],
    ]
    for i in range(4):
        both = matmul(x_mine[...], mine[i]) + matmul(x_other[...], other[i])
        for j in (0, 1):
            part = jnp.where(ids[...] == order[2 * i + j], both[:, j * size : (j + 1) * size], 0.0)
            out[...] = part if i + j == 0 else out[...] + part


def dx_kernel(dy, back, own, near, far_a, far_b, *rest):
    *adapter, here, there = rest
    rows, width = here.shape
    cols = own.shape[1]
    tile = far_a.shape[0] // 2
    for t in range(width // tile):
        span = slice(t * tile, (t + 1) * tile)
        far = (far_a, far_b)[t // 2]
        part = slice((t % 2) * tile, (t % 2 + 1) * tile)
        base = contract_final_axis(dy[:, :cols], own[span, :])
        base += contract_final_axis(dy[:, cols : 2 * cols], near[span, :])
        base += contract_final_axis(dy[:, 2 * cols :], far[part, :])
        lora, start = 0.0, 0
        for piece in adapter:
            stop = start + piece.shape[1]
            lora += contract_final_axis(back[:, start:stop], piece[span, :])
            start = stop
        total = (base + lora.astype(bf16).astype(f32)).astype(bf16)
        here[:, span] = total[:rows]
        there[:, span] = total[rows:]


def y_kernel(flags, x_mine, x_other, *rest):
    mine, other, (keep, send) = rest[:4], rest[4:8], rest[8:]
    cols = mine[0].shape[1]
    half = mine[2].shape[0]

    def store(block, pair, place):
        kept = flags[0] == (1 if pair else 0)

        @pl.when(kept)
        def _():
            keep[place] = block

        @pl.when(jnp.logical_not(kept))
        def _():
            send[place] = block

    for i in (0, 1):
        block = matmul(x_mine[...], mine[i][...]) + matmul(x_other[...], other[i][...])
        store(block, True, (flags[1] + i) % 2)
    for i in (0, 1):
        span = slice(i * cols, (i + 1) * cols)
        block = 0.0
        for tokens, parts in ((x_mine, mine), (x_other, other)):
            block += matmul(tokens[:, :half], parts[2][:, span])
            block += matmul(tokens[:, half:], parts[3][:, span])
        store(block, False, (flags[2] + i) % 2)


def body_line(
    tokens,
    cotangent,
    frozen_value_weight,
    adapter_down_weight,
    adapter_up_weight,
    token_adapter,
    rank_step_count,
):
    rows, width = tokens.shape
    kv = cotangent.shape[1]
    cols = frozen_value_weight.shape[1]
    down = adapter_down_weight[0]
    up = adapter_up_weight[0]
    rank_limit = down.shape[1]
    wide = 2 * rank_limit
    quarter = width // 2
    eighth = quarter // 2
    part = eighth // 2
    kvq = kv // 2
    z, x = lax.axis_index("fsdp"), lax.axis_index("own")
    y, c = lax.axis_index("rep"), lax.axis_index("tp")
    first_pair = z < 2
    is_middle = (z == 1) | (z == 2)
    line = [z, z + 1 - 2 * (z % 2), jnp.where(first_pair, 2, 1), jnp.where(first_pair, 3, 0)]
    adapters = jnp.stack([2 * t + o for t in line for o in (x, 1 - x)]).astype(jnp.int32)
    number = adapters.shape[0]
    natural = jnp.arange(number, dtype=jnp.int32)

    latest = []

    def step(*values):
        if latest:
            values = lax.optimization_barrier((*values, latest[0]))[: len(values)]
        return values[0] if len(values) == 1 else values

    def done(value):
        latest[:] = [value]
        return value

    def cut(value, start, size, axis):
        return lax.dynamic_slice_in_dim(value, start, size, axis)

    def features(value, side, half, axis):
        return cut(value, side * quarter + half * eighth, eighth, axis)

    def spread(ids, value, order):
        out = jax.ShapeDtypeStruct((value.shape[0], number * rank_limit), bf16)
        return kernel_call(spread_kernel, [out], ids, value, scalars=order)[0]

    def join(*values):
        return jnp.concatenate(values, axis=1)

    weight_here = done(features(frozen_value_weight, x, y, 0))
    weight_near = along(weight_here, NEIGHBOURS)
    down_got = swap(done(features(step(down), 1 - x, y, 0)), "own")
    ids_row = token_adapter[:, 0].astype(bf16)[None, :]
    packet = done(
        jnp.concatenate(
            [step(cotangent), jnp.broadcast_to(jnp.concatenate([ids_row, ids_row], axis=1), (16, kv))]
        )
    )
    packet = swap(packet, "own")
    up_sent = jnp.broadcast_to(
        step(up).reshape(rank_limit, 2, kvq).transpose(1, 0, 2)[None], (4, 2, rank_limit, kvq)
    ).reshape(number, rank_limit, kvq)
    up_all = lax.all_to_all(
        done(up_sent), ("fsdp", "own"), split_axis=0, concat_axis=0, tiled=True
    ).reshape(number * rank_limit, kvq)
    sent = done(features(step(tokens), 1 - x, y, 1))
    x_there = [swap(sent, "own")]
    sent = done(features(step(tokens), 1 - x, 1 - y, 1))
    x_there.append(swap(sent, "own"))
    down_piece = done(join(features(down, x, y, 0), step(down_got)))
    down_near = along(down_piece, NEIGHBOURS)
    weight_near = step(weight_near)
    crossing = done(join(weight_here[:part], weight_near[:part]))
    crossed_a = along(crossing, MIDDLE)
    weight_near_other = swap(weight_near, "rep")

    packet = step(packet)
    dy_half = jnp.concatenate([cotangent, packet[:rows]], axis=0)
    ids = jnp.concatenate([token_adapter[:, 0], packet[rows, :rows].astype(jnp.int32)])[:, None]
    ranks = rank_limit // 8 * rank_step_count
    token_rank = jnp.sum(
        jnp.where(ids == natural[None, :], ranks[None, :], 0), axis=1, keepdims=True
    )
    token_scale = 16.0 / token_rank.astype(f32)
    keep = jnp.arange(rank_limit, dtype=jnp.int32)[None, :] < token_rank
    dy_quarter = cut(dy_half, x * kvq, kvq, 1)
    dy_tp = swap(done(dy_half), "tp")

    compact = jax.ShapeDtypeStruct((2 * rows, rank_limit), f32)

    def sum_own(total):
        return jnp.roll(swap(total, "own"), rows, axis=0)

    up_all, dy_quarter = step(up_all, dy_quarter)
    back_part = done(kernel_call(back_kernel, [compact], ids, dy_quarter, up_all)[0])
    back_tp = swap(back_part, "tp")
    near = step(down_near)
    down_near = near
    crossing = done(join(down_piece, near))
    down_crossed = along(crossing, MIDDLE)
    down_other = swap(crossing, "rep")
    back_part = done(back_part + step(back_tp))
    back_own = sum_own(back_part)
    crossing = done(join(step(weight_here)[part:], weight_near[part:]))
    crossed_b = along(crossing, MIDDLE)
    x_mine = done(jnp.concatenate([features(tokens, x, y, 1), step(x_there[0])], axis=0))
    x_in = [along(x_mine, INWARD)]
    back = back_part + step(back_own)
    back = (token_scale * jnp.where(keep, back, 0.0)).astype(bf16)
    back_in = done(join(back, jnp.broadcast_to(ids.astype(bf16), back.shape)))
    back_in = along(back_in, INWARD)
    x_other = done(
        jnp.concatenate([features(tokens, x, 1 - y, 1), step(x_there[1])], axis=0)
    )
    x_in.append(along(x_other, INWARD))
    x_both = [x_mine, x_other]
    outer_a = along(step(crossed_a), OUTWARD)
    back_wide = done(spread(ids, step(back), adapters))

    dy_tp = step(dy_tp)
    dy_full = jnp.where(c == 0, join(dy_half, dy_tp), join(dy_tp, dy_half))
    dy_line = done(join(*[cut(dy_full, t * cols, cols, 1) for t in line]))

    down_outer = along(step(down_crossed), OUTWARD)
    back_in, down_other = step(back_in, down_other)
    in_ids = back_in[:, rank_limit : rank_limit + 1].astype(jnp.int32)
    back_in_wide = done(spread(in_ids, back_in[:, :rank_limit], adapters))

    outer_a, crossed_a, weight_near_other = step(outer_a, crossed_a, weight_near_other)
    far_a = done(jnp.where(is_middle, crossed_a, outer_a))
    far_a_other = swap(far_a, "rep")

    def total(half, first, last):
        span = slice(first * wide, last * wide)
        return contract_first(x_both[half], back_wide[:, span])

    def total_in(half, first, last):
        span = slice(first * wide, last * wide)
        return contract_first(x_in[half], back_in_wide[:, span])

    def to_middle(half):
        x_in[half] = step(x_in[half])
        return along(
            done((total(half, 2, 4) + total_in(half, 2, 4)).astype(bf16)), MIDDLE
        )

    def to_end(half, crossed):
        crossed = step(crossed)
        sums = total(half, 1, 2) + crossed[:, wide:].astype(f32)
        return along(done(sums.astype(bf16)), OUTWARD)

    def finish(half, crossed, outer):
        outer = step(outer)
        grad = total(half, 0, 1) + total_in(half, 0, 1)
        grad = (grad + crossed[:, :wide].astype(f32) + outer.astype(f32)).astype(bf16)
        here, there = grad[:, :rank_limit], grad[:, rank_limit:]
        done(here)
        return here, swap(there, "own")

    middle = [to_middle(0)]
    outer_b = along(step(crossed_b), OUTWARD)
    down_outer, down_crossed, far_a_other = step(down_outer, down_crossed, far_a_other)
    down_far = done(jnp.where(is_middle, down_crossed, down_outer))
    down_far_other = swap(down_far, "rep")
    middle.append(to_middle(1))
    outer_b, crossed_b = step(outer_b, crossed_b)
    far_b = done(jnp.where(is_middle, crossed_b, outer_b))
    far_b_other = swap(far_b, "rep")

    half_grad = [jax.ShapeDtypeStruct((rows, eighth), bf16)] * 2
    dx_mine, dx_sent = kernel_call(
        dx_kernel,
        half_grad,
        step(dy_line),
        back_wide,
        weight_here,
        weight_near,
        far_a,
        far_b,
        down_piece,
        down_near,
        down_far,
    )
    dx_mine_got = swap(done(dx_sent), "own")
    outward = [to_end(0, middle[0])]

    down_far_other, dx_mine_got = step(down_far_other, dx_mine_got)
    low_part = done(
        kernel_call(
            low_kernel,
            [compact],
            ids,
            x_mine,
            x_other,
            down_piece,
            down_near,
            down_far,
            down_other,
            down_far_other,
            scalars=adapters,
        )[0]
    )
    low_tp = swap(low_part, "tp")
    low_part = done(low_part + step(low_tp))
    low_own = sum_own(low_part)
    weight_other = features(frozen_value_weight, x, 1 - y, 0)
    grads = [finish(0, middle[0], outward[0])]

    far_b_other = step(far_b_other)
    dx_other, dx_sent = kernel_call(
        dx_kernel,
        half_grad,
        step(dy_line),
        back_wide,
        weight_other,
        weight_near_other,
        far_a_other,
        far_b_other,
        down_other,
        down_far_other,
    )
    dx_other_got = swap(done(dx_sent), "own")
    outward.append(to_end(1, middle[1]))

    low_own, grad_got = step(low_own, grads[0][1])
    low = jnp.where(keep, low_part + low_own, 0.0).astype(bf16)
    low_wide = done(spread(ids, low, natural))
    up_part = done(contract_first(step(low_wide), dy_quarter).astype(bf16))
    up_got = lax.all_to_all(
        up_part.reshape(4, 2, rank_limit, kvq), "fsdp", split_axis=0, concat_axis=0, tiled=True
    )
    delta = done((token_scale * matmul(step(low_wide), up_all)).astype(bf16))

    flags = jnp.stack([(c == 0) == first_pair, z % 2 == 1, z >= 2]).astype(jnp.int32)
    y_keep, y_sent = kernel_call(
        y_kernel,
        [jax.ShapeDtypeStruct((2, 2 * rows, cols), f32)] * 2,
        step(x_mine),
        x_other,
        weight_here,
        weight_near,
        far_a,
        far_b,
        weight_other,
        weight_near_other,
        far_a_other,
        far_b_other,
        scalars=flags,
    )
    y_got = swap(done(y_sent), "tp")
    chosen = jnp.arange(2)[:, None, None] == x
    y_got, dx_other_got = step(y_got, dx_other_got)
    y_sum = y_keep + y_got + jnp.where(chosen, delta[None].astype(f32), 0.0)
    y_got = swap(done(y_sum[:, rows:].astype(bf16)), "own")
    grads.append(finish(1, middle[1], outward[1]))

    up_sum = jnp.sum(step(up_got).astype(f32), axis=0)
    own_ranks = cut(ranks, 2 * z, 2, 0).astype(f32)
    up_sum = done(((16.0 / own_ranks)[:, None, None] * up_sum).astype(bf16))
    up_mine = cut(up_sum, x, 1, 0)
    up_theirs = swap(cut(up_sum, 1 - x, 1, 0), "own")

    def in_place(here, there, axis):
        blocks = jnp.concatenate(here + there, axis=axis)
        size = blocks.shape[axis] // 4
        return jnp.concatenate(
            [
                cut(blocks, (2 * ((i + x) % 2) + (j + y) % 2) * size, size, axis)
                for i in (0, 1)
                for j in (0, 1)
            ],
            axis=axis,
        )

    input_grad = done(in_place([step(dx_mine), dx_other], [dx_mine_got, dx_other_got], 1))
    y_sum = y_sum[:, :rows] + step(y_got).astype(f32)
    projected = done(join(y_sum[0], y_sum[1]).astype(bf16))
    second = step(grads[1][1])
    down_gradient = done(in_place([grads[0][0], grads[1][0]], [grad_got, second], 0)[None])
    up_theirs = step(up_theirs)
    up_gradient = jnp.where(
        x == 0,
        jnp.concatenate([up_mine, up_theirs], axis=2),
        jnp.concatenate([up_theirs, up_mine], axis=2),
    )
    return (projected, input_grad, down_gradient, up_gradient)


def body_routed(
    tokens,
    cotangent,
    frozen_value_weight,
    adapter_down_weight,
    adapter_up_weight,
    token_adapter,
    rank_step_count,
):
    rows, width_halved = tokens.shape
    half_kv = cotangent.shape[1]
    owning_adapters = lax.axis_size(("fsdp", "own"))
    greatest_rank = 3 * rows // (2 * owning_adapters)
    ids = token_adapter[:, 0]
    table = (ids[:, None] == jnp.arange(owning_adapters, dtype=jnp.int32)[None, :]).astype(
        f32
    )
    order = jnp.arange(rows, dtype=jnp.int32)
    earlier = (order[:, None] > order[None, :]).astype(f32)
    before = jnp.dot(earlier, table, precision=lax.Precision.HIGHEST)
    place = jnp.sum(before * table, axis=1).astype(jnp.int32)
    slot = ids * greatest_rank + place
    source_rows = jnp.full((owning_adapters * greatest_rank,), rows, jnp.int32).at[slot].set(order)
    padded_x = jnp.concatenate([tokens, jnp.zeros((1, width_halved), bf16)], axis=0)
    padded_dy = jnp.concatenate([cotangent, jnp.zeros((1, half_kv), bf16)], axis=0)
    send_x = jnp.take(padded_x, source_rows, axis=0)
    send_dy = jnp.take(padded_dy, source_rows, axis=0)
    recv_x, recv_dy = (
        lax.all_to_all(
            send_x.reshape(owning_adapters, greatest_rank, width_halved),
            ("fsdp", "own"),
            split_axis=0,
            concat_axis=0,
            tiled=True,
        ),
        lax.all_to_all(
            send_dy.reshape(owning_adapters, greatest_rank, half_kv),
            ("fsdp", "own"),
            split_axis=0,
            concat_axis=0,
            tiled=True,
        ),
    )
    flat_x = recv_x.reshape(owning_adapters * greatest_rank, width_halved)
    flat_dy = recv_dy.reshape(owning_adapters * greatest_rank, half_kv)
    dy_full = lax.all_gather(cotangent, "tp", axis=1, tiled=True)
    whole = lax.all_gather(frozen_value_weight, "fsdp", axis=1, tiled=True)
    partial_y = jnp.dot(tokens, whole, preferred_element_type=f32)
    base_dx = contract_final_axis(dy_full, whole)
    base_y = lax.psum_scatter(partial_y, "tp", scatter_dimension=1, tiled=True)
    down_matrix = adapter_down_weight[0]
    up_matrix = adapter_up_weight[0]
    part_low = jnp.dot(flat_x, down_matrix, preferred_element_type=f32)
    part_back = contract_final_axis(flat_dy, up_matrix)
    low_sum, back_sum = lax.psum((part_low, part_back), "tp")
    width_rank = down_matrix.shape[1]
    rank = width_rank // 8 * rank_step_count[lax.axis_index(("fsdp", "own"))]
    keep = jnp.arange(width_rank, dtype=jnp.int32)[None, :] < rank
    scale = 16.0 / rank.astype(f32)
    low = jnp.where(keep, low_sum, 0.0).astype(bf16)
    backward_pass = (scale * jnp.where(keep, back_sum, 0.0)).astype(bf16)
    delta = (scale * jnp.dot(low, up_matrix, preferred_element_type=f32)).astype(
        bf16
    )
    adapter_input_gradient = contract_final_axis(backward_pass, down_matrix).astype(bf16)
    down_gradient = contract_first(flat_x, backward_pass).astype(bf16)[None]
    up_gradient = (scale * contract_first(low, flat_dy)).astype(bf16)[None]
    home_delta, home_dx = (
        lax.all_to_all(
            delta.reshape(owning_adapters, greatest_rank, half_kv),
            ("fsdp", "own"),
            split_axis=0,
            concat_axis=0,
            tiled=True,
        ),
        lax.all_to_all(
            adapter_input_gradient.reshape(owning_adapters, greatest_rank, width_halved),
            ("fsdp", "own"),
            split_axis=0,
            concat_axis=0,
            tiled=True,
        ),
    )
    adapter_delta_rows = jnp.take(
        home_delta.reshape(owning_adapters * greatest_rank, half_kv), slot, axis=0
    )
    input_gradient_rows = jnp.take(
        home_dx.reshape(owning_adapters * greatest_rank, width_halved), slot, axis=0
    )
    projected = (base_y + adapter_delta_rows.astype(f32)).astype(bf16)
    input_grad = (base_dx + input_gradient_rows.astype(f32)).astype(bf16)
    return (projected, input_grad, down_gradient, up_gradient)


def solution(mesh):
    placed = (
        P(("rep", "fsdp", "own"), "tp"),
        P(("rep", "fsdp", "own"), "tp"),
        P("tp", "fsdp"),
        P(("fsdp", "own"), "tp", None),
        P(("fsdp", "own"), None, "tp"),
        P(("rep", "fsdp", "own"), None),
        P(),
    )
    line = mesh.shape["fsdp"] == 4 and mesh.shape["own"] == 2 and mesh.shape["rep"] == 2
    return jax.shard_map(
        body_line if line else body_routed,
        mesh=mesh,
        in_specs=placed,
        out_specs=(
            P(("rep", "fsdp", "own"), "tp"),
            P(("rep", "fsdp", "own"), "tp"),
            P(("rep", "fsdp", "own"), "tp", None),
            P(("rep", "fsdp", "own"), None, "tp"),
        ),
        check_vma=False,
    )
```

```python
import jax
import jax.numpy as jnp
from jax import lax
from jax.experimental import pallas as pl
from jax.experimental.pallas import tpu as pltpu
from jax.sharding import PartitionSpec as P

bf16 = jnp.bfloat16
f32 = jnp.float32


def contract_first(left, right):
    return lax.dot_general(
        left, right, (((0,), (0,)), ((), ())), preferred_element_type=f32
    )


def contract_final_axis(left, right):
    return lax.dot_general(
        left, right, (((1,), (1,)), ((), ())), preferred_element_type=f32
    )


def matmul(left, right):
    return jnp.dot(left, right, preferred_element_type=f32)


PAIR = [(0, 1), (1, 0)]
NEIGHBOURS = [(0, 1), (1, 0), (2, 3), (3, 2)]
MIDDLE = [(1, 2), (2, 1)]
OUTWARD = [(1, 0), (2, 3)]
INWARD = [(0, 1), (3, 2)]


def swap(value, axis):
    return lax.ppermute(value, axis, PAIR)


def along(value, pairs):
    return lax.ppermute(value, "fsdp", pairs)


def kernel_call(body, outs, *operands, scalars=None, scratch=(), space=pltpu.VMEM):
    specs = [pl.BlockSpec(memory_space=space)] * len(operands)
    if scalars is not None:
        operands = (scalars, *operands)
        specs = [pl.BlockSpec(memory_space=pltpu.SMEM), *specs]
    return pl.pallas_call(
        body,
        out_shape=list(outs),
        in_specs=specs,
        out_specs=[pl.BlockSpec(memory_space=space)] * len(outs),
        scratch_shapes=list(scratch),
        compiler_params=pltpu.CompilerParams(vmem_limit_bytes=28 * 2**20),
        cost_estimate=pl.CostEstimate(flops=0, bytes_accessed=0, transcendentals=0),
    )(*operands)


def copy_call(plan, outs, scalars, *operands):
    count = len(plan(None, [None] * len(operands), [None] * len(outs)))

    def body(numbers, *refs):
        sems = refs[-1]
        pairs = plan(numbers, refs[: len(operands)], refs[len(operands) : -1])
        copies = [pltpu.make_async_copy(a, b, sems.at[i]) for i, (a, b) in enumerate(pairs)]
        for copy in copies:
            copy.start()
        for copy in copies:
            copy.wait()

    return kernel_call(
        body,
        outs,
        *operands,
        scalars=scalars,
        scratch=[pltpu.SemaphoreType.DMA((count,))],
        space=pl.ANY,
    )


def view(ref, *spans):
    if ref is None:
        return None
    index = tuple(
        pl.ds(start if isinstance(start, int) else pl.multiple_of(start, 128), size)
        for start, size in spans
    )
    return ref.at[index]


def at(numbers, i):
    return None if numbers is None else numbers[i]


def ranks_of(ranks, ids):
    total = jnp.zeros(ids.shape, f32)
    for a in range(ranks.shape[0]):
        total = jnp.where(ids == a, ranks[a].astype(f32), total)
    return total


def kept(ids, ranks, value):
    rank = ranks_of(ranks, ids)
    column = lax.broadcasted_iota(jnp.int32, value.shape, 1).astype(f32)
    return jnp.where(column < rank, value, 0.0), 16.0 / rank


def roll_rows(value):
    half = value.shape[0] // 2
    return jnp.concatenate([value[half:], value[:half]], axis=0)


def back_kernel(ids, dy, up, out):
    size = out.shape[1]
    token = ids[...].astype(f32)
    for i in range(0, up.shape[0] // size, 2):
        both = contract_final_axis(dy[...], up[i * size : (i + 2) * size, :])
        for j in (0, 1):
            part = jnp.where(token == i + j, both[:, j * size : (j + 1) * size], 0.0)
            out[...] = part if i + j == 0 else out[...] + part


def spread_into(out, token, value, order):
    size = value.shape[1]
    for i in range(out.shape[1] // size):
        a = order[i].astype(f32)
        out[:, i * size : (i + 1) * size] = jnp.where(token == a, value, 0.0).astype(bf16)


def back_end_kernel(numbers, ids, part, got, wide, sent):
    token = ids[...].astype(f32)
    count = numbers.shape[0] // 2
    ranks, order = [numbers[i] for i in range(count)], [numbers[count + i] for i in range(count)]
    value, scale = kept(token, jnp.stack(ranks), part[...] + roll_rows(got[...]))
    value = (scale * value).astype(bf16)
    size = value.shape[1]
    sent[:, :size] = value
    sent[:, size:] = ids[...]
    spread_into(wide, token, value.astype(f32), order)


def spread_in_kernel(numbers, packet, wide):
    size = packet.shape[1] // 2
    count = numbers.shape[0] // 2
    order = [numbers[count + i] for i in range(count)]
    spread_into(wide, packet[:, size:].astype(f32), packet[:, :size].astype(f32), order)


def low_kernel(numbers, ids, x_mine, x_other, own, near, far, own_near_other, far_other, out):
    size = out.shape[1]
    wide = 2 * size
    token = ids[...].astype(f32)
    mine = [own[...], near[...], far[:, :wide], far[:, wide:]]
    other = [
        own_near_other[:, :wide],
        own_near_other[:, wide:],
        far_other[:, :wide],
        far_other[:, wide:],
    ]
    for i in range(4):
        both = matmul(x_mine[...], mine[i]) + matmul(x_other[...], other[i])
        for j in (0, 1):
            place = numbers[numbers.shape[0] // 2 + 2 * i + j].astype(f32)
            part = jnp.where(token == place, both[:, j * size : (j + 1) * size], 0.0)
            out[...] = part if i + j == 0 else out[...] + part


def low_end_kernel(numbers, ids, part, got, up, wide, delta):
    token = ids[...].astype(f32)
    count = numbers.shape[0] // 2
    ranks = jnp.stack([numbers[i] for i in range(count)])
    value, scale = kept(token, ranks, part[...] + roll_rows(got[...]))
    value = value.astype(bf16).astype(f32)
    spread_into(wide, token, value, [jnp.int32(i) for i in range(count)])
    delta[...] = (scale[:, :1] * matmul(wide[...], up[...])).astype(bf16)


def dx_kernel(dy, back, own, near, far, *rest):
    *adapter, here, there = rest
    rows, width = here.shape
    cols = own.shape[1]
    tile = min(cols, width)
    for t in range(width // tile):
        span = slice(t * tile, (t + 1) * tile)
        base = contract_final_axis(dy[:, :cols], own[span, :])
        base += contract_final_axis(dy[:, cols : 2 * cols], near[span, :])
        base += contract_final_axis(dy[:, 2 * cols :], far[span, :])
        lora, start = 0.0, 0
        for piece in adapter:
            stop = start + piece.shape[1]
            lora += contract_final_axis(back[:, start:stop], piece[span, :])
            start = stop
        total = (base + lora.astype(bf16).astype(f32)).astype(bf16)
        here[:, span] = total[:rows]
        there[:, span] = total[rows:]


def y_kernel(flags, tokens, own, near, far, *rest):
    *before, keep, send = rest
    cols = own.shape[1]

    def store(pair, first, part):
        mine = flags[0] == (1 if pair else 0)
        for i in (0, 1):
            place = (first + i) % 2
            block = matmul(tokens[...], part(i))

            @pl.when(mine)
            def _():
                keep[place] = block + before[0][place] if before else block

            @pl.when(jnp.logical_not(mine))
            def _():
                send[place] = block + before[1][place] if before else block

    store(True, flags[1], lambda i: (own, near)[i][...])
    store(False, flags[2], lambda i: far[:, i * cols : (i + 1) * cols])


def y_sum_kernel(flags, keep, got, delta, here, there):
    rows = here.shape[1]
    for i in (0, 1):
        added = jnp.where(flags[3] == i, delta[...].astype(f32), 0.0)
        total = keep[i] + got[i] + added
        here[i] = total[:rows]
        there[i] = total[rows:].astype(bf16)


def y_end_kernel(here, got, out):
    cols = here.shape[2]
    for i in (0, 1):
        out[:, i * cols : (i + 1) * cols] = (here[i] + got[i].astype(f32)).astype(bf16)


def body_line(
    tokens,
    cotangent,
    frozen_value_weight,
    adapter_down_weight,
    adapter_up_weight,
    token_adapter,
    rank_step_count,
):
    rows, width = tokens.shape
    kv = cotangent.shape[1]
    cols = frozen_value_weight.shape[1]
    down = adapter_down_weight[0]
    up = adapter_up_weight[0]
    size = down.shape[1]
    wide = 2 * size
    quarter = width // 2
    eighth = quarter // 2
    kvq = kv // 2
    both = 2 * rows
    z, x = lax.axis_index("fsdp"), lax.axis_index("own")
    y, c = lax.axis_index("rep"), lax.axis_index("tp")
    first_pair = z < 2
    is_middle = (z == 1) | (z == 2)
    line = [z, z + 1 - 2 * (z % 2), jnp.where(first_pair, 2, 1), jnp.where(first_pair, 3, 0)]
    adapters = jnp.stack([2 * t + o for t in line for o in (x, 1 - x)]).astype(jnp.int32)
    number = adapters.shape[0]
    starts = jnp.stack(
        [side * quarter + half * eighth for side in (x, 1 - x) for half in (y, 1 - y)]
    ).astype(jnp.int32)
    ranks = size // 8 * rank_step_count
    numbers = jnp.concatenate([ranks, adapters])
    flags = jnp.stack([(c == 0) == first_pair, z % 2 == 1, z >= 2, x == 1]).astype(jnp.int32)

    latest = []

    def step(*values):
        if latest:
            values = lax.optimization_barrier((*values, latest[0]))[: len(values)]
        return values[0] if len(values) == 1 else values

    def done(value):
        latest[:] = [value]
        return value

    def like(*shape, kind=bf16):
        return jax.ShapeDtypeStruct(shape, kind)

    def cut(value, start, length, axis):
        return lax.dynamic_slice_in_dim(value, start, length, axis)

    def join(*values):
        return jnp.concatenate(values, axis=1)

    def rows_at(i, value, length):
        out = like(length, value.shape[1])
        return copy_call(
            lambda n, a, o: [(view(a[0], (at(n, i), length), (0, value.shape[1])), o[0])],
            [out],
            starts,
            value,
        )[0]

    def columns_at(i, value):
        out = like(value.shape[0], eighth)
        return copy_call(
            lambda n, a, o: [(view(a[0], (0, value.shape[0]), (at(n, i), eighth)), o[0])],
            [out],
            starts,
            value,
        )[0]

    def side_by_side(*values):
        widths = [v.shape[1] for v in values]
        length = values[0].shape[0]
        return copy_call(
            lambda n, a, o: [
                (a[i], view(o[0], (0, length), (sum(widths[:i]), widths[i])))
                for i in range(len(values))
            ],
            [like(length, sum(widths))],
            starts,
            *values,
        )[0]

    def tokens_of(i, value, got):
        return copy_call(
            lambda n, a, o: [
                (view(a[0], (0, rows), (at(n, i), eighth)), view(o[0], (0, rows), (0, eighth))),
                (a[1], view(o[0], (rows, rows), (0, eighth))),
            ],
            [like(both, eighth)],
            starts,
            value,
            got,
        )[0]

    down_got = swap(done(rows_at(2, down, eighth)), "own")
    ids_here = jnp.broadcast_to(token_adapter.astype(bf16), (rows, size))
    packet = swap(done(join(step(cotangent), ids_here)), "own")
    x_got = [swap(done(columns_at(2, step(tokens))), "own")]
    x_got.append(swap(done(columns_at(3, step(tokens))), "own"))
    down_piece = done(
        copy_call(
            lambda n, a, o: [
                (view(a[0], (at(n, 0), eighth), (0, size)), view(o[0], (0, eighth), (0, size))),
                (a[1], view(o[0], (0, eighth), (size, size))),
            ],
            [like(eighth, wide)],
            starts,
            down,
            step(down_got),
        )[0]
    )
    down_near = along(down_piece, NEIGHBOURS)
    up_sent = jnp.broadcast_to(
        step(up).reshape(size, 2, kvq).transpose(1, 0, 2)[None], (4, 2, size, kvq)
    ).reshape(number, size, kvq)
    up_all = lax.all_to_all(
        done(up_sent), ("fsdp", "own"), split_axis=0, concat_axis=0, tiled=True
    ).reshape(number * size, kvq)
    weight_here = done(rows_at(0, step(frozen_value_weight), eighth))
    weight_near = along(weight_here, NEIGHBOURS)

    packet = step(packet)
    dy_half = jnp.concatenate([cotangent, packet[:, :kv]], axis=0)
    ids = jnp.concatenate([ids_here, packet[:, kv:]], axis=0)
    dy_quarter = cut(dy_half, x * kvq, kvq, 1)
    dy_tp = swap(done(dy_half), "tp")

    down_near = step(down_near)
    crossing = done(side_by_side(down_piece, down_near))
    down_crossed = along(crossing, MIDDLE)
    down_other = swap(crossing, "rep")

    compact = like(both, size, kind=f32)
    up_all, dy_quarter = step(up_all, dy_quarter)
    back_part = done(kernel_call(back_kernel, [compact], ids, dy_quarter, up_all)[0])
    back_tp = swap(back_part, "tp")
    x_mine = done(tokens_of(0, tokens, step(x_got[0])))
    back_part = done(back_part + step(back_tp))
    back_got = swap(back_part, "own")
    x_in = [along(x_mine, INWARD)]
    weight_near = step(weight_near)
    crossing = done(side_by_side(weight_here, weight_near))
    weight_crossed = along(crossing, MIDDLE)
    weight_near_other = swap(weight_near, "rep")
    back_wide, back_sent = kernel_call(
        back_end_kernel,
        [like(both, number * size), like(both, wide)],
        ids,
        back_part,
        step(back_got),
        scalars=numbers,
    )
    back_in = along(done(back_sent), INWARD)
    x_other = done(tokens_of(1, tokens, step(x_got[1])))
    x_in.append(along(x_other, INWARD))
    x_both = [x_mine, x_other]

    dy_tp = step(dy_tp)
    dy_full = jnp.where(c == 0, join(dy_half, dy_tp), join(dy_tp, dy_half))
    dy_line = done(join(*[cut(dy_full, t * cols, cols, 1) for t in line]))
    weight_other = done(rows_at(1, step(frozen_value_weight), eighth))

    def total(half, first, last):
        return contract_first(x_both[half], back_wide[:, first * wide : last * wide])

    def total_in(half, first, last):
        return contract_first(x_in[half], back_in_wide[:, first * wide : last * wide])

    def to_middle(half, *others):
        x_in[half], *_ = step(x_in[half], back_in_wide, *others)
        sums = total(half, 2, 4) + total_in(half, 2, 4)
        return along(done(sums.astype(bf16)), MIDDLE)

    def to_end(half, crossed):
        crossed = step(crossed)
        sums = total(half, 1, 2) + crossed[:, wide:].astype(f32)
        return along(done(sums.astype(bf16)), OUTWARD)

    def finish(half, crossed, outer, *others):
        outer, *_ = step(outer, x_mine, *others)
        grad = total(half, 0, 1) + total_in(half, 0, 1)
        grad = (grad + crossed[:, :wide].astype(f32) + outer.astype(f32)).astype(bf16)
        here, there = grad[:, :size], grad[:, size:]
        done(here)
        return here, swap(there, "own")

    down_crossed, back_in, down_other = step(down_crossed, back_in, down_other)
    down_outer = along(down_crossed, OUTWARD)
    back_in_wide = done(
        kernel_call(
            spread_in_kernel, [like(both, number * size)], back_in, scalars=numbers
        )[0]
    )
    middle = [to_middle(0)]
    weight_crossed, weight_near_other = step(weight_crossed, weight_near_other)
    weight_outer = along(weight_crossed, OUTWARD)
    down_outer = step(down_outer)
    down_far = done(jnp.where(is_middle, down_crossed, down_outer))
    down_far_other = swap(down_far, "rep")
    middle.append(to_middle(1))
    outward = [to_end(0, middle[0])]
    weight_outer = step(weight_outer)
    weight_far = done(jnp.where(is_middle, weight_crossed, weight_outer))
    weight_far_other = swap(weight_far, "rep")

    low_part = done(
        kernel_call(
            low_kernel,
            [compact],
            ids,
            x_mine,
            x_other,
            down_piece,
            down_near,
            down_far,
            down_other,
            step(down_far_other),
            scalars=numbers,
        )[0]
    )
    low_tp = swap(low_part, "tp")
    half_grad = [like(rows, eighth)] * 2
    dx_mine, dx_sent = kernel_call(
        dx_kernel,
        half_grad,
        step(dy_line),
        back_wide,
        weight_here,
        weight_near,
        weight_far,
        down_piece,
        down_near,
        down_far,
    )
    done(dx_mine)
    low_part = done(low_part + step(low_tp))
    low_got = swap(low_part, "own")
    dx_mine_got = swap(dx_sent, "own")
    grads = [finish(0, middle[0], outward[0])]
    blocks = [like(2, both, cols, kind=f32)] * 2
    y_first = kernel_call(
        y_kernel, blocks, step(x_mine), weight_here, weight_near, weight_far, scalars=flags
    )
    done(y_first[0])
    low_wide, delta = kernel_call(
        low_end_kernel,
        [like(both, number * size), like(both, kvq)],
        ids,
        low_part,
        step(low_got),
        up_all,
        scalars=numbers,
    )
    up_part = done(contract_first(low_wide, dy_quarter).astype(bf16))
    up_got = lax.all_to_all(
        up_part.reshape(4, 2, size, kvq), "fsdp", split_axis=0, concat_axis=0, tiled=True
    )
    outward.append(to_end(1, middle[1]))

    weight_far_other, dx_mine_got = step(weight_far_other, dx_mine_got)
    y_keep, y_sent = kernel_call(
        y_kernel,
        blocks,
        x_other,
        weight_other,
        weight_near_other,
        weight_far_other,
        *y_first,
        scalars=flags,
    )
    y_got = swap(done(y_sent), "tp")
    dx_other, dx_sent = kernel_call(
        dx_kernel,
        half_grad,
        step(dy_line),
        back_wide,
        weight_other,
        weight_near_other,
        weight_far_other,
        down_other,
        down_far_other,
    )
    dx_other_got = swap(done(dx_sent), "own")
    y_here, y_sent = kernel_call(
        y_sum_kernel,
        [like(2, rows, cols, kind=f32), like(2, rows, cols)],
        y_keep,
        step(y_got),
        delta,
        scalars=flags,
    )
    y_got = swap(done(y_sent), "own")
    grads.append(finish(1, middle[1], outward[1], grads[0][1]))

    up_sum = jnp.sum(step(up_got).astype(f32), axis=0)
    own_ranks = cut(ranks, 2 * z, 2, 0).astype(f32)
    up_sum = done(((16.0 / own_ranks)[:, None, None] * up_sum).astype(bf16))
    up_mine = cut(up_sum, x, 1, 0)
    up_theirs = swap(cut(up_sum, 1 - x, 1, 0), "own")

    def in_place(axis, out, *pieces):
        def plan(n, a, o):
            spans = [[(0, length) for length in out.shape] for _ in range(4)]
            for i in range(4):
                spans[i][axis] = (at(n, i), eighth)
            return [(a[i], view(o[0], *spans[i])) for i in range(4)]

        return copy_call(plan, [out], starts, *pieces)[0]

    dx_other_got, _ = step(dx_other_got, dx_mine)
    input_grad = done(
        in_place(1, like(rows, width), dx_mine, dx_other, dx_mine_got, dx_other_got)
    )
    projected = done(kernel_call(y_end_kernel, [like(rows, kv)], y_here, step(y_got))[0])
    down_gradient = done(
        in_place(
            0, like(width, size), grads[0][0], grads[1][0], grads[0][1], step(grads[1][1])
        )[None]
    )
    up_theirs = step(up_theirs)
    up_gradient = jnp.where(
        x == 0,
        jnp.concatenate([up_mine, up_theirs], axis=2),
        jnp.concatenate([up_theirs, up_mine], axis=2),
    )
    return (projected, input_grad, down_gradient, up_gradient)


def body_routed(
    tokens,
    cotangent,
    frozen_value_weight,
    adapter_down_weight,
    adapter_up_weight,
    token_adapter,
    rank_step_count,
):
    rows, width_halved = tokens.shape
    half_kv = cotangent.shape[1]
    owning_adapters = lax.axis_size(("fsdp", "own"))
    greatest_rank = 3 * rows // (2 * owning_adapters)
    ids = token_adapter[:, 0]
    table = (ids[:, None] == jnp.arange(owning_adapters, dtype=jnp.int32)[None, :]).astype(
        f32
    )
    order = jnp.arange(rows, dtype=jnp.int32)
    earlier = (order[:, None] > order[None, :]).astype(f32)
    before = jnp.dot(earlier, table, precision=lax.Precision.HIGHEST)
    place = jnp.sum(before * table, axis=1).astype(jnp.int32)
    slot = ids * greatest_rank + place
    source_rows = jnp.full((owning_adapters * greatest_rank,), rows, jnp.int32).at[slot].set(order)
    padded_x = jnp.concatenate([tokens, jnp.zeros((1, width_halved), bf16)], axis=0)
    padded_dy = jnp.concatenate([cotangent, jnp.zeros((1, half_kv), bf16)], axis=0)
    send_x = jnp.take(padded_x, source_rows, axis=0)
    send_dy = jnp.take(padded_dy, source_rows, axis=0)
    recv_x, recv_dy = (
        lax.all_to_all(
            send_x.reshape(owning_adapters, greatest_rank, width_halved),
            ("fsdp", "own"),
            split_axis=0,
            concat_axis=0,
            tiled=True,
        ),
        lax.all_to_all(
            send_dy.reshape(owning_adapters, greatest_rank, half_kv),
            ("fsdp", "own"),
            split_axis=0,
            concat_axis=0,
            tiled=True,
        ),
    )
    flat_x = recv_x.reshape(owning_adapters * greatest_rank, width_halved)
    flat_dy = recv_dy.reshape(owning_adapters * greatest_rank, half_kv)
    dy_full = lax.all_gather(cotangent, "tp", axis=1, tiled=True)
    whole = lax.all_gather(frozen_value_weight, "fsdp", axis=1, tiled=True)
    partial_y = jnp.dot(tokens, whole, preferred_element_type=f32)
    base_dx = contract_final_axis(dy_full, whole)
    base_y = lax.psum_scatter(partial_y, "tp", scatter_dimension=1, tiled=True)
    down_matrix = adapter_down_weight[0]
    up_matrix = adapter_up_weight[0]
    part_low = jnp.dot(flat_x, down_matrix, preferred_element_type=f32)
    part_back = contract_final_axis(flat_dy, up_matrix)
    low_sum, back_sum = lax.psum((part_low, part_back), "tp")
    width_rank = down_matrix.shape[1]
    rank = width_rank // 8 * rank_step_count[lax.axis_index(("fsdp", "own"))]
    keep = jnp.arange(width_rank, dtype=jnp.int32)[None, :] < rank
    scale = 16.0 / rank.astype(f32)
    low = jnp.where(keep, low_sum, 0.0).astype(bf16)
    backward_pass = (scale * jnp.where(keep, back_sum, 0.0)).astype(bf16)
    delta = (scale * jnp.dot(low, up_matrix, preferred_element_type=f32)).astype(
        bf16
    )
    adapter_input_gradient = contract_final_axis(backward_pass, down_matrix).astype(bf16)
    down_gradient = contract_first(flat_x, backward_pass).astype(bf16)[None]
    up_gradient = (scale * contract_first(low, flat_dy)).astype(bf16)[None]
    home_delta, home_dx = (
        lax.all_to_all(
            delta.reshape(owning_adapters, greatest_rank, half_kv),
            ("fsdp", "own"),
            split_axis=0,
            concat_axis=0,
            tiled=True,
        ),
        lax.all_to_all(
            adapter_input_gradient.reshape(owning_adapters, greatest_rank, width_halved),
            ("fsdp", "own"),
            split_axis=0,
            concat_axis=0,
            tiled=True,
        ),
    )
    adapter_delta_rows = jnp.take(
        home_delta.reshape(owning_adapters * greatest_rank, half_kv), slot, axis=0
    )
    input_gradient_rows = jnp.take(
        home_dx.reshape(owning_adapters * greatest_rank, width_halved), slot, axis=0
    )
    projected = (base_y + adapter_delta_rows.astype(f32)).astype(bf16)
    input_grad = (base_dx + input_gradient_rows.astype(f32)).astype(bf16)
    return (projected, input_grad, down_gradient, up_gradient)


def solution(mesh):
    placed = (
        P(("rep", "fsdp", "own"), "tp"),
        P(("rep", "fsdp", "own"), "tp"),
        P("tp", "fsdp"),
        P(("fsdp", "own"), "tp", None),
        P(("fsdp", "own"), None, "tp"),
        P(("rep", "fsdp", "own"), None),
        P(),
    )
    line = mesh.shape["fsdp"] == 4 and mesh.shape["own"] == 2 and mesh.shape["rep"] == 2
    return jax.shard_map(
        body_line if line else body_routed,
        mesh=mesh,
        in_specs=placed,
        out_specs=(
            P(("rep", "fsdp", "own"), "tp"),
            P(("rep", "fsdp", "own"), "tp"),
            P(("rep", "fsdp", "own"), "tp", None),
            P(("rep", "fsdp", "own"), None, "tp"),
        ),
        check_vma=False,
    )
```

```python
import jax
import jax.numpy as jnp
from jax import lax
from jax.experimental import pallas as pl
from jax.experimental.pallas import tpu as pltpu
from jax.sharding import PartitionSpec as P

bf16 = jnp.bfloat16
f32 = jnp.float32


def contract_first(left, right):
    return lax.dot_general(
        left, right, (((0,), (0,)), ((), ())), preferred_element_type=f32
    )


def contract_final_axis(left, right):
    return lax.dot_general(
        left, right, (((1,), (1,)), ((), ())), preferred_element_type=f32
    )


def matmul(left, right):
    return jnp.dot(left, right, preferred_element_type=f32)


PAIR = [(0, 1), (1, 0)]
NEIGHBOURS = [(0, 1), (1, 0), (2, 3), (3, 2)]
MIDDLE = [(1, 2), (2, 1)]
OUTWARD = [(1, 0), (2, 3)]
INWARD = [(0, 1), (3, 2)]


def swap(value, axis):
    return lax.ppermute(value, axis, PAIR)


def along(value, pairs):
    return lax.ppermute(value, "fsdp", pairs)


def kernel_call(body, outs, *operands, scalars=None, scratch=(), space=pltpu.VMEM):
    specs = [pl.BlockSpec(memory_space=space)] * len(operands)
    if scalars is not None:
        operands = (scalars, *operands)
        specs = [pl.BlockSpec(memory_space=pltpu.SMEM), *specs]
    return pl.pallas_call(
        body,
        out_shape=list(outs),
        in_specs=specs,
        out_specs=[pl.BlockSpec(memory_space=pltpu.VMEM)] * len(outs),
        scratch_shapes=list(scratch),
        compiler_params=pltpu.CompilerParams(vmem_limit_bytes=28 * 2**20),
        cost_estimate=pl.CostEstimate(flops=0, bytes_accessed=0, transcendentals=0),
    )(*operands)


def copy_call(plan, outs, scalars, *operands):
    count = len(plan(None, [None] * len(operands), [None] * len(outs)))

    def body(numbers, *refs):
        sems = refs[-1]
        pairs = plan(numbers, refs[: len(operands)], refs[len(operands) : -1])
        copies = [pltpu.make_async_copy(a, b, sems.at[i]) for i, (a, b) in enumerate(pairs)]
        for copy in copies:
            copy.start()
        for copy in copies:
            copy.wait()

    return kernel_call(
        body,
        outs,
        *operands,
        scalars=scalars,
        scratch=[pltpu.SemaphoreType.DMA((count,))],
        space=pl.ANY,
    )


def view(ref, *spans):
    if ref is None:
        return None
    index = tuple(
        pl.ds(start if isinstance(start, int) else pl.multiple_of(start, 128), size)
        for start, size in spans
    )
    return ref.at[index]


def at(numbers, i):
    return None if numbers is None else numbers[i]


def ranks_of(ranks, ids):
    total = jnp.zeros(ids.shape, f32)
    for a in range(ranks.shape[0]):
        total = jnp.where(ids == a, ranks[a].astype(f32), total)
    return total


def kept(ids, ranks, value):
    rank = ranks_of(ranks, ids)
    column = lax.broadcasted_iota(jnp.int32, value.shape, 1).astype(f32)
    return jnp.where(column < rank, value, 0.0), 16.0 / rank


def roll_rows(value):
    half = value.shape[0] // 2
    return jnp.concatenate([value[half:], value[:half]], axis=0)


def back_kernel(ids, dy, up, out):
    size = out.shape[1]
    token = ids[...].astype(f32)
    for i in range(0, up.shape[0] // size, 2):
        both = contract_final_axis(dy[...], up[i * size : (i + 2) * size, :])
        for j in (0, 1):
            part = jnp.where(token == i + j, both[:, j * size : (j + 1) * size], 0.0)
            out[...] = part if i + j == 0 else out[...] + part


def spread_into(out, token, value, order):
    size = value.shape[1]
    for i in range(out.shape[1] // size):
        a = order[i].astype(f32)
        out[:, i * size : (i + 1) * size] = jnp.where(token == a, value, 0.0).astype(bf16)


def back_end_kernel(numbers, ids, part, got, wide, sent):
    token = ids[...].astype(f32)
    count = numbers.shape[0] // 2
    ranks, order = [numbers[i] for i in range(count)], [numbers[count + i] for i in range(count)]
    value, scale = kept(token, jnp.stack(ranks), part[...] + roll_rows(got[...]))
    value = (scale * value).astype(bf16)
    size = value.shape[1]
    sent[:, :size] = value
    sent[:, size:] = ids[...]
    spread_into(wide, token, value.astype(f32), order)


def spread_in_kernel(numbers, packet, wide):
    size = packet.shape[1] // 2
    count = numbers.shape[0] // 2
    order = [numbers[count + i] for i in range(count)]
    spread_into(wide, packet[:, size:].astype(f32), packet[:, :size].astype(f32), order)


def low_kernel(numbers, ids, x_mine, x_other, own, near, far, own_near_other, far_other, out):
    size = out.shape[1]
    wide = 2 * size
    token = ids[...].astype(f32)
    mine = [own[...], near[...], far[:, :wide], far[:, wide:]]
    other = [
        own_near_other[:, :wide],
        own_near_other[:, wide:],
        far_other[:, :wide],
        far_other[:, wide:],
    ]
    for i in range(4):
        both = matmul(x_mine[...], mine[i]) + matmul(x_other[...], other[i])
        for j in (0, 1):
            place = numbers[numbers.shape[0] // 2 + 2 * i + j].astype(f32)
            part = jnp.where(token == place, both[:, j * size : (j + 1) * size], 0.0)
            out[...] = part if i + j == 0 else out[...] + part


def low_end_kernel(numbers, ids, part, got, up, wide, delta):
    token = ids[...].astype(f32)
    count = numbers.shape[0] // 2
    ranks = jnp.stack([numbers[i] for i in range(count)])
    value, scale = kept(token, ranks, part[...] + roll_rows(got[...]))
    value = value.astype(bf16).astype(f32)
    spread_into(wide, token, value, [jnp.int32(i) for i in range(count)])
    delta[...] = (scale[:, :1] * matmul(wide[...], up[...])).astype(bf16)


def dx_kernel(dy, back, own, near, far, *rest):
    *adapter, here, there = rest
    rows, width = here.shape
    cols = own.shape[1]
    tile = min(cols, width)
    for t in range(width // tile):
        span = slice(t * tile, (t + 1) * tile)
        base = contract_final_axis(dy[:, :cols], own[span, :])
        base += contract_final_axis(dy[:, cols : 2 * cols], near[span, :])
        base += contract_final_axis(dy[:, 2 * cols :], far[span, :])
        lora, start = 0.0, 0
        for piece in adapter:
            stop = start + piece.shape[1]
            lora += contract_final_axis(back[:, start:stop], piece[span, :])
            start = stop
        total = (base + lora.astype(bf16).astype(f32)).astype(bf16)
        here[:, span] = total[:rows]
        there[:, span] = total[rows:]


def y_kernel(flags, tokens, own, near, far, *rest):
    *before, keep, send = rest
    cols = own.shape[1]

    def store(pair, first, part):
        mine = flags[0] == (1 if pair else 0)
        for i in (0, 1):
            place = (first + i) % 2
            block = matmul(tokens[...], part(i))

            @pl.when(mine)
            def _():
                keep[place] = block + before[0][place] if before else block

            @pl.when(jnp.logical_not(mine))
            def _():
                send[place] = block + before[1][place] if before else block

    store(True, flags[1], lambda i: (own, near)[i][...])
    store(False, flags[2], lambda i: far[:, i * cols : (i + 1) * cols])


def y_sum_kernel(flags, keep, got, delta, here, there):
    rows = here.shape[1]
    for i in (0, 1):
        added = jnp.where(flags[3] == i, delta[...].astype(f32), 0.0)
        total = keep[i] + got[i] + added
        here[i] = total[:rows]
        there[i] = total[rows:].astype(bf16)


def y_end_kernel(here, got, out):
    cols = here.shape[2]
    for i in (0, 1):
        out[:, i * cols : (i + 1) * cols] = (here[i] + got[i].astype(f32)).astype(bf16)


def body_line(
    tokens,
    cotangent,
    frozen_value_weight,
    adapter_down_weight,
    adapter_up_weight,
    token_adapter,
    rank_step_count,
):
    rows, width = tokens.shape
    kv = cotangent.shape[1]
    cols = frozen_value_weight.shape[1]
    down = adapter_down_weight[0]
    up = adapter_up_weight[0]
    size = down.shape[1]
    wide = 2 * size
    quarter = width // 2
    eighth = quarter // 2
    kvq = kv // 2
    both = 2 * rows
    z, x = lax.axis_index("fsdp"), lax.axis_index("own")
    y, c = lax.axis_index("rep"), lax.axis_index("tp")
    first_pair = z < 2
    is_middle = (z == 1) | (z == 2)
    line = [z, z + 1 - 2 * (z % 2), jnp.where(first_pair, 2, 1), jnp.where(first_pair, 3, 0)]
    adapters = jnp.stack([2 * t + o for t in line for o in (x, 1 - x)]).astype(jnp.int32)
    number = adapters.shape[0]
    starts = jnp.stack(
        [side * quarter + half * eighth for side in (x, 1 - x) for half in (y, 1 - y)]
    ).astype(jnp.int32)
    ranks = size // 8 * rank_step_count
    numbers = jnp.concatenate([ranks, adapters])
    flags = jnp.stack([(c == 0) == first_pair, z % 2 == 1, z >= 2, x == 1]).astype(jnp.int32)

    latest = []

    def step(*values):
        if latest:
            values = lax.optimization_barrier((*values, latest[0]))[: len(values)]
        return values[0] if len(values) == 1 else values

    def done(value):
        latest[:] = [value]
        return value

    def like(*shape, kind=bf16):
        return jax.ShapeDtypeStruct(shape, kind)

    def cut(value, start, length, axis):
        return lax.dynamic_slice_in_dim(value, start, length, axis)

    def join(*values):
        return jnp.concatenate(values, axis=1)

    def rows_at(i, value, length):
        out = like(length, value.shape[1])
        return copy_call(
            lambda n, a, o: [(view(a[0], (at(n, i), length), (0, value.shape[1])), o[0])],
            [out],
            starts,
            value,
        )[0]

    def columns_at(i, value):
        out = like(value.shape[0], eighth)
        return copy_call(
            lambda n, a, o: [(view(a[0], (0, value.shape[0]), (at(n, i), eighth)), o[0])],
            [out],
            starts,
            value,
        )[0]

    def side_by_side(*values):
        widths = [v.shape[1] for v in values]
        length = values[0].shape[0]
        return copy_call(
            lambda n, a, o: [
                (a[i], view(o[0], (0, length), (sum(widths[:i]), widths[i])))
                for i in range(len(values))
            ],
            [like(length, sum(widths))],
            starts,
            *values,
        )[0]

    def tokens_of(i, value, got):
        return copy_call(
            lambda n, a, o: [
                (view(a[0], (0, rows), (at(n, i), eighth)), view(o[0], (0, rows), (0, eighth))),
                (a[1], view(o[0], (rows, rows), (0, eighth))),
            ],
            [like(both, eighth)],
            starts,
            value,
            got,
        )[0]

    down_got = swap(done(rows_at(2, down, eighth)), "own")
    up_sent = jnp.broadcast_to(
        step(up).reshape(size, 2, kvq).transpose(1, 0, 2)[None], (4, 2, size, kvq)
    ).reshape(number, size, kvq)
    up_all = lax.all_to_all(
        done(up_sent), ("fsdp", "own"), split_axis=0, concat_axis=0, tiled=True
    ).reshape(number * size, kvq)
    down_piece = done(
        copy_call(
            lambda n, a, o: [
                (view(a[0], (at(n, 0), eighth), (0, size)), view(o[0], (0, eighth), (0, size))),
                (a[1], view(o[0], (0, eighth), (size, size))),
            ],
            [like(eighth, wide)],
            starts,
            down,
            step(down_got),
        )[0]
    )
    down_near = along(down_piece, NEIGHBOURS)
    ids_here = jnp.broadcast_to(token_adapter.astype(bf16), (rows, size))
    packet = swap(done(join(step(cotangent), ids_here)), "own")
    x_got = [swap(done(columns_at(2, step(tokens))), "own")]
    weight_here = done(rows_at(0, step(frozen_value_weight), eighth))
    weight_near = along(weight_here, NEIGHBOURS)

    packet = step(packet)
    dy_half = jnp.concatenate([cotangent, packet[:, :kv]], axis=0)
    ids = jnp.concatenate([ids_here, packet[:, kv:]], axis=0)
    dy_quarter = cut(dy_half, x * kvq, kvq, 1)
    dy_tp = swap(done(dy_half), "tp")

    down_near = step(down_near)
    crossing = done(side_by_side(down_piece, down_near))
    down_crossed = along(crossing, MIDDLE)
    down_other = swap(crossing, "rep")

    compact = like(both, size, kind=f32)
    up_all, dy_quarter = step(up_all, dy_quarter)
    back_part = done(kernel_call(back_kernel, [compact], ids, dy_quarter, up_all)[0])
    back_tp = swap(back_part, "tp")
    x_mine = done(tokens_of(0, tokens, step(x_got[0])))
    back_part = done(back_part + step(back_tp))
    back_got = swap(back_part, "own")
    x_got.append(swap(done(columns_at(3, step(tokens))), "own"))
    x_in = [along(x_mine, INWARD)]
    weight_near = step(weight_near)
    crossing = done(side_by_side(weight_here, weight_near))
    weight_crossed = along(crossing, MIDDLE)
    weight_near_other = swap(weight_near, "rep")
    back_wide, back_sent = kernel_call(
        back_end_kernel,
        [like(both, number * size), like(both, wide)],
        ids,
        back_part,
        step(back_got),
        scalars=numbers,
    )
    back_in = along(done(back_sent), INWARD)
    x_other = done(tokens_of(1, tokens, step(x_got[1])))
    x_in.append(along(x_other, INWARD))
    x_both = [x_mine, x_other]

    dy_tp = step(dy_tp)
    dy_full = jnp.where(c == 0, join(dy_half, dy_tp), join(dy_tp, dy_half))
    dy_line = done(join(*[cut(dy_full, t * cols, cols, 1) for t in line]))
    weight_other = done(rows_at(1, step(frozen_value_weight), eighth))

    def total(half, first, last):
        return contract_first(x_both[half], back_wide[:, first * wide : last * wide])

    def total_in(half, first, last):
        return contract_first(x_in[half], back_in_wide[:, first * wide : last * wide])

    def to_middle(half, *others):
        x_in[half], *_ = step(x_in[half], back_in_wide, *others)
        sums = total(half, 2, 4) + total_in(half, 2, 4)
        return along(done(sums.astype(bf16)), MIDDLE)

    def to_end(half, crossed):
        crossed = step(crossed)
        sums = total(half, 1, 2) + crossed[:, wide:].astype(f32)
        return along(done(sums.astype(bf16)), OUTWARD)

    def finish(half, crossed, outer, *others):
        outer, *_ = step(outer, x_mine, *others)
        grad = total(half, 0, 1) + total_in(half, 0, 1)
        grad = (grad + crossed[:, :wide].astype(f32) + outer.astype(f32)).astype(bf16)
        here, there = grad[:, :size], grad[:, size:]
        done(here)
        return here, swap(there, "own")

    down_crossed, back_in, down_other = step(down_crossed, back_in, down_other)
    down_outer = along(down_crossed, OUTWARD)
    back_in_wide = done(
        kernel_call(
            spread_in_kernel, [like(both, number * size)], back_in, scalars=numbers
        )[0]
    )
    middle = [to_middle(0)]
    weight_crossed, weight_near_other = step(weight_crossed, weight_near_other)
    weight_outer = along(weight_crossed, OUTWARD)
    down_outer = step(down_outer)
    down_far = done(jnp.where(is_middle, down_crossed, down_outer))
    down_far_other = swap(down_far, "rep")
    middle.append(to_middle(1))
    outward = [to_end(0, middle[0])]
    weight_outer = step(weight_outer)
    weight_far = done(jnp.where(is_middle, weight_crossed, weight_outer))
    weight_far_other = swap(weight_far, "rep")

    low_part = done(
        kernel_call(
            low_kernel,
            [compact],
            ids,
            x_mine,
            x_other,
            down_piece,
            down_near,
            down_far,
            down_other,
            step(down_far_other),
            scalars=numbers,
        )[0]
    )
    low_tp = swap(low_part, "tp")
    blocks = [like(2, both, cols, kind=f32)] * 2
    y_first = kernel_call(
        y_kernel, blocks, step(x_mine), weight_here, weight_near, weight_far, scalars=flags
    )
    done(y_first[0])
    low_part = done(low_part + step(low_tp))
    low_got = swap(low_part, "own")
    half_grad = [like(rows, eighth)] * 2
    dx_mine, dx_sent = kernel_call(
        dx_kernel,
        half_grad,
        step(dy_line),
        back_wide,
        weight_here,
        weight_near,
        weight_far,
        down_piece,
        down_near,
        down_far,
    )
    done(dx_mine)
    dx_mine_got = swap(dx_sent, "own")
    grads = [finish(0, middle[0], outward[0])]
    low_wide, delta = kernel_call(
        low_end_kernel,
        [like(both, number * size), like(both, kvq)],
        ids,
        low_part,
        step(low_got),
        up_all,
        scalars=numbers,
    )
    up_part = done(contract_first(low_wide, dy_quarter).astype(bf16))
    up_got = lax.all_to_all(
        up_part.reshape(4, 2, size, kvq), "fsdp", split_axis=0, concat_axis=0, tiled=True
    )
    outward.append(to_end(1, middle[1]))

    weight_far_other, dx_mine_got = step(weight_far_other, dx_mine_got)
    y_keep, y_sent = kernel_call(
        y_kernel,
        blocks,
        x_other,
        weight_other,
        weight_near_other,
        weight_far_other,
        *y_first,
        scalars=flags,
    )
    y_got = swap(done(y_sent), "tp")
    dx_other, dx_sent = kernel_call(
        dx_kernel,
        half_grad,
        step(dy_line),
        back_wide,
        weight_other,
        weight_near_other,
        weight_far_other,
        down_other,
        down_far_other,
    )
    dx_other_got = swap(done(dx_sent), "own")
    y_here, y_sent = kernel_call(
        y_sum_kernel,
        [like(2, rows, cols, kind=f32), like(2, rows, cols)],
        y_keep,
        step(y_got),
        delta,
        scalars=flags,
    )
    y_got = swap(done(y_sent), "own")
    grads.append(finish(1, middle[1], outward[1], grads[0][1]))

    up_sum = jnp.sum(step(up_got).astype(f32), axis=0)
    own_ranks = cut(ranks, 2 * z, 2, 0).astype(f32)
    up_sum = done(((16.0 / own_ranks)[:, None, None] * up_sum).astype(bf16))
    up_mine = cut(up_sum, x, 1, 0)
    up_theirs = swap(cut(up_sum, 1 - x, 1, 0), "own")

    def in_place(axis, out, *pieces):
        def plan(n, a, o):
            spans = [[(0, length) for length in out.shape] for _ in range(4)]
            for i in range(4):
                spans[i][axis] = (at(n, i), eighth)
            return [(a[i], view(o[0], *spans[i])) for i in range(4)]

        return copy_call(plan, [out], starts, *pieces)[0]

    dx_other_got, _ = step(dx_other_got, dx_mine)
    input_grad = done(
        in_place(1, like(rows, width), dx_mine, dx_other, dx_mine_got, dx_other_got)
    )
    projected = done(kernel_call(y_end_kernel, [like(rows, kv)], y_here, step(y_got))[0])
    down_gradient = done(
        in_place(
            0, like(width, size), grads[0][0], grads[1][0], grads[0][1], step(grads[1][1])
        )[None]
    )
    up_theirs = step(up_theirs)
    up_gradient = jnp.where(
        x == 0,
        jnp.concatenate([up_mine, up_theirs], axis=2),
        jnp.concatenate([up_theirs, up_mine], axis=2),
    )
    return (projected, input_grad, down_gradient, up_gradient)


def body_routed(
    tokens,
    cotangent,
    frozen_value_weight,
    adapter_down_weight,
    adapter_up_weight,
    token_adapter,
    rank_step_count,
):
    rows, width_halved = tokens.shape
    half_kv = cotangent.shape[1]
    owning_adapters = lax.axis_size(("fsdp", "own"))
    greatest_rank = 3 * rows // (2 * owning_adapters)
    ids = token_adapter[:, 0]
    table = (ids[:, None] == jnp.arange(owning_adapters, dtype=jnp.int32)[None, :]).astype(
        f32
    )
    order = jnp.arange(rows, dtype=jnp.int32)
    earlier = (order[:, None] > order[None, :]).astype(f32)
    before = jnp.dot(earlier, table, precision=lax.Precision.HIGHEST)
    place = jnp.sum(before * table, axis=1).astype(jnp.int32)
    slot = ids * greatest_rank + place
    source_rows = jnp.full((owning_adapters * greatest_rank,), rows, jnp.int32).at[slot].set(order)
    padded_x = jnp.concatenate([tokens, jnp.zeros((1, width_halved), bf16)], axis=0)
    padded_dy = jnp.concatenate([cotangent, jnp.zeros((1, half_kv), bf16)], axis=0)
    send_x = jnp.take(padded_x, source_rows, axis=0)
    send_dy = jnp.take(padded_dy, source_rows, axis=0)
    recv_x, recv_dy = (
        lax.all_to_all(
            send_x.reshape(owning_adapters, greatest_rank, width_halved),
            ("fsdp", "own"),
            split_axis=0,
            concat_axis=0,
            tiled=True,
        ),
        lax.all_to_all(
            send_dy.reshape(owning_adapters, greatest_rank, half_kv),
            ("fsdp", "own"),
            split_axis=0,
            concat_axis=0,
            tiled=True,
        ),
    )
    flat_x = recv_x.reshape(owning_adapters * greatest_rank, width_halved)
    flat_dy = recv_dy.reshape(owning_adapters * greatest_rank, half_kv)
    dy_full = lax.all_gather(cotangent, "tp", axis=1, tiled=True)
    whole = lax.all_gather(frozen_value_weight, "fsdp", axis=1, tiled=True)
    partial_y = jnp.dot(tokens, whole, preferred_element_type=f32)
    base_dx = contract_final_axis(dy_full, whole)
    base_y = lax.psum_scatter(partial_y, "tp", scatter_dimension=1, tiled=True)
    down_matrix = adapter_down_weight[0]
    up_matrix = adapter_up_weight[0]
    part_low = jnp.dot(flat_x, down_matrix, preferred_element_type=f32)
    part_back = contract_final_axis(flat_dy, up_matrix)
    low_sum, back_sum = lax.psum((part_low, part_back), "tp")
    width_rank = down_matrix.shape[1]
    rank = width_rank // 8 * rank_step_count[lax.axis_index(("fsdp", "own"))]
    keep = jnp.arange(width_rank, dtype=jnp.int32)[None, :] < rank
    scale = 16.0 / rank.astype(f32)
    low = jnp.where(keep, low_sum, 0.0).astype(bf16)
    backward_pass = (scale * jnp.where(keep, back_sum, 0.0)).astype(bf16)
    delta = (scale * jnp.dot(low, up_matrix, preferred_element_type=f32)).astype(
        bf16
    )
    adapter_input_gradient = contract_final_axis(backward_pass, down_matrix).astype(bf16)
    down_gradient = contract_first(flat_x, backward_pass).astype(bf16)[None]
    up_gradient = (scale * contract_first(low, flat_dy)).astype(bf16)[None]
    home_delta, home_dx = (
        lax.all_to_all(
            delta.reshape(owning_adapters, greatest_rank, half_kv),
            ("fsdp", "own"),
            split_axis=0,
            concat_axis=0,
            tiled=True,
        ),
        lax.all_to_all(
            adapter_input_gradient.reshape(owning_adapters, greatest_rank, width_halved),
            ("fsdp", "own"),
            split_axis=0,
            concat_axis=0,
            tiled=True,
        ),
    )
    adapter_delta_rows = jnp.take(
        home_delta.reshape(owning_adapters * greatest_rank, half_kv), slot, axis=0
    )
    input_gradient_rows = jnp.take(
        home_dx.reshape(owning_adapters * greatest_rank, width_halved), slot, axis=0
    )
    projected = (base_y + adapter_delta_rows.astype(f32)).astype(bf16)
    input_grad = (base_dx + input_gradient_rows.astype(f32)).astype(bf16)
    return (projected, input_grad, down_gradient, up_gradient)


def solution(mesh):
    placed = (
        P(("rep", "fsdp", "own"), "tp"),
        P(("rep", "fsdp", "own"), "tp"),
        P("tp", "fsdp"),
        P(("fsdp", "own"), "tp", None),
        P(("fsdp", "own"), None, "tp"),
        P(("rep", "fsdp", "own"), None),
        P(),
    )
    line = mesh.shape["fsdp"] == 4 and mesh.shape["own"] == 2 and mesh.shape["rep"] == 2
    return jax.shard_map(
        body_line if line else body_routed,
        mesh=mesh,
        in_specs=placed,
        out_specs=(
            P(("rep", "fsdp", "own"), "tp"),
            P(("rep", "fsdp", "own"), "tp"),
            P(("rep", "fsdp", "own"), "tp", None),
            P(("rep", "fsdp", "own"), None, "tp"),
        ),
        check_vma=False,
    )
```

```python
import jax
import jax.numpy as jnp
from jax import lax
from jax.experimental import pallas as pl
from jax.experimental.pallas import tpu as pltpu
from jax.sharding import PartitionSpec as P

bf16 = jnp.bfloat16
f32 = jnp.float32


def contract_first(left, right):
    return lax.dot_general(
        left, right, (((0,), (0,)), ((), ())), preferred_element_type=f32
    )


def contract_final_axis(left, right):
    return lax.dot_general(
        left, right, (((1,), (1,)), ((), ())), preferred_element_type=f32
    )


def matmul(left, right):
    return jnp.dot(left, right, preferred_element_type=f32)


PAIR = [(0, 1), (1, 0)]
NEIGHBOURS = [(0, 1), (1, 0), (2, 3), (3, 2)]
MIDDLE = [(1, 2), (2, 1)]
OUTWARD = [(1, 0), (2, 3)]
INWARD = [(0, 1), (3, 2)]


def swap(value, axis):
    return lax.ppermute(value, axis, PAIR)


def along(value, pairs):
    return lax.ppermute(value, "fsdp", pairs)


def kernel_call(body, outs, *operands, scalars=None, scratch=(), space=pltpu.VMEM):
    specs = [pl.BlockSpec(memory_space=space)] * len(operands)
    if scalars is not None:
        operands = (scalars, *operands)
        specs = [pl.BlockSpec(memory_space=pltpu.SMEM), *specs]
    return pl.pallas_call(
        body,
        out_shape=list(outs),
        in_specs=specs,
        out_specs=[pl.BlockSpec(memory_space=pltpu.VMEM)] * len(outs),
        scratch_shapes=list(scratch),
        compiler_params=pltpu.CompilerParams(vmem_limit_bytes=28 * 2**20),
        cost_estimate=pl.CostEstimate(flops=0, bytes_accessed=0, transcendentals=0),
    )(*operands)


def copy_call(plan, outs, scalars, *operands):
    count = len(plan(None, [None] * len(operands), [None] * len(outs)))

    def body(numbers, *refs):
        sems = refs[-1]
        pairs = plan(numbers, refs[: len(operands)], refs[len(operands) : -1])
        copies = [pltpu.make_async_copy(a, b, sems.at[i]) for i, (a, b) in enumerate(pairs)]
        for copy in copies:
            copy.start()
        for copy in copies:
            copy.wait()

    return kernel_call(
        body,
        outs,
        *operands,
        scalars=scalars,
        scratch=[pltpu.SemaphoreType.DMA((count,))],
        space=pl.ANY,
    )


def view(ref, *spans):
    if ref is None:
        return None
    index = tuple(
        pl.ds(start if isinstance(start, int) else pl.multiple_of(start, 128), size)
        for start, size in spans
    )
    return ref.at[index]


def at(numbers, i):
    return None if numbers is None else numbers[i]


def ranks_of(ranks, ids):
    total = jnp.zeros(ids.shape, f32)
    for a in range(ranks.shape[0]):
        total = jnp.where(ids == a, ranks[a].astype(f32), total)
    return total


def kept(ids, ranks, value):
    rank = ranks_of(ranks, ids)
    column = lax.broadcasted_iota(jnp.int32, value.shape, 1).astype(f32)
    return jnp.where(column < rank, value, 0.0), 16.0 / rank


def roll_rows(value):
    half = value.shape[0] // 2
    return jnp.concatenate([value[half:], value[:half]], axis=0)


def back_kernel(ids, dy, up, out):
    size = out.shape[1]
    token = ids[...].astype(f32)
    for i in range(0, up.shape[0] // size, 2):
        both = contract_final_axis(dy[...], up[i * size : (i + 2) * size, :])
        for j in (0, 1):
            part = jnp.where(token == i + j, both[:, j * size : (j + 1) * size], 0.0)
            out[...] = part if i + j == 0 else out[...] + part


def spread_into(out, token, value, order):
    size = value.shape[1]
    for i in range(out.shape[1] // size):
        a = order[i].astype(f32)
        out[:, i * size : (i + 1) * size] = jnp.where(token == a, value, 0.0).astype(bf16)


def back_end_kernel(numbers, ids, part, got, wide, sent):
    token = ids[...].astype(f32)
    count = numbers.shape[0] // 2
    ranks, order = [numbers[i] for i in range(count)], [numbers[count + i] for i in range(count)]
    value, scale = kept(token, jnp.stack(ranks), part[...] + roll_rows(got[...]))
    value = (scale * value).astype(bf16)
    size = value.shape[1]
    sent[:, :size] = value
    sent[:, size:] = ids[...]
    spread_into(wide, token, value.astype(f32), order)


def spread_in_kernel(numbers, packet, wide):
    size = packet.shape[1] // 2
    count = numbers.shape[0] // 2
    order = [numbers[count + i] for i in range(count)]
    spread_into(wide, packet[:, size:].astype(f32), packet[:, :size].astype(f32), order)


def low_kernel(numbers, ids, x_mine, x_other, own, near, far, own_near_other, far_other, out):
    size = out.shape[1]
    wide = 2 * size
    token = ids[...].astype(f32)
    mine = [own[...], near[...], far[:, :wide], far[:, wide:]]
    other = [
        own_near_other[:, :wide],
        own_near_other[:, wide:],
        far_other[:, :wide],
        far_other[:, wide:],
    ]
    for i in range(4):
        both = matmul(x_mine[...], mine[i]) + matmul(x_other[...], other[i])
        for j in (0, 1):
            place = numbers[numbers.shape[0] // 2 + 2 * i + j].astype(f32)
            part = jnp.where(token == place, both[:, j * size : (j + 1) * size], 0.0)
            out[...] = part if i + j == 0 else out[...] + part


def low_end_kernel(numbers, ids, part, got, up, dy, wide, delta, grad):
    token = ids[...].astype(f32)
    count = numbers.shape[0] // 2
    ranks = jnp.stack([numbers[i] for i in range(count)])
    value, scale = kept(token, ranks, part[...] + roll_rows(got[...]))
    value = value.astype(bf16).astype(f32)
    spread_into(wide, token, value, [jnp.int32(i) for i in range(count)])
    grad[...] = contract_first(wide[...], dy[...]).astype(bf16)
    delta[...] = (scale[:, :1] * matmul(wide[...], up[...])).astype(bf16)


def to_middle_kernel(x_here, back, x_in, back_in, out):
    half = back.shape[1] // 2
    sums = contract_first(x_here[...], back[:, half:])
    out[...] = (sums + contract_first(x_in[...], back_in[:, half:])).astype(bf16)


def to_end_kernel(x_here, back, crossed, out):
    wide = out.shape[1]
    sums = contract_first(x_here[...], back[:, wide : 2 * wide])
    out[...] = (sums + crossed[:, wide:].astype(f32)).astype(bf16)


def finish_kernel(x_here, back, x_in, back_in, crossed, outer, here, there):
    size = here.shape[1]
    wide = 2 * size
    sums = contract_first(x_here[...], back[:, :wide])
    sums += contract_first(x_in[...], back_in[:, :wide])
    sums += crossed[:, :wide].astype(f32) + outer[...].astype(f32)
    here[...] = sums[:, :size].astype(bf16)
    there[...] = sums[:, size:].astype(bf16)


def up_sent_kernel(up, out):
    cols = out.shape[2]
    for i in range(out.shape[0]):
        out[i] = up[:, (i % 2) * cols : (i % 2 + 1) * cols]


def packet_kernel(flags, here, ids_here, packet, half, ids, quarter):
    rows, kv = here.shape
    half[:rows] = here[...]
    half[rows:] = packet[:, :kv]
    ids[:rows] = ids_here[...]
    ids[rows:] = packet[:, kv:]
    cols = quarter.shape[1]
    span = pl.ds(pl.multiple_of(flags[3] * cols, 128), cols)
    quarter[:rows] = here[:, span]
    quarter[rows:] = packet[:, span]


def dy_line_kernel(places, here, got, out):
    cols = out.shape[1] // 4
    for i in range(4):
        place = places[i]
        span = pl.ds(pl.multiple_of((place % 2) * cols, 128), cols)
        own = place // 2 == places[4]

        @pl.when(own)
        def _():
            out[:, i * cols : (i + 1) * cols] = here[:, span]

        @pl.when(jnp.logical_not(own))
        def _():
            out[:, i * cols : (i + 1) * cols] = got[:, span]


def far_kernel(flags, crossed, outer, out):
    @pl.when(flags[4] == 1)
    def _():
        out[...] = crossed[...]

    @pl.when(flags[4] == 0)
    def _():
        out[...] = outer[...]


def up_sum_kernel(numbers, got, here, there):
    count = numbers.shape[0] // 2
    for i, out in enumerate((here, there)):
        adapter = numbers[count + i]
        rank = jnp.float32(1.0)
        for a in range(count):
            rank = jnp.where(adapter == a, numbers[a].astype(f32), rank)
        part = got[0, adapter % 2].astype(f32)
        for source in range(1, got.shape[0]):
            part += got[source, adapter % 2].astype(f32)
        out[...] = (jnp.full(part.shape, 16.0, f32) / rank * part).astype(bf16)


def up_place_kernel(flags, here, there, out):
    cols = here.shape[1]
    out[:, pl.ds(pl.multiple_of(flags[3] * cols, 128), cols)] = here[...]
    out[:, pl.ds(pl.multiple_of((1 - flags[3]) * cols, 128), cols)] = there[...]


def add_kernel(left, right, out):
    out[...] = left[...] + right[...]


def dx_kernel(dy, back, own, near, far, *rest):
    *adapter, here, there = rest
    rows, width = here.shape
    cols = own.shape[1]
    tile = min(cols, width)
    for t in range(width // tile):
        span = slice(t * tile, (t + 1) * tile)
        base = contract_final_axis(dy[:, :cols], own[span, :])
        base += contract_final_axis(dy[:, cols : 2 * cols], near[span, :])
        base += contract_final_axis(dy[:, 2 * cols :], far[span, :])
        lora, start = 0.0, 0
        for piece in adapter:
            stop = start + piece.shape[1]
            lora += contract_final_axis(back[:, start:stop], piece[span, :])
            start = stop
        total = (base + lora.astype(bf16).astype(f32)).astype(bf16)
        here[:, span] = total[:rows]
        there[:, span] = total[rows:]


def y_kernel(flags, tokens, own, near, far, *rest):
    *before, keep, send = rest
    cols = own.shape[1]

    def store(pair, first, part):
        mine = flags[0] == (1 if pair else 0)
        for i in (0, 1):
            place = (first + i) % 2
            block = matmul(tokens[...], part(i))

            @pl.when(mine)
            def _():
                keep[place] = block + before[0][place] if before else block

            @pl.when(jnp.logical_not(mine))
            def _():
                send[place] = block + before[1][place] if before else block

    store(True, flags[1], lambda i: (own, near)[i][...])
    store(False, flags[2], lambda i: far[:, i * cols : (i + 1) * cols])


def y_sum_kernel(flags, keep, got, delta, here, there):
    rows = here.shape[1]
    for i in (0, 1):
        added = jnp.where(flags[3] == i, delta[...].astype(f32), 0.0)
        total = keep[i] + got[i] + added
        here[i] = total[:rows]
        there[i] = total[rows:].astype(bf16)


def y_end_kernel(here, got, out):
    cols = here.shape[2]
    for i in (0, 1):
        out[:, i * cols : (i + 1) * cols] = (here[i] + got[i].astype(f32)).astype(bf16)


def body_line(
    tokens,
    cotangent,
    frozen_value_weight,
    adapter_down_weight,
    adapter_up_weight,
    token_adapter,
    rank_step_count,
):
    rows, width = tokens.shape
    kv = cotangent.shape[1]
    cols = frozen_value_weight.shape[1]
    down = adapter_down_weight[0]
    up = adapter_up_weight[0]
    size = down.shape[1]
    wide = 2 * size
    quarter = width // 2
    eighth = quarter // 2
    kvq = kv // 2
    both = 2 * rows
    z, x = lax.axis_index("fsdp"), lax.axis_index("own")
    y, c = lax.axis_index("rep"), lax.axis_index("tp")
    first_pair = z < 2
    is_middle = (z == 1) | (z == 2)
    line = [z, z + 1 - 2 * (z % 2), jnp.where(first_pair, 2, 1), jnp.where(first_pair, 3, 0)]
    adapters = jnp.stack([2 * t + o for t in line for o in (x, 1 - x)]).astype(jnp.int32)
    number = adapters.shape[0]
    starts = jnp.stack(
        [side * quarter + half * eighth for side in (x, 1 - x) for half in (y, 1 - y)]
    ).astype(jnp.int32)
    ranks = size // 8 * rank_step_count
    numbers = jnp.concatenate([ranks, adapters])
    flags = jnp.stack([(c == 0) == first_pair, z % 2 == 1, z >= 2, x == 1, is_middle])
    flags = flags.astype(jnp.int32)
    places = jnp.stack([*line, c]).astype(jnp.int32)

    latest = []

    def step(*values):
        if latest:
            values = lax.optimization_barrier((*values, latest[0]))[: len(values)]
        return values[0] if len(values) == 1 else values

    def done(value):
        latest[:] = [value]
        return value

    def like(*shape, kind=bf16):
        return jax.ShapeDtypeStruct(shape, kind)

    def join(*values):
        return jnp.concatenate(values, axis=1)

    def rows_at(i, value, length):
        out = like(length, value.shape[1])
        return copy_call(
            lambda n, a, o: [(view(a[0], (at(n, i), length), (0, value.shape[1])), o[0])],
            [out],
            starts,
            value,
        )[0]

    def columns_at(i, value):
        out = like(value.shape[0], eighth)
        return copy_call(
            lambda n, a, o: [(view(a[0], (0, value.shape[0]), (at(n, i), eighth)), o[0])],
            [out],
            starts,
            value,
        )[0]

    def side_by_side(*values):
        widths = [v.shape[1] for v in values]
        length = values[0].shape[0]
        return copy_call(
            lambda n, a, o: [
                (a[i], view(o[0], (0, length), (sum(widths[:i]), widths[i])))
                for i in range(len(values))
            ],
            [like(length, sum(widths))],
            starts,
            *values,
        )[0]

    def tokens_of(i, value, got):
        return copy_call(
            lambda n, a, o: [
                (view(a[0], (0, rows), (at(n, i), eighth)), view(o[0], (0, rows), (0, eighth))),
                (a[1], view(o[0], (rows, rows), (0, eighth))),
            ],
            [like(both, eighth)],
            starts,
            value,
            got,
        )[0]

    down_got = swap(done(rows_at(2, down, eighth)), "own")
    ids_here = jnp.broadcast_to(token_adapter.astype(bf16), (rows, size))
    packet = swap(done(join(step(cotangent), ids_here)), "own")
    x_got = [swap(done(columns_at(2, step(tokens))), "own")]
    down_piece = done(
        copy_call(
            lambda n, a, o: [
                (view(a[0], (at(n, 0), eighth), (0, size)), view(o[0], (0, eighth), (0, size))),
                (a[1], view(o[0], (0, eighth), (size, size))),
            ],
            [like(eighth, wide)],
            starts,
            down,
            step(down_got),
        )[0]
    )
    down_near = along(down_piece, NEIGHBOURS)
    up, packet = step(up, packet)
    up_sent = kernel_call(up_sent_kernel, [like(number, size, kvq)], up)[0]
    up_all = lax.all_to_all(
        done(up_sent), ("fsdp", "own"), split_axis=0, concat_axis=0, tiled=True
    ).reshape(number * size, kvq)
    weight_here = done(rows_at(0, step(frozen_value_weight), eighth))
    weight_near = along(weight_here, NEIGHBOURS)

    dy_half, ids, dy_quarter = kernel_call(
        packet_kernel,
        [like(both, kv), like(both, size), like(both, kvq)],
        cotangent,
        ids_here,
        step(packet),
        scalars=flags,
    )
    done(dy_quarter)
    dy_tp = swap(dy_half, "tp")

    down_near, x_got[0] = step(down_near, x_got[0])
    crossing = done(side_by_side(down_piece, down_near))
    down_crossed = along(crossing, MIDDLE)
    down_other = swap(crossing, "rep")
    x_mine = done(tokens_of(0, tokens, step(x_got[0])))
    x_in = [along(x_mine, INWARD)]
    dy_line = done(
        kernel_call(
            dy_line_kernel, [like(both, 2 * kv)], dy_half, step(dy_tp), scalars=places
        )[0]
    )

    compact = like(both, size, kind=f32)
    up_all = step(up_all)
    back_part = done(kernel_call(back_kernel, [compact], ids, dy_quarter, up_all)[0])
    back_tp = swap(back_part, "tp")
    weight_near = step(weight_near)
    crossing = done(side_by_side(weight_here, weight_near))
    weight_crossed = along(crossing, MIDDLE)
    back_part = done(kernel_call(add_kernel, [compact], back_part, step(back_tp))[0])
    back_got = swap(back_part, "own")
    sent, down_other = step(tokens, down_other)
    x_got.append(swap(done(columns_at(3, sent)), "own"))
    weight_other = done(rows_at(1, step(frozen_value_weight), eighth))
    back_wide, back_sent = kernel_call(
        back_end_kernel,
        [like(both, number * size), like(both, wide)],
        ids,
        back_part,
        step(back_got),
        scalars=numbers,
    )
    back_in = along(done(back_sent), INWARD)
    down_crossed = done(step(down_crossed))
    down_outer = along(down_crossed, OUTWARD)
    x_other = done(tokens_of(1, tokens, step(x_got[1])))
    x_in.append(along(x_other, INWARD))
    x_both = [x_mine, x_other]

    def to_middle(half):
        x_in[half] = step(x_in[half])
        sums = kernel_call(
            to_middle_kernel,
            [like(eighth, 2 * wide)],
            x_both[half],
            back_wide,
            x_in[half],
            back_in_wide,
        )[0]
        return along(done(sums), MIDDLE)

    def to_end(half, crossed):
        sums = kernel_call(
            to_end_kernel, [like(eighth, wide)], x_both[half], back_wide, step(crossed)
        )[0]
        return along(done(sums), OUTWARD)

    def finish(half, crossed, outer, *others):
        outer, *_ = step(outer, x_mine, *others)
        here, there = kernel_call(
            finish_kernel,
            [like(eighth, size)] * 2,
            x_both[half],
            back_wide,
            x_in[half],
            back_in_wide,
            crossed,
            outer,
        )
        done(here)
        return here, swap(there, "own")

    def far_of(crossed, outer):
        out = like(*crossed.shape)
        return kernel_call(far_kernel, [out], crossed, outer, scalars=flags)[0]

    back_in_wide = done(
        kernel_call(
            spread_in_kernel, [like(both, number * size)], step(back_in), scalars=numbers
        )[0]
    )
    middle = [to_middle(0)]
    weight_near_other = swap(step(weight_near), "rep")
    weight_crossed = done(step(weight_crossed))
    weight_outer = along(weight_crossed, OUTWARD)
    down_outer, weight_near_other = step(down_outer, weight_near_other)
    down_far = done(far_of(down_crossed, down_outer))
    down_far_other = swap(down_far, "rep")
    middle.append(to_middle(1))
    outward = [to_end(0, middle[0])]
    weight_far = done(far_of(weight_crossed, step(weight_outer)))
    weight_far_other = swap(weight_far, "rep")

    low_part = done(
        kernel_call(
            low_kernel,
            [compact],
            ids,
            x_mine,
            x_other,
            down_piece,
            down_near,
            down_far,
            down_other,
            step(down_far_other),
            scalars=numbers,
        )[0]
    )
    low_tp = swap(low_part, "tp")
    blocks = [like(2, both, cols, kind=f32)] * 2
    y_first = kernel_call(
        y_kernel, blocks, step(x_mine), weight_here, weight_near, weight_far, scalars=flags
    )
    done(y_first[0])
    low_part = done(low_part + step(low_tp))
    low_got = swap(low_part, "own")
    half_grad = [like(rows, eighth)] * 2
    dx_mine, dx_sent = kernel_call(
        dx_kernel,
        half_grad,
        step(dy_line),
        back_wide,
        weight_here,
        weight_near,
        weight_far,
        down_piece,
        down_near,
        down_far,
    )
    done(dx_mine)
    dx_mine_got = swap(dx_sent, "own")
    grads = [finish(0, middle[0], outward[0])]
    _, delta, up_part = kernel_call(
        low_end_kernel,
        [like(both, number * size), like(both, kvq), like(number * size, kvq)],
        ids,
        low_part,
        step(low_got),
        up_all,
        dy_quarter,
        scalars=numbers,
    )
    up_got = lax.all_to_all(
        done(up_part).reshape(4, 2, size, kvq), "fsdp", split_axis=0, concat_axis=0, tiled=True
    )
    outward.append(to_end(1, middle[1]))
    weight_far_other, dx_mine_got, grad_got = step(weight_far_other, dx_mine_got, grads[0][1])
    dx_other, dx_sent = kernel_call(
        dx_kernel,
        half_grad,
        dy_line,
        back_wide,
        weight_other,
        weight_near_other,
        weight_far_other,
        down_other,
        down_far_other,
    )
    dx_other_got = swap(done(dx_sent), "own")
    y_keep, y_sent = kernel_call(
        y_kernel,
        blocks,
        step(x_other),
        weight_other,
        weight_near_other,
        weight_far_other,
        *y_first,
        scalars=flags,
    )
    y_got = swap(done(y_sent), "tp")
    y_here, y_sent = kernel_call(
        y_sum_kernel,
        [like(2, rows, cols, kind=f32), like(2, rows, cols)],
        y_keep,
        step(y_got),
        delta,
        scalars=flags,
    )
    y_got = swap(done(y_sent), "own")
    up_mine, up_theirs = kernel_call(
        up_sum_kernel, [like(size, kvq)] * 2, step(up_got), scalars=numbers
    )
    up_theirs = swap(done(up_theirs), "own")
    grads.append(finish(1, middle[1], outward[1]))

    def in_place(axis, out, *pieces):
        def plan(n, a, o):
            spans = [[(0, length) for length in out.shape] for _ in range(4)]
            for i in range(4):
                spans[i][axis] = (at(n, i), eighth)
            return [(a[i], view(o[0], *spans[i])) for i in range(4)]

        return copy_call(plan, [out], starts, *pieces)[0]

    dx_other_got, _ = step(dx_other_got, dx_mine)
    input_grad = done(
        in_place(1, like(rows, width), dx_mine, dx_other, dx_mine_got, dx_other_got)
    )
    projected = done(kernel_call(y_end_kernel, [like(rows, kv)], y_here, step(y_got))[0])
    down_gradient = done(
        in_place(
            0, like(width, size), grads[0][0], grads[1][0], grad_got, step(grads[1][1])
        )[None]
    )
    up_gradient = kernel_call(
        up_place_kernel, [like(size, kv)], up_mine, step(up_theirs), scalars=flags
    )[0][None]
    return (projected, input_grad, down_gradient, up_gradient)


def body_routed(
    tokens,
    cotangent,
    frozen_value_weight,
    adapter_down_weight,
    adapter_up_weight,
    token_adapter,
    rank_step_count,
):
    rows, width_halved = tokens.shape
    half_kv = cotangent.shape[1]
    owning_adapters = lax.axis_size(("fsdp", "own"))
    greatest_rank = 3 * rows // (2 * owning_adapters)
    ids = token_adapter[:, 0]
    table = (ids[:, None] == jnp.arange(owning_adapters, dtype=jnp.int32)[None, :]).astype(
        f32
    )
    order = jnp.arange(rows, dtype=jnp.int32)
    earlier = (order[:, None] > order[None, :]).astype(f32)
    before = jnp.dot(earlier, table, precision=lax.Precision.HIGHEST)
    place = jnp.sum(before * table, axis=1).astype(jnp.int32)
    slot = ids * greatest_rank + place
    source_rows = jnp.full((owning_adapters * greatest_rank,), rows, jnp.int32).at[slot].set(order)
    padded_x = jnp.concatenate([tokens, jnp.zeros((1, width_halved), bf16)], axis=0)
    padded_dy = jnp.concatenate([cotangent, jnp.zeros((1, half_kv), bf16)], axis=0)
    send_x = jnp.take(padded_x, source_rows, axis=0)
    send_dy = jnp.take(padded_dy, source_rows, axis=0)
    recv_x, recv_dy = (
        lax.all_to_all(
            send_x.reshape(owning_adapters, greatest_rank, width_halved),
            ("fsdp", "own"),
            split_axis=0,
            concat_axis=0,
            tiled=True,
        ),
        lax.all_to_all(
            send_dy.reshape(owning_adapters, greatest_rank, half_kv),
            ("fsdp", "own"),
            split_axis=0,
            concat_axis=0,
            tiled=True,
        ),
    )
    flat_x = recv_x.reshape(owning_adapters * greatest_rank, width_halved)
    flat_dy = recv_dy.reshape(owning_adapters * greatest_rank, half_kv)
    dy_full = lax.all_gather(cotangent, "tp", axis=1, tiled=True)
    whole = lax.all_gather(frozen_value_weight, "fsdp", axis=1, tiled=True)
    partial_y = jnp.dot(tokens, whole, preferred_element_type=f32)
    base_dx = contract_final_axis(dy_full, whole)
    base_y = lax.psum_scatter(partial_y, "tp", scatter_dimension=1, tiled=True)
    down_matrix = adapter_down_weight[0]
    up_matrix = adapter_up_weight[0]
    part_low = jnp.dot(flat_x, down_matrix, preferred_element_type=f32)
    part_back = contract_final_axis(flat_dy, up_matrix)
    low_sum, back_sum = lax.psum((part_low, part_back), "tp")
    width_rank = down_matrix.shape[1]
    rank = width_rank // 8 * rank_step_count[lax.axis_index(("fsdp", "own"))]
    keep = jnp.arange(width_rank, dtype=jnp.int32)[None, :] < rank
    scale = 16.0 / rank.astype(f32)
    low = jnp.where(keep, low_sum, 0.0).astype(bf16)
    backward_pass = (scale * jnp.where(keep, back_sum, 0.0)).astype(bf16)
    delta = (scale * jnp.dot(low, up_matrix, preferred_element_type=f32)).astype(
        bf16
    )
    adapter_input_gradient = contract_final_axis(backward_pass, down_matrix).astype(bf16)
    down_gradient = contract_first(flat_x, backward_pass).astype(bf16)[None]
    up_gradient = (scale * contract_first(low, flat_dy)).astype(bf16)[None]
    home_delta, home_dx = (
        lax.all_to_all(
            delta.reshape(owning_adapters, greatest_rank, half_kv),
            ("fsdp", "own"),
            split_axis=0,
            concat_axis=0,
            tiled=True,
        ),
        lax.all_to_all(
            adapter_input_gradient.reshape(owning_adapters, greatest_rank, width_halved),
            ("fsdp", "own"),
            split_axis=0,
            concat_axis=0,
            tiled=True,
        ),
    )
    adapter_delta_rows = jnp.take(
        home_delta.reshape(owning_adapters * greatest_rank, half_kv), slot, axis=0
    )
    input_gradient_rows = jnp.take(
        home_dx.reshape(owning_adapters * greatest_rank, width_halved), slot, axis=0
    )
    projected = (base_y + adapter_delta_rows.astype(f32)).astype(bf16)
    input_grad = (base_dx + input_gradient_rows.astype(f32)).astype(bf16)
    return (projected, input_grad, down_gradient, up_gradient)


def solution(mesh):
    placed = (
        P(("rep", "fsdp", "own"), "tp"),
        P(("rep", "fsdp", "own"), "tp"),
        P("tp", "fsdp"),
        P(("fsdp", "own"), "tp", None),
        P(("fsdp", "own"), None, "tp"),
        P(("rep", "fsdp", "own"), None),
        P(),
    )
    line = mesh.shape["fsdp"] == 4 and mesh.shape["own"] == 2 and mesh.shape["rep"] == 2
    return jax.shard_map(
        body_line if line else body_routed,
        mesh=mesh,
        in_specs=placed,
        out_specs=(
            P(("rep", "fsdp", "own"), "tp"),
            P(("rep", "fsdp", "own"), "tp"),
            P(("rep", "fsdp", "own"), "tp", None),
            P(("rep", "fsdp", "own"), None, "tp"),
        ),
        check_vma=False,
    )
```

```python
import jax
import jax.numpy as jnp
from jax import lax
from jax.experimental import pallas as pl
from jax.experimental.pallas import tpu as pltpu
from jax.sharding import PartitionSpec as P

bf16 = jnp.bfloat16
f32 = jnp.float32


def contract_first(left, right):
    return lax.dot_general(
        left, right, (((0,), (0,)), ((), ())), preferred_element_type=f32
    )


def contract_final_axis(left, right):
    return lax.dot_general(
        left, right, (((1,), (1,)), ((), ())), preferred_element_type=f32
    )


def matmul(left, right):
    return jnp.dot(left, right, preferred_element_type=f32)


PAIR = [(0, 1), (1, 0)]
NEIGHBOURS = [(0, 1), (1, 0), (2, 3), (3, 2)]
MIDDLE = [(1, 2), (2, 1)]
OUTWARD = [(1, 0), (2, 3)]
INWARD = [(0, 1), (3, 2)]


def swap(value, axis):
    return lax.ppermute(value, axis, PAIR)


def along(value, pairs):
    return lax.ppermute(value, "fsdp", pairs)


def kernel_call(body, outs, *operands, scalars=None, scratch=(), space=pltpu.VMEM):
    specs = [pl.BlockSpec(memory_space=space)] * len(operands)
    if scalars is not None:
        operands = (scalars, *operands)
        specs = [pl.BlockSpec(memory_space=pltpu.SMEM), *specs]
    return pl.pallas_call(
        body,
        out_shape=list(outs),
        in_specs=specs,
        out_specs=[pl.BlockSpec(memory_space=pltpu.VMEM)] * len(outs),
        scratch_shapes=list(scratch),
        compiler_params=pltpu.CompilerParams(vmem_limit_bytes=28 * 2**20),
        cost_estimate=pl.CostEstimate(flops=0, bytes_accessed=0, transcendentals=0),
    )(*operands)


def copy_call(plan, outs, scalars, *operands):
    count = len(plan(None, [None] * len(operands), [None] * len(outs)))

    def body(numbers, *refs):
        sems = refs[-1]
        pairs = plan(numbers, refs[: len(operands)], refs[len(operands) : -1])
        copies = [pltpu.make_async_copy(a, b, sems.at[i]) for i, (a, b) in enumerate(pairs)]
        for copy in copies:
            copy.start()
        for copy in copies:
            copy.wait()

    return kernel_call(
        body,
        outs,
        *operands,
        scalars=scalars,
        scratch=[pltpu.SemaphoreType.DMA((count,))],
        space=pl.ANY,
    )


def view(ref, *spans):
    if ref is None:
        return None
    index = tuple(
        pl.ds(start if isinstance(start, int) else pl.multiple_of(start, 128), size)
        for start, size in spans
    )
    return ref.at[index]


def at(numbers, i):
    return None if numbers is None else numbers[i]


def ranks_of(ranks, ids):
    total = jnp.zeros(ids.shape, f32)
    for a in range(ranks.shape[0]):
        total = jnp.where(ids == a, ranks[a].astype(f32), total)
    return total


def kept(ids, ranks, value):
    rank = ranks_of(ranks, ids)
    column = lax.broadcasted_iota(jnp.int32, value.shape, 1).astype(f32)
    return jnp.where(column < rank, value, 0.0), 16.0 / rank


def roll_rows(value):
    half = value.shape[0] // 2
    return jnp.concatenate([value[half:], value[:half]], axis=0)


def back_kernel(numbers, ids, dy, *rest):
    *ups, out = rest
    size = out.shape[1]
    token = ids[...].astype(f32)
    first = 2 * (numbers.shape[0] // 3)
    for i, up in enumerate(ups):
        both = contract_final_axis(dy[...], up[...])
        for j in (0, 1):
            place = numbers[first + 2 * i + j].astype(f32)
            part = jnp.where(token == place, both[:, j * size : (j + 1) * size], 0.0)
            out[...] = part if i + j == 0 else out[...] + part


def spread_into(out, token, value, order):
    size = value.shape[1]
    for i in range(out.shape[1] // size):
        a = order[i].astype(f32)
        out[:, i * size : (i + 1) * size] = jnp.where(token == a, value, 0.0).astype(bf16)


def back_end_kernel(numbers, ids, part, got, wide, sent):
    token = ids[...].astype(f32)
    count = numbers.shape[0] // 3
    ranks, order = [numbers[i] for i in range(count)], [numbers[count + i] for i in range(count)]
    value, scale = kept(token, jnp.stack(ranks), part[...] + roll_rows(got[...]))
    value = (scale * value).astype(bf16)
    size = value.shape[1]
    sent[:, :size] = value
    sent[:, size:] = ids[...]
    spread_into(wide, token, value.astype(f32), order)


def spread_in_kernel(numbers, packet, wide):
    size = packet.shape[1] // 2
    count = numbers.shape[0] // 3
    order = [numbers[count + i] for i in range(count)]
    spread_into(wide, packet[:, size:].astype(f32), packet[:, :size].astype(f32), order)


def low_kernel(numbers, ids, x_mine, x_other, own, near, far, own_near_other, far_other, out):
    size = out.shape[1]
    wide = 2 * size
    token = ids[...].astype(f32)
    mine = [own[...], near[...], far[:, :wide], far[:, wide:]]
    other = [
        own_near_other[:, :wide],
        own_near_other[:, wide:],
        far_other[:, :wide],
        far_other[:, wide:],
    ]
    for i in range(4):
        both = matmul(x_mine[...], mine[i]) + matmul(x_other[...], other[i])
        for j in (0, 1):
            place = numbers[numbers.shape[0] // 3 + 2 * i + j].astype(f32)
            part = jnp.where(token == place, both[:, j * size : (j + 1) * size], 0.0)
            out[...] = part if i + j == 0 else out[...] + part


def low_end_kernel(numbers, ids, part, got, dy, *rest):
    *ups, delta, first, second, third, fourth = rest
    token = ids[...].astype(f32)
    count = numbers.shape[0] // 3
    size = part.shape[1]
    ranks = jnp.stack([numbers[i] for i in range(count)])
    value, scale = kept(token, ranks, part[...] + roll_rows(got[...]))
    value = value.astype(bf16).astype(f32)
    total = 0.0
    for i, out in enumerate((first, second, third, fourth)):
        wide = jnp.concatenate(
            [
                jnp.where(token == numbers[2 * count + 2 * i + j].astype(f32), value, 0.0)
                for j in (0, 1)
            ],
            axis=1,
        ).astype(bf16)
        out[...] = contract_first(wide, dy[...]).astype(bf16)
        total += matmul(wide, ups[i][...])
    delta[...] = (scale[:, :1] * total).astype(bf16)


def to_middle_kernel(x_here, back, x_in, back_in, out):
    half = back.shape[1] // 2
    sums = contract_first(x_here[...], back[:, half:])
    out[...] = (sums + contract_first(x_in[...], back_in[:, half:])).astype(bf16)


def to_end_kernel(x_here, back, crossed, out):
    wide = out.shape[1]
    sums = contract_first(x_here[...], back[:, wide : 2 * wide])
    out[...] = (sums + crossed[:, wide:].astype(f32)).astype(bf16)


def finish_kernel(x_here, back, x_in, back_in, crossed, outer, here, there):
    size = here.shape[1]
    wide = 2 * size
    sums = contract_first(x_here[...], back[:, :wide])
    sums += contract_first(x_in[...], back_in[:, :wide])
    sums += crossed[:, :wide].astype(f32) + outer[...].astype(f32)
    here[...] = sums[:, :size].astype(bf16)
    there[...] = sums[:, size:].astype(bf16)


def packet_kernel(flags, cotangent, adapters, up, out):
    rows, kv = cotangent.shape
    size = up.shape[0]
    half = up.shape[1] // 2
    count = rows // size
    cols = half // count
    out[:, :kv] = cotangent[...]
    numbers = jnp.broadcast_to(adapters[...].astype(f32), (rows, size))
    out[:, kv : kv + size] = numbers.astype(bf16)
    for i in range(count):
        start = pl.multiple_of((1 - flags[3]) * half + i * cols, 128)
        out[i * size : (i + 1) * size, kv + size :] = up[:, pl.ds(start, cols)]


def unpack_kernel(flags, here, ids_here, up_here, packet, half, ids, quarter, up):
    rows, kv = here.shape
    size = up_here.shape[0]
    half[:rows] = here[...]
    half[rows:] = packet[:, :kv]
    ids[:rows] = ids_here[:, kv : kv + size]
    ids[rows:] = packet[:, kv : kv + size]
    cols = quarter.shape[1]
    span = pl.ds(pl.multiple_of(flags[3] * cols, 128), cols)
    quarter[:rows] = here[:, span]
    quarter[rows:] = packet[:, span]
    up[:size] = up_here[:, span]
    part = cols * size // rows
    for i in range(rows // size):
        up[size:, i * part : (i + 1) * part] = packet[i * size : (i + 1) * size, kv + size :]


def dy_line_kernel(places, here, got, out):
    cols = out.shape[1] // 4
    for i in range(4):
        place = places[i]
        span = pl.ds(pl.multiple_of((place % 2) * cols, 128), cols)
        own = place // 2 == places[4]

        @pl.when(own)
        def _():
            out[:, i * cols : (i + 1) * cols] = here[:, span]

        @pl.when(jnp.logical_not(own))
        def _():
            out[:, i * cols : (i + 1) * cols] = got[:, span]


def far_kernel(flags, crossed, outer, out):
    @pl.when(flags[4] == 1)
    def _():
        out[...] = crossed[...]

    @pl.when(flags[4] == 0)
    def _():
        out[...] = outer[...]


def up_sum_kernel(numbers, first, second, third, fourth, here, there):
    count = numbers.shape[0] // 3
    size = here.shape[0]
    for i, out in enumerate((here, there)):
        adapter = numbers[count + i]
        rank = jnp.float32(1.0)
        for a in range(count):
            rank = jnp.where(adapter == a, numbers[a].astype(f32), rank)
        span = slice(i * size, (i + 1) * size)
        part = sum(v[span, :].astype(f32) for v in (first, second, third, fourth))
        out[...] = (jnp.full(part.shape, 16.0, f32) / rank * part).astype(bf16)


def up_place_kernel(flags, here, there, out):
    cols = here.shape[1]
    out[:, pl.ds(pl.multiple_of(flags[3] * cols, 128), cols)] = here[...]
    out[:, pl.ds(pl.multiple_of((1 - flags[3]) * cols, 128), cols)] = there[...]


def add_kernel(left, right, out):
    out[...] = left[...] + right[...]


def dx_kernel(dy, back, own, near, far, *rest):
    *adapter, here, there = rest
    rows, width = here.shape
    cols = own.shape[1]
    tile = min(cols, width)
    for t in range(width // tile):
        span = slice(t * tile, (t + 1) * tile)
        base = contract_final_axis(dy[:, :cols], own[span, :])
        base += contract_final_axis(dy[:, cols : 2 * cols], near[span, :])
        base += contract_final_axis(dy[:, 2 * cols :], far[span, :])
        lora, start = 0.0, 0
        for piece in adapter:
            stop = start + piece.shape[1]
            lora += contract_final_axis(back[:, start:stop], piece[span, :])
            start = stop
        total = (base + lora.astype(bf16).astype(f32)).astype(bf16)
        here[:, span] = total[:rows]
        there[:, span] = total[rows:]


def y_kernel(flags, tokens, own, near, far, *rest):
    *before, keep, send = rest
    cols = own.shape[1]

    def store(pair, first, part):
        mine = flags[0] == (1 if pair else 0)
        for i in (0, 1):
            place = (first + i) % 2
            block = matmul(tokens[...], part(i))

            @pl.when(mine)
            def _():
                keep[place] = block + before[0][place] if before else block

            @pl.when(jnp.logical_not(mine))
            def _():
                send[place] = block + before[1][place] if before else block

    store(True, flags[1], lambda i: (own, near)[i][...])
    store(False, flags[2], lambda i: far[:, i * cols : (i + 1) * cols])


def y_sum_kernel(flags, keep, got, delta, here, there):
    rows = here.shape[1]
    for i in (0, 1):
        added = jnp.where(flags[3] == i, delta[...].astype(f32), 0.0)
        total = keep[i] + got[i] + added
        here[i] = total[:rows]
        there[i] = total[rows:].astype(bf16)


def y_end_kernel(here, got, out):
    cols = here.shape[2]
    for i in (0, 1):
        out[:, i * cols : (i + 1) * cols] = (here[i] + got[i].astype(f32)).astype(bf16)


def body_line(
    tokens,
    cotangent,
    frozen_value_weight,
    adapter_down_weight,
    adapter_up_weight,
    token_adapter,
    rank_step_count,
):
    rows, width = tokens.shape
    kv = cotangent.shape[1]
    cols = frozen_value_weight.shape[1]
    down = adapter_down_weight[0]
    up = adapter_up_weight[0]
    size = down.shape[1]
    wide = 2 * size
    quarter = width // 2
    eighth = quarter // 2
    kvq = kv // 2
    both = 2 * rows
    z, x = lax.axis_index("fsdp"), lax.axis_index("own")
    y, c = lax.axis_index("rep"), lax.axis_index("tp")
    first_pair = z < 2
    is_middle = (z == 1) | (z == 2)
    line = [z, z + 1 - 2 * (z % 2), jnp.where(first_pair, 2, 1), jnp.where(first_pair, 3, 0)]
    adapters = jnp.stack([2 * t + o for t in line for o in (x, 1 - x)]).astype(jnp.int32)
    number = adapters.shape[0]
    starts = jnp.stack(
        [side * quarter + half * eighth for side in (x, 1 - x) for half in (y, 1 - y)]
    ).astype(jnp.int32)
    ranks = size // 8 * rank_step_count
    ring = jnp.stack([2 * ((z + k) % 4) + o for k in range(4) for o in (x, 1 - x)])
    numbers = jnp.concatenate([ranks, adapters, ring.astype(jnp.int32)])
    flags = jnp.stack([(c == 0) == first_pair, z % 2 == 1, z >= 2, x == 1, is_middle])
    flags = flags.astype(jnp.int32)
    places = jnp.stack([*line, c]).astype(jnp.int32)

    latest = []

    def step(*values):
        if latest:
            values = lax.optimization_barrier((*values, latest[0]))[: len(values)]
        return values[0] if len(values) == 1 else values

    def done(value):
        latest[:] = [value]
        return value

    def like(*shape, kind=bf16):
        return jax.ShapeDtypeStruct(shape, kind)

    def around(value, shift):
        return along(value, [(i, (i + shift) % 4) for i in range(4)])

    def rows_at(i, value, length):
        out = like(length, value.shape[1])
        return copy_call(
            lambda n, a, o: [(view(a[0], (at(n, i), length), (0, value.shape[1])), o[0])],
            [out],
            starts,
            value,
        )[0]

    def columns_at(i, value):
        out = like(value.shape[0], eighth)
        return copy_call(
            lambda n, a, o: [(view(a[0], (0, value.shape[0]), (at(n, i), eighth)), o[0])],
            [out],
            starts,
            value,
        )[0]

    def side_by_side(*values):
        widths = [v.shape[1] for v in values]
        length = values[0].shape[0]
        return copy_call(
            lambda n, a, o: [
                (a[i], view(o[0], (0, length), (sum(widths[:i]), widths[i])))
                for i in range(len(values))
            ],
            [like(length, sum(widths))],
            starts,
            *values,
        )[0]

    def tokens_of(i, value, got):
        return copy_call(
            lambda n, a, o: [
                (view(a[0], (0, rows), (at(n, i), eighth)), view(o[0], (0, rows), (0, eighth))),
                (a[1], view(o[0], (rows, rows), (0, eighth))),
            ],
            [like(both, eighth)],
            starts,
            value,
            got,
        )[0]

    down_got = swap(done(rows_at(2, down, eighth)), "own")
    packet_here = done(
        kernel_call(
            packet_kernel,
            [like(rows, kv + size + kvq * size // rows)],
            step(cotangent),
            token_adapter,
            up,
            scalars=flags,
        )[0]
    )
    packet = swap(packet_here, "own")
    down_piece = done(
        copy_call(
            lambda n, a, o: [
                (view(a[0], (at(n, 0), eighth), (0, size)), view(o[0], (0, eighth), (0, size))),
                (a[1], view(o[0], (0, eighth), (size, size))),
            ],
            [like(eighth, wide)],
            starts,
            down,
            step(down_got),
        )[0]
    )
    down_near = along(down_piece, NEIGHBOURS)
    x_got = [swap(done(columns_at(2, step(tokens))), "own")]
    dy_half, ids, dy_quarter, up_piece = kernel_call(
        unpack_kernel,
        [like(both, kv), like(both, size), like(both, kvq), like(wide, kvq)],
        cotangent,
        packet_here,
        up,
        step(packet),
        scalars=flags,
    )
    ups = [done(up_piece)] + [around(up_piece, 4 - k) for k in (1, 2, 3)]

    crossing = done(side_by_side(down_piece, step(down_near)))
    down_crossed = along(crossing, MIDDLE)
    x_mine = done(tokens_of(0, tokens, step(x_got[0])))
    x_in = [along(x_mine, INWARD)]
    compact = like(both, size, kind=f32)
    dy_quarter, *ups = step(dy_quarter, *ups)
    back_part = done(
        kernel_call(back_kernel, [compact], ids, dy_quarter, *ups, scalars=numbers)[0]
    )
    back_tp = swap(back_part, "tp")
    weight_here = done(rows_at(0, step(frozen_value_weight), eighth))
    weight_near = along(weight_here, NEIGHBOURS)
    back_part = done(kernel_call(add_kernel, [compact], back_part, step(back_tp))[0])
    back_got = swap(back_part, "own")
    dy_tp = swap(step(dy_half), "tp")
    weight_other = done(rows_at(1, step(frozen_value_weight), eighth))
    weight_near = step(weight_near)
    weight_crossed = along(done(side_by_side(weight_here, weight_near)), MIDDLE)
    back_wide, back_sent = kernel_call(
        back_end_kernel,
        [like(both, number * size), like(both, wide)],
        ids,
        back_part,
        step(back_got),
        scalars=numbers,
    )
    back_in = along(done(back_sent), INWARD)
    x_got.append(swap(done(columns_at(3, step(tokens))), "own"))
    dy_line = done(
        kernel_call(
            dy_line_kernel, [like(both, 2 * kv)], dy_half, step(dy_tp), scalars=places
        )[0]
    )
    down_crossed = done(step(down_crossed))
    down_outer = along(down_crossed, OUTWARD)
    x_other = done(tokens_of(1, tokens, step(x_got[1])))
    x_in.append(along(x_other, INWARD))
    x_both = [x_mine, x_other]

    def to_middle(half):
        x_in[half] = step(x_in[half])
        sums = kernel_call(
            to_middle_kernel,
            [like(eighth, 2 * wide)],
            x_both[half],
            back_wide,
            x_in[half],
            back_in_wide,
        )[0]
        return along(done(sums), MIDDLE)

    def to_end(half, crossed):
        sums = kernel_call(
            to_end_kernel, [like(eighth, wide)], x_both[half], back_wide, step(crossed)
        )[0]
        return along(done(sums), OUTWARD)

    def finish(half, crossed, outer, *others):
        outer, *_ = step(outer, x_mine, *others)
        here, there = kernel_call(
            finish_kernel,
            [like(eighth, size)] * 2,
            x_both[half],
            back_wide,
            x_in[half],
            back_in_wide,
            crossed,
            outer,
        )
        done(here)
        return here, swap(there, "own")

    def far_of(crossed, outer):
        out = like(*crossed.shape)
        return kernel_call(far_kernel, [out], crossed, outer, scalars=flags)[0]

    back_in_wide = done(
        kernel_call(
            spread_in_kernel, [like(both, number * size)], step(back_in), scalars=numbers
        )[0]
    )
    middle = [to_middle(0)]
    down_other = swap(step(crossing), "rep")
    down_outer = step(down_outer)
    down_far = done(far_of(down_crossed, down_outer))
    down_far_other = swap(down_far, "rep")
    weight_crossed = done(step(weight_crossed))
    weight_outer = along(weight_crossed, OUTWARD)
    middle.append(to_middle(1))
    middle[0], down_other = step(middle[0], down_other)
    outward = [to_end(0, middle[0])]
    weight_near_other = swap(step(weight_near), "rep")
    weight_far = done(far_of(weight_crossed, step(weight_outer)))
    weight_far_other = swap(weight_far, "rep")
    half_grad = [like(rows, eighth)] * 2
    dy_line, weight_near_other = step(dy_line, weight_near_other)
    dx_mine, dx_sent = kernel_call(
        dx_kernel,
        half_grad,
        dy_line,
        back_wide,
        weight_here,
        weight_near,
        weight_far,
        down_piece,
        down_near,
        down_far,
    )
    dx_mine_got = swap(done(dx_sent), "own")

    low_part = done(
        kernel_call(
            low_kernel,
            [compact],
            ids,
            x_mine,
            x_other,
            down_piece,
            down_near,
            down_far,
            down_other,
            step(down_far_other),
            scalars=numbers,
        )[0]
    )
    low_tp = swap(low_part, "tp")
    blocks = [like(2, both, cols, kind=f32)] * 2
    y_first = kernel_call(
        y_kernel, blocks, step(x_mine), weight_here, weight_near, weight_far, scalars=flags
    )
    done(y_first[0])
    low_part = done(kernel_call(add_kernel, [compact], low_part, step(low_tp))[0])
    low_got = swap(low_part, "own")
    outward.append(to_end(1, middle[1]))
    low_got, dx_mine_got = step(low_got, dx_mine_got)
    delta, *up_parts = kernel_call(
        low_end_kernel,
        [like(both, kvq)] + [like(wide, kvq)] * 4,
        ids,
        low_part,
        low_got,
        dy_quarter,
        *ups,
        scalars=numbers,
    )
    done(delta)
    up_got = [around(up_parts[k], k) for k in (1, 2, 3)]
    grads = [finish(0, middle[0], outward[0])]
    dx_other, dx_sent = kernel_call(
        dx_kernel,
        half_grad,
        dy_line,
        back_wide,
        weight_other,
        weight_near_other,
        step(weight_far_other),
        down_other,
        down_far_other,
    )
    dx_other_got = swap(done(dx_sent), "own")
    y_keep, y_sent = kernel_call(
        y_kernel,
        blocks,
        step(x_other),
        weight_other,
        weight_near_other,
        weight_far_other,
        *y_first,
        scalars=flags,
    )
    y_got = swap(done(y_sent), "tp")
    grads.append(finish(1, middle[1], outward[1], *up_got))
    up_mine, up_theirs = kernel_call(
        up_sum_kernel, [like(size, kvq)] * 2, step(up_parts[0]), *up_got, scalars=numbers
    )
    up_theirs = swap(done(up_theirs), "own")
    y_here, y_sent = kernel_call(
        y_sum_kernel,
        [like(2, rows, cols, kind=f32), like(2, rows, cols)],
        y_keep,
        step(y_got),
        delta,
        scalars=flags,
    )
    y_got = swap(done(y_sent), "own")
    grad_got = grads[0][1]

    def in_place(axis, out, *pieces):
        def plan(n, a, o):
            spans = [[(0, length) for length in out.shape] for _ in range(4)]
            for i in range(4):
                spans[i][axis] = (at(n, i), eighth)
            return [(a[i], view(o[0], *spans[i])) for i in range(4)]

        return copy_call(plan, [out], starts, *pieces)[0]

    dx_other_got, _ = step(dx_other_got, dx_mine)
    input_grad = done(
        in_place(1, like(rows, width), dx_mine, dx_other, dx_mine_got, dx_other_got)
    )
    projected = done(kernel_call(y_end_kernel, [like(rows, kv)], y_here, step(y_got))[0])
    down_gradient = done(
        in_place(
            0, like(width, size), grads[0][0], grads[1][0], grad_got, step(grads[1][1])
        )[None]
    )
    up_gradient = kernel_call(
        up_place_kernel, [like(size, kv)], up_mine, step(up_theirs), scalars=flags
    )[0][None]
    return (projected, input_grad, down_gradient, up_gradient)


def body_routed(
    tokens,
    cotangent,
    frozen_value_weight,
    adapter_down_weight,
    adapter_up_weight,
    token_adapter,
    rank_step_count,
):
    rows, width_halved = tokens.shape
    half_kv = cotangent.shape[1]
    owning_adapters = lax.axis_size(("fsdp", "own"))
    greatest_rank = 3 * rows // (2 * owning_adapters)
    ids = token_adapter[:, 0]
    table = (ids[:, None] == jnp.arange(owning_adapters, dtype=jnp.int32)[None, :]).astype(
        f32
    )
    order = jnp.arange(rows, dtype=jnp.int32)
    earlier = (order[:, None] > order[None, :]).astype(f32)
    before = jnp.dot(earlier, table, precision=lax.Precision.HIGHEST)
    place = jnp.sum(before * table, axis=1).astype(jnp.int32)
    slot = ids * greatest_rank + place
    source_rows = jnp.full((owning_adapters * greatest_rank,), rows, jnp.int32).at[slot].set(order)
    padded_x = jnp.concatenate([tokens, jnp.zeros((1, width_halved), bf16)], axis=0)
    padded_dy = jnp.concatenate([cotangent, jnp.zeros((1, half_kv), bf16)], axis=0)
    send_x = jnp.take(padded_x, source_rows, axis=0)
    send_dy = jnp.take(padded_dy, source_rows, axis=0)
    recv_x, recv_dy = (
        lax.all_to_all(
            send_x.reshape(owning_adapters, greatest_rank, width_halved),
            ("fsdp", "own"),
            split_axis=0,
            concat_axis=0,
            tiled=True,
        ),
        lax.all_to_all(
            send_dy.reshape(owning_adapters, greatest_rank, half_kv),
            ("fsdp", "own"),
            split_axis=0,
            concat_axis=0,
            tiled=True,
        ),
    )
    flat_x = recv_x.reshape(owning_adapters * greatest_rank, width_halved)
    flat_dy = recv_dy.reshape(owning_adapters * greatest_rank, half_kv)
    dy_full = lax.all_gather(cotangent, "tp", axis=1, tiled=True)
    whole = lax.all_gather(frozen_value_weight, "fsdp", axis=1, tiled=True)
    partial_y = jnp.dot(tokens, whole, preferred_element_type=f32)
    base_dx = contract_final_axis(dy_full, whole)
    base_y = lax.psum_scatter(partial_y, "tp", scatter_dimension=1, tiled=True)
    down_matrix = adapter_down_weight[0]
    up_matrix = adapter_up_weight[0]
    part_low = jnp.dot(flat_x, down_matrix, preferred_element_type=f32)
    part_back = contract_final_axis(flat_dy, up_matrix)
    low_sum, back_sum = lax.psum((part_low, part_back), "tp")
    width_rank = down_matrix.shape[1]
    rank = width_rank // 8 * rank_step_count[lax.axis_index(("fsdp", "own"))]
    keep = jnp.arange(width_rank, dtype=jnp.int32)[None, :] < rank
    scale = 16.0 / rank.astype(f32)
    low = jnp.where(keep, low_sum, 0.0).astype(bf16)
    backward_pass = (scale * jnp.where(keep, back_sum, 0.0)).astype(bf16)
    delta = (scale * jnp.dot(low, up_matrix, preferred_element_type=f32)).astype(
        bf16
    )
    adapter_input_gradient = contract_final_axis(backward_pass, down_matrix).astype(bf16)
    down_gradient = contract_first(flat_x, backward_pass).astype(bf16)[None]
    up_gradient = (scale * contract_first(low, flat_dy)).astype(bf16)[None]
    home_delta, home_dx = (
        lax.all_to_all(
            delta.reshape(owning_adapters, greatest_rank, half_kv),
            ("fsdp", "own"),
            split_axis=0,
            concat_axis=0,
            tiled=True,
        ),
        lax.all_to_all(
            adapter_input_gradient.reshape(owning_adapters, greatest_rank, width_halved),
            ("fsdp", "own"),
            split_axis=0,
            concat_axis=0,
            tiled=True,
        ),
    )
    adapter_delta_rows = jnp.take(
        home_delta.reshape(owning_adapters * greatest_rank, half_kv), slot, axis=0
    )
    input_gradient_rows = jnp.take(
        home_dx.reshape(owning_adapters * greatest_rank, width_halved), slot, axis=0
    )
    projected = (base_y + adapter_delta_rows.astype(f32)).astype(bf16)
    input_grad = (base_dx + input_gradient_rows.astype(f32)).astype(bf16)
    return (projected, input_grad, down_gradient, up_gradient)


def solution(mesh):
    placed = (
        P(("rep", "fsdp", "own"), "tp"),
        P(("rep", "fsdp", "own"), "tp"),
        P("tp", "fsdp"),
        P(("fsdp", "own"), "tp", None),
        P(("fsdp", "own"), None, "tp"),
        P(("rep", "fsdp", "own"), None),
        P(),
    )
    line = mesh.shape["fsdp"] == 4 and mesh.shape["own"] == 2 and mesh.shape["rep"] == 2
    return jax.shard_map(
        body_line if line else body_routed,
        mesh=mesh,
        in_specs=placed,
        out_specs=(
            P(("rep", "fsdp", "own"), "tp"),
            P(("rep", "fsdp", "own"), "tp"),
            P(("rep", "fsdp", "own"), "tp", None),
            P(("rep", "fsdp", "own"), None, "tp"),
        ),
        check_vma=False,
    )
```

```python
import jax
import jax.numpy as jnp
from jax import lax
from jax.experimental import pallas as pl
from jax.experimental.pallas import tpu as pltpu
from jax.sharding import PartitionSpec as P

bf16 = jnp.bfloat16
f32 = jnp.float32


def contract_first(left, right):
    return lax.dot_general(
        left, right, (((0,), (0,)), ((), ())), preferred_element_type=f32
    )


def contract_final_axis(left, right):
    return lax.dot_general(
        left, right, (((1,), (1,)), ((), ())), preferred_element_type=f32
    )


def matmul(left, right):
    return jnp.dot(left, right, preferred_element_type=f32)


PAIR = [(0, 1), (1, 0)]
NEIGHBOURS = [(0, 1), (1, 0), (2, 3), (3, 2)]
MIDDLE = [(1, 2), (2, 1)]
OUTWARD = [(1, 0), (2, 3)]
INWARD = [(0, 1), (3, 2)]


def swap(value, axis):
    return lax.ppermute(value, axis, PAIR)


def along(value, pairs):
    return lax.ppermute(value, "fsdp", pairs)


def kernel_call(body, outs, *operands, scalars=None, scratch=(), space=pltpu.VMEM):
    specs = [pl.BlockSpec(memory_space=space)] * len(operands)
    if scalars is not None:
        operands = (scalars, *operands)
        specs = [pl.BlockSpec(memory_space=pltpu.SMEM), *specs]
    return pl.pallas_call(
        body,
        out_shape=list(outs),
        in_specs=specs,
        out_specs=[pl.BlockSpec(memory_space=pltpu.VMEM)] * len(outs),
        scratch_shapes=list(scratch),
        compiler_params=pltpu.CompilerParams(vmem_limit_bytes=28 * 2**20),
        cost_estimate=pl.CostEstimate(flops=0, bytes_accessed=0, transcendentals=0),
    )(*operands)


def copy_call(plan, outs, scalars, *operands):
    count = len(plan(None, [None] * len(operands), [None] * len(outs)))

    def body(numbers, *refs):
        sems = refs[-1]
        pairs = plan(numbers, refs[: len(operands)], refs[len(operands) : -1])
        copies = [pltpu.make_async_copy(a, b, sems.at[i]) for i, (a, b) in enumerate(pairs)]
        for copy in copies:
            copy.start()
        for copy in copies:
            copy.wait()

    return kernel_call(
        body,
        outs,
        *operands,
        scalars=scalars,
        scratch=[pltpu.SemaphoreType.DMA((count,))],
        space=pl.ANY,
    )


def view(ref, *spans):
    if ref is None:
        return None
    index = tuple(
        pl.ds(start if isinstance(start, int) else pl.multiple_of(start, 128), size)
        for start, size in spans
    )
    return ref.at[index]


def at(numbers, i):
    return None if numbers is None else numbers[i]


def ranks_of(ranks, ids):
    total = jnp.zeros(ids.shape, f32)
    for a in range(ranks.shape[0]):
        total = jnp.where(ids == a, ranks[a].astype(f32), total)
    return total


def kept(ids, ranks, value):
    rank = ranks_of(ranks, ids)
    column = lax.broadcasted_iota(jnp.int32, value.shape, 1).astype(f32)
    return jnp.where(column < rank, value, 0.0), 16.0 / rank


def roll_rows(value):
    half = value.shape[0] // 2
    return jnp.concatenate([value[half:], value[:half]], axis=0)


def back_kernel(ids, dy, up, out):
    size = out.shape[1]
    token = ids[...].astype(f32)
    for i in range(0, up.shape[0] // size, 2):
        both = contract_final_axis(dy[...], up[i * size : (i + 2) * size, :])
        for j in (0, 1):
            part = jnp.where(token == i + j, both[:, j * size : (j + 1) * size], 0.0)
            out[...] = part if i + j == 0 else out[...] + part


def spread_into(out, token, value, order):
    size = value.shape[1]
    for i in range(out.shape[1] // size):
        a = order[i].astype(f32)
        out[:, i * size : (i + 1) * size] = jnp.where(token == a, value, 0.0).astype(bf16)


def back_end_kernel(numbers, ids, part, got, wide, sent):
    token = ids[...].astype(f32)
    count = numbers.shape[0] // 2
    ranks, order = [numbers[i] for i in range(count)], [numbers[count + i] for i in range(count)]
    value, scale = kept(token, jnp.stack(ranks), part[...] + roll_rows(got[...]))
    value = (scale * value).astype(bf16)
    size = value.shape[1]
    sent[:, :size] = value
    sent[:, size:] = ids[...]
    spread_into(wide, token, value.astype(f32), order)


def spread_in_kernel(numbers, packet, wide):
    size = packet.shape[1] // 2
    count = numbers.shape[0] // 2
    order = [numbers[count + i] for i in range(count)]
    spread_into(wide, packet[:, size:].astype(f32), packet[:, :size].astype(f32), order)


def low_kernel(numbers, ids, x_mine, x_other, own, near, far, own_near_other, far_other, out):
    size = out.shape[1]
    wide = 2 * size
    token = ids[...].astype(f32)
    mine = [own[...], near[...], far[:, :wide], far[:, wide:]]
    other = [
        own_near_other[:, :wide],
        own_near_other[:, wide:],
        far_other[:, :wide],
        far_other[:, wide:],
    ]
    for i in range(4):
        both = matmul(x_mine[...], mine[i]) + matmul(x_other[...], other[i])
        for j in (0, 1):
            place = numbers[numbers.shape[0] // 2 + 2 * i + j].astype(f32)
            part = jnp.where(token == place, both[:, j * size : (j + 1) * size], 0.0)
            out[...] = part if i + j == 0 else out[...] + part


def low_end_kernel(numbers, ids, part, got, up, dy, wide, delta, grad):
    token = ids[...].astype(f32)
    count = numbers.shape[0] // 2
    ranks = jnp.stack([numbers[i] for i in range(count)])
    value, scale = kept(token, ranks, part[...] + roll_rows(got[...]))
    value = value.astype(bf16).astype(f32)
    spread_into(wide, token, value, [jnp.int32(i) for i in range(count)])
    grad[...] = contract_first(wide[...], dy[...]).astype(bf16)
    delta[...] = (scale[:, :1] * matmul(wide[...], up[...])).astype(bf16)


def to_middle_kernel(x_here, back, x_in, back_in, out):
    half = back.shape[1] // 2
    sums = contract_first(x_here[...], back[:, half:])
    out[...] = (sums + contract_first(x_in[...], back_in[:, half:])).astype(bf16)


def to_end_kernel(x_here, back, crossed, out):
    wide = out.shape[1]
    sums = contract_first(x_here[...], back[:, wide : 2 * wide])
    out[...] = (sums + crossed[:, wide:].astype(f32)).astype(bf16)


def finish_kernel(x_here, back, x_in, back_in, crossed, outer, here, there):
    size = here.shape[1]
    wide = 2 * size
    sums = contract_first(x_here[...], back[:, :wide])
    sums += contract_first(x_in[...], back_in[:, :wide])
    sums += crossed[:, :wide].astype(f32) + outer[...].astype(f32)
    here[...] = sums[:, :size].astype(bf16)
    there[...] = sums[:, size:].astype(bf16)


def up_sent_kernel(up, out):
    cols = out.shape[2]
    for i in range(out.shape[0]):
        out[i] = up[:, (i % 2) * cols : (i % 2 + 1) * cols]


def packet_kernel(cotangent, adapters, out):
    rows, kv = cotangent.shape
    size = out.shape[1] - kv
    out[:, :kv] = cotangent[...]
    numbers = jnp.broadcast_to(adapters[...].astype(f32), (rows, size))
    out[:, kv:] = numbers.astype(bf16)


def unpack_kernel(flags, here, there, half, ids, quarter):
    rows = here.shape[0]
    kv = half.shape[1]
    cols = quarter.shape[1]
    span = pl.ds(pl.multiple_of(flags[3] * cols, 128), cols)
    for i, packet in enumerate((here, there)):
        place = slice(i * rows, (i + 1) * rows)
        half[place] = packet[:, :kv]
        ids[place] = packet[:, kv:]
        quarter[place] = packet[:, span]


def dy_line_kernel(places, here, got, out):
    cols = out.shape[1] // 4
    for i in range(4):
        place = places[i]
        span = pl.ds(pl.multiple_of((place % 2) * cols, 128), cols)
        own = place // 2 == places[4]

        @pl.when(own)
        def _():
            out[:, i * cols : (i + 1) * cols] = here[:, span]

        @pl.when(jnp.logical_not(own))
        def _():
            out[:, i * cols : (i + 1) * cols] = got[:, span]


def far_kernel(flags, crossed, outer, out):
    @pl.when(flags[4] == 1)
    def _():
        out[...] = crossed[...]

    @pl.when(flags[4] == 0)
    def _():
        out[...] = outer[...]


def up_sum_kernel(numbers, got, here, there):
    count = numbers.shape[0] // 2
    for i, out in enumerate((here, there)):
        adapter = numbers[count + i]
        rank = jnp.float32(1.0)
        for a in range(count):
            rank = jnp.where(adapter == a, numbers[a].astype(f32), rank)
        part = got[0, adapter % 2].astype(f32)
        for source in range(1, got.shape[0]):
            part += got[source, adapter % 2].astype(f32)
        out[...] = (jnp.full(part.shape, 16.0, f32) / rank * part).astype(bf16)


def up_place_kernel(flags, here, there, out):
    cols = here.shape[1]
    out[:, pl.ds(pl.multiple_of(flags[3] * cols, 128), cols)] = here[...]
    out[:, pl.ds(pl.multiple_of((1 - flags[3]) * cols, 128), cols)] = there[...]


def add_kernel(left, right, out):
    out[...] = left[...] + right[...]


def dx_kernel(dy, back, own, near, far, *rest):
    *adapter, here, there = rest
    rows, width = here.shape
    cols = own.shape[1]
    tile = min(cols, width)
    for t in range(width // tile):
        span = slice(t * tile, (t + 1) * tile)
        base = contract_final_axis(dy[:, :cols], own[span, :])
        base += contract_final_axis(dy[:, cols : 2 * cols], near[span, :])
        base += contract_final_axis(dy[:, 2 * cols :], far[span, :])
        lora, start = 0.0, 0
        for piece in adapter:
            stop = start + piece.shape[1]
            lora += contract_final_axis(back[:, start:stop], piece[span, :])
            start = stop
        total = (base + lora.astype(bf16).astype(f32)).astype(bf16)
        here[:, span] = total[:rows]
        there[:, span] = total[rows:]


def y_kernel(flags, tokens, own, near, far, *rest):
    *before, keep, send = rest
    cols = own.shape[1]

    def store(pair, first, part):
        mine = flags[0] == (1 if pair else 0)
        for i in (0, 1):
            place = (first + i) % 2
            block = matmul(tokens[...], part(i))

            @pl.when(mine)
            def _():
                keep[place] = block + before[0][place] if before else block

            @pl.when(jnp.logical_not(mine))
            def _():
                send[place] = block + before[1][place] if before else block

    store(True, flags[1], lambda i: (own, near)[i][...])
    store(False, flags[2], lambda i: far[:, i * cols : (i + 1) * cols])


def y_sum_kernel(flags, keep, got, delta, here, there):
    rows = here.shape[1]
    for i in (0, 1):
        added = jnp.where(flags[3] == i, delta[...].astype(f32), 0.0)
        total = keep[i] + got[i] + added
        here[i] = total[:rows]
        there[i] = total[rows:].astype(bf16)


def y_end_kernel(here, got, out):
    cols = here.shape[2]
    for i in (0, 1):
        out[:, i * cols : (i + 1) * cols] = (here[i] + got[i].astype(f32)).astype(bf16)


def body_line(
    tokens,
    cotangent,
    frozen_value_weight,
    adapter_down_weight,
    adapter_up_weight,
    token_adapter,
    rank_step_count,
):
    rows, width = tokens.shape
    kv = cotangent.shape[1]
    cols = frozen_value_weight.shape[1]
    down = adapter_down_weight[0]
    up = adapter_up_weight[0]
    size = down.shape[1]
    wide = 2 * size
    quarter = width // 2
    eighth = quarter // 2
    kvq = kv // 2
    both = 2 * rows
    z, x = lax.axis_index("fsdp"), lax.axis_index("own")
    y, c = lax.axis_index("rep"), lax.axis_index("tp")
    first_pair = z < 2
    is_middle = (z == 1) | (z == 2)
    line = [z, z + 1 - 2 * (z % 2), jnp.where(first_pair, 2, 1), jnp.where(first_pair, 3, 0)]
    adapters = jnp.stack([2 * t + o for t in line for o in (x, 1 - x)]).astype(jnp.int32)
    number = adapters.shape[0]
    starts = jnp.stack(
        [side * quarter + half * eighth for side in (x, 1 - x) for half in (y, 1 - y)]
    ).astype(jnp.int32)
    ranks = size // 8 * rank_step_count
    numbers = jnp.concatenate([ranks, adapters])
    flags = jnp.stack([(c == 0) == first_pair, z % 2 == 1, z >= 2, x == 1, is_middle])
    flags = flags.astype(jnp.int32)
    places = jnp.stack([*line, c]).astype(jnp.int32)

    latest = []

    def step(*values):
        if latest:
            values = lax.optimization_barrier((*values, latest[0]))[: len(values)]
        return values[0] if len(values) == 1 else values

    def done(value):
        latest[:] = [value]
        return value

    def like(*shape, kind=bf16):
        return jax.ShapeDtypeStruct(shape, kind)

    def rows_at(i, value, length):
        out = like(length, value.shape[1])
        return copy_call(
            lambda n, a, o: [(view(a[0], (at(n, i), length), (0, value.shape[1])), o[0])],
            [out],
            starts,
            value,
        )[0]

    def columns_at(i, value):
        out = like(value.shape[0], eighth)
        return copy_call(
            lambda n, a, o: [(view(a[0], (0, value.shape[0]), (at(n, i), eighth)), o[0])],
            [out],
            starts,
            value,
        )[0]

    def side_by_side(*values):
        widths = [v.shape[1] for v in values]
        length = values[0].shape[0]
        return copy_call(
            lambda n, a, o: [
                (a[i], view(o[0], (0, length), (sum(widths[:i]), widths[i])))
                for i in range(len(values))
            ],
            [like(length, sum(widths))],
            starts,
            *values,
        )[0]

    def tokens_of(i, value, got):
        return copy_call(
            lambda n, a, o: [
                (view(a[0], (0, rows), (at(n, i), eighth)), view(o[0], (0, rows), (0, eighth))),
                (a[1], view(o[0], (rows, rows), (0, eighth))),
            ],
            [like(both, eighth)],
            starts,
            value,
            got,
        )[0]

    down_got = swap(done(rows_at(2, down, eighth)), "own")
    packet_here = done(
        kernel_call(packet_kernel, [like(rows, kv + size)], step(cotangent), token_adapter)[0]
    )
    packet = swap(packet_here, "own")
    down_piece = done(
        copy_call(
            lambda n, a, o: [
                (view(a[0], (at(n, 0), eighth), (0, size)), view(o[0], (0, eighth), (0, size))),
                (a[1], view(o[0], (0, eighth), (size, size))),
            ],
            [like(eighth, wide)],
            starts,
            down,
            step(down_got),
        )[0]
    )
    down_near = along(down_piece, NEIGHBOURS)
    up, packet = step(up, packet)
    up_sent = kernel_call(up_sent_kernel, [like(number, size, kvq)], up)[0]
    up_all = lax.all_to_all(
        done(up_sent), ("fsdp", "own"), split_axis=0, concat_axis=0, tiled=True
    ).reshape(number * size, kvq)
    x_got = [swap(done(columns_at(2, step(tokens))), "own")]
    weight_here = done(rows_at(0, step(frozen_value_weight), eighth))
    weight_near = along(weight_here, NEIGHBOURS)
    dy_half, ids, dy_quarter = kernel_call(
        unpack_kernel,
        [like(both, kv), like(both, size), like(both, kvq)],
        step(packet_here),
        packet,
        scalars=flags,
    )
    done(dy_quarter)

    crossing = done(side_by_side(down_piece, step(down_near)))
    down_crossed = along(crossing, MIDDLE)
    down_other = swap(crossing, "rep")
    x_mine = done(tokens_of(0, tokens, step(x_got[0])))
    x_in = [along(x_mine, INWARD)]
    compact = like(both, size, kind=f32)
    up_all = step(up_all)
    back_part = done(kernel_call(back_kernel, [compact], ids, dy_quarter, up_all)[0])
    back_tp = swap(back_part, "tp")
    crossing = done(side_by_side(weight_here, step(weight_near)))
    weight_crossed = along(crossing, MIDDLE)
    back_part = done(kernel_call(add_kernel, [compact], back_part, step(back_tp))[0])
    back_got = swap(back_part, "own")
    sent, down_other = step(frozen_value_weight, down_other)
    weight_other = done(rows_at(1, sent, eighth))
    weight_near_other = swap(step(weight_near), "rep")
    back_wide, back_sent = kernel_call(
        back_end_kernel,
        [like(both, number * size), like(both, wide)],
        ids,
        back_part,
        step(back_got),
        scalars=numbers,
    )
    back_in = along(done(back_sent), INWARD)
    down_crossed = done(step(down_crossed))
    down_outer = along(down_crossed, OUTWARD)
    sent, weight_near_other = step(tokens, weight_near_other)
    x_got.append(swap(done(columns_at(3, sent)), "own"))
    dy_tp = swap(step(dy_half), "tp")
    dy_line = done(
        kernel_call(dy_line_kernel, [like(both, 2 * kv)], dy_half, dy_tp, scalars=places)[0]
    )

    def to_middle(half):
        x_in[half] = step(x_in[half])
        sums = kernel_call(
            to_middle_kernel,
            [like(eighth, 2 * wide)],
            x_both[half],
            back_wide,
            x_in[half],
            back_in_wide,
        )[0]
        return along(done(sums), MIDDLE)

    def to_end(half, crossed):
        sums = kernel_call(
            to_end_kernel, [like(eighth, wide)], x_both[half], back_wide, step(crossed)
        )[0]
        return along(done(sums), OUTWARD)

    def finish(half, crossed, outer, *others):
        outer, *_ = step(outer, x_mine, *others)
        here, there = kernel_call(
            finish_kernel,
            [like(eighth, size)] * 2,
            x_both[half],
            back_wide,
            x_in[half],
            back_in_wide,
            crossed,
            outer,
        )
        return done(here), swap(there, "own")

    def far_of(crossed, outer):
        out = like(*crossed.shape)
        return kernel_call(far_kernel, [out], crossed, outer, scalars=flags)[0]

    back_in_wide = done(
        kernel_call(
            spread_in_kernel, [like(both, number * size)], step(back_in), scalars=numbers
        )[0]
    )
    x_both = [x_mine]
    middle = [to_middle(0)]
    x_both.append(done(tokens_of(1, tokens, step(x_got[1]))))
    x_other = x_both[1]
    x_in.append(along(x_other, INWARD))
    weight_crossed = done(step(weight_crossed))
    weight_outer = along(weight_crossed, OUTWARD)
    down_far = done(far_of(down_crossed, step(down_outer)))
    down_far_other = swap(down_far, "rep")
    middle.append(to_middle(1))
    outward = [to_end(0, middle[0])]
    weight_far = done(far_of(weight_crossed, step(weight_outer)))
    weight_far_other = swap(weight_far, "rep")
    half_grad = [like(rows, eighth)] * 2
    dx_mine, dx_mine_sent = kernel_call(
        dx_kernel,
        half_grad,
        step(dy_line),
        back_wide,
        weight_here,
        weight_near,
        weight_far,
        down_piece,
        down_near,
        down_far,
    )
    done(dx_mine)

    low_part = done(
        kernel_call(
            low_kernel,
            [compact],
            ids,
            x_mine,
            x_other,
            down_piece,
            down_near,
            down_far,
            down_other,
            step(down_far_other),
            scalars=numbers,
        )[0]
    )
    low_tp = swap(low_part, "tp")
    blocks = [like(2, both, cols, kind=f32)] * 2
    y_first = kernel_call(
        y_kernel, blocks, step(x_mine), weight_here, weight_near, weight_far, scalars=flags
    )
    done(y_first[0])
    low_part = done(kernel_call(add_kernel, [compact], low_part, step(low_tp))[0])
    low_got = swap(low_part, "own")
    grads = [finish(0, middle[0], outward[0])]
    low_got = step(low_got)
    dx_mine_got = swap(step(dx_mine_sent, low_got)[0], "own")
    _, delta, up_part = kernel_call(
        low_end_kernel,
        [like(both, number * size), like(both, kvq), like(number * size, kvq)],
        ids,
        low_part,
        low_got,
        up_all,
        dy_quarter,
        scalars=numbers,
    )
    up_got = lax.all_to_all(
        done(up_part).reshape(4, 2, size, kvq), "fsdp", split_axis=0, concat_axis=0, tiled=True
    )
    outward.append(to_end(1, middle[1]))
    weight_far_other, grad_got = step(weight_far_other, grads[0][1])
    dx_other, dx_sent = kernel_call(
        dx_kernel,
        half_grad,
        dy_line,
        back_wide,
        weight_other,
        weight_near_other,
        weight_far_other,
        down_other,
        down_far_other,
    )
    dx_other_got = swap(done(dx_sent), "own")
    up_got, dx_mine_got = step(up_got, dx_mine_got)
    up_mine, up_theirs = kernel_call(
        up_sum_kernel, [like(size, kvq)] * 2, up_got, scalars=numbers
    )
    up_theirs = swap(done(up_theirs), "own")
    y_keep, y_sent = kernel_call(
        y_kernel,
        blocks,
        step(x_other),
        weight_other,
        weight_near_other,
        weight_far_other,
        *y_first,
        scalars=flags,
    )
    y_got = swap(done(y_sent), "tp")
    grads.append(finish(1, middle[1], outward[1]))
    y_here, y_sent = kernel_call(
        y_sum_kernel,
        [like(2, rows, cols, kind=f32), like(2, rows, cols)],
        y_keep,
        step(y_got),
        delta,
        scalars=flags,
    )
    y_got = swap(done(y_sent), "own")

    def in_place(axis, out, *pieces):
        def plan(n, a, o):
            spans = [[(0, length) for length in out.shape] for _ in range(4)]
            for i in range(4):
                spans[i][axis] = (at(n, i), eighth)
            return [(a[i], view(o[0], *spans[i])) for i in range(4)]

        return copy_call(plan, [out], starts, *pieces)[0]

    dx_other_got, _ = step(dx_other_got, dx_mine)
    input_grad = done(
        in_place(1, like(rows, width), dx_mine, dx_other, dx_mine_got, dx_other_got)
    )
    projected = done(kernel_call(y_end_kernel, [like(rows, kv)], y_here, step(y_got))[0])
    down_gradient = done(
        in_place(
            0, like(width, size), grads[0][0], grads[1][0], grad_got, step(grads[1][1])
        )[None]
    )
    up_gradient = kernel_call(
        up_place_kernel, [like(size, kv)], up_mine, step(up_theirs), scalars=flags
    )[0][None]
    return (projected, input_grad, down_gradient, up_gradient)


def body_routed(
    tokens,
    cotangent,
    frozen_value_weight,
    adapter_down_weight,
    adapter_up_weight,
    token_adapter,
    rank_step_count,
):
    rows, width_halved = tokens.shape
    half_kv = cotangent.shape[1]
    owning_adapters = lax.axis_size(("fsdp", "own"))
    greatest_rank = 3 * rows // (2 * owning_adapters)
    ids = token_adapter[:, 0]
    table = (ids[:, None] == jnp.arange(owning_adapters, dtype=jnp.int32)[None, :]).astype(
        f32
    )
    order = jnp.arange(rows, dtype=jnp.int32)
    earlier = (order[:, None] > order[None, :]).astype(f32)
    before = jnp.dot(earlier, table, precision=lax.Precision.HIGHEST)
    place = jnp.sum(before * table, axis=1).astype(jnp.int32)
    slot = ids * greatest_rank + place
    source_rows = jnp.full((owning_adapters * greatest_rank,), rows, jnp.int32).at[slot].set(order)
    padded_x = jnp.concatenate([tokens, jnp.zeros((1, width_halved), bf16)], axis=0)
    padded_dy = jnp.concatenate([cotangent, jnp.zeros((1, half_kv), bf16)], axis=0)
    send_x = jnp.take(padded_x, source_rows, axis=0)
    send_dy = jnp.take(padded_dy, source_rows, axis=0)
    recv_x, recv_dy = (
        lax.all_to_all(
            send_x.reshape(owning_adapters, greatest_rank, width_halved),
            ("fsdp", "own"),
            split_axis=0,
            concat_axis=0,
            tiled=True,
        ),
        lax.all_to_all(
            send_dy.reshape(owning_adapters, greatest_rank, half_kv),
            ("fsdp", "own"),
            split_axis=0,
            concat_axis=0,
            tiled=True,
        ),
    )
    flat_x = recv_x.reshape(owning_adapters * greatest_rank, width_halved)
    flat_dy = recv_dy.reshape(owning_adapters * greatest_rank, half_kv)
    dy_full = lax.all_gather(cotangent, "tp", axis=1, tiled=True)
    whole = lax.all_gather(frozen_value_weight, "fsdp", axis=1, tiled=True)
    partial_y = jnp.dot(tokens, whole, preferred_element_type=f32)
    base_dx = contract_final_axis(dy_full, whole)
    base_y = lax.psum_scatter(partial_y, "tp", scatter_dimension=1, tiled=True)
    down_matrix = adapter_down_weight[0]
    up_matrix = adapter_up_weight[0]
    part_low = jnp.dot(flat_x, down_matrix, preferred_element_type=f32)
    part_back = contract_final_axis(flat_dy, up_matrix)
    low_sum, back_sum = lax.psum((part_low, part_back), "tp")
    width_rank = down_matrix.shape[1]
    rank = width_rank // 8 * rank_step_count[lax.axis_index(("fsdp", "own"))]
    keep = jnp.arange(width_rank, dtype=jnp.int32)[None, :] < rank
    scale = 16.0 / rank.astype(f32)
    low = jnp.where(keep, low_sum, 0.0).astype(bf16)
    backward_pass = (scale * jnp.where(keep, back_sum, 0.0)).astype(bf16)
    delta = (scale * jnp.dot(low, up_matrix, preferred_element_type=f32)).astype(
        bf16
    )
    adapter_input_gradient = contract_final_axis(backward_pass, down_matrix).astype(bf16)
    down_gradient = contract_first(flat_x, backward_pass).astype(bf16)[None]
    up_gradient = (scale * contract_first(low, flat_dy)).astype(bf16)[None]
    home_delta, home_dx = (
        lax.all_to_all(
            delta.reshape(owning_adapters, greatest_rank, half_kv),
            ("fsdp", "own"),
            split_axis=0,
            concat_axis=0,
            tiled=True,
        ),
        lax.all_to_all(
            adapter_input_gradient.reshape(owning_adapters, greatest_rank, width_halved),
            ("fsdp", "own"),
            split_axis=0,
            concat_axis=0,
            tiled=True,
        ),
    )
    adapter_delta_rows = jnp.take(
        home_delta.reshape(owning_adapters * greatest_rank, half_kv), slot, axis=0
    )
    input_gradient_rows = jnp.take(
        home_dx.reshape(owning_adapters * greatest_rank, width_halved), slot, axis=0
    )
    projected = (base_y + adapter_delta_rows.astype(f32)).astype(bf16)
    input_grad = (base_dx + input_gradient_rows.astype(f32)).astype(bf16)
    return (projected, input_grad, down_gradient, up_gradient)


def solution(mesh):
    placed = (
        P(("rep", "fsdp", "own"), "tp"),
        P(("rep", "fsdp", "own"), "tp"),
        P("tp", "fsdp"),
        P(("fsdp", "own"), "tp", None),
        P(("fsdp", "own"), None, "tp"),
        P(("rep", "fsdp", "own"), None),
        P(),
    )
    line = mesh.shape["fsdp"] == 4 and mesh.shape["own"] == 2 and mesh.shape["rep"] == 2
    return jax.shard_map(
        body_line if line else body_routed,
        mesh=mesh,
        in_specs=placed,
        out_specs=(
            P(("rep", "fsdp", "own"), "tp"),
            P(("rep", "fsdp", "own"), "tp"),
            P(("rep", "fsdp", "own"), "tp", None),
            P(("rep", "fsdp", "own"), None, "tp"),
        ),
        check_vma=False,
    )
```

```python
import jax
import jax.numpy as jnp
from jax import lax
from jax.experimental import pallas as pl
from jax.experimental.pallas import tpu as pltpu
from jax.sharding import PartitionSpec as P

bf16 = jnp.bfloat16
f32 = jnp.float32


def contract_first(left, right):
    return lax.dot_general(
        left, right, (((0,), (0,)), ((), ())), preferred_element_type=f32
    )


def contract_final_axis(left, right):
    return lax.dot_general(
        left, right, (((1,), (1,)), ((), ())), preferred_element_type=f32
    )


def matmul(left, right):
    return jnp.dot(left, right, preferred_element_type=f32)


PAIR = [(0, 1), (1, 0)]
NEIGHBOURS = [(0, 1), (1, 0), (2, 3), (3, 2)]
MIDDLE = [(1, 2), (2, 1)]
OUTWARD = [(1, 0), (2, 3)]
INWARD = [(0, 1), (3, 2)]


def swap(value, axis):
    return lax.ppermute(value, axis, PAIR)


def along(value, pairs):
    return lax.ppermute(value, "fsdp", pairs)


def kernel_call(body, outs, *operands, scalars=None, scratch=(), space=pltpu.VMEM):
    specs = [pl.BlockSpec(memory_space=space)] * len(operands)
    if scalars is not None:
        operands = (scalars, *operands)
        specs = [pl.BlockSpec(memory_space=pltpu.SMEM), *specs]
    return pl.pallas_call(
        body,
        out_shape=list(outs),
        in_specs=specs,
        out_specs=[pl.BlockSpec(memory_space=pltpu.VMEM)] * len(outs),
        scratch_shapes=list(scratch),
        compiler_params=pltpu.CompilerParams(vmem_limit_bytes=28 * 2**20),
        cost_estimate=pl.CostEstimate(flops=0, bytes_accessed=0, transcendentals=0),
    )(*operands)


def copy_call(plan, outs, scalars, *operands):
    count = len(plan(None, [None] * len(operands), [None] * len(outs)))

    def body(numbers, *refs):
        sems = refs[-1]
        pairs = plan(numbers, refs[: len(operands)], refs[len(operands) : -1])
        copies = [pltpu.make_async_copy(a, b, sems.at[i]) for i, (a, b) in enumerate(pairs)]
        for copy in copies:
            copy.start()
        for copy in copies:
            copy.wait()

    return kernel_call(
        body,
        outs,
        *operands,
        scalars=scalars,
        scratch=[pltpu.SemaphoreType.DMA((count,))],
        space=pl.ANY,
    )


def view(ref, *spans):
    if ref is None:
        return None
    index = tuple(
        pl.ds(start if isinstance(start, int) else pl.multiple_of(start, 128), size)
        for start, size in spans
    )
    return ref.at[index]


def at(numbers, i):
    return None if numbers is None else numbers[i]


def ranks_of(ranks, ids):
    total = jnp.zeros(ids.shape, f32)
    for a in range(ranks.shape[0]):
        total = jnp.where(ids == a, ranks[a].astype(f32), total)
    return total


def kept(ids, ranks, value):
    rank = ranks_of(ranks, ids)
    column = lax.broadcasted_iota(jnp.int32, value.shape, 1).astype(f32)
    return jnp.where(column < rank, value, 0.0), 16.0 / rank


def roll_rows(value):
    half = value.shape[0] // 2
    return jnp.concatenate([value[half:], value[:half]], axis=0)


def back_kernel(ids, dy, up, out):
    size = out.shape[1]
    token = ids[...].astype(f32)
    for i in range(0, up.shape[0] // size, 2):
        both = contract_final_axis(dy[...], up[i * size : (i + 2) * size, :])
        for j in (0, 1):
            part = jnp.where(token == i + j, both[:, j * size : (j + 1) * size], 0.0)
            out[...] = part if i + j == 0 else out[...] + part


def spread_into(out, token, value, order):
    size = value.shape[1]
    for i in range(out.shape[1] // size):
        a = order[i].astype(f32)
        out[:, i * size : (i + 1) * size] = jnp.where(token == a, value, 0.0).astype(bf16)


def back_end_kernel(numbers, ids, part, got, wide, sent):
    token = ids[...].astype(f32)
    count = numbers.shape[0] // 3
    ranks, order = [numbers[i] for i in range(count)], [numbers[count + i] for i in range(count)]
    value, scale = kept(token, jnp.stack(ranks), part[...] + roll_rows(got[...]))
    value = (scale * value).astype(bf16)
    size = value.shape[1]
    sent[:, :size] = value
    sent[:, size:] = ids[...]
    spread_into(wide, token, value.astype(f32), order)


def spread_in_kernel(numbers, packet, wide):
    size = packet.shape[1] // 2
    count = numbers.shape[0] // 3
    order = [numbers[count + i] for i in range(count)]
    spread_into(wide, packet[:, size:].astype(f32), packet[:, :size].astype(f32), order)


def low_kernel(numbers, ids, x_mine, x_other, own, near, far, own_near_other, far_other, out):
    size = out.shape[1]
    wide = 2 * size
    token = ids[...].astype(f32)
    mine = [own[...], near[...], far[:, :wide], far[:, wide:]]
    other = [
        own_near_other[:, :wide],
        own_near_other[:, wide:],
        far_other[:, :wide],
        far_other[:, wide:],
    ]
    for i in range(4):
        both = matmul(x_mine[...], mine[i]) + matmul(x_other[...], other[i])
        for j in (0, 1):
            place = numbers[numbers.shape[0] // 3 + 2 * i + j].astype(f32)
            part = jnp.where(token == place, both[:, j * size : (j + 1) * size], 0.0)
            out[...] = part if i + j == 0 else out[...] + part


def low_end_kernel(numbers, ids, part, got, up, dy, delta, *grads):
    token = ids[...].astype(f32)
    count = numbers.shape[0] // 3
    size = part.shape[1]
    ranks = jnp.stack([numbers[i] for i in range(count)])
    value, scale = kept(token, ranks, part[...] + roll_rows(got[...]))
    value = value.astype(bf16).astype(f32)

    def pair(first, second):
        return jnp.concatenate(
            [jnp.where(token == a, value, 0.0) for a in (first, second)], axis=1
        ).astype(bf16)

    total = 0.0
    for i, out in enumerate(grads):
        places = [numbers[2 * count + 2 * i + j].astype(f32) for j in (0, 1)]
        out[...] = contract_first(pair(*places), dy[...]).astype(bf16)
        total += matmul(pair(2 * i, 2 * i + 1), up[2 * i * size : 2 * (i + 1) * size, :])
    delta[...] = (scale[:, :1] * total).astype(bf16)


def to_middle_kernel(x_here, back, x_in, back_in, out):
    half = back.shape[1] // 2
    sums = contract_first(x_here[...], back[:, half:])
    out[...] = (sums + contract_first(x_in[...], back_in[:, half:])).astype(bf16)


def to_end_kernel(x_here, back, crossed, out):
    wide = out.shape[1]
    sums = contract_first(x_here[...], back[:, wide : 2 * wide])
    out[...] = (sums + crossed[:, wide:].astype(f32)).astype(bf16)


def finish_kernel(x_here, back, x_in, back_in, crossed, outer, here, there):
    size = here.shape[1]
    wide = 2 * size
    sums = contract_first(x_here[...], back[:, :wide])
    sums += contract_first(x_in[...], back_in[:, :wide])
    sums += crossed[:, :wide].astype(f32) + outer[...].astype(f32)
    here[...] = sums[:, :size].astype(bf16)
    there[...] = sums[:, size:].astype(bf16)


def up_sent_kernel(up, out):
    cols = out.shape[2]
    for i in range(out.shape[0]):
        out[i] = up[:, (i % 2) * cols : (i % 2 + 1) * cols]


def packet_kernel(cotangent, adapters, out):
    rows, kv = cotangent.shape
    size = out.shape[1] - kv
    out[:, :kv] = cotangent[...]
    numbers = jnp.broadcast_to(adapters[...].astype(f32), (rows, size))
    out[:, kv:] = numbers.astype(bf16)


def unpack_kernel(flags, here, there, half, ids, quarter):
    rows = here.shape[0]
    kv = half.shape[1]
    cols = quarter.shape[1]
    span = pl.ds(pl.multiple_of(flags[3] * cols, 128), cols)
    for i, packet in enumerate((here, there)):
        place = slice(i * rows, (i + 1) * rows)
        half[place] = packet[:, :kv]
        ids[place] = packet[:, kv:]
        quarter[place] = packet[:, span]


def dy_line_kernel(places, here, got, out):
    cols = out.shape[1] // 4
    for i in range(4):
        place = places[i]
        span = pl.ds(pl.multiple_of((place % 2) * cols, 128), cols)
        own = place // 2 == places[4]

        @pl.when(own)
        def _():
            out[:, i * cols : (i + 1) * cols] = here[:, span]

        @pl.when(jnp.logical_not(own))
        def _():
            out[:, i * cols : (i + 1) * cols] = got[:, span]


def far_kernel(flags, crossed, outer, out):
    @pl.when(flags[4] == 1)
    def _():
        out[...] = crossed[...]

    @pl.when(flags[4] == 0)
    def _():
        out[...] = outer[...]


def up_sum_kernel(numbers, first, second, third, fourth, here, there):
    count = numbers.shape[0] // 3
    size = here.shape[0]
    for i, out in enumerate((here, there)):
        adapter = numbers[count + i]
        rank = jnp.float32(1.0)
        for a in range(count):
            rank = jnp.where(adapter == a, numbers[a].astype(f32), rank)
        span = slice(i * size, (i + 1) * size)
        part = sum(v[span, :].astype(f32) for v in (first, second, third, fourth))
        out[...] = (jnp.full(part.shape, 16.0, f32) / rank * part).astype(bf16)


def up_place_kernel(flags, here, there, out):
    cols = here.shape[1]
    out[:, pl.ds(pl.multiple_of(flags[3] * cols, 128), cols)] = here[...]
    out[:, pl.ds(pl.multiple_of((1 - flags[3]) * cols, 128), cols)] = there[...]


def add_kernel(left, right, out):
    out[...] = left[...] + right[...]


def dx_kernel(dy, back, own, near, far, *rest):
    *adapter, here, there = rest
    rows, width = here.shape
    cols = own.shape[1]
    tile = min(cols, width)
    for t in range(width // tile):
        span = slice(t * tile, (t + 1) * tile)
        base = contract_final_axis(dy[:, :cols], own[span, :])
        base += contract_final_axis(dy[:, cols : 2 * cols], near[span, :])
        base += contract_final_axis(dy[:, 2 * cols :], far[span, :])
        lora, start = 0.0, 0
        for piece in adapter:
            stop = start + piece.shape[1]
            lora += contract_final_axis(back[:, start:stop], piece[span, :])
            start = stop
        total = (base + lora.astype(bf16).astype(f32)).astype(bf16)
        here[:, span] = total[:rows]
        there[:, span] = total[rows:]


def y_kernel(flags, tokens, own, near, far, *rest):
    *before, keep, send = rest
    cols = own.shape[1]

    def store(pair, first, part):
        mine = flags[0] == (1 if pair else 0)
        for i in (0, 1):
            place = (first + i) % 2
            block = matmul(tokens[...], part(i))

            @pl.when(mine)
            def _():
                keep[place] = block + before[0][place] if before else block

            @pl.when(jnp.logical_not(mine))
            def _():
                send[place] = block + before[1][place] if before else block

    store(True, flags[1], lambda i: (own, near)[i][...])
    store(False, flags[2], lambda i: far[:, i * cols : (i + 1) * cols])


def y_sum_kernel(flags, keep, got, delta, here, there):
    rows = here.shape[1]
    for i in (0, 1):
        added = jnp.where(flags[3] == i, delta[...].astype(f32), 0.0)
        total = keep[i] + got[i] + added
        here[i] = total[:rows]
        there[i] = total[rows:].astype(bf16)


def y_end_kernel(here, got, out):
    cols = here.shape[2]
    for i in (0, 1):
        out[:, i * cols : (i + 1) * cols] = (here[i] + got[i].astype(f32)).astype(bf16)


def body_line(
    tokens,
    cotangent,
    frozen_value_weight,
    adapter_down_weight,
    adapter_up_weight,
    token_adapter,
    rank_step_count,
):
    rows, width = tokens.shape
    kv = cotangent.shape[1]
    cols = frozen_value_weight.shape[1]
    down = adapter_down_weight[0]
    up = adapter_up_weight[0]
    size = down.shape[1]
    wide = 2 * size
    quarter = width // 2
    eighth = quarter // 2
    kvq = kv // 2
    both = 2 * rows
    z, x = lax.axis_index("fsdp"), lax.axis_index("own")
    y, c = lax.axis_index("rep"), lax.axis_index("tp")
    first_pair = z < 2
    is_middle = (z == 1) | (z == 2)
    line = [z, z + 1 - 2 * (z % 2), jnp.where(first_pair, 2, 1), jnp.where(first_pair, 3, 0)]
    adapters = jnp.stack([2 * t + o for t in line for o in (x, 1 - x)]).astype(jnp.int32)
    number = adapters.shape[0]
    starts = jnp.stack(
        [side * quarter + half * eighth for side in (x, 1 - x) for half in (y, 1 - y)]
    ).astype(jnp.int32)
    ranks = size // 8 * rank_step_count
    ring = jnp.stack([2 * ((z + k) % 4) + o for k in range(4) for o in (x, 1 - x)])
    numbers = jnp.concatenate([ranks, adapters, ring.astype(jnp.int32)])
    flags = jnp.stack([(c == 0) == first_pair, z % 2 == 1, z >= 2, x == 1, is_middle])
    flags = flags.astype(jnp.int32)
    places = jnp.stack([*line, c]).astype(jnp.int32)

    latest = []

    def step(*values):
        if latest:
            values = lax.optimization_barrier((*values, latest[0]))[: len(values)]
        return values[0] if len(values) == 1 else values

    def done(value):
        latest[:] = [value]
        return value

    def like(*shape, kind=bf16):
        return jax.ShapeDtypeStruct(shape, kind)

    def around(value, shift):
        return along(value, [(i, (i + shift) % 4) for i in range(4)])

    def rows_at(i, value, length):
        out = like(length, value.shape[1])
        return copy_call(
            lambda n, a, o: [(view(a[0], (at(n, i), length), (0, value.shape[1])), o[0])],
            [out],
            starts,
            value,
        )[0]

    def columns_at(i, value):
        out = like(value.shape[0], eighth)
        return copy_call(
            lambda n, a, o: [(view(a[0], (0, value.shape[0]), (at(n, i), eighth)), o[0])],
            [out],
            starts,
            value,
        )[0]

    def side_by_side(*values):
        widths = [v.shape[1] for v in values]
        length = values[0].shape[0]
        return copy_call(
            lambda n, a, o: [
                (a[i], view(o[0], (0, length), (sum(widths[:i]), widths[i])))
                for i in range(len(values))
            ],
            [like(length, sum(widths))],
            starts,
            *values,
        )[0]

    def tokens_of(i, value, got):
        return copy_call(
            lambda n, a, o: [
                (view(a[0], (0, rows), (at(n, i), eighth)), view(o[0], (0, rows), (0, eighth))),
                (a[1], view(o[0], (rows, rows), (0, eighth))),
            ],
            [like(both, eighth)],
            starts,
            value,
            got,
        )[0]

    up_sent = kernel_call(up_sent_kernel, [like(number, size, kvq)], up)[0]
    up_all = lax.all_to_all(
        done(up_sent), ("fsdp", "own"), split_axis=0, concat_axis=0, tiled=True
    ).reshape(number * size, kvq)
    down_got = swap(done(rows_at(2, step(down), eighth)), "own")
    packet_here = done(
        kernel_call(packet_kernel, [like(rows, kv + size)], step(cotangent), token_adapter)[0]
    )
    packet = swap(packet_here, "own")
    down_piece = done(
        copy_call(
            lambda n, a, o: [
                (view(a[0], (at(n, 0), eighth), (0, size)), view(o[0], (0, eighth), (0, size))),
                (a[1], view(o[0], (0, eighth), (size, size))),
            ],
            [like(eighth, wide)],
            starts,
            down,
            step(down_got),
        )[0]
    )
    down_near = along(down_piece, NEIGHBOURS)
    x_got = [swap(done(columns_at(2, step(tokens))), "own")]
    weight_here = done(rows_at(0, step(frozen_value_weight), eighth))
    weight_near = along(weight_here, NEIGHBOURS)
    dy_half, ids, dy_quarter = kernel_call(
        unpack_kernel,
        [like(both, kv), like(both, size), like(both, kvq)],
        packet_here,
        step(packet),
        scalars=flags,
    )
    done(dy_quarter)
    down_near, x_got[0] = step(down_near, x_got[0])
    crossing = done(side_by_side(down_piece, down_near))
    down_crossed = along(crossing, MIDDLE)
    down_other = swap(crossing, "rep")
    x_mine = done(tokens_of(0, tokens, step(x_got[0])))
    x_in = [along(x_mine, INWARD)]
    compact = like(both, size, kind=f32)
    up_all = step(up_all)
    back_part = done(kernel_call(back_kernel, [compact], ids, dy_quarter, up_all)[0])
    back_tp = swap(back_part, "tp")
    back_part = done(kernel_call(add_kernel, [compact], back_part, step(back_tp))[0])
    back_got = swap(back_part, "own")
    crossing = done(side_by_side(weight_here, step(weight_near)))
    weight_crossed = along(crossing, MIDDLE)
    sent, down_other = step(frozen_value_weight, down_other)
    weight_other = done(rows_at(1, sent, eighth))
    weight_near_other = swap(step(weight_near), "rep")
    back_wide, back_sent = kernel_call(
        back_end_kernel,
        [like(both, number * size), like(both, wide)],
        ids,
        back_part,
        step(back_got),
        scalars=numbers,
    )
    back_in = along(done(back_sent), INWARD)
    down_crossed = done(step(down_crossed))
    down_outer = along(down_crossed, OUTWARD)
    sent, weight_near_other = step(tokens, weight_near_other)
    x_got.append(swap(done(columns_at(3, sent)), "own"))
    dy_tp = swap(step(dy_half), "tp")
    dy_line = done(
        kernel_call(dy_line_kernel, [like(both, 2 * kv)], dy_half, dy_tp, scalars=places)[0]
    )

    def to_middle(half):
        x_in[half] = step(x_in[half])
        sums = kernel_call(
            to_middle_kernel,
            [like(eighth, 2 * wide)],
            x_both[half],
            back_wide,
            x_in[half],
            back_in_wide,
        )[0]
        return along(done(sums), MIDDLE)

    def to_end(half, crossed):
        sums = kernel_call(
            to_end_kernel, [like(eighth, wide)], x_both[half], back_wide, step(crossed)
        )[0]
        return along(done(sums), OUTWARD)

    def finish(half, crossed, outer, *others):
        outer, *_ = step(outer, x_mine, *others)
        here, there = kernel_call(
            finish_kernel,
            [like(eighth, size)] * 2,
            x_both[half],
            back_wide,
            x_in[half],
            back_in_wide,
            crossed,
            outer,
        )
        return done(here), there

    def far_of(crossed, outer):
        out = like(*crossed.shape)
        return kernel_call(far_kernel, [out], crossed, outer, scalars=flags)[0]

    back_in_wide = done(
        kernel_call(
            spread_in_kernel, [like(both, number * size)], step(back_in), scalars=numbers
        )[0]
    )
    x_both = [x_mine]
    middle = [to_middle(0)]
    x_both.append(done(tokens_of(1, tokens, step(x_got[1]))))
    x_other = x_both[1]
    x_in.append(along(x_other, INWARD))
    weight_crossed = done(step(weight_crossed))
    weight_outer = along(weight_crossed, OUTWARD)
    down_far = done(far_of(down_crossed, step(down_outer)))
    down_far_other = swap(down_far, "rep")
    middle.append(to_middle(1))
    outward = [to_end(0, middle[0])]
    weight_far = done(far_of(weight_crossed, step(weight_outer)))
    weight_far_other = swap(weight_far, "rep")
    half_grad = [like(rows, eighth)] * 2
    dx_mine, dx_sent = kernel_call(
        dx_kernel,
        half_grad,
        step(dy_line),
        back_wide,
        weight_here,
        weight_near,
        weight_far,
        down_piece,
        down_near,
        down_far,
    )
    dx_mine_got = swap(done(dx_sent), "own")

    low_part = done(
        kernel_call(
            low_kernel,
            [compact],
            ids,
            x_mine,
            x_other,
            down_piece,
            down_near,
            down_far,
            down_other,
            step(down_far_other),
            scalars=numbers,
        )[0]
    )
    low_tp = swap(low_part, "tp")
    grad_here, grad_sent = finish(0, middle[0], outward[0])
    blocks = [like(2, both, cols, kind=f32)] * 2
    y_first = kernel_call(
        y_kernel, blocks, step(x_mine), weight_here, weight_near, weight_far, scalars=flags
    )
    done(y_first[0])
    low_tp, dx_mine_got = step(low_tp, dx_mine_got)
    low_part = done(kernel_call(add_kernel, [compact], low_part, low_tp)[0])
    low_got = swap(low_part, "own")
    outward.append(to_end(1, middle[1]))
    low_got = step(low_got)
    grad_got = swap(lax.optimization_barrier((grad_sent, low_got))[0], "own")
    delta, *up_parts = kernel_call(
        low_end_kernel,
        [like(both, kvq)] + [like(wide, kvq)] * 4,
        ids,
        low_part,
        low_got,
        up_all,
        dy_quarter,
        scalars=numbers,
    )
    done(delta)
    up_got = [around(up_parts[k], k) for k in (1, 2, 3)]
    dx_other, dx_sent = kernel_call(
        dx_kernel,
        half_grad,
        dy_line,
        back_wide,
        weight_other,
        weight_near_other,
        step(weight_far_other),
        down_other,
        down_far_other,
    )
    dx_other_got = swap(done(dx_sent), "own")
    grad_last, grad_sent = finish(1, middle[1], outward[1])
    grad_last_got = swap(grad_sent, "own")
    up_got = step(*up_got)
    up_mine, up_theirs = kernel_call(
        up_sum_kernel, [like(size, kvq)] * 2, up_parts[0], *up_got, scalars=numbers
    )
    up_theirs = swap(done(up_theirs), "own")
    y_keep, y_sent = kernel_call(
        y_kernel,
        blocks,
        step(x_other),
        weight_other,
        weight_near_other,
        weight_far_other,
        *y_first,
        scalars=flags,
    )
    y_got = swap(done(y_sent), "tp")
    y_here, y_sent = kernel_call(
        y_sum_kernel,
        [like(2, rows, cols, kind=f32), like(2, rows, cols)],
        y_keep,
        step(y_got),
        delta,
        scalars=flags,
    )
    y_got = swap(done(y_sent), "own")

    def in_place(axis, out, *pieces):
        def plan(n, a, o):
            spans = [[(0, length) for length in out.shape] for _ in range(4)]
            for i in range(4):
                spans[i][axis] = (at(n, i), eighth)
            return [(a[i], view(o[0], *spans[i])) for i in range(4)]

        return copy_call(plan, [out], starts, *pieces)[0]

    dx_other_got, _ = step(dx_other_got, dx_mine)
    input_grad = done(
        in_place(1, like(rows, width), dx_mine, dx_other, dx_mine_got, dx_other_got)
    )
    projected = done(kernel_call(y_end_kernel, [like(rows, kv)], y_here, step(y_got))[0])
    down_gradient = done(
        in_place(
            0, like(width, size), grad_here, grad_last, grad_got, step(grad_last_got)
        )[None]
    )
    up_gradient = kernel_call(
        up_place_kernel, [like(size, kv)], up_mine, step(up_theirs), scalars=flags
    )[0][None]
    return (projected, input_grad, down_gradient, up_gradient)


def body_routed(
    tokens,
    cotangent,
    frozen_value_weight,
    adapter_down_weight,
    adapter_up_weight,
    token_adapter,
    rank_step_count,
):
    rows, width_halved = tokens.shape
    half_kv = cotangent.shape[1]
    owning_adapters = lax.axis_size(("fsdp", "own"))
    greatest_rank = 3 * rows // (2 * owning_adapters)
    ids = token_adapter[:, 0]
    table = (ids[:, None] == jnp.arange(owning_adapters, dtype=jnp.int32)[None, :]).astype(
        f32
    )
    order = jnp.arange(rows, dtype=jnp.int32)
    earlier = (order[:, None] > order[None, :]).astype(f32)
    before = jnp.dot(earlier, table, precision=lax.Precision.HIGHEST)
    place = jnp.sum(before * table, axis=1).astype(jnp.int32)
    slot = ids * greatest_rank + place
    source_rows = jnp.full((owning_adapters * greatest_rank,), rows, jnp.int32).at[slot].set(order)
    padded_x = jnp.concatenate([tokens, jnp.zeros((1, width_halved), bf16)], axis=0)
    padded_dy = jnp.concatenate([cotangent, jnp.zeros((1, half_kv), bf16)], axis=0)
    send_x = jnp.take(padded_x, source_rows, axis=0)
    send_dy = jnp.take(padded_dy, source_rows, axis=0)
    recv_x, recv_dy = (
        lax.all_to_all(
            send_x.reshape(owning_adapters, greatest_rank, width_halved),
            ("fsdp", "own"),
            split_axis=0,
            concat_axis=0,
            tiled=True,
        ),
        lax.all_to_all(
            send_dy.reshape(owning_adapters, greatest_rank, half_kv),
            ("fsdp", "own"),
            split_axis=0,
            concat_axis=0,
            tiled=True,
        ),
    )
    flat_x = recv_x.reshape(owning_adapters * greatest_rank, width_halved)
    flat_dy = recv_dy.reshape(owning_adapters * greatest_rank, half_kv)
    dy_full = lax.all_gather(cotangent, "tp", axis=1, tiled=True)
    whole = lax.all_gather(frozen_value_weight, "fsdp", axis=1, tiled=True)
    partial_y = jnp.dot(tokens, whole, preferred_element_type=f32)
    base_dx = contract_final_axis(dy_full, whole)
    base_y = lax.psum_scatter(partial_y, "tp", scatter_dimension=1, tiled=True)
    down_matrix = adapter_down_weight[0]
    up_matrix = adapter_up_weight[0]
    part_low = jnp.dot(flat_x, down_matrix, preferred_element_type=f32)
    part_back = contract_final_axis(flat_dy, up_matrix)
    low_sum, back_sum = lax.psum((part_low, part_back), "tp")
    width_rank = down_matrix.shape[1]
    rank = width_rank // 8 * rank_step_count[lax.axis_index(("fsdp", "own"))]
    keep = jnp.arange(width_rank, dtype=jnp.int32)[None, :] < rank
    scale = 16.0 / rank.astype(f32)
    low = jnp.where(keep, low_sum, 0.0).astype(bf16)
    backward_pass = (scale * jnp.where(keep, back_sum, 0.0)).astype(bf16)
    delta = (scale * jnp.dot(low, up_matrix, preferred_element_type=f32)).astype(
        bf16
    )
    adapter_input_gradient = contract_final_axis(backward_pass, down_matrix).astype(bf16)
    down_gradient = contract_first(flat_x, backward_pass).astype(bf16)[None]
    up_gradient = (scale * contract_first(low, flat_dy)).astype(bf16)[None]
    home_delta, home_dx = (
        lax.all_to_all(
            delta.reshape(owning_adapters, greatest_rank, half_kv),
            ("fsdp", "own"),
            split_axis=0,
            concat_axis=0,
            tiled=True,
        ),
        lax.all_to_all(
            adapter_input_gradient.reshape(owning_adapters, greatest_rank, width_halved),
            ("fsdp", "own"),
            split_axis=0,
            concat_axis=0,
            tiled=True,
        ),
    )
    adapter_delta_rows = jnp.take(
        home_delta.reshape(owning_adapters * greatest_rank, half_kv), slot, axis=0
    )
    input_gradient_rows = jnp.take(
        home_dx.reshape(owning_adapters * greatest_rank, width_halved), slot, axis=0
    )
    projected = (base_y + adapter_delta_rows.astype(f32)).astype(bf16)
    input_grad = (base_dx + input_gradient_rows.astype(f32)).astype(bf16)
    return (projected, input_grad, down_gradient, up_gradient)


def solution(mesh):
    placed = (
        P(("rep", "fsdp", "own"), "tp"),
        P(("rep", "fsdp", "own"), "tp"),
        P("tp", "fsdp"),
        P(("fsdp", "own"), "tp", None),
        P(("fsdp", "own"), None, "tp"),
        P(("rep", "fsdp", "own"), None),
        P(),
    )
    line = mesh.shape["fsdp"] == 4 and mesh.shape["own"] == 2 and mesh.shape["rep"] == 2
    return jax.shard_map(
        body_line if line else body_routed,
        mesh=mesh,
        in_specs=placed,
        out_specs=(
            P(("rep", "fsdp", "own"), "tp"),
            P(("rep", "fsdp", "own"), "tp"),
            P(("rep", "fsdp", "own"), "tp", None),
            P(("rep", "fsdp", "own"), None, "tp"),
        ),
        check_vma=False,
    )
```

```python
import jax
import jax.numpy as jnp
from jax import lax
from jax.experimental import pallas as pl
from jax.experimental.pallas import tpu as pltpu
from jax.sharding import PartitionSpec as P

bf16 = jnp.bfloat16
f32 = jnp.float32


def contract_first(left, right):
    return lax.dot_general(
        left, right, (((0,), (0,)), ((), ())), preferred_element_type=f32
    )


def contract_final_axis(left, right):
    return lax.dot_general(
        left, right, (((1,), (1,)), ((), ())), preferred_element_type=f32
    )


def matmul(left, right):
    return jnp.dot(left, right, preferred_element_type=f32)


PAIR = [(0, 1), (1, 0)]
NEIGHBOURS = [(0, 1), (1, 0), (2, 3), (3, 2)]
MIDDLE = [(1, 2), (2, 1)]
OUTWARD = [(1, 0), (2, 3)]
INWARD = [(0, 1), (3, 2)]


def swap(value, axis):
    return lax.ppermute(value, axis, PAIR)


def along(value, pairs):
    return lax.ppermute(value, "fsdp", pairs)


def kernel_call(body, outs, *operands, scalars=None, scratch=(), space=pltpu.VMEM):
    specs = [pl.BlockSpec(memory_space=space)] * len(operands)
    if scalars is not None:
        operands = (scalars, *operands)
        specs = [pl.BlockSpec(memory_space=pltpu.SMEM), *specs]
    return pl.pallas_call(
        body,
        out_shape=list(outs),
        in_specs=specs,
        out_specs=[pl.BlockSpec(memory_space=pltpu.VMEM)] * len(outs),
        scratch_shapes=list(scratch),
        compiler_params=pltpu.CompilerParams(vmem_limit_bytes=28 * 2**20),
        cost_estimate=pl.CostEstimate(flops=0, bytes_accessed=0, transcendentals=0),
    )(*operands)


def copy_call(plan, outs, scalars, *operands):
    count = len(plan(None, [None] * len(operands), [None] * len(outs)))

    def body(numbers, *refs):
        sems = refs[-1]
        pairs = plan(numbers, refs[: len(operands)], refs[len(operands) : -1])
        copies = [pltpu.make_async_copy(a, b, sems.at[i]) for i, (a, b) in enumerate(pairs)]
        for copy in copies:
            copy.start()
        for copy in copies:
            copy.wait()

    return kernel_call(
        body,
        outs,
        *operands,
        scalars=scalars,
        scratch=[pltpu.SemaphoreType.DMA((count,))],
        space=pl.ANY,
    )


def view(ref, *spans):
    if ref is None:
        return None
    index = tuple(
        pl.ds(start if isinstance(start, int) else pl.multiple_of(start, 128), size)
        for start, size in spans
    )
    return ref.at[index]


def at(numbers, i):
    return None if numbers is None else numbers[i]


def ranks_of(ranks, ids):
    total = jnp.zeros(ids.shape, f32)
    for a in range(ranks.shape[0]):
        total = jnp.where(ids == a, ranks[a].astype(f32), total)
    return total


def kept(ids, ranks, value):
    rank = ranks_of(ranks, ids)
    column = lax.broadcasted_iota(jnp.int32, value.shape, 1).astype(f32)
    return jnp.where(column < rank, value, 0.0), 16.0 / rank


def roll_rows(value):
    half = value.shape[0] // 2
    return jnp.concatenate([value[half:], value[:half]], axis=0)


def back_kernel(ids, dy, up, out):
    size = out.shape[1]
    token = ids[...].astype(f32)
    for i in range(0, up.shape[0] // size, 2):
        both = contract_final_axis(dy[...], up[i * size : (i + 2) * size, :])
        for j in (0, 1):
            part = jnp.where(token == i + j, both[:, j * size : (j + 1) * size], 0.0)
            out[...] = part if i + j == 0 else out[...] + part


def spread_into(out, token, value, order):
    size = value.shape[1]
    for i in range(out.shape[1] // size):
        a = order[i].astype(f32)
        out[:, i * size : (i + 1) * size] = jnp.where(token == a, value, 0.0).astype(bf16)


def back_end_kernel(numbers, ids, part, got, wide, sent):
    token = ids[...].astype(f32)
    count = numbers.shape[0] // 3
    ranks, order = [numbers[i] for i in range(count)], [numbers[count + i] for i in range(count)]
    value, scale = kept(token, jnp.stack(ranks), part[...] + roll_rows(got[...]))
    value = (scale * value).astype(bf16)
    size = value.shape[1]
    sent[:, :size] = value
    sent[:, size:] = ids[...]
    spread_into(wide, token, value.astype(f32), order)


def spread_in_kernel(numbers, packet, wide):
    size = packet.shape[1] // 2
    count = numbers.shape[0] // 3
    order = [numbers[count + i] for i in range(count)]
    spread_into(wide, packet[:, size:].astype(f32), packet[:, :size].astype(f32), order)


def low_kernel(numbers, ids, x_mine, x_other, own, near, far, own_near_other, far_other, out):
    size = out.shape[1]
    wide = 2 * size
    token = ids[...].astype(f32)
    mine = [own[...], near[...], far[:, :wide], far[:, wide:]]
    other = [
        own_near_other[:, :wide],
        own_near_other[:, wide:],
        far_other[:, :wide],
        far_other[:, wide:],
    ]
    for i in range(4):
        both = matmul(x_mine[...], mine[i]) + matmul(x_other[...], other[i])
        for j in (0, 1):
            place = numbers[numbers.shape[0] // 3 + 2 * i + j].astype(f32)
            part = jnp.where(token == place, both[:, j * size : (j + 1) * size], 0.0)
            out[...] = part if i + j == 0 else out[...] + part


def low_end_kernel(numbers, ids, part, got, up, dy, delta, *grads):
    token = ids[...].astype(f32)
    count = numbers.shape[0] // 3
    size = part.shape[1]
    ranks = jnp.stack([numbers[i] for i in range(count)])
    value, scale = kept(token, ranks, part[...] + roll_rows(got[...]))
    value = value.astype(bf16).astype(f32)

    def pair(first, second):
        return jnp.concatenate(
            [jnp.where(token == a, value, 0.0) for a in (first, second)], axis=1
        ).astype(bf16)

    total = 0.0
    for i, out in enumerate(grads):
        places = [numbers[2 * count + 2 * i + j].astype(f32) for j in (0, 1)]
        out[...] = contract_first(pair(*places), dy[...]).astype(bf16)
        total += matmul(pair(2 * i, 2 * i + 1), up[2 * i * size : 2 * (i + 1) * size, :])
    delta[...] = (scale[:, :1] * total).astype(bf16)


def to_middle_kernel(x_here, back, x_in, back_in, out):
    half = back.shape[1] // 2
    sums = contract_first(x_here[...], back[:, half:])
    out[...] = (sums + contract_first(x_in[...], back_in[:, half:])).astype(bf16)


def to_end_kernel(x_here, back, crossed, out):
    wide = out.shape[1]
    sums = contract_first(x_here[...], back[:, wide : 2 * wide])
    out[...] = (sums + crossed[:, wide:].astype(f32)).astype(bf16)


def finish_kernel(x_here, back, x_in, back_in, crossed, outer, here, there):
    size = here.shape[1]
    wide = 2 * size
    sums = contract_first(x_here[...], back[:, :wide])
    sums += contract_first(x_in[...], back_in[:, :wide])
    sums += crossed[:, :wide].astype(f32) + outer[...].astype(f32)
    here[...] = sums[:, :size].astype(bf16)
    there[...] = sums[:, size:].astype(bf16)


def up_sent_kernel(up, out):
    cols = out.shape[2]
    for i in range(out.shape[0]):
        out[i] = up[:, (i % 2) * cols : (i % 2 + 1) * cols]


def packet_kernel(cotangent, adapters, out):
    rows, kv = cotangent.shape
    size = out.shape[1] - kv
    out[:, :kv] = cotangent[...]
    numbers = jnp.broadcast_to(adapters[...].astype(f32), (rows, size))
    out[:, kv:] = numbers.astype(bf16)


def unpack_kernel(flags, here, there, half, ids, quarter):
    rows = here.shape[0]
    kv = half.shape[1]
    cols = quarter.shape[1]
    span = pl.ds(pl.multiple_of(flags[3] * cols, 128), cols)
    for i, packet in enumerate((here, there)):
        place = slice(i * rows, (i + 1) * rows)
        half[place] = packet[:, :kv]
        ids[place] = packet[:, kv:]
        quarter[place] = packet[:, span]


def dy_line_kernel(places, here, got, out):
    cols = out.shape[1] // 4
    for i in range(4):
        place = places[i]
        span = pl.ds(pl.multiple_of((place % 2) * cols, 128), cols)
        own = place // 2 == places[4]

        @pl.when(own)
        def _():
            out[:, i * cols : (i + 1) * cols] = here[:, span]

        @pl.when(jnp.logical_not(own))
        def _():
            out[:, i * cols : (i + 1) * cols] = got[:, span]


def far_kernel(flags, crossed, outer, out):
    @pl.when(flags[4] == 1)
    def _():
        out[...] = crossed[...]

    @pl.when(flags[4] == 0)
    def _():
        out[...] = outer[...]


def up_sum_kernel(numbers, first, second, third, fourth, here, there):
    count = numbers.shape[0] // 3
    size = here.shape[0]
    for i, out in enumerate((here, there)):
        adapter = numbers[count + i]
        rank = jnp.float32(1.0)
        for a in range(count):
            rank = jnp.where(adapter == a, numbers[a].astype(f32), rank)
        span = slice(i * size, (i + 1) * size)
        part = sum(v[span, :].astype(f32) for v in (first, second, third, fourth))
        out[...] = (jnp.full(part.shape, 16.0, f32) / rank * part).astype(bf16)


def up_place_kernel(flags, here, there, out):
    cols = here.shape[1]
    out[:, pl.ds(pl.multiple_of(flags[3] * cols, 128), cols)] = here[...]
    out[:, pl.ds(pl.multiple_of((1 - flags[3]) * cols, 128), cols)] = there[...]


def add_kernel(left, right, out):
    out[...] = left[...] + right[...]


def dx_kernel(dy, back, own, near, far, *rest):
    *adapter, here, there = rest
    rows, width = here.shape
    cols = own.shape[1]
    tile = min(cols, width)
    for t in range(width // tile):
        span = slice(t * tile, (t + 1) * tile)
        base = contract_final_axis(dy[:, :cols], own[span, :])
        base += contract_final_axis(dy[:, cols : 2 * cols], near[span, :])
        base += contract_final_axis(dy[:, 2 * cols :], far[span, :])
        lora, start = 0.0, 0
        for piece in adapter:
            stop = start + piece.shape[1]
            lora += contract_final_axis(back[:, start:stop], piece[span, :])
            start = stop
        total = (base + lora.astype(bf16).astype(f32)).astype(bf16)
        here[:, span] = total[:rows]
        there[:, span] = total[rows:]


def y_kernel(flags, tokens, own, near, far, *rest):
    *before, keep, send = rest
    cols = own.shape[1]

    def store(pair, first, part):
        mine = flags[0] == (1 if pair else 0)
        for i in (0, 1):
            place = (first + i) % 2
            block = matmul(tokens[...], part(i))

            @pl.when(mine)
            def _():
                keep[place] = block + before[0][place] if before else block

            @pl.when(jnp.logical_not(mine))
            def _():
                send[place] = block + before[1][place] if before else block

    store(True, flags[1], lambda i: (own, near)[i][...])
    store(False, flags[2], lambda i: far[:, i * cols : (i + 1) * cols])


def y_sum_kernel(flags, keep, got, delta, here, there):
    rows = here.shape[1]
    for i in (0, 1):
        added = jnp.where(flags[3] == i, delta[...].astype(f32), 0.0)
        total = keep[i] + got[i] + added
        here[i] = total[:rows]
        there[i] = total[rows:].astype(bf16)


def y_end_kernel(here, got, out):
    cols = here.shape[2]
    for i in (0, 1):
        out[:, i * cols : (i + 1) * cols] = (here[i] + got[i].astype(f32)).astype(bf16)


def body_line(
    tokens,
    cotangent,
    frozen_value_weight,
    adapter_down_weight,
    adapter_up_weight,
    token_adapter,
    rank_step_count,
):
    rows, width = tokens.shape
    kv = cotangent.shape[1]
    cols = frozen_value_weight.shape[1]
    down = adapter_down_weight[0]
    up = adapter_up_weight[0]
    size = down.shape[1]
    wide = 2 * size
    quarter = width // 2
    eighth = quarter // 2
    kvq = kv // 2
    both = 2 * rows
    z, x = lax.axis_index("fsdp"), lax.axis_index("own")
    y, c = lax.axis_index("rep"), lax.axis_index("tp")
    first_pair = z < 2
    is_middle = (z == 1) | (z == 2)
    line = [z, z + 1 - 2 * (z % 2), jnp.where(first_pair, 2, 1), jnp.where(first_pair, 3, 0)]
    adapters = jnp.stack([2 * t + o for t in line for o in (x, 1 - x)]).astype(jnp.int32)
    number = adapters.shape[0]
    starts = jnp.stack(
        [side * quarter + half * eighth for side in (x, 1 - x) for half in (y, 1 - y)]
    ).astype(jnp.int32)
    ranks = size // 8 * rank_step_count
    ring = jnp.stack([2 * ((z + k) % 4) + o for k in range(4) for o in (x, 1 - x)])
    numbers = jnp.concatenate([ranks, adapters, ring.astype(jnp.int32)])
    flags = jnp.stack([(c == 0) == first_pair, z % 2 == 1, z >= 2, x == 1, is_middle])
    flags = flags.astype(jnp.int32)
    places = jnp.stack([*line, c]).astype(jnp.int32)

    latest = []

    def step(*values):
        if latest:
            values = lax.optimization_barrier((*values, latest[0]))[: len(values)]
        return values[0] if len(values) == 1 else values

    def done(value):
        latest[:] = [value]
        return value

    def like(*shape, kind=bf16):
        return jax.ShapeDtypeStruct(shape, kind)

    def around(value, shift):
        return along(value, [(i, (i + shift) % 4) for i in range(4)])

    def rows_at(i, value, length):
        out = like(length, value.shape[1])
        return copy_call(
            lambda n, a, o: [(view(a[0], (at(n, i), length), (0, value.shape[1])), o[0])],
            [out],
            starts,
            value,
        )[0]

    def columns_at(i, value):
        out = like(value.shape[0], eighth)
        return copy_call(
            lambda n, a, o: [(view(a[0], (0, value.shape[0]), (at(n, i), eighth)), o[0])],
            [out],
            starts,
            value,
        )[0]

    def side_by_side(*values):
        widths = [v.shape[1] for v in values]
        length = values[0].shape[0]
        return copy_call(
            lambda n, a, o: [
                (a[i], view(o[0], (0, length), (sum(widths[:i]), widths[i])))
                for i in range(len(values))
            ],
            [like(length, sum(widths))],
            starts,
            *values,
        )[0]

    def tokens_of(i, value, got):
        return copy_call(
            lambda n, a, o: [
                (view(a[0], (0, rows), (at(n, i), eighth)), view(o[0], (0, rows), (0, eighth))),
                (a[1], view(o[0], (rows, rows), (0, eighth))),
            ],
            [like(both, eighth)],
            starts,
            value,
            got,
        )[0]

    up_sent = kernel_call(up_sent_kernel, [like(number, size, kvq)], up)[0]
    up_all = lax.all_to_all(
        done(up_sent), ("fsdp", "own"), split_axis=0, concat_axis=0, tiled=True
    ).reshape(number * size, kvq)
    down_got = swap(done(rows_at(2, step(down), eighth)), "own")
    packet_here = done(
        kernel_call(packet_kernel, [like(rows, kv + size)], step(cotangent), token_adapter)[0]
    )
    packet = swap(packet_here, "own")
    x_got = [swap(done(columns_at(2, step(tokens))), "own")]
    down_piece = done(
        copy_call(
            lambda n, a, o: [
                (view(a[0], (at(n, 0), eighth), (0, size)), view(o[0], (0, eighth), (0, size))),
                (a[1], view(o[0], (0, eighth), (size, size))),
            ],
            [like(eighth, wide)],
            starts,
            down,
            step(down_got),
        )[0]
    )
    down_near = along(down_piece, NEIGHBOURS)
    packet, up_all = step(packet, up_all)
    dy_half, ids, dy_quarter = kernel_call(
        unpack_kernel,
        [like(both, kv), like(both, size), like(both, kvq)],
        packet_here,
        packet,
        scalars=flags,
    )
    compact = like(both, size, kind=f32)
    back_part = done(kernel_call(back_kernel, [compact], ids, dy_quarter, up_all)[0])
    back_tp = swap(back_part, "tp")
    weight_here = done(rows_at(0, step(frozen_value_weight), eighth))
    weight_near = along(weight_here, NEIGHBOURS)
    back_part = done(kernel_call(add_kernel, [compact], back_part, step(back_tp))[0])
    back_got = swap(back_part, "own")
    down_near, x_got[0] = step(down_near, x_got[0])
    crossing = done(side_by_side(down_piece, down_near))
    down_crossed = along(crossing, MIDDLE)
    down_other = swap(crossing, "rep")
    x_mine = done(tokens_of(0, tokens, step(x_got[0])))
    x_in = [along(x_mine, INWARD)]
    back_wide, back_sent = kernel_call(
        back_end_kernel,
        [like(both, number * size), like(both, wide)],
        ids,
        back_part,
        step(back_got),
        scalars=numbers,
    )
    back_in = along(done(back_sent), INWARD)
    crossing = done(side_by_side(weight_here, step(weight_near)))
    weight_crossed = along(crossing, MIDDLE)
    back_in_wide = done(
        kernel_call(
            spread_in_kernel, [like(both, number * size)], step(back_in), scalars=numbers
        )[0]
    )
    x_got.append(swap(done(columns_at(3, step(tokens))), "own"))
    weight_other = done(rows_at(1, step(frozen_value_weight), eighth))
    down_crossed = done(step(down_crossed))
    down_outer = along(down_crossed, OUTWARD)
    weight_near, down_other = step(weight_near, down_other)
    weight_near_other = swap(done(weight_near), "rep")
    x_other = done(tokens_of(1, tokens, step(x_got[1])))
    x_in.append(along(x_other, INWARD))
    x_both = [x_mine, x_other]

    def to_middle(half):
        x_in[half] = step(x_in[half])
        sums = kernel_call(
            to_middle_kernel,
            [like(eighth, 2 * wide)],
            x_both[half],
            back_wide,
            x_in[half],
            back_in_wide,
        )[0]
        return along(done(sums), MIDDLE)

    def to_end(half, crossed):
        sums = kernel_call(
            to_end_kernel, [like(eighth, wide)], x_both[half], back_wide, step(crossed)
        )[0]
        return along(done(sums), OUTWARD)

    def finish(half, crossed, outer, *others):
        outer, *_ = step(outer, x_mine, *others)
        here, there = kernel_call(
            finish_kernel,
            [like(eighth, size)] * 2,
            x_both[half],
            back_wide,
            x_in[half],
            back_in_wide,
            crossed,
            outer,
        )
        return done(here), there

    def far_of(crossed, outer):
        out = like(*crossed.shape)
        return kernel_call(far_kernel, [out], crossed, outer, scalars=flags)[0]

    middle = [to_middle(0)]
    weight_crossed = done(step(weight_crossed))
    weight_outer = along(weight_crossed, OUTWARD)
    dy_half, weight_near_other = step(dy_half, weight_near_other)
    dy_tp = swap(dy_half, "tp")
    dy_line = done(
        kernel_call(
            dy_line_kernel, [like(both, 2 * kv)], dy_half, step(dy_tp), scalars=places
        )[0]
    )
    down_far = done(far_of(down_crossed, step(down_outer)))
    down_far_other = swap(down_far, "rep")
    middle.append(to_middle(1))
    outward = [to_end(0, middle[0])]
    weight_far = done(far_of(weight_crossed, step(weight_outer)))
    weight_far_other = swap(weight_far, "rep")
    half_grad = [like(rows, eighth)] * 2
    dx_mine, dx_sent = kernel_call(
        dx_kernel,
        half_grad,
        step(dy_line),
        back_wide,
        weight_here,
        weight_near,
        weight_far,
        down_piece,
        down_near,
        down_far,
    )
    dx_mine_got = swap(done(dx_sent), "own")

    low_part = done(
        kernel_call(
            low_kernel,
            [compact],
            ids,
            x_mine,
            x_other,
            down_piece,
            down_near,
            down_far,
            down_other,
            step(down_far_other),
            scalars=numbers,
        )[0]
    )
    low_tp = swap(low_part, "tp")
    grad_here, grad_sent = finish(0, middle[0], outward[0])
    grad_got = swap(grad_sent, "own")
    blocks = [like(2, both, cols, kind=f32)] * 2
    y_first = kernel_call(
        y_kernel, blocks, step(x_mine), weight_here, weight_near, weight_far, scalars=flags
    )
    done(y_first[0])
    low_tp, dx_mine_got = step(low_tp, dx_mine_got)
    low_part = done(kernel_call(add_kernel, [compact], low_part, low_tp)[0])
    low_got = swap(low_part, "own")
    outward.append(to_end(1, middle[1]))
    low_got, grad_got = step(low_got, grad_got)
    delta, *up_parts = kernel_call(
        low_end_kernel,
        [like(both, kvq)] + [like(wide, kvq)] * 4,
        ids,
        low_part,
        low_got,
        up_all,
        dy_quarter,
        scalars=numbers,
    )
    done(delta)
    up_got = [around(up_parts[k], k) for k in (1, 2, 3)]
    dx_other, dx_sent = kernel_call(
        dx_kernel,
        half_grad,
        dy_line,
        back_wide,
        weight_other,
        weight_near_other,
        step(weight_far_other),
        down_other,
        down_far_other,
    )
    dx_other_got = swap(done(dx_sent), "own")
    grad_last, grad_sent = finish(1, middle[1], outward[1])
    grad_last_got = swap(grad_sent, "own")
    up_got = step(*up_got)
    up_mine, up_theirs = kernel_call(
        up_sum_kernel, [like(size, kvq)] * 2, up_parts[0], *up_got, scalars=numbers
    )
    up_theirs = swap(done(up_theirs), "own")
    x_other, dx_other_got = step(x_other, dx_other_got)
    y_keep, y_sent = kernel_call(
        y_kernel,
        blocks,
        x_other,
        weight_other,
        weight_near_other,
        weight_far_other,
        *y_first,
        scalars=flags,
    )
    y_got = swap(done(y_sent), "tp")
    y_got, grad_last_got = step(y_got, grad_last_got)
    y_here, y_sent = kernel_call(
        y_sum_kernel,
        [like(2, rows, cols, kind=f32), like(2, rows, cols)],
        y_keep,
        y_got,
        delta,
        scalars=flags,
    )
    y_got = swap(done(y_sent), "own")

    def in_place(axis, out, *pieces):
        def plan(n, a, o):
            spans = [[(0, length) for length in out.shape] for _ in range(4)]
            for i in range(4):
                spans[i][axis] = (at(n, i), eighth)
            return [(a[i], view(o[0], *spans[i])) for i in range(4)]

        return copy_call(plan, [out], starts, *pieces)[0]

    dx_other_got, _ = step(dx_other_got, dx_mine)
    input_grad = done(
        in_place(1, like(rows, width), dx_mine, dx_other, dx_mine_got, dx_other_got)
    )
    projected = done(kernel_call(y_end_kernel, [like(rows, kv)], y_here, step(y_got))[0])
    down_gradient = done(
        in_place(
            0, like(width, size), grad_here, grad_last, grad_got, step(grad_last_got)
        )[None]
    )
    up_gradient = kernel_call(
        up_place_kernel, [like(size, kv)], up_mine, step(up_theirs), scalars=flags
    )[0][None]
    return (projected, input_grad, down_gradient, up_gradient)


def body_routed(
    tokens,
    cotangent,
    frozen_value_weight,
    adapter_down_weight,
    adapter_up_weight,
    token_adapter,
    rank_step_count,
):
    rows, width_halved = tokens.shape
    half_kv = cotangent.shape[1]
    owning_adapters = lax.axis_size(("fsdp", "own"))
    greatest_rank = 3 * rows // (2 * owning_adapters)
    ids = token_adapter[:, 0]
    table = (ids[:, None] == jnp.arange(owning_adapters, dtype=jnp.int32)[None, :]).astype(
        f32
    )
    order = jnp.arange(rows, dtype=jnp.int32)
    earlier = (order[:, None] > order[None, :]).astype(f32)
    before = jnp.dot(earlier, table, precision=lax.Precision.HIGHEST)
    place = jnp.sum(before * table, axis=1).astype(jnp.int32)
    slot = ids * greatest_rank + place
    source_rows = jnp.full((owning_adapters * greatest_rank,), rows, jnp.int32).at[slot].set(order)
    padded_x = jnp.concatenate([tokens, jnp.zeros((1, width_halved), bf16)], axis=0)
    padded_dy = jnp.concatenate([cotangent, jnp.zeros((1, half_kv), bf16)], axis=0)
    send_x = jnp.take(padded_x, source_rows, axis=0)
    send_dy = jnp.take(padded_dy, source_rows, axis=0)
    recv_x, recv_dy = (
        lax.all_to_all(
            send_x.reshape(owning_adapters, greatest_rank, width_halved),
            ("fsdp", "own"),
            split_axis=0,
            concat_axis=0,
            tiled=True,
        ),
        lax.all_to_all(
            send_dy.reshape(owning_adapters, greatest_rank, half_kv),
            ("fsdp", "own"),
            split_axis=0,
            concat_axis=0,
            tiled=True,
        ),
    )
    flat_x = recv_x.reshape(owning_adapters * greatest_rank, width_halved)
    flat_dy = recv_dy.reshape(owning_adapters * greatest_rank, half_kv)
    dy_full = lax.all_gather(cotangent, "tp", axis=1, tiled=True)
    whole = lax.all_gather(frozen_value_weight, "fsdp", axis=1, tiled=True)
    partial_y = jnp.dot(tokens, whole, preferred_element_type=f32)
    base_dx = contract_final_axis(dy_full, whole)
    base_y = lax.psum_scatter(partial_y, "tp", scatter_dimension=1, tiled=True)
    down_matrix = adapter_down_weight[0]
    up_matrix = adapter_up_weight[0]
    part_low = jnp.dot(flat_x, down_matrix, preferred_element_type=f32)
    part_back = contract_final_axis(flat_dy, up_matrix)
    low_sum, back_sum = lax.psum((part_low, part_back), "tp")
    width_rank = down_matrix.shape[1]
    rank = width_rank // 8 * rank_step_count[lax.axis_index(("fsdp", "own"))]
    keep = jnp.arange(width_rank, dtype=jnp.int32)[None, :] < rank
    scale = 16.0 / rank.astype(f32)
    low = jnp.where(keep, low_sum, 0.0).astype(bf16)
    backward_pass = (scale * jnp.where(keep, back_sum, 0.0)).astype(bf16)
    delta = (scale * jnp.dot(low, up_matrix, preferred_element_type=f32)).astype(
        bf16
    )
    adapter_input_gradient = contract_final_axis(backward_pass, down_matrix).astype(bf16)
    down_gradient = contract_first(flat_x, backward_pass).astype(bf16)[None]
    up_gradient = (scale * contract_first(low, flat_dy)).astype(bf16)[None]
    home_delta, home_dx = (
        lax.all_to_all(
            delta.reshape(owning_adapters, greatest_rank, half_kv),
            ("fsdp", "own"),
            split_axis=0,
            concat_axis=0,
            tiled=True,
        ),
        lax.all_to_all(
            adapter_input_gradient.reshape(owning_adapters, greatest_rank, width_halved),
            ("fsdp", "own"),
            split_axis=0,
            concat_axis=0,
            tiled=True,
        ),
    )
    adapter_delta_rows = jnp.take(
        home_delta.reshape(owning_adapters * greatest_rank, half_kv), slot, axis=0
    )
    input_gradient_rows = jnp.take(
        home_dx.reshape(owning_adapters * greatest_rank, width_halved), slot, axis=0
    )
    projected = (base_y + adapter_delta_rows.astype(f32)).astype(bf16)
    input_grad = (base_dx + input_gradient_rows.astype(f32)).astype(bf16)
    return (projected, input_grad, down_gradient, up_gradient)


def solution(mesh):
    placed = (
        P(("rep", "fsdp", "own"), "tp"),
        P(("rep", "fsdp", "own"), "tp"),
        P("tp", "fsdp"),
        P(("fsdp", "own"), "tp", None),
        P(("fsdp", "own"), None, "tp"),
        P(("rep", "fsdp", "own"), None),
        P(),
    )
    line = mesh.shape["fsdp"] == 4 and mesh.shape["own"] == 2 and mesh.shape["rep"] == 2
    return jax.shard_map(
        body_line if line else body_routed,
        mesh=mesh,
        in_specs=placed,
        out_specs=(
            P(("rep", "fsdp", "own"), "tp"),
            P(("rep", "fsdp", "own"), "tp"),
            P(("rep", "fsdp", "own"), "tp", None),
            P(("rep", "fsdp", "own"), None, "tp"),
        ),
        check_vma=False,
    )
```

```python
import jax
import jax.numpy as jnp
from jax import lax
from jax.experimental import pallas as pl
from jax.experimental.pallas import tpu as pltpu
from jax.sharding import PartitionSpec as P

bf16 = jnp.bfloat16
f32 = jnp.float32


def contract_first(left, right):
    return lax.dot_general(
        left, right, (((0,), (0,)), ((), ())), preferred_element_type=f32
    )


def contract_final_axis(left, right):
    return lax.dot_general(
        left, right, (((1,), (1,)), ((), ())), preferred_element_type=f32
    )


def matmul(left, right):
    return jnp.dot(left, right, preferred_element_type=f32)


PAIR = [(0, 1), (1, 0)]
NEIGHBOURS = [(0, 1), (1, 0), (2, 3), (3, 2)]
MIDDLE = [(1, 2), (2, 1)]
OUTWARD = [(1, 0), (2, 3)]
INWARD = [(0, 1), (3, 2)]


def swap(value, axis):
    return lax.ppermute(value, axis, PAIR)


def along(value, pairs):
    return lax.ppermute(value, "fsdp", pairs)


def kernel_call(body, outs, *operands, scalars=None, scratch=(), space=pltpu.VMEM):
    specs = [pl.BlockSpec(memory_space=space)] * len(operands)
    if scalars is not None:
        operands = (scalars, *operands)
        specs = [pl.BlockSpec(memory_space=pltpu.SMEM), *specs]
    return pl.pallas_call(
        body,
        out_shape=list(outs),
        in_specs=specs,
        out_specs=[pl.BlockSpec(memory_space=pltpu.VMEM)] * len(outs),
        scratch_shapes=list(scratch),
        compiler_params=pltpu.CompilerParams(vmem_limit_bytes=28 * 2**20),
        cost_estimate=pl.CostEstimate(flops=0, bytes_accessed=0, transcendentals=0),
    )(*operands)


def copy_call(plan, outs, scalars, *operands):
    count = len(plan(None, [None] * len(operands), [None] * len(outs)))

    def body(numbers, *refs):
        sems = refs[-1]
        pairs = plan(numbers, refs[: len(operands)], refs[len(operands) : -1])
        copies = [pltpu.make_async_copy(a, b, sems.at[i]) for i, (a, b) in enumerate(pairs)]
        for copy in copies:
            copy.start()
        for copy in copies:
            copy.wait()

    return kernel_call(
        body,
        outs,
        *operands,
        scalars=scalars,
        scratch=[pltpu.SemaphoreType.DMA((count,))],
        space=pl.ANY,
    )


def view(ref, *spans):
    if ref is None:
        return None
    index = tuple(
        pl.ds(start if isinstance(start, int) else pl.multiple_of(start, 128), size)
        for start, size in spans
    )
    return ref.at[index]


def at(numbers, i):
    return None if numbers is None else numbers[i]


def ranks_of(ranks, ids):
    total = jnp.zeros(ids.shape, f32)
    for a in range(ranks.shape[0]):
        total = jnp.where(ids == a, ranks[a].astype(f32), total)
    return total


def kept(ids, ranks, value):
    rank = ranks_of(ranks, ids)
    column = lax.broadcasted_iota(jnp.int32, value.shape, 1).astype(f32)
    return jnp.where(column < rank, value, 0.0), 16.0 / rank


def roll_rows(value):
    half = value.shape[0] // 2
    return jnp.concatenate([value[half:], value[:half]], axis=0)


def back_kernel(ids, dy, up, out):
    size = out.shape[1]
    token = ids[...].astype(f32)
    for i in range(0, up.shape[0] // size, 2):
        both = contract_final_axis(dy[...], up[i * size : (i + 2) * size, :])
        for j in (0, 1):
            part = jnp.where(token == i + j, both[:, j * size : (j + 1) * size], 0.0)
            out[...] = part if i + j == 0 else out[...] + part


def spread_into(out, token, value, order):
    size = value.shape[1]
    for i in range(out.shape[1] // size):
        a = order[i].astype(f32)
        out[:, i * size : (i + 1) * size] = jnp.where(token == a, value, 0.0).astype(bf16)


def back_end_kernel(numbers, ids, part, got, wide, sent):
    token = ids[...].astype(f32)
    count = numbers.shape[0] // 3
    ranks, order = [numbers[i] for i in range(count)], [numbers[count + i] for i in range(count)]
    value, scale = kept(token, jnp.stack(ranks), part[...] + roll_rows(got[...]))
    value = (scale * value).astype(bf16)
    size = value.shape[1]
    sent[:, :size] = value
    sent[:, size:] = ids[...]
    spread_into(wide, token, value.astype(f32), order)


def spread_in_kernel(numbers, packet, wide):
    size = packet.shape[1] // 2
    count = numbers.shape[0] // 3
    order = [numbers[count + i] for i in range(count)]
    spread_into(wide, packet[:, size:].astype(f32), packet[:, :size].astype(f32), order)


def low_kernel(numbers, ids, x_mine, x_other, own, near, far, own_near_other, far_other, out):
    size = out.shape[1]
    wide = 2 * size
    token = ids[...].astype(f32)
    mine = [own[...], near[...], far[:, :wide], far[:, wide:]]
    other = [
        own_near_other[:, :wide],
        own_near_other[:, wide:],
        far_other[:, :wide],
        far_other[:, wide:],
    ]
    for i in range(4):
        both = matmul(x_mine[...], mine[i]) + matmul(x_other[...], other[i])
        for j in (0, 1):
            place = numbers[numbers.shape[0] // 3 + 2 * i + j].astype(f32)
            part = jnp.where(token == place, both[:, j * size : (j + 1) * size], 0.0)
            out[...] = part if i + j == 0 else out[...] + part


def low_end_kernel(numbers, ids, part, got, up, dy, delta, *grads):
    token = ids[...].astype(f32)
    count = numbers.shape[0] // 3
    size = part.shape[1]
    ranks = jnp.stack([numbers[i] for i in range(count)])
    value, scale = kept(token, ranks, part[...] + roll_rows(got[...]))
    value = value.astype(bf16).astype(f32)

    def pair(first, second):
        return jnp.concatenate(
            [jnp.where(token == a, value, 0.0) for a in (first, second)], axis=1
        ).astype(bf16)

    total = 0.0
    for i, out in enumerate(grads):
        places = [numbers[2 * count + 2 * i + j].astype(f32) for j in (0, 1)]
        out[...] = contract_first(pair(*places), dy[...]).astype(bf16)
        total += matmul(pair(2 * i, 2 * i + 1), up[2 * i * size : 2 * (i + 1) * size, :])
    delta[...] = (scale[:, :1] * total).astype(bf16)


def to_middle_kernel(x_here, back, x_in, back_in, out):
    half = back.shape[1] // 2
    sums = contract_first(x_here[...], back[:, half:])
    out[...] = (sums + contract_first(x_in[...], back_in[:, half:])).astype(bf16)


def to_end_kernel(x_here, back, crossed, out):
    wide = out.shape[1]
    sums = contract_first(x_here[...], back[:, wide : 2 * wide])
    out[...] = (sums + crossed[:, wide:].astype(f32)).astype(bf16)


def finish_kernel(x_here, back, x_in, back_in, crossed, outer, here, there):
    size = here.shape[1]
    wide = 2 * size
    sums = contract_first(x_here[...], back[:, :wide])
    sums += contract_first(x_in[...], back_in[:, :wide])
    sums += crossed[:, :wide].astype(f32) + outer[...].astype(f32)
    here[...] = sums[:, :size].astype(bf16)
    there[...] = sums[:, size:].astype(bf16)


def up_sent_kernel(up, out):
    cols = out.shape[2]
    for i in range(out.shape[0]):
        out[i] = up[:, (i % 2) * cols : (i % 2 + 1) * cols]


def packet_kernel(cotangent, adapters, out):
    rows, kv = cotangent.shape
    size = out.shape[1] - kv
    out[:, :kv] = cotangent[...]
    numbers = jnp.broadcast_to(adapters[...].astype(f32), (rows, size))
    out[:, kv:] = numbers.astype(bf16)


def unpack_kernel(flags, here, there, half, ids, quarter):
    rows = here.shape[0]
    kv = half.shape[1]
    cols = quarter.shape[1]
    span = pl.ds(pl.multiple_of(flags[3] * cols, 128), cols)
    for i, packet in enumerate((here, there)):
        place = slice(i * rows, (i + 1) * rows)
        half[place] = packet[:, :kv]
        ids[place] = packet[:, kv:]
        quarter[place] = packet[:, span]


def dy_line_kernel(places, here, got, out):
    cols = out.shape[1] // 4
    for i in range(4):
        place = places[i]
        span = pl.ds(pl.multiple_of((place % 2) * cols, 128), cols)
        own = place // 2 == places[4]

        @pl.when(own)
        def _():
            out[:, i * cols : (i + 1) * cols] = here[:, span]

        @pl.when(jnp.logical_not(own))
        def _():
            out[:, i * cols : (i + 1) * cols] = got[:, span]


def far_kernel(flags, crossed, outer, out):
    @pl.when(flags[4] == 1)
    def _():
        out[...] = crossed[...]

    @pl.when(flags[4] == 0)
    def _():
        out[...] = outer[...]


def up_sum_kernel(numbers, first, second, third, fourth, here, there):
    count = numbers.shape[0] // 3
    size = here.shape[0]
    for i, out in enumerate((here, there)):
        adapter = numbers[count + i]
        rank = jnp.float32(1.0)
        for a in range(count):
            rank = jnp.where(adapter == a, numbers[a].astype(f32), rank)
        span = slice(i * size, (i + 1) * size)
        part = sum(v[span, :].astype(f32) for v in (first, second, third, fourth))
        out[...] = (jnp.full(part.shape, 16.0, f32) / rank * part).astype(bf16)


def up_place_kernel(flags, here, there, out):
    cols = here.shape[1]
    out[:, pl.ds(pl.multiple_of(flags[3] * cols, 128), cols)] = here[...]
    out[:, pl.ds(pl.multiple_of((1 - flags[3]) * cols, 128), cols)] = there[...]


def add_kernel(left, right, out):
    out[...] = left[...] + right[...]


def dx_kernel(dy, back, own, near, far, *rest):
    *adapter, here, there = rest
    rows, width = here.shape
    cols = own.shape[1]
    tile = min(cols, width)
    for t in range(width // tile):
        span = slice(t * tile, (t + 1) * tile)
        base = contract_final_axis(dy[:, :cols], own[span, :])
        base += contract_final_axis(dy[:, cols : 2 * cols], near[span, :])
        base += contract_final_axis(dy[:, 2 * cols :], far[span, :])
        lora, start = 0.0, 0
        for piece in adapter:
            stop = start + piece.shape[1]
            lora += contract_final_axis(back[:, start:stop], piece[span, :])
            start = stop
        total = (base + lora.astype(bf16).astype(f32)).astype(bf16)
        here[:, span] = total[:rows]
        there[:, span] = total[rows:]


def y_kernel(flags, tokens, own, near, far, *rest):
    *before, keep, send = rest
    cols = own.shape[1]

    def store(pair, first, part):
        mine = flags[0] == (1 if pair else 0)
        for i in (0, 1):
            place = (first + i) % 2
            block = matmul(tokens[...], part(i))

            @pl.when(mine)
            def _():
                keep[place] = block + before[0][place] if before else block

            @pl.when(jnp.logical_not(mine))
            def _():
                send[place] = block + before[1][place] if before else block

    store(True, flags[1], lambda i: (own, near)[i][...])
    store(False, flags[2], lambda i: far[:, i * cols : (i + 1) * cols])


def y_sum_kernel(flags, keep, got, delta, here, there):
    rows = here.shape[1]
    for i in (0, 1):
        added = jnp.where(flags[3] == i, delta[...].astype(f32), 0.0)
        total = keep[i] + got[i] + added
        here[i] = total[:rows]
        there[i] = total[rows:].astype(bf16)


def y_end_kernel(here, got, out):
    cols = here.shape[2]
    for i in (0, 1):
        out[:, i * cols : (i + 1) * cols] = (here[i] + got[i].astype(f32)).astype(bf16)


def body_line(
    tokens,
    cotangent,
    frozen_value_weight,
    adapter_down_weight,
    adapter_up_weight,
    token_adapter,
    rank_step_count,
):
    rows, width = tokens.shape
    kv = cotangent.shape[1]
    cols = frozen_value_weight.shape[1]
    down = adapter_down_weight[0]
    up = adapter_up_weight[0]
    size = down.shape[1]
    wide = 2 * size
    quarter = width // 2
    eighth = quarter // 2
    kvq = kv // 2
    both = 2 * rows
    z, x = lax.axis_index("fsdp"), lax.axis_index("own")
    y, c = lax.axis_index("rep"), lax.axis_index("tp")
    first_pair = z < 2
    is_middle = (z == 1) | (z == 2)
    line = [z, z + 1 - 2 * (z % 2), jnp.where(first_pair, 2, 1), jnp.where(first_pair, 3, 0)]
    adapters = jnp.stack([2 * t + o for t in line for o in (x, 1 - x)]).astype(jnp.int32)
    number = adapters.shape[0]
    starts = jnp.stack(
        [side * quarter + half * eighth for side in (x, 1 - x) for half in (y, 1 - y)]
    ).astype(jnp.int32)
    ranks = size // 8 * rank_step_count
    ring = jnp.stack([2 * ((z + k) % 4) + o for k in range(4) for o in (x, 1 - x)])
    numbers = jnp.concatenate([ranks, adapters, ring.astype(jnp.int32)])
    flags = jnp.stack([(c == 0) == first_pair, z % 2 == 1, z >= 2, x == 1, is_middle])
    flags = flags.astype(jnp.int32)
    places = jnp.stack([*line, c]).astype(jnp.int32)

    latest = []

    def step(*values):
        if latest:
            values = lax.optimization_barrier((*values, latest[0]))[: len(values)]
        return values[0] if len(values) == 1 else values

    def done(value):
        latest[:] = [value]
        return value

    def like(*shape, kind=bf16):
        return jax.ShapeDtypeStruct(shape, kind)

    def around(value, shift):
        return along(value, [(i, (i + shift) % 4) for i in range(4)])

    def rows_at(i, value, length):
        out = like(length, value.shape[1])
        return copy_call(
            lambda n, a, o: [(view(a[0], (at(n, i), length), (0, value.shape[1])), o[0])],
            [out],
            starts,
            value,
        )[0]

    def columns_at(i, value):
        out = like(value.shape[0], eighth)
        return copy_call(
            lambda n, a, o: [(view(a[0], (0, value.shape[0]), (at(n, i), eighth)), o[0])],
            [out],
            starts,
            value,
        )[0]

    def side_by_side(*values):
        widths = [v.shape[1] for v in values]
        length = values[0].shape[0]
        return copy_call(
            lambda n, a, o: [
                (a[i], view(o[0], (0, length), (sum(widths[:i]), widths[i])))
                for i in range(len(values))
            ],
            [like(length, sum(widths))],
            starts,
            *values,
        )[0]

    def tokens_of(i, value, got):
        return copy_call(
            lambda n, a, o: [
                (view(a[0], (0, rows), (at(n, i), eighth)), view(o[0], (0, rows), (0, eighth))),
                (a[1], view(o[0], (rows, rows), (0, eighth))),
            ],
            [like(both, eighth)],
            starts,
            value,
            got,
        )[0]

    down_got = swap(done(rows_at(2, down, eighth)), "own")
    packet_here = done(
        kernel_call(packet_kernel, [like(rows, kv + size)], step(cotangent), token_adapter)[0]
    )
    packet = swap(packet_here, "own")
    down_got, packet = step(down_got, packet)
    down_piece = done(
        copy_call(
            lambda n, a, o: [
                (view(a[0], (at(n, 0), eighth), (0, size)), view(o[0], (0, eighth), (0, size))),
                (a[1], view(o[0], (0, eighth), (size, size))),
            ],
            [like(eighth, wide)],
            starts,
            down,
            down_got,
        )[0]
    )
    down_near = along(down_piece, NEIGHBOURS)
    up_sent = kernel_call(up_sent_kernel, [like(number, size, kvq)], step(up))[0]
    up_all = lax.all_to_all(
        done(up_sent), ("fsdp", "own"), split_axis=0, concat_axis=0, tiled=True
    ).reshape(number * size, kvq)
    dy_half, ids, dy_quarter = kernel_call(
        unpack_kernel,
        [like(both, kv), like(both, size), like(both, kvq)],
        packet_here,
        step(packet),
        scalars=flags,
    )
    done(dy_quarter)
    x_got = [swap(done(columns_at(2, step(tokens))), "own")]
    weight_here = done(rows_at(0, step(frozen_value_weight), eighth))
    weight_near = along(weight_here, NEIGHBOURS)
    crossing = done(side_by_side(down_piece, step(down_near)))
    down_crossed = along(crossing, MIDDLE)
    compact = like(both, size, kind=f32)
    back_part = done(
        kernel_call(back_kernel, [compact], ids, dy_quarter, step(up_all))[0]
    )
    back_tp = swap(back_part, "tp")
    down_other = swap(crossing, "rep")
    crossing = done(side_by_side(weight_here, step(weight_near)))
    weight_crossed = along(crossing, MIDDLE)
    back_part = done(kernel_call(add_kernel, [compact], back_part, step(back_tp))[0])
    back_got = swap(back_part, "own")
    back_got, x_got[0] = step(back_got, x_got[0])
    back_wide, back_sent = kernel_call(
        back_end_kernel,
        [like(both, number * size), like(both, wide)],
        ids,
        back_part,
        back_got,
        scalars=numbers,
    )
    back_in = along(done(back_sent), INWARD)
    x_got.append(swap(done(columns_at(3, step(tokens))), "own"))
    x_mine = done(tokens_of(0, tokens, step(x_got[0])))
    back_in, down_crossed = step(back_in, down_crossed)
    back_in_wide = done(
        kernel_call(
            spread_in_kernel, [like(both, number * size)], back_in, scalars=numbers
        )[0]
    )
    down_outer = along(down_crossed, OUTWARD)
    x_in = [along(step(x_mine), INWARD)]
    weight_other = done(rows_at(1, step(frozen_value_weight), eighth))
    weight_near, down_other = step(weight_near, down_other)
    weight_near_other = swap(done(weight_near), "rep")
    x_other = done(tokens_of(1, tokens, step(x_got[1])))
    x_in.append(along(x_other, INWARD))
    x_both = [x_mine, x_other]

    def to_middle(half):
        x_in[half] = step(x_in[half])
        sums = kernel_call(
            to_middle_kernel,
            [like(eighth, 2 * wide)],
            x_both[half],
            back_wide,
            x_in[half],
            back_in_wide,
        )[0]
        return along(done(sums), MIDDLE)

    def to_end(half, crossed):
        sums = kernel_call(
            to_end_kernel, [like(eighth, wide)], x_both[half], back_wide, step(crossed)
        )[0]
        return along(done(sums), OUTWARD)

    def finish(half, crossed, outer, *others):
        outer, *_ = step(outer, x_mine, *others)
        here, there = kernel_call(
            finish_kernel,
            [like(eighth, size)] * 2,
            x_both[half],
            back_wide,
            x_in[half],
            back_in_wide,
            crossed,
            outer,
        )
        return done(here), there

    def far_of(crossed, outer):
        out = like(*crossed.shape)
        return kernel_call(far_kernel, [out], crossed, outer, scalars=flags)[0]

    middle = [to_middle(0)]
    weight_crossed = done(step(weight_crossed))
    weight_outer = along(weight_crossed, OUTWARD)
    dy_half, weight_near_other = step(dy_half, weight_near_other)
    dy_tp = swap(dy_half, "tp")
    dy_line = done(
        kernel_call(
            dy_line_kernel, [like(both, 2 * kv)], dy_half, step(dy_tp), scalars=places
        )[0]
    )
    down_far = done(far_of(down_crossed, step(down_outer)))
    down_far_other = swap(down_far, "rep")
    middle.append(to_middle(1))
    outward = [to_end(0, middle[0])]
    weight_far = done(far_of(weight_crossed, step(weight_outer)))
    weight_far_other = swap(weight_far, "rep")
    half_grad = [like(rows, eighth)] * 2
    dx_mine, dx_sent = kernel_call(
        dx_kernel,
        half_grad,
        step(dy_line),
        back_wide,
        weight_here,
        weight_near,
        weight_far,
        down_piece,
        down_near,
        down_far,
    )
    dx_mine_got = swap(done(dx_sent), "own")

    low_part = done(
        kernel_call(
            low_kernel,
            [compact],
            ids,
            x_mine,
            x_other,
            down_piece,
            down_near,
            down_far,
            down_other,
            step(down_far_other),
            scalars=numbers,
        )[0]
    )
    low_tp = swap(low_part, "tp")
    grad_here, grad_sent = finish(0, middle[0], outward[0])
    grad_got = swap(grad_sent, "own")
    blocks = [like(2, both, cols, kind=f32)] * 2
    y_first = kernel_call(
        y_kernel, blocks, step(x_mine), weight_here, weight_near, weight_far, scalars=flags
    )
    done(y_first[0])
    low_tp, dx_mine_got = step(low_tp, dx_mine_got)
    low_part = done(kernel_call(add_kernel, [compact], low_part, low_tp)[0])
    low_got = swap(low_part, "own")
    outward.append(to_end(1, middle[1]))
    low_got, grad_got = step(low_got, grad_got)
    delta, *up_parts = kernel_call(
        low_end_kernel,
        [like(both, kvq)] + [like(wide, kvq)] * 4,
        ids,
        low_part,
        low_got,
        up_all,
        dy_quarter,
        scalars=numbers,
    )
    done(delta)
    up_got = [around(up_parts[k], k) for k in (1, 2, 3)]
    dx_other, dx_sent = kernel_call(
        dx_kernel,
        half_grad,
        dy_line,
        back_wide,
        weight_other,
        weight_near_other,
        step(weight_far_other),
        down_other,
        down_far_other,
    )
    dx_other_got = swap(done(dx_sent), "own")
    grad_last, grad_sent = finish(1, middle[1], outward[1])
    grad_last_got = swap(grad_sent, "own")
    up_got = step(*up_got)
    up_mine, up_theirs = kernel_call(
        up_sum_kernel, [like(size, kvq)] * 2, up_parts[0], *up_got, scalars=numbers
    )
    up_theirs = swap(done(up_theirs), "own")
    x_other, dx_other_got = step(x_other, dx_other_got)
    y_keep, y_sent = kernel_call(
        y_kernel,
        blocks,
        x_other,
        weight_other,
        weight_near_other,
        weight_far_other,
        *y_first,
        scalars=flags,
    )
    y_got = swap(done(y_sent), "tp")
    y_got, grad_last_got = step(y_got, grad_last_got)
    y_here, y_sent = kernel_call(
        y_sum_kernel,
        [like(2, rows, cols, kind=f32), like(2, rows, cols)],
        y_keep,
        y_got,
        delta,
        scalars=flags,
    )
    y_got = swap(done(y_sent), "own")

    def in_place(axis, out, *pieces):
        def plan(n, a, o):
            spans = [[(0, length) for length in out.shape] for _ in range(4)]
            for i in range(4):
                spans[i][axis] = (at(n, i), eighth)
            return [(a[i], view(o[0], *spans[i])) for i in range(4)]

        return copy_call(plan, [out], starts, *pieces)[0]

    dx_other_got, _ = step(dx_other_got, dx_mine)
    input_grad = done(
        in_place(1, like(rows, width), dx_mine, dx_other, dx_mine_got, dx_other_got)
    )
    projected = done(kernel_call(y_end_kernel, [like(rows, kv)], y_here, step(y_got))[0])
    down_gradient = done(
        in_place(
            0, like(width, size), grad_here, grad_last, grad_got, step(grad_last_got)
        )[None]
    )
    up_gradient = kernel_call(
        up_place_kernel, [like(size, kv)], up_mine, step(up_theirs), scalars=flags
    )[0][None]
    return (projected, input_grad, down_gradient, up_gradient)


def body_routed(
    tokens,
    cotangent,
    frozen_value_weight,
    adapter_down_weight,
    adapter_up_weight,
    token_adapter,
    rank_step_count,
):
    rows, width_halved = tokens.shape
    half_kv = cotangent.shape[1]
    owning_adapters = lax.axis_size(("fsdp", "own"))
    greatest_rank = 3 * rows // (2 * owning_adapters)
    ids = token_adapter[:, 0]
    table = (ids[:, None] == jnp.arange(owning_adapters, dtype=jnp.int32)[None, :]).astype(
        f32
    )
    order = jnp.arange(rows, dtype=jnp.int32)
    earlier = (order[:, None] > order[None, :]).astype(f32)
    before = jnp.dot(earlier, table, precision=lax.Precision.HIGHEST)
    place = jnp.sum(before * table, axis=1).astype(jnp.int32)
    slot = ids * greatest_rank + place
    source_rows = jnp.full((owning_adapters * greatest_rank,), rows, jnp.int32).at[slot].set(order)
    padded_x = jnp.concatenate([tokens, jnp.zeros((1, width_halved), bf16)], axis=0)
    padded_dy = jnp.concatenate([cotangent, jnp.zeros((1, half_kv), bf16)], axis=0)
    send_x = jnp.take(padded_x, source_rows, axis=0)
    send_dy = jnp.take(padded_dy, source_rows, axis=0)
    recv_x, recv_dy = (
        lax.all_to_all(
            send_x.reshape(owning_adapters, greatest_rank, width_halved),
            ("fsdp", "own"),
            split_axis=0,
            concat_axis=0,
            tiled=True,
        ),
        lax.all_to_all(
            send_dy.reshape(owning_adapters, greatest_rank, half_kv),
            ("fsdp", "own"),
            split_axis=0,
            concat_axis=0,
            tiled=True,
        ),
    )
    flat_x = recv_x.reshape(owning_adapters * greatest_rank, width_halved)
    flat_dy = recv_dy.reshape(owning_adapters * greatest_rank, half_kv)
    dy_full = lax.all_gather(cotangent, "tp", axis=1, tiled=True)
    whole = lax.all_gather(frozen_value_weight, "fsdp", axis=1, tiled=True)
    partial_y = jnp.dot(tokens, whole, preferred_element_type=f32)
    base_dx = contract_final_axis(dy_full, whole)
    base_y = lax.psum_scatter(partial_y, "tp", scatter_dimension=1, tiled=True)
    down_matrix = adapter_down_weight[0]
    up_matrix = adapter_up_weight[0]
    part_low = jnp.dot(flat_x, down_matrix, preferred_element_type=f32)
    part_back = contract_final_axis(flat_dy, up_matrix)
    low_sum, back_sum = lax.psum((part_low, part_back), "tp")
    width_rank = down_matrix.shape[1]
    rank = width_rank // 8 * rank_step_count[lax.axis_index(("fsdp", "own"))]
    keep = jnp.arange(width_rank, dtype=jnp.int32)[None, :] < rank
    scale = 16.0 / rank.astype(f32)
    low = jnp.where(keep, low_sum, 0.0).astype(bf16)
    backward_pass = (scale * jnp.where(keep, back_sum, 0.0)).astype(bf16)
    delta = (scale * jnp.dot(low, up_matrix, preferred_element_type=f32)).astype(
        bf16
    )
    adapter_input_gradient = contract_final_axis(backward_pass, down_matrix).astype(bf16)
    down_gradient = contract_first(flat_x, backward_pass).astype(bf16)[None]
    up_gradient = (scale * contract_first(low, flat_dy)).astype(bf16)[None]
    home_delta, home_dx = (
        lax.all_to_all(
            delta.reshape(owning_adapters, greatest_rank, half_kv),
            ("fsdp", "own"),
            split_axis=0,
            concat_axis=0,
            tiled=True,
        ),
        lax.all_to_all(
            adapter_input_gradient.reshape(owning_adapters, greatest_rank, width_halved),
            ("fsdp", "own"),
            split_axis=0,
            concat_axis=0,
            tiled=True,
        ),
    )
    adapter_delta_rows = jnp.take(
        home_delta.reshape(owning_adapters * greatest_rank, half_kv), slot, axis=0
    )
    input_gradient_rows = jnp.take(
        home_dx.reshape(owning_adapters * greatest_rank, width_halved), slot, axis=0
    )
    projected = (base_y + adapter_delta_rows.astype(f32)).astype(bf16)
    input_grad = (base_dx + input_gradient_rows.astype(f32)).astype(bf16)
    return (projected, input_grad, down_gradient, up_gradient)


def solution(mesh):
    placed = (
        P(("rep", "fsdp", "own"), "tp"),
        P(("rep", "fsdp", "own"), "tp"),
        P("tp", "fsdp"),
        P(("fsdp", "own"), "tp", None),
        P(("fsdp", "own"), None, "tp"),
        P(("rep", "fsdp", "own"), None),
        P(),
    )
    line = mesh.shape["fsdp"] == 4 and mesh.shape["own"] == 2 and mesh.shape["rep"] == 2
    return jax.shard_map(
        body_line if line else body_routed,
        mesh=mesh,
        in_specs=placed,
        out_specs=(
            P(("rep", "fsdp", "own"), "tp"),
            P(("rep", "fsdp", "own"), "tp"),
            P(("rep", "fsdp", "own"), "tp", None),
            P(("rep", "fsdp", "own"), None, "tp"),
        ),
        check_vma=False,
    )
```

```python
import jax
import jax.numpy as jnp
from jax import lax
from jax.experimental import pallas as pl
from jax.experimental.pallas import tpu as pltpu
from jax.sharding import PartitionSpec as P

bf16 = jnp.bfloat16
f32 = jnp.float32


def contract_first(left, right):
    return lax.dot_general(
        left, right, (((0,), (0,)), ((), ())), preferred_element_type=f32
    )


def contract_final_axis(left, right):
    return lax.dot_general(
        left, right, (((1,), (1,)), ((), ())), preferred_element_type=f32
    )


def matmul(left, right):
    return jnp.dot(left, right, preferred_element_type=f32)


PAIR = [(0, 1), (1, 0)]
NEIGHBOURS = [(0, 1), (1, 0), (2, 3), (3, 2)]
MIDDLE = [(1, 2), (2, 1)]
OUTWARD = [(1, 0), (2, 3)]
INWARD = [(0, 1), (3, 2)]


def swap(value, axis):
    return lax.ppermute(value, axis, PAIR)


def along(value, pairs):
    return lax.ppermute(value, "fsdp", pairs)


def kernel_call(body, outs, *operands, scalars=None, scratch=(), space=pltpu.VMEM):
    specs = [pl.BlockSpec(memory_space=space)] * len(operands)
    if scalars is not None:
        operands = (scalars, *operands)
        specs = [pl.BlockSpec(memory_space=pltpu.SMEM), *specs]
    return pl.pallas_call(
        body,
        out_shape=list(outs),
        in_specs=specs,
        out_specs=[pl.BlockSpec(memory_space=pltpu.VMEM)] * len(outs),
        scratch_shapes=list(scratch),
        compiler_params=pltpu.CompilerParams(vmem_limit_bytes=28 * 2**20),
        cost_estimate=pl.CostEstimate(flops=0, bytes_accessed=0, transcendentals=0),
    )(*operands)


def copy_call(plan, outs, scalars, *operands):
    count = len(plan(None, [None] * len(operands), [None] * len(outs)))

    def body(numbers, *refs):
        sems = refs[-1]
        pairs = plan(numbers, refs[: len(operands)], refs[len(operands) : -1])
        copies = [pltpu.make_async_copy(a, b, sems.at[i]) for i, (a, b) in enumerate(pairs)]
        for copy in copies:
            copy.start()
        for copy in copies:
            copy.wait()

    return kernel_call(
        body,
        outs,
        *operands,
        scalars=scalars,
        scratch=[pltpu.SemaphoreType.DMA((count,))],
        space=pl.ANY,
    )


def view(ref, *spans):
    if ref is None:
        return None
    index = tuple(
        pl.ds(start if isinstance(start, int) else pl.multiple_of(start, 128), size)
        for start, size in spans
    )
    return ref.at[index]


def at(numbers, i):
    return None if numbers is None else numbers[i]


def ranks_of(ranks, ids):
    total = jnp.zeros(ids.shape, f32)
    for a in range(ranks.shape[0]):
        total = jnp.where(ids == a, ranks[a].astype(f32), total)
    return total


def kept(ids, ranks, value):
    rank = ranks_of(ranks, ids)
    column = lax.broadcasted_iota(jnp.int32, value.shape, 1).astype(f32)
    return jnp.where(column < rank, value, 0.0), 16.0 / rank


def roll_rows(value):
    half = value.shape[0] // 2
    return jnp.concatenate([value[half:], value[:half]], axis=0)


def back_kernel(ids, dy, up, out):
    size = out.shape[1]
    token = ids[...].astype(f32)
    for i in range(0, up.shape[0] // size, 2):
        both = contract_final_axis(dy[...], up[i * size : (i + 2) * size, :])
        for j in (0, 1):
            part = jnp.where(token == i + j, both[:, j * size : (j + 1) * size], 0.0)
            out[...] = part if i + j == 0 else out[...] + part


def spread_into(out, token, value, order):
    size = value.shape[1]
    for i in range(out.shape[1] // size):
        a = order[i].astype(f32)
        out[:, i * size : (i + 1) * size] = jnp.where(token == a, value, 0.0).astype(bf16)


def back_end_kernel(numbers, ids, part, got, wide, sent):
    token = ids[...].astype(f32)
    count = numbers.shape[0] // 3
    ranks, order = [numbers[i] for i in range(count)], [numbers[count + i] for i in range(count)]
    value, scale = kept(token, jnp.stack(ranks), part[...] + roll_rows(got[...]))
    value = (scale * value).astype(bf16)
    size = value.shape[1]
    sent[:, :size] = value
    sent[:, size:] = ids[...]
    spread_into(wide, token, value.astype(f32), order)


def spread_in_kernel(numbers, packet, wide):
    size = packet.shape[1] // 2
    count = numbers.shape[0] // 3
    order = [numbers[count + i] for i in range(count)]
    spread_into(wide, packet[:, size:].astype(f32), packet[:, :size].astype(f32), order)


def low_kernel(numbers, ids, x_mine, x_other, own, near, far, own_near_other, far_other, out):
    size = out.shape[1]
    wide = 2 * size
    token = ids[...].astype(f32)
    mine = [own[...], near[...], far[:, :wide], far[:, wide:]]
    other = [
        own_near_other[:, :wide],
        own_near_other[:, wide:],
        far_other[:, :wide],
        far_other[:, wide:],
    ]
    for i in range(4):
        both = matmul(x_mine[...], mine[i]) + matmul(x_other[...], other[i])
        for j in (0, 1):
            place = numbers[numbers.shape[0] // 3 + 2 * i + j].astype(f32)
            part = jnp.where(token == place, both[:, j * size : (j + 1) * size], 0.0)
            out[...] = part if i + j == 0 else out[...] + part


def low_end_kernel(numbers, ids, part, got, up, dy, delta, *grads):
    token = ids[...].astype(f32)
    count = numbers.shape[0] // 3
    size = part.shape[1]
    ranks = jnp.stack([numbers[i] for i in range(count)])
    value, scale = kept(token, ranks, part[...] + roll_rows(got[...]))
    value = value.astype(bf16).astype(f32)

    def pair(first, second):
        return jnp.concatenate(
            [jnp.where(token == a, value, 0.0) for a in (first, second)], axis=1
        ).astype(bf16)

    total = 0.0
    for i, out in enumerate(grads):
        places = [numbers[2 * count + 2 * i + j].astype(f32) for j in (0, 1)]
        out[...] = contract_first(pair(*places), dy[...]).astype(bf16)
        total += matmul(pair(2 * i, 2 * i + 1), up[2 * i * size : 2 * (i + 1) * size, :])
    delta[...] = (scale[:, :1] * total).astype(bf16)


def to_middle_kernel(x_here, back, x_in, back_in, out):
    half = back.shape[1] // 2
    sums = contract_first(x_here[...], back[:, half:])
    out[...] = (sums + contract_first(x_in[...], back_in[:, half:])).astype(bf16)


def to_end_kernel(x_here, back, crossed, out):
    wide = out.shape[1]
    sums = contract_first(x_here[...], back[:, wide : 2 * wide])
    out[...] = (sums + crossed[:, wide:].astype(f32)).astype(bf16)


def finish_kernel(x_here, back, x_in, back_in, crossed, outer, here, there):
    size = here.shape[1]
    wide = 2 * size
    sums = contract_first(x_here[...], back[:, :wide])
    sums += contract_first(x_in[...], back_in[:, :wide])
    sums += crossed[:, :wide].astype(f32) + outer[...].astype(f32)
    here[...] = sums[:, :size].astype(bf16)
    there[...] = sums[:, size:].astype(bf16)


def up_sent_kernel(up, out):
    cols = out.shape[2]
    for i in range(out.shape[0]):
        out[i] = up[:, (i % 2) * cols : (i % 2 + 1) * cols]


def packet_kernel(cotangent, adapters, out):
    rows, kv = cotangent.shape
    size = out.shape[1] - kv
    out[:, :kv] = cotangent[...]
    numbers = jnp.broadcast_to(adapters[...].astype(f32), (rows, size))
    out[:, kv:] = numbers.astype(bf16)


def unpack_kernel(flags, here, there, half, ids, quarter):
    rows = here.shape[0]
    kv = half.shape[1]
    cols = quarter.shape[1]
    span = pl.ds(pl.multiple_of(flags[3] * cols, 128), cols)
    for i, packet in enumerate((here, there)):
        place = slice(i * rows, (i + 1) * rows)
        half[place] = packet[:, :kv]
        ids[place] = packet[:, kv:]
        quarter[place] = packet[:, span]


def dy_line_kernel(places, here, got, out):
    cols = out.shape[1] // 4
    for i in range(4):
        place = places[i]
        span = pl.ds(pl.multiple_of((place % 2) * cols, 128), cols)
        own = place // 2 == places[4]

        @pl.when(own)
        def _():
            out[:, i * cols : (i + 1) * cols] = here[:, span]

        @pl.when(jnp.logical_not(own))
        def _():
            out[:, i * cols : (i + 1) * cols] = got[:, span]


def far_kernel(flags, crossed, outer, out):
    @pl.when(flags[4] == 1)
    def _():
        out[...] = crossed[...]

    @pl.when(flags[4] == 0)
    def _():
        out[...] = outer[...]


def up_sum_kernel(numbers, first, second, third, fourth, here, there):
    count = numbers.shape[0] // 3
    size = here.shape[0]
    for i, out in enumerate((here, there)):
        adapter = numbers[count + i]
        rank = jnp.float32(1.0)
        for a in range(count):
            rank = jnp.where(adapter == a, numbers[a].astype(f32), rank)
        span = slice(i * size, (i + 1) * size)
        part = sum(v[span, :].astype(f32) for v in (first, second, third, fourth))
        out[...] = (jnp.full(part.shape, 16.0, f32) / rank * part).astype(bf16)


def up_place_kernel(flags, here, there, out):
    cols = here.shape[1]
    out[:, pl.ds(pl.multiple_of(flags[3] * cols, 128), cols)] = here[...]
    out[:, pl.ds(pl.multiple_of((1 - flags[3]) * cols, 128), cols)] = there[...]


def add_kernel(left, right, out):
    out[...] = left[...] + right[...]


def dx_kernel(dy, back, own, near, far, *rest):
    *adapter, here, there = rest
    rows, width = here.shape
    cols = own.shape[1]
    tile = min(cols, width)
    for t in range(width // tile):
        span = slice(t * tile, (t + 1) * tile)
        base = contract_final_axis(dy[:, :cols], own[span, :])
        base += contract_final_axis(dy[:, cols : 2 * cols], near[span, :])
        base += contract_final_axis(dy[:, 2 * cols :], far[span, :])
        lora, start = 0.0, 0
        for piece in adapter:
            stop = start + piece.shape[1]
            lora += contract_final_axis(back[:, start:stop], piece[span, :])
            start = stop
        total = (base + lora.astype(bf16).astype(f32)).astype(bf16)
        here[:, span] = total[:rows]
        there[:, span] = total[rows:]


def y_kernel(flags, tokens, own, near, far, *rest):
    *before, keep, send = rest
    cols = own.shape[1]

    def store(pair, first, part):
        mine = flags[0] == (1 if pair else 0)
        for i in (0, 1):
            place = (first + i) % 2
            block = matmul(tokens[...], part(i))

            @pl.when(mine)
            def _():
                keep[place] = block + before[0][place] if before else block

            @pl.when(jnp.logical_not(mine))
            def _():
                send[place] = block + before[1][place] if before else block

    store(True, flags[1], lambda i: (own, near)[i][...])
    store(False, flags[2], lambda i: far[:, i * cols : (i + 1) * cols])


def y_sum_kernel(flags, keep, got, delta, here, there):
    rows = here.shape[1]
    for i in (0, 1):
        added = jnp.where(flags[3] == i, delta[...].astype(f32), 0.0)
        total = keep[i] + got[i] + added
        here[i] = total[:rows]
        there[i] = total[rows:].astype(bf16)


def y_end_kernel(here, got, out):
    cols = here.shape[2]
    for i in (0, 1):
        out[:, i * cols : (i + 1) * cols] = (here[i] + got[i].astype(f32)).astype(bf16)


def body_line(
    tokens,
    cotangent,
    frozen_value_weight,
    adapter_down_weight,
    adapter_up_weight,
    token_adapter,
    rank_step_count,
):
    rows, width = tokens.shape
    kv = cotangent.shape[1]
    cols = frozen_value_weight.shape[1]
    down = adapter_down_weight[0]
    up = adapter_up_weight[0]
    size = down.shape[1]
    wide = 2 * size
    quarter = width // 2
    eighth = quarter // 2
    kvq = kv // 2
    both = 2 * rows
    z, x = lax.axis_index("fsdp"), lax.axis_index("own")
    y, c = lax.axis_index("rep"), lax.axis_index("tp")
    first_pair = z < 2
    is_middle = (z == 1) | (z == 2)
    line = [z, z + 1 - 2 * (z % 2), jnp.where(first_pair, 2, 1), jnp.where(first_pair, 3, 0)]
    adapters = jnp.stack([2 * t + o for t in line for o in (x, 1 - x)]).astype(jnp.int32)
    number = adapters.shape[0]
    starts = jnp.stack(
        [side * quarter + half * eighth for side in (x, 1 - x) for half in (y, 1 - y)]
    ).astype(jnp.int32)
    ranks = size // 8 * rank_step_count
    ring = jnp.stack([2 * ((z + k) % 4) + o for k in range(4) for o in (x, 1 - x)])
    numbers = jnp.concatenate([ranks, adapters, ring.astype(jnp.int32)])
    flags = jnp.stack([(c == 0) == first_pair, z % 2 == 1, z >= 2, x == 1, is_middle])
    flags = flags.astype(jnp.int32)
    places = jnp.stack([*line, c]).astype(jnp.int32)

    latest = []

    def step(*values):
        if latest:
            values = lax.optimization_barrier((*values, latest[0]))[: len(values)]
        return values[0] if len(values) == 1 else values

    def done(value):
        latest[:] = [value]
        return value

    def like(*shape, kind=bf16):
        return jax.ShapeDtypeStruct(shape, kind)

    def around(value, shift):
        return along(value, [(i, (i + shift) % 4) for i in range(4)])

    def rows_at(i, value, length):
        out = like(length, value.shape[1])
        return copy_call(
            lambda n, a, o: [(view(a[0], (at(n, i), length), (0, value.shape[1])), o[0])],
            [out],
            starts,
            value,
        )[0]

    def columns_at(i, value):
        out = like(value.shape[0], eighth)
        return copy_call(
            lambda n, a, o: [(view(a[0], (0, value.shape[0]), (at(n, i), eighth)), o[0])],
            [out],
            starts,
            value,
        )[0]

    def side_by_side(*values):
        widths = [v.shape[1] for v in values]
        length = values[0].shape[0]
        return copy_call(
            lambda n, a, o: [
                (a[i], view(o[0], (0, length), (sum(widths[:i]), widths[i])))
                for i in range(len(values))
            ],
            [like(length, sum(widths))],
            starts,
            *values,
        )[0]

    def tokens_of(i, value, got):
        return copy_call(
            lambda n, a, o: [
                (view(a[0], (0, rows), (at(n, i), eighth)), view(o[0], (0, rows), (0, eighth))),
                (a[1], view(o[0], (rows, rows), (0, eighth))),
            ],
            [like(both, eighth)],
            starts,
            value,
            got,
        )[0]

    up_sent = kernel_call(up_sent_kernel, [like(number, size, kvq)], up)[0]
    up_all = lax.all_to_all(
        done(up_sent), ("fsdp", "own"), split_axis=0, concat_axis=0, tiled=True
    ).reshape(number * size, kvq)
    down_got = swap(done(rows_at(2, step(down), eighth)), "own")
    packet_here = done(
        kernel_call(packet_kernel, [like(rows, kv + size)], step(cotangent), token_adapter)[0]
    )
    packet = swap(packet_here, "own")
    x_got = [swap(done(columns_at(2, step(tokens))), "own")]
    down_piece = done(
        copy_call(
            lambda n, a, o: [
                (view(a[0], (at(n, 0), eighth), (0, size)), view(o[0], (0, eighth), (0, size))),
                (a[1], view(o[0], (0, eighth), (size, size))),
            ],
            [like(eighth, wide)],
            starts,
            down,
            step(down_got),
        )[0]
    )
    down_near = along(down_piece, NEIGHBOURS)
    packet, up_all = step(packet, up_all)
    dy_half, ids, dy_quarter = kernel_call(
        unpack_kernel,
        [like(both, kv), like(both, size), like(both, kvq)],
        packet_here,
        packet,
        scalars=flags,
    )
    compact = like(both, size, kind=f32)
    back_part = done(kernel_call(back_kernel, [compact], ids, dy_quarter, up_all)[0])
    back_tp = swap(back_part, "tp")
    weight_here = done(rows_at(0, step(frozen_value_weight), eighth))
    weight_near = along(weight_here, NEIGHBOURS)
    back_part = done(kernel_call(add_kernel, [compact], back_part, step(back_tp))[0])
    back_got = swap(back_part, "own")
    down_near, x_got[0] = step(down_near, x_got[0])
    crossing = done(side_by_side(down_piece, down_near))
    down_crossed = along(crossing, MIDDLE)
    down_other = swap(crossing, "rep")
    back_wide, back_sent = kernel_call(
        back_end_kernel,
        [like(both, number * size), like(both, wide)],
        ids,
        back_part,
        step(back_got),
        scalars=numbers,
    )
    back_in = along(done(back_sent), INWARD)
    crossing = done(side_by_side(weight_here, step(weight_near)))
    weight_crossed = along(crossing, MIDDLE)
    x_got.append(swap(done(columns_at(3, step(tokens))), "own"))
    back_in_wide = done(
        kernel_call(
            spread_in_kernel, [like(both, number * size)], step(back_in), scalars=numbers
        )[0]
    )
    x_mine = done(tokens_of(0, tokens, step(x_got[0])))
    x_in = [along(x_mine, INWARD)]
    weight_other = done(rows_at(1, step(frozen_value_weight), eighth))
    down_crossed = done(step(down_crossed))
    down_outer = along(down_crossed, OUTWARD)
    weight_near, down_other = step(weight_near, down_other)
    weight_near_other = swap(done(weight_near), "rep")
    x_other = done(tokens_of(1, tokens, step(x_got[1])))
    x_in.append(along(x_other, INWARD))
    x_both = [x_mine, x_other]

    def to_middle(half):
        x_in[half] = step(x_in[half])
        sums = kernel_call(
            to_middle_kernel,
            [like(eighth, 2 * wide)],
            x_both[half],
            back_wide,
            x_in[half],
            back_in_wide,
        )[0]
        return along(done(sums), MIDDLE)

    def to_end(half, crossed):
        sums = kernel_call(
            to_end_kernel, [like(eighth, wide)], x_both[half], back_wide, step(crossed)
        )[0]
        return along(done(sums), OUTWARD)

    def finish(half, crossed, outer, *others):
        outer, *_ = step(outer, x_mine, *others)
        here, there = kernel_call(
            finish_kernel,
            [like(eighth, size)] * 2,
            x_both[half],
            back_wide,
            x_in[half],
            back_in_wide,
            crossed,
            outer,
        )
        return done(here), there

    def far_of(crossed, outer):
        out = like(*crossed.shape)
        return kernel_call(far_kernel, [out], crossed, outer, scalars=flags)[0]

    middle = [to_middle(0)]
    weight_crossed = done(step(weight_crossed))
    weight_outer = along(weight_crossed, OUTWARD)
    dy_half, weight_near_other = step(dy_half, weight_near_other)
    dy_tp = swap(dy_half, "tp")
    dy_line = done(
        kernel_call(
            dy_line_kernel, [like(both, 2 * kv)], dy_half, step(dy_tp), scalars=places
        )[0]
    )
    down_far = done(far_of(down_crossed, step(down_outer)))
    down_far_other = swap(down_far, "rep")
    middle.append(to_middle(1))
    outward = [to_end(0, middle[0])]
    weight_far = done(far_of(weight_crossed, step(weight_outer)))
    weight_far_other = swap(weight_far, "rep")
    half_grad = [like(rows, eighth)] * 2
    dx_mine, dx_sent = kernel_call(
        dx_kernel,
        half_grad,
        step(dy_line),
        back_wide,
        weight_here,
        weight_near,
        weight_far,
        down_piece,
        down_near,
        down_far,
    )
    dx_mine_got = swap(done(dx_sent), "own")

    low_part = done(
        kernel_call(
            low_kernel,
            [compact],
            ids,
            x_mine,
            x_other,
            down_piece,
            down_near,
            down_far,
            down_other,
            step(down_far_other),
            scalars=numbers,
        )[0]
    )
    low_tp = swap(low_part, "tp")
    grad_here, grad_sent = finish(0, middle[0], outward[0])
    grad_got = swap(grad_sent, "own")
    blocks = [like(2, both, cols, kind=f32)] * 2
    y_first = kernel_call(
        y_kernel, blocks, step(x_mine), weight_here, weight_near, weight_far, scalars=flags
    )
    done(y_first[0])
    low_tp, dx_mine_got = step(low_tp, dx_mine_got)
    low_part = done(kernel_call(add_kernel, [compact], low_part, low_tp)[0])
    low_got = swap(low_part, "own")
    outward.append(to_end(1, middle[1]))
    low_got, grad_got = step(low_got, grad_got)
    delta, *up_parts = kernel_call(
        low_end_kernel,
        [like(both, kvq)] + [like(wide, kvq)] * 4,
        ids,
        low_part,
        low_got,
        up_all,
        dy_quarter,
        scalars=numbers,
    )
    done(delta)
    up_got = [around(up_parts[k], k) for k in (1, 2, 3)]
    dx_other, dx_sent = kernel_call(
        dx_kernel,
        half_grad,
        dy_line,
        back_wide,
        weight_other,
        weight_near_other,
        step(weight_far_other),
        down_other,
        down_far_other,
    )
    dx_other_got = swap(done(dx_sent), "own")
    grad_last, grad_sent = finish(1, middle[1], outward[1])
    grad_last_got = swap(grad_sent, "own")
    up_got = step(*up_got)
    up_mine, up_theirs = kernel_call(
        up_sum_kernel, [like(size, kvq)] * 2, up_parts[0], *up_got, scalars=numbers
    )
    up_theirs = swap(done(up_theirs), "own")
    x_other, dx_other_got = step(x_other, dx_other_got)
    y_keep, y_sent = kernel_call(
        y_kernel,
        blocks,
        x_other,
        weight_other,
        weight_near_other,
        weight_far_other,
        *y_first,
        scalars=flags,
    )
    y_got = swap(done(y_sent), "tp")
    y_got, grad_last_got = step(y_got, grad_last_got)
    y_here, y_sent = kernel_call(
        y_sum_kernel,
        [like(2, rows, cols, kind=f32), like(2, rows, cols)],
        y_keep,
        y_got,
        delta,
        scalars=flags,
    )
    y_got = swap(done(y_sent), "own")

    def in_place(axis, out, *pieces):
        def plan(n, a, o):
            spans = [[(0, length) for length in out.shape] for _ in range(4)]
            for i in range(4):
                spans[i][axis] = (at(n, i), eighth)
            return [(a[i], view(o[0], *spans[i])) for i in range(4)]

        return copy_call(plan, [out], starts, *pieces)[0]

    dx_other_got, _ = step(dx_other_got, dx_mine)
    input_grad = done(
        in_place(1, like(rows, width), dx_mine, dx_other, dx_mine_got, dx_other_got)
    )
    projected = done(kernel_call(y_end_kernel, [like(rows, kv)], y_here, step(y_got))[0])
    down_gradient = done(
        in_place(
            0, like(width, size), grad_here, grad_last, grad_got, step(grad_last_got)
        )[None]
    )
    up_gradient = kernel_call(
        up_place_kernel, [like(size, kv)], up_mine, step(up_theirs), scalars=flags
    )[0][None]
    return (projected, input_grad, down_gradient, up_gradient)


def body_routed(
    tokens,
    cotangent,
    frozen_value_weight,
    adapter_down_weight,
    adapter_up_weight,
    token_adapter,
    rank_step_count,
):
    rows, width_halved = tokens.shape
    half_kv = cotangent.shape[1]
    owning_adapters = lax.axis_size(("fsdp", "own"))
    greatest_rank = 3 * rows // (2 * owning_adapters)
    ids = token_adapter[:, 0]
    table = (ids[:, None] == jnp.arange(owning_adapters, dtype=jnp.int32)[None, :]).astype(
        f32
    )
    order = jnp.arange(rows, dtype=jnp.int32)
    earlier = (order[:, None] > order[None, :]).astype(f32)
    before = jnp.dot(earlier, table, precision=lax.Precision.HIGHEST)
    place = jnp.sum(before * table, axis=1).astype(jnp.int32)
    slot = ids * greatest_rank + place
    source_rows = jnp.full((owning_adapters * greatest_rank,), rows, jnp.int32).at[slot].set(order)
    padded_x = jnp.concatenate([tokens, jnp.zeros((1, width_halved), bf16)], axis=0)
    padded_dy = jnp.concatenate([cotangent, jnp.zeros((1, half_kv), bf16)], axis=0)
    send_x = jnp.take(padded_x, source_rows, axis=0)
    send_dy = jnp.take(padded_dy, source_rows, axis=0)
    recv_x, recv_dy = (
        lax.all_to_all(
            send_x.reshape(owning_adapters, greatest_rank, width_halved),
            ("fsdp", "own"),
            split_axis=0,
            concat_axis=0,
            tiled=True,
        ),
        lax.all_to_all(
            send_dy.reshape(owning_adapters, greatest_rank, half_kv),
            ("fsdp", "own"),
            split_axis=0,
            concat_axis=0,
            tiled=True,
        ),
    )
    flat_x = recv_x.reshape(owning_adapters * greatest_rank, width_halved)
    flat_dy = recv_dy.reshape(owning_adapters * greatest_rank, half_kv)
    dy_full = lax.all_gather(cotangent, "tp", axis=1, tiled=True)
    whole = lax.all_gather(frozen_value_weight, "fsdp", axis=1, tiled=True)
    partial_y = jnp.dot(tokens, whole, preferred_element_type=f32)
    base_dx = contract_final_axis(dy_full, whole)
    base_y = lax.psum_scatter(partial_y, "tp", scatter_dimension=1, tiled=True)
    down_matrix = adapter_down_weight[0]
    up_matrix = adapter_up_weight[0]
    part_low = jnp.dot(flat_x, down_matrix, preferred_element_type=f32)
    part_back = contract_final_axis(flat_dy, up_matrix)
    low_sum, back_sum = lax.psum((part_low, part_back), "tp")
    width_rank = down_matrix.shape[1]
    rank = width_rank // 8 * rank_step_count[lax.axis_index(("fsdp", "own"))]
    keep = jnp.arange(width_rank, dtype=jnp.int32)[None, :] < rank
    scale = 16.0 / rank.astype(f32)
    low = jnp.where(keep, low_sum, 0.0).astype(bf16)
    backward_pass = (scale * jnp.where(keep, back_sum, 0.0)).astype(bf16)
    delta = (scale * jnp.dot(low, up_matrix, preferred_element_type=f32)).astype(
        bf16
    )
    adapter_input_gradient = contract_final_axis(backward_pass, down_matrix).astype(bf16)
    down_gradient = contract_first(flat_x, backward_pass).astype(bf16)[None]
    up_gradient = (scale * contract_first(low, flat_dy)).astype(bf16)[None]
    home_delta, home_dx = (
        lax.all_to_all(
            delta.reshape(owning_adapters, greatest_rank, half_kv),
            ("fsdp", "own"),
            split_axis=0,
            concat_axis=0,
            tiled=True,
        ),
        lax.all_to_all(
            adapter_input_gradient.reshape(owning_adapters, greatest_rank, width_halved),
            ("fsdp", "own"),
            split_axis=0,
            concat_axis=0,
            tiled=True,
        ),
    )
    adapter_delta_rows = jnp.take(
        home_delta.reshape(owning_adapters * greatest_rank, half_kv), slot, axis=0
    )
    input_gradient_rows = jnp.take(
        home_dx.reshape(owning_adapters * greatest_rank, width_halved), slot, axis=0
    )
    projected = (base_y + adapter_delta_rows.astype(f32)).astype(bf16)
    input_grad = (base_dx + input_gradient_rows.astype(f32)).astype(bf16)
    return (projected, input_grad, down_gradient, up_gradient)


def solution(mesh):
    placed = (
        P(("rep", "fsdp", "own"), "tp"),
        P(("rep", "fsdp", "own"), "tp"),
        P("tp", "fsdp"),
        P(("fsdp", "own"), "tp", None),
        P(("fsdp", "own"), None, "tp"),
        P(("rep", "fsdp", "own"), None),
        P(),
    )
    line = mesh.shape["fsdp"] == 4 and mesh.shape["own"] == 2 and mesh.shape["rep"] == 2
    return jax.shard_map(
        body_line if line else body_routed,
        mesh=mesh,
        in_specs=placed,
        out_specs=(
            P(("rep", "fsdp", "own"), "tp"),
            P(("rep", "fsdp", "own"), "tp"),
            P(("rep", "fsdp", "own"), "tp", None),
            P(("rep", "fsdp", "own"), None, "tp"),
        ),
        check_vma=False,
    )
```

```python
import jax
import jax.numpy as jnp
from jax import lax
from jax.experimental import pallas as pl
from jax.experimental.pallas import tpu as pltpu
from jax.sharding import PartitionSpec as P

bf16 = jnp.bfloat16
f32 = jnp.float32


def contract_first(left, right):
    return lax.dot_general(
        left, right, (((0,), (0,)), ((), ())), preferred_element_type=f32
    )


def contract_final_axis(left, right):
    return lax.dot_general(
        left, right, (((1,), (1,)), ((), ())), preferred_element_type=f32
    )


def matmul(left, right):
    return jnp.dot(left, right, preferred_element_type=f32)


PAIR = [(0, 1), (1, 0)]
NEIGHBOURS = [(0, 1), (1, 0), (2, 3), (3, 2)]
MIDDLE = [(1, 2), (2, 1)]
OUTWARD = [(1, 0), (2, 3)]
INWARD = [(0, 1), (3, 2)]


def swap(value, axis):
    return lax.ppermute(value, axis, PAIR)


def along(value, pairs):
    return lax.ppermute(value, "fsdp", pairs)


def kernel_call(body, outs, *operands, scalars=None, scratch=(), space=pltpu.VMEM):
    specs = [pl.BlockSpec(memory_space=space)] * len(operands)
    if scalars is not None:
        operands = (scalars, *operands)
        specs = [pl.BlockSpec(memory_space=pltpu.SMEM), *specs]
    return pl.pallas_call(
        body,
        out_shape=list(outs),
        in_specs=specs,
        out_specs=[pl.BlockSpec(memory_space=pltpu.VMEM)] * len(outs),
        scratch_shapes=list(scratch),
        compiler_params=pltpu.CompilerParams(vmem_limit_bytes=28 * 2**20),
        cost_estimate=pl.CostEstimate(flops=0, bytes_accessed=0, transcendentals=0),
    )(*operands)


def copy_call(plan, outs, scalars, *operands):
    count = len(plan(None, [None] * len(operands), [None] * len(outs)))

    def body(numbers, *refs):
        sems = refs[-1]
        pairs = plan(numbers, refs[: len(operands)], refs[len(operands) : -1])
        copies = [pltpu.make_async_copy(a, b, sems.at[i]) for i, (a, b) in enumerate(pairs)]
        for copy in copies:
            copy.start()
        for copy in copies:
            copy.wait()

    return kernel_call(
        body,
        outs,
        *operands,
        scalars=scalars,
        scratch=[pltpu.SemaphoreType.DMA((count,))],
        space=pl.ANY,
    )


def view(ref, *spans):
    if ref is None:
        return None
    index = tuple(
        pl.ds(start if isinstance(start, int) else pl.multiple_of(start, 128), size)
        for start, size in spans
    )
    return ref.at[index]


def at(numbers, i):
    return None if numbers is None else numbers[i]


def ranks_of(ranks, ids):
    total = jnp.zeros(ids.shape, f32)
    for a in range(ranks.shape[0]):
        total = jnp.where(ids == a, ranks[a].astype(f32), total)
    return total


def kept(ids, ranks, value):
    rank = ranks_of(ranks, ids)
    column = lax.broadcasted_iota(jnp.int32, value.shape, 1).astype(f32)
    return jnp.where(column < rank, value, 0.0), 16.0 / rank


def roll_rows(value):
    half = value.shape[0] // 2
    return jnp.concatenate([value[half:], value[:half]], axis=0)


def back_kernel(ids, dy, up, out):
    size = out.shape[1]
    token = ids[...].astype(f32)
    for i in range(0, up.shape[0] // size, 2):
        both = contract_final_axis(dy[...], up[i * size : (i + 2) * size, :])
        for j in (0, 1):
            part = jnp.where(token == i + j, both[:, j * size : (j + 1) * size], 0.0)
            out[...] = part if i + j == 0 else out[...] + part


def spread_into(out, token, value, order):
    size = value.shape[1]
    for i in range(out.shape[1] // size):
        a = order[i].astype(f32)
        out[:, i * size : (i + 1) * size] = jnp.where(token == a, value, 0.0).astype(bf16)


def back_end_kernel(numbers, ids, part, got, wide, sent):
    token = ids[...].astype(f32)
    count = numbers.shape[0] // 3
    ranks, order = [numbers[i] for i in range(count)], [numbers[count + i] for i in range(count)]
    value, scale = kept(token, jnp.stack(ranks), part[...] + roll_rows(got[...]))
    value = (scale * value).astype(bf16)
    size = value.shape[1]
    sent[:, :size] = value
    sent[:, size:] = ids[...]
    spread_into(wide, token, value.astype(f32), order)


def spread_in_kernel(numbers, packet, wide):
    size = packet.shape[1] // 2
    count = numbers.shape[0] // 3
    order = [numbers[count + i] for i in range(count)]
    spread_into(wide, packet[:, size:].astype(f32), packet[:, :size].astype(f32), order)


def low_kernel(numbers, ids, x_mine, x_other, own, near, far, own_near_other, far_other, out):
    size = out.shape[1]
    wide = 2 * size
    token = ids[...].astype(f32)
    mine = [own[...], near[...], far[:, :wide], far[:, wide:]]
    other = [
        own_near_other[:, :wide],
        own_near_other[:, wide:],
        far_other[:, :wide],
        far_other[:, wide:],
    ]
    for i in range(4):
        both = matmul(x_mine[...], mine[i]) + matmul(x_other[...], other[i])
        for j in (0, 1):
            place = numbers[numbers.shape[0] // 3 + 2 * i + j].astype(f32)
            part = jnp.where(token == place, both[:, j * size : (j + 1) * size], 0.0)
            out[...] = part if i + j == 0 else out[...] + part


def low_end_kernel(numbers, ids, part, got, up, dy, delta, *grads):
    token = ids[...].astype(f32)
    count = numbers.shape[0] // 3
    size = part.shape[1]
    ranks = jnp.stack([numbers[i] for i in range(count)])
    value, scale = kept(token, ranks, part[...] + roll_rows(got[...]))
    value = value.astype(bf16).astype(f32)

    def pair(first, second):
        return jnp.concatenate(
            [jnp.where(token == a, value, 0.0) for a in (first, second)], axis=1
        ).astype(bf16)

    total = 0.0
    for i, out in enumerate(grads):
        places = [numbers[2 * count + 2 * i + j].astype(f32) for j in (0, 1)]
        out[...] = contract_first(pair(*places), dy[...]).astype(bf16)
        total += matmul(pair(2 * i, 2 * i + 1), up[2 * i * size : 2 * (i + 1) * size, :])
    delta[...] = (scale[:, :1] * total).astype(bf16)


def to_middle_kernel(x_here, back, x_in, back_in, out):
    half = back.shape[1] // 2
    sums = contract_first(x_here[...], back[:, half:])
    out[...] = (sums + contract_first(x_in[...], back_in[:, half:])).astype(bf16)


def to_end_kernel(x_here, back, crossed, out):
    wide = out.shape[1]
    sums = contract_first(x_here[...], back[:, wide : 2 * wide])
    out[...] = (sums + crossed[:, wide:].astype(f32)).astype(bf16)


def finish_kernel(x_here, back, x_in, back_in, crossed, outer, here, there):
    size = here.shape[1]
    wide = 2 * size
    sums = contract_first(x_here[...], back[:, :wide])
    sums += contract_first(x_in[...], back_in[:, :wide])
    sums += crossed[:, :wide].astype(f32) + outer[...].astype(f32)
    here[...] = sums[:, :size].astype(bf16)
    there[...] = sums[:, size:].astype(bf16)


def up_sent_kernel(up, out):
    cols = out.shape[2]
    for i in range(out.shape[0]):
        out[i] = up[:, (i % 2) * cols : (i % 2 + 1) * cols]


def packet_kernel(cotangent, adapters, out):
    rows, kv = cotangent.shape
    size = out.shape[1] - kv
    out[:, :kv] = cotangent[...]
    numbers = jnp.broadcast_to(adapters[...].astype(f32), (rows, size))
    out[:, kv:] = numbers.astype(bf16)


def unpack_kernel(flags, here, there, half, ids, quarter):
    rows = here.shape[0]
    kv = half.shape[1]
    cols = quarter.shape[1]
    span = pl.ds(pl.multiple_of(flags[3] * cols, 128), cols)
    for i, packet in enumerate((here, there)):
        place = slice(i * rows, (i + 1) * rows)
        half[place] = packet[:, :kv]
        ids[place] = packet[:, kv:]
        quarter[place] = packet[:, span]


def dy_line_kernel(places, here, got, out):
    cols = out.shape[1] // 4
    for i in range(4):
        place = places[i]
        span = pl.ds(pl.multiple_of((place % 2) * cols, 128), cols)
        own = place // 2 == places[4]

        @pl.when(own)
        def _():
            out[:, i * cols : (i + 1) * cols] = here[:, span]

        @pl.when(jnp.logical_not(own))
        def _():
            out[:, i * cols : (i + 1) * cols] = got[:, span]


def far_kernel(flags, crossed, outer, out):
    @pl.when(flags[4] == 1)
    def _():
        out[...] = crossed[...]

    @pl.when(flags[4] == 0)
    def _():
        out[...] = outer[...]


def up_sum_kernel(numbers, first, second, third, fourth, here, there):
    count = numbers.shape[0] // 3
    size = here.shape[0]
    for i, out in enumerate((here, there)):
        adapter = numbers[count + i]
        rank = jnp.float32(1.0)
        for a in range(count):
            rank = jnp.where(adapter == a, numbers[a].astype(f32), rank)
        span = slice(i * size, (i + 1) * size)
        part = sum(v[span, :].astype(f32) for v in (first, second, third, fourth))
        out[...] = (jnp.full(part.shape, 16.0, f32) / rank * part).astype(bf16)


def up_place_kernel(flags, here, there, out):
    cols = here.shape[1]
    out[:, pl.ds(pl.multiple_of(flags[3] * cols, 128), cols)] = here[...]
    out[:, pl.ds(pl.multiple_of((1 - flags[3]) * cols, 128), cols)] = there[...]


def add_kernel(left, right, out):
    out[...] = left[...] + right[...]


def dx_kernel(dy, back, own, near, far, *rest):
    *adapter, here, there = rest
    rows, width = here.shape
    cols = own.shape[1]
    tile = min(cols, width)
    for t in range(width // tile):
        span = slice(t * tile, (t + 1) * tile)
        base = contract_final_axis(dy[:, :cols], own[span, :])
        base += contract_final_axis(dy[:, cols : 2 * cols], near[span, :])
        base += contract_final_axis(dy[:, 2 * cols :], far[span, :])
        lora, start = 0.0, 0
        for piece in adapter:
            stop = start + piece.shape[1]
            lora += contract_final_axis(back[:, start:stop], piece[span, :])
            start = stop
        total = (base + lora.astype(bf16).astype(f32)).astype(bf16)
        here[:, span] = total[:rows]
        there[:, span] = total[rows:]


def y_kernel(flags, tokens, own, near, far, *rest):
    *before, keep, send = rest
    cols = own.shape[1]

    def store(pair, first, part):
        mine = flags[0] == (1 if pair else 0)
        for i in (0, 1):
            place = (first + i) % 2
            block = matmul(tokens[...], part(i))

            @pl.when(mine)
            def _():
                keep[place] = block + before[0][place] if before else block

            @pl.when(jnp.logical_not(mine))
            def _():
                send[place] = block + before[1][place] if before else block

    store(True, flags[1], lambda i: (own, near)[i][...])
    store(False, flags[2], lambda i: far[:, i * cols : (i + 1) * cols])


def y_sum_kernel(flags, keep, got, delta, here, there):
    rows = here.shape[1]
    for i in (0, 1):
        added = jnp.where(flags[3] == i, delta[...].astype(f32), 0.0)
        total = keep[i] + got[i] + added
        here[i] = total[:rows]
        there[i] = total[rows:].astype(bf16)


def y_end_kernel(here, got, out):
    cols = here.shape[2]
    for i in (0, 1):
        out[:, i * cols : (i + 1) * cols] = (here[i] + got[i].astype(f32)).astype(bf16)


def body_line(
    tokens,
    cotangent,
    frozen_value_weight,
    adapter_down_weight,
    adapter_up_weight,
    token_adapter,
    rank_step_count,
):
    rows, width = tokens.shape
    kv = cotangent.shape[1]
    cols = frozen_value_weight.shape[1]
    down = adapter_down_weight[0]
    up = adapter_up_weight[0]
    size = down.shape[1]
    wide = 2 * size
    quarter = width // 2
    eighth = quarter // 2
    kvq = kv // 2
    both = 2 * rows
    z, x = lax.axis_index("fsdp"), lax.axis_index("own")
    y, c = lax.axis_index("rep"), lax.axis_index("tp")
    first_pair = z < 2
    is_middle = (z == 1) | (z == 2)
    line = [z, z + 1 - 2 * (z % 2), jnp.where(first_pair, 2, 1), jnp.where(first_pair, 3, 0)]
    adapters = jnp.stack([2 * t + o for t in line for o in (x, 1 - x)]).astype(jnp.int32)
    number = adapters.shape[0]
    starts = jnp.stack(
        [side * quarter + half * eighth for side in (x, 1 - x) for half in (y, 1 - y)]
    ).astype(jnp.int32)
    ranks = size // 8 * rank_step_count
    ring = jnp.stack([2 * ((z + k) % 4) + o for k in range(4) for o in (x, 1 - x)])
    numbers = jnp.concatenate([ranks, adapters, ring.astype(jnp.int32)])
    flags = jnp.stack([(c == 0) == first_pair, z % 2 == 1, z >= 2, x == 1, is_middle])
    flags = flags.astype(jnp.int32)
    places = jnp.stack([*line, c]).astype(jnp.int32)

    latest = []

    def step(*values):
        if latest:
            values = lax.optimization_barrier((*values, latest[0]))[: len(values)]
        return values[0] if len(values) == 1 else values

    def done(value):
        latest[:] = [value]
        return value

    def like(*shape, kind=bf16):
        return jax.ShapeDtypeStruct(shape, kind)

    def around(value, shift):
        return along(value, [(i, (i + shift) % 4) for i in range(4)])

    def rows_at(i, value, length):
        out = like(length, value.shape[1])
        return copy_call(
            lambda n, a, o: [(view(a[0], (at(n, i), length), (0, value.shape[1])), o[0])],
            [out],
            starts,
            value,
        )[0]

    def columns_at(i, value):
        out = like(value.shape[0], eighth)
        return copy_call(
            lambda n, a, o: [(view(a[0], (0, value.shape[0]), (at(n, i), eighth)), o[0])],
            [out],
            starts,
            value,
        )[0]

    def side_by_side(*values):
        widths = [v.shape[1] for v in values]
        length = values[0].shape[0]
        return copy_call(
            lambda n, a, o: [
                (a[i], view(o[0], (0, length), (sum(widths[:i]), widths[i])))
                for i in range(len(values))
            ],
            [like(length, sum(widths))],
            starts,
            *values,
        )[0]

    def tokens_of(i, value, got):
        return copy_call(
            lambda n, a, o: [
                (view(a[0], (0, rows), (at(n, i), eighth)), view(o[0], (0, rows), (0, eighth))),
                (a[1], view(o[0], (rows, rows), (0, eighth))),
            ],
            [like(both, eighth)],
            starts,
            value,
            got,
        )[0]

    up_sent = kernel_call(up_sent_kernel, [like(number, size, kvq)], up)[0]
    up_all = lax.all_to_all(
        done(up_sent), ("fsdp", "own"), split_axis=0, concat_axis=0, tiled=True
    ).reshape(number * size, kvq)
    down_got = swap(done(rows_at(2, step(down), eighth)), "own")
    packet_here = done(
        kernel_call(packet_kernel, [like(rows, kv + size)], step(cotangent), token_adapter)[0]
    )
    packet = swap(packet_here, "own")
    x_got = [swap(done(columns_at(2, step(tokens))), "own")]
    down_piece = done(
        copy_call(
            lambda n, a, o: [
                (view(a[0], (at(n, 0), eighth), (0, size)), view(o[0], (0, eighth), (0, size))),
                (a[1], view(o[0], (0, eighth), (size, size))),
            ],
            [like(eighth, wide)],
            starts,
            down,
            step(down_got),
        )[0]
    )
    down_near = along(down_piece, NEIGHBOURS)
    packet, up_all = step(packet, up_all)
    dy_half, ids, dy_quarter = kernel_call(
        unpack_kernel,
        [like(both, kv), like(both, size), like(both, kvq)],
        packet_here,
        packet,
        scalars=flags,
    )
    compact = like(both, size, kind=f32)
    back_part = done(kernel_call(back_kernel, [compact], ids, dy_quarter, up_all)[0])
    back_tp = swap(back_part, "tp")
    dy_tp = swap(dy_half, "tp")
    weight_here = done(rows_at(0, step(frozen_value_weight), eighth))
    weight_near = along(weight_here, NEIGHBOURS)
    back_part = done(kernel_call(add_kernel, [compact], back_part, step(back_tp))[0])
    back_got = swap(back_part, "own")
    dy_line = done(
        kernel_call(
            dy_line_kernel, [like(both, 2 * kv)], dy_half, step(dy_tp), scalars=places
        )[0]
    )
    down_near, x_got[0] = step(down_near, x_got[0])
    crossing = done(side_by_side(down_piece, down_near))
    down_crossed = along(crossing, MIDDLE)
    down_other = swap(crossing, "rep")
    back_wide, back_sent = kernel_call(
        back_end_kernel,
        [like(both, number * size), like(both, wide)],
        ids,
        back_part,
        step(back_got),
        scalars=numbers,
    )
    back_in = along(done(back_sent), INWARD)
    crossing = done(side_by_side(weight_here, step(weight_near)))
    weight_crossed = along(crossing, MIDDLE)
    x_got.append(swap(done(columns_at(3, step(tokens))), "own"))
    back_in_wide = done(
        kernel_call(
            spread_in_kernel, [like(both, number * size)], step(back_in), scalars=numbers
        )[0]
    )
    x_mine = done(tokens_of(0, tokens, step(x_got[0])))
    x_in = [along(x_mine, INWARD)]
    weight_other = done(rows_at(1, step(frozen_value_weight), eighth))
    down_crossed = done(step(down_crossed))
    down_outer = along(down_crossed, OUTWARD)
    weight_near, down_other = step(weight_near, down_other)
    weight_near_other = swap(done(weight_near), "rep")
    x_other = done(tokens_of(1, tokens, step(x_got[1])))
    x_in.append(along(x_other, INWARD))
    x_both = [x_mine, x_other]

    def to_middle(half):
        x_in[half] = step(x_in[half])
        sums = kernel_call(
            to_middle_kernel,
            [like(eighth, 2 * wide)],
            x_both[half],
            back_wide,
            x_in[half],
            back_in_wide,
        )[0]
        return along(done(sums), MIDDLE)

    def to_end(half, crossed):
        sums = kernel_call(
            to_end_kernel, [like(eighth, wide)], x_both[half], back_wide, step(crossed)
        )[0]
        return along(done(sums), OUTWARD)

    def finish(half, crossed, outer, *others):
        outer, *_ = step(outer, x_mine, *others)
        here, there = kernel_call(
            finish_kernel,
            [like(eighth, size)] * 2,
            x_both[half],
            back_wide,
            x_in[half],
            back_in_wide,
            crossed,
            outer,
        )
        return done(here), there

    def far_of(crossed, outer):
        out = like(*crossed.shape)
        return kernel_call(far_kernel, [out], crossed, outer, scalars=flags)[0]

    middle = [to_middle(0)]
    weight_crossed = done(step(weight_crossed))
    weight_outer = along(weight_crossed, OUTWARD)
    down_outer, weight_near_other = step(down_outer, weight_near_other)
    down_far = done(far_of(down_crossed, down_outer))
    down_far_other = swap(down_far, "rep")
    middle.append(to_middle(1))
    outward = [to_end(0, middle[0])]
    weight_far = done(far_of(weight_crossed, step(weight_outer)))
    weight_far_other = swap(weight_far, "rep")
    half_grad = [like(rows, eighth)] * 2
    low_part = done(
        kernel_call(
            low_kernel,
            [compact],
            ids,
            x_mine,
            x_other,
            down_piece,
            down_near,
            down_far,
            down_other,
            step(down_far_other),
            scalars=numbers,
        )[0]
    )
    low_tp = swap(low_part, "tp")
    blocks = [like(2, both, cols, kind=f32)] * 2
    y_first = kernel_call(
        y_kernel, blocks, step(x_mine), weight_here, weight_near, weight_far, scalars=flags
    )
    done(y_first[0])
    low_part = done(kernel_call(add_kernel, [compact], low_part, step(low_tp))[0])
    low_got = swap(low_part, "own")
    dx_mine, dx_sent = kernel_call(
        dx_kernel,
        half_grad,
        step(dy_line),
        back_wide,
        weight_here,
        weight_near,
        weight_far,
        down_piece,
        down_near,
        down_far,
    )
    dx_mine_got = swap(done(dx_sent), "own")
    grad_here, grad_sent = finish(0, middle[0], outward[0])
    grad_got = swap(grad_sent, "own")
    outward.append(to_end(1, middle[1]))
    low_got = step(low_got)
    delta, *up_parts = kernel_call(
        low_end_kernel,
        [like(both, kvq)] + [like(wide, kvq)] * 4,
        ids,
        low_part,
        low_got,
        up_all,
        dy_quarter,
        scalars=numbers,
    )
    done(delta)
    up_got = [around(up_parts[k], k) for k in (1, 2, 3)]
    weight_far_other, dx_mine_got = step(weight_far_other, dx_mine_got)
    dx_other, dx_sent = kernel_call(
        dx_kernel,
        half_grad,
        dy_line,
        back_wide,
        weight_other,
        weight_near_other,
        weight_far_other,
        down_other,
        down_far_other,
    )
    dx_other_got = swap(done(dx_sent), "own")
    grad_last, grad_sent = finish(1, middle[1], outward[1], grad_got)
    grad_last_got = swap(grad_sent, "own")
    up_got = step(*up_got)
    up_mine, up_theirs = kernel_call(
        up_sum_kernel, [like(size, kvq)] * 2, up_parts[0], *up_got, scalars=numbers
    )
    up_theirs = swap(done(up_theirs), "own")
    x_other, dx_other_got = step(x_other, dx_other_got)
    y_keep, y_sent = kernel_call(
        y_kernel,
        blocks,
        x_other,
        weight_other,
        weight_near_other,
        weight_far_other,
        *y_first,
        scalars=flags,
    )
    y_got = swap(done(y_sent), "tp")
    y_got, grad_last_got = step(y_got, grad_last_got)
    y_here, y_sent = kernel_call(
        y_sum_kernel,
        [like(2, rows, cols, kind=f32), like(2, rows, cols)],
        y_keep,
        y_got,
        delta,
        scalars=flags,
    )
    y_got = swap(done(y_sent), "own")

    def in_place(axis, out, *pieces):
        def plan(n, a, o):
            spans = [[(0, length) for length in out.shape] for _ in range(4)]
            for i in range(4):
                spans[i][axis] = (at(n, i), eighth)
            return [(a[i], view(o[0], *spans[i])) for i in range(4)]

        return copy_call(plan, [out], starts, *pieces)[0]

    dx_other_got, _ = step(dx_other_got, dx_mine)
    input_grad = done(
        in_place(1, like(rows, width), dx_mine, dx_other, dx_mine_got, dx_other_got)
    )
    projected = done(kernel_call(y_end_kernel, [like(rows, kv)], y_here, step(y_got))[0])
    down_gradient = done(
        in_place(
            0, like(width, size), grad_here, grad_last, grad_got, step(grad_last_got)
        )[None]
    )
    up_gradient = kernel_call(
        up_place_kernel, [like(size, kv)], up_mine, step(up_theirs), scalars=flags
    )[0][None]
    return (projected, input_grad, down_gradient, up_gradient)


def body_routed(
    tokens,
    cotangent,
    frozen_value_weight,
    adapter_down_weight,
    adapter_up_weight,
    token_adapter,
    rank_step_count,
):
    rows, width_halved = tokens.shape
    half_kv = cotangent.shape[1]
    owning_adapters = lax.axis_size(("fsdp", "own"))
    greatest_rank = 3 * rows // (2 * owning_adapters)
    ids = token_adapter[:, 0]
    table = (ids[:, None] == jnp.arange(owning_adapters, dtype=jnp.int32)[None, :]).astype(
        f32
    )
    order = jnp.arange(rows, dtype=jnp.int32)
    earlier = (order[:, None] > order[None, :]).astype(f32)
    before = jnp.dot(earlier, table, precision=lax.Precision.HIGHEST)
    place = jnp.sum(before * table, axis=1).astype(jnp.int32)
    slot = ids * greatest_rank + place
    source_rows = jnp.full((owning_adapters * greatest_rank,), rows, jnp.int32).at[slot].set(order)
    padded_x = jnp.concatenate([tokens, jnp.zeros((1, width_halved), bf16)], axis=0)
    padded_dy = jnp.concatenate([cotangent, jnp.zeros((1, half_kv), bf16)], axis=0)
    send_x = jnp.take(padded_x, source_rows, axis=0)
    send_dy = jnp.take(padded_dy, source_rows, axis=0)
    recv_x, recv_dy = (
        lax.all_to_all(
            send_x.reshape(owning_adapters, greatest_rank, width_halved),
            ("fsdp", "own"),
            split_axis=0,
            concat_axis=0,
            tiled=True,
        ),
        lax.all_to_all(
            send_dy.reshape(owning_adapters, greatest_rank, half_kv),
            ("fsdp", "own"),
            split_axis=0,
            concat_axis=0,
            tiled=True,
        ),
    )
    flat_x = recv_x.reshape(owning_adapters * greatest_rank, width_halved)
    flat_dy = recv_dy.reshape(owning_adapters * greatest_rank, half_kv)
    dy_full = lax.all_gather(cotangent, "tp", axis=1, tiled=True)
    whole = lax.all_gather(frozen_value_weight, "fsdp", axis=1, tiled=True)
    partial_y = jnp.dot(tokens, whole, preferred_element_type=f32)
    base_dx = contract_final_axis(dy_full, whole)
    base_y = lax.psum_scatter(partial_y, "tp", scatter_dimension=1, tiled=True)
    down_matrix = adapter_down_weight[0]
    up_matrix = adapter_up_weight[0]
    part_low = jnp.dot(flat_x, down_matrix, preferred_element_type=f32)
    part_back = contract_final_axis(flat_dy, up_matrix)
    low_sum, back_sum = lax.psum((part_low, part_back), "tp")
    width_rank = down_matrix.shape[1]
    rank = width_rank // 8 * rank_step_count[lax.axis_index(("fsdp", "own"))]
    keep = jnp.arange(width_rank, dtype=jnp.int32)[None, :] < rank
    scale = 16.0 / rank.astype(f32)
    low = jnp.where(keep, low_sum, 0.0).astype(bf16)
    backward_pass = (scale * jnp.where(keep, back_sum, 0.0)).astype(bf16)
    delta = (scale * jnp.dot(low, up_matrix, preferred_element_type=f32)).astype(
        bf16
    )
    adapter_input_gradient = contract_final_axis(backward_pass, down_matrix).astype(bf16)
    down_gradient = contract_first(flat_x, backward_pass).astype(bf16)[None]
    up_gradient = (scale * contract_first(low, flat_dy)).astype(bf16)[None]
    home_delta, home_dx = (
        lax.all_to_all(
            delta.reshape(owning_adapters, greatest_rank, half_kv),
            ("fsdp", "own"),
            split_axis=0,
            concat_axis=0,
            tiled=True,
        ),
        lax.all_to_all(
            adapter_input_gradient.reshape(owning_adapters, greatest_rank, width_halved),
            ("fsdp", "own"),
            split_axis=0,
            concat_axis=0,
            tiled=True,
        ),
    )
    adapter_delta_rows = jnp.take(
        home_delta.reshape(owning_adapters * greatest_rank, half_kv), slot, axis=0
    )
    input_gradient_rows = jnp.take(
        home_dx.reshape(owning_adapters * greatest_rank, width_halved), slot, axis=0
    )
    projected = (base_y + adapter_delta_rows.astype(f32)).astype(bf16)
    input_grad = (base_dx + input_gradient_rows.astype(f32)).astype(bf16)
    return (projected, input_grad, down_gradient, up_gradient)


def solution(mesh):
    placed = (
        P(("rep", "fsdp", "own"), "tp"),
        P(("rep", "fsdp", "own"), "tp"),
        P("tp", "fsdp"),
        P(("fsdp", "own"), "tp", None),
        P(("fsdp", "own"), None, "tp"),
        P(("rep", "fsdp", "own"), None),
        P(),
    )
    line = mesh.shape["fsdp"] == 4 and mesh.shape["own"] == 2 and mesh.shape["rep"] == 2
    return jax.shard_map(
        body_line if line else body_routed,
        mesh=mesh,
        in_specs=placed,
        out_specs=(
            P(("rep", "fsdp", "own"), "tp"),
            P(("rep", "fsdp", "own"), "tp"),
            P(("rep", "fsdp", "own"), "tp", None),
            P(("rep", "fsdp", "own"), None, "tp"),
        ),
        check_vma=False,
    )
```

```python
import jax
import jax.numpy as jnp
from jax import lax
from jax.experimental import pallas as pl
from jax.experimental.pallas import tpu as pltpu
from jax.sharding import PartitionSpec as P

bf16 = jnp.bfloat16
f32 = jnp.float32


def contract_first(left, right):
    return lax.dot_general(
        left, right, (((0,), (0,)), ((), ())), preferred_element_type=f32
    )


def contract_final_axis(left, right):
    return lax.dot_general(
        left, right, (((1,), (1,)), ((), ())), preferred_element_type=f32
    )


def matmul(left, right):
    return jnp.dot(left, right, preferred_element_type=f32)


PAIR = [(0, 1), (1, 0)]
NEIGHBOURS = [(0, 1), (1, 0), (2, 3), (3, 2)]
MIDDLE = [(1, 2), (2, 1)]
OUTWARD = [(1, 0), (2, 3)]
INWARD = [(0, 1), (3, 2)]


def swap(value, axis):
    return lax.ppermute(value, axis, PAIR)


def along(value, pairs):
    return lax.ppermute(value, "fsdp", pairs)


def kernel_call(body, outs, *operands, scalars=None, scratch=(), space=pltpu.VMEM):
    specs = [pl.BlockSpec(memory_space=space)] * len(operands)
    if scalars is not None:
        operands = (scalars, *operands)
        specs = [pl.BlockSpec(memory_space=pltpu.SMEM), *specs]
    return pl.pallas_call(
        body,
        out_shape=list(outs),
        in_specs=specs,
        out_specs=[pl.BlockSpec(memory_space=pltpu.VMEM)] * len(outs),
        scratch_shapes=list(scratch),
        compiler_params=pltpu.CompilerParams(vmem_limit_bytes=28 * 2**20),
        cost_estimate=pl.CostEstimate(flops=0, bytes_accessed=0, transcendentals=0),
    )(*operands)


def copy_call(plan, outs, scalars, *operands):
    count = len(plan(None, [None] * len(operands), [None] * len(outs)))

    def body(numbers, *refs):
        sems = refs[-1]
        pairs = plan(numbers, refs[: len(operands)], refs[len(operands) : -1])
        copies = [pltpu.make_async_copy(a, b, sems.at[i]) for i, (a, b) in enumerate(pairs)]
        for copy in copies:
            copy.start()
        for copy in copies:
            copy.wait()

    return kernel_call(
        body,
        outs,
        *operands,
        scalars=scalars,
        scratch=[pltpu.SemaphoreType.DMA((count,))],
        space=pl.ANY,
    )


def view(ref, *spans):
    if ref is None:
        return None
    index = tuple(
        pl.ds(start if isinstance(start, int) else pl.multiple_of(start, 128), size)
        for start, size in spans
    )
    return ref.at[index]


def at(numbers, i):
    return None if numbers is None else numbers[i]


def ranks_of(ranks, ids):
    total = jnp.zeros(ids.shape, f32)
    for a in range(ranks.shape[0]):
        total = jnp.where(ids == a, ranks[a].astype(f32), total)
    return total


def kept(ids, ranks, value):
    rank = ranks_of(ranks, ids)
    column = lax.broadcasted_iota(jnp.int32, value.shape, 1).astype(f32)
    return jnp.where(column < rank, value, 0.0), 16.0 / rank


def roll_rows(value):
    half = value.shape[0] // 2
    return jnp.concatenate([value[half:], value[:half]], axis=0)


def back_kernel(ids, dy, up, out):
    size = out.shape[1]
    token = ids[...].astype(f32)
    for i in range(0, up.shape[0] // size, 2):
        both = contract_final_axis(dy[...], up[i * size : (i + 2) * size, :])
        for j in (0, 1):
            part = jnp.where(token == i + j, both[:, j * size : (j + 1) * size], 0.0)
            out[...] = part if i + j == 0 else out[...] + part


def spread_into(out, token, value, order):
    size = value.shape[1]
    for i in range(out.shape[1] // size):
        a = order[i].astype(f32)
        out[:, i * size : (i + 1) * size] = jnp.where(token == a, value, 0.0).astype(bf16)


def back_end_kernel(numbers, ids, part, got, wide, sent):
    token = ids[...].astype(f32)
    count = numbers.shape[0] // 3
    ranks, order = [numbers[i] for i in range(count)], [numbers[count + i] for i in range(count)]
    value, scale = kept(token, jnp.stack(ranks), part[...] + roll_rows(got[...]))
    value = (scale * value).astype(bf16)
    size = value.shape[1]
    sent[:, :size] = value
    sent[:, size:] = ids[...]
    spread_into(wide, token, value.astype(f32), order)


def spread_in_kernel(numbers, packet, wide):
    size = packet.shape[1] // 2
    count = numbers.shape[0] // 3
    order = [numbers[count + i] for i in range(count)]
    spread_into(wide, packet[:, size:].astype(f32), packet[:, :size].astype(f32), order)


def low_kernel(numbers, ids, x_mine, x_other, own, near, far, own_near_other, far_other, out):
    size = out.shape[1]
    wide = 2 * size
    token = ids[...].astype(f32)
    mine = [own[...], near[...], far[:, :wide], far[:, wide:]]
    other = [
        own_near_other[:, :wide],
        own_near_other[:, wide:],
        far_other[:, :wide],
        far_other[:, wide:],
    ]
    for i in range(4):
        both = matmul(x_mine[...], mine[i]) + matmul(x_other[...], other[i])
        for j in (0, 1):
            place = numbers[numbers.shape[0] // 3 + 2 * i + j].astype(f32)
            part = jnp.where(token == place, both[:, j * size : (j + 1) * size], 0.0)
            out[...] = part if i + j == 0 else out[...] + part


def low_end_kernel(numbers, ids, part, got, up, dy, delta, *grads):
    token = ids[...].astype(f32)
    count = numbers.shape[0] // 3
    size = part.shape[1]
    ranks = jnp.stack([numbers[i] for i in range(count)])
    value, scale = kept(token, ranks, part[...] + roll_rows(got[...]))
    value = value.astype(bf16).astype(f32)

    def pair(first, second):
        return jnp.concatenate(
            [jnp.where(token == a, value, 0.0) for a in (first, second)], axis=1
        ).astype(bf16)

    total = 0.0
    for i, out in enumerate(grads):
        places = [numbers[2 * count + 2 * i + j].astype(f32) for j in (0, 1)]
        out[...] = contract_first(pair(*places), dy[...]).astype(bf16)
        total += matmul(pair(2 * i, 2 * i + 1), up[2 * i * size : 2 * (i + 1) * size, :])
    delta[...] = (scale[:, :1] * total).astype(bf16)


def to_middle_kernel(x_here, back, x_in, back_in, out):
    half = back.shape[1] // 2
    sums = contract_first(x_here[...], back[:, half:])
    out[...] = (sums + contract_first(x_in[...], back_in[:, half:])).astype(bf16)


def to_end_kernel(x_here, back, crossed, out):
    wide = out.shape[1]
    sums = contract_first(x_here[...], back[:, wide : 2 * wide])
    out[...] = (sums + crossed[:, wide:].astype(f32)).astype(bf16)


def finish_kernel(x_here, back, x_in, back_in, crossed, outer, here, there):
    size = here.shape[1]
    wide = 2 * size
    sums = contract_first(x_here[...], back[:, :wide])
    sums += contract_first(x_in[...], back_in[:, :wide])
    sums += crossed[:, :wide].astype(f32) + outer[...].astype(f32)
    here[...] = sums[:, :size].astype(bf16)
    there[...] = sums[:, size:].astype(bf16)


def up_sent_kernel(up, out):
    cols = out.shape[2]
    for i in range(out.shape[0]):
        out[i] = up[:, (i % 2) * cols : (i % 2 + 1) * cols]


def packet_kernel(cotangent, adapters, out):
    rows, kv = cotangent.shape
    size = out.shape[1] - kv
    out[:, :kv] = cotangent[...]
    numbers = jnp.broadcast_to(adapters[...].astype(f32), (rows, size))
    out[:, kv:] = numbers.astype(bf16)


def unpack_kernel(flags, here, there, half, ids, quarter):
    rows = here.shape[0]
    kv = half.shape[1]
    cols = quarter.shape[1]
    span = pl.ds(pl.multiple_of(flags[3] * cols, 128), cols)
    for i, packet in enumerate((here, there)):
        place = slice(i * rows, (i + 1) * rows)
        half[place] = packet[:, :kv]
        ids[place] = packet[:, kv:]
        quarter[place] = packet[:, span]


def dy_line_kernel(places, here, got, out):
    cols = out.shape[1] // 4
    for i in range(4):
        place = places[i]
        span = pl.ds(pl.multiple_of((place % 2) * cols, 128), cols)
        own = place // 2 == places[4]

        @pl.when(own)
        def _():
            out[:, i * cols : (i + 1) * cols] = here[:, span]

        @pl.when(jnp.logical_not(own))
        def _():
            out[:, i * cols : (i + 1) * cols] = got[:, span]


def far_kernel(flags, crossed, outer, out):
    @pl.when(flags[4] == 1)
    def _():
        out[...] = crossed[...]

    @pl.when(flags[4] == 0)
    def _():
        out[...] = outer[...]


def up_sum_kernel(numbers, first, second, third, fourth, here, there):
    count = numbers.shape[0] // 3
    size = here.shape[0]
    for i, out in enumerate((here, there)):
        adapter = numbers[count + i]
        rank = jnp.float32(1.0)
        for a in range(count):
            rank = jnp.where(adapter == a, numbers[a].astype(f32), rank)
        span = slice(i * size, (i + 1) * size)
        part = sum(v[span, :].astype(f32) for v in (first, second, third, fourth))
        out[...] = (jnp.full(part.shape, 16.0, f32) / rank * part).astype(bf16)


def up_place_kernel(flags, here, there, out):
    cols = here.shape[1]
    out[:, pl.ds(pl.multiple_of(flags[3] * cols, 128), cols)] = here[...]
    out[:, pl.ds(pl.multiple_of((1 - flags[3]) * cols, 128), cols)] = there[...]


def add_kernel(left, right, out):
    out[...] = left[...] + right[...]


def dx_kernel(dy, back, own, near, far, *rest):
    *adapter, here, there = rest
    rows, width = here.shape
    cols = own.shape[1]
    tile = min(cols, width)
    for t in range(width // tile):
        span = slice(t * tile, (t + 1) * tile)
        base = contract_final_axis(dy[:, :cols], own[span, :])
        base += contract_final_axis(dy[:, cols : 2 * cols], near[span, :])
        base += contract_final_axis(dy[:, 2 * cols :], far[span, :])
        lora, start = 0.0, 0
        for piece in adapter:
            stop = start + piece.shape[1]
            lora += contract_final_axis(back[:, start:stop], piece[span, :])
            start = stop
        total = (base + lora.astype(bf16).astype(f32)).astype(bf16)
        here[:, span] = total[:rows]
        there[:, span] = total[rows:]


def y_kernel(flags, tokens, own, near, far, *rest):
    *before, keep, send = rest
    cols = own.shape[1]

    def store(pair, first, part):
        mine = flags[0] == (1 if pair else 0)
        for i in (0, 1):
            place = (first + i) % 2
            block = matmul(tokens[...], part(i))

            @pl.when(mine)
            def _():
                keep[place] = block + before[0][place] if before else block

            @pl.when(jnp.logical_not(mine))
            def _():
                send[place] = block + before[1][place] if before else block

    store(True, flags[1], lambda i: (own, near)[i][...])
    store(False, flags[2], lambda i: far[:, i * cols : (i + 1) * cols])


def y_sum_kernel(flags, keep, got, delta, here, there):
    rows = here.shape[1]
    for i in (0, 1):
        added = jnp.where(flags[3] == i, delta[...].astype(f32), 0.0)
        total = keep[i] + got[i] + added
        here[i] = total[:rows]
        there[i] = total[rows:].astype(bf16)


def y_end_kernel(here, got, out):
    cols = here.shape[2]
    for i in (0, 1):
        out[:, i * cols : (i + 1) * cols] = (here[i] + got[i].astype(f32)).astype(bf16)


def body_line(
    tokens,
    cotangent,
    frozen_value_weight,
    adapter_down_weight,
    adapter_up_weight,
    token_adapter,
    rank_step_count,
):
    rows, width = tokens.shape
    kv = cotangent.shape[1]
    cols = frozen_value_weight.shape[1]
    down = adapter_down_weight[0]
    up = adapter_up_weight[0]
    size = down.shape[1]
    wide = 2 * size
    quarter = width // 2
    eighth = quarter // 2
    kvq = kv // 2
    both = 2 * rows
    z, x = lax.axis_index("fsdp"), lax.axis_index("own")
    y, c = lax.axis_index("rep"), lax.axis_index("tp")
    first_pair = z < 2
    is_middle = (z == 1) | (z == 2)
    line = [z, z + 1 - 2 * (z % 2), jnp.where(first_pair, 2, 1), jnp.where(first_pair, 3, 0)]
    adapters = jnp.stack([2 * t + o for t in line for o in (x, 1 - x)]).astype(jnp.int32)
    number = adapters.shape[0]
    starts = jnp.stack(
        [side * quarter + half * eighth for side in (x, 1 - x) for half in (y, 1 - y)]
    ).astype(jnp.int32)
    ranks = size // 8 * rank_step_count
    ring = jnp.stack([2 * ((z + k) % 4) + o for k in range(4) for o in (x, 1 - x)])
    numbers = jnp.concatenate([ranks, adapters, ring.astype(jnp.int32)])
    flags = jnp.stack([(c == 0) == first_pair, z % 2 == 1, z >= 2, x == 1, is_middle])
    flags = flags.astype(jnp.int32)
    places = jnp.stack([*line, c]).astype(jnp.int32)

    latest = []

    def step(*values):
        if latest:
            values = lax.optimization_barrier((*values, latest[0]))[: len(values)]
        return values[0] if len(values) == 1 else values

    def done(value):
        latest[:] = [value]
        return value

    def like(*shape, kind=bf16):
        return jax.ShapeDtypeStruct(shape, kind)

    def around(value, shift):
        return along(value, [(i, (i + shift) % 4) for i in range(4)])

    def rows_at(i, value, length):
        out = like(length, value.shape[1])
        return copy_call(
            lambda n, a, o: [(view(a[0], (at(n, i), length), (0, value.shape[1])), o[0])],
            [out],
            starts,
            value,
        )[0]

    def columns_at(i, value):
        out = like(value.shape[0], eighth)
        return copy_call(
            lambda n, a, o: [(view(a[0], (0, value.shape[0]), (at(n, i), eighth)), o[0])],
            [out],
            starts,
            value,
        )[0]

    def side_by_side(*values):
        widths = [v.shape[1] for v in values]
        length = values[0].shape[0]
        return copy_call(
            lambda n, a, o: [
                (a[i], view(o[0], (0, length), (sum(widths[:i]), widths[i])))
                for i in range(len(values))
            ],
            [like(length, sum(widths))],
            starts,
            *values,
        )[0]

    def tokens_of(i, value, got):
        return copy_call(
            lambda n, a, o: [
                (view(a[0], (0, rows), (at(n, i), eighth)), view(o[0], (0, rows), (0, eighth))),
                (a[1], view(o[0], (rows, rows), (0, eighth))),
            ],
            [like(both, eighth)],
            starts,
            value,
            got,
        )[0]

    up_sent = kernel_call(up_sent_kernel, [like(number, size, kvq)], up)[0]
    up_all = lax.all_to_all(
        done(up_sent), ("fsdp", "own"), split_axis=0, concat_axis=0, tiled=True
    ).reshape(number * size, kvq)
    down_got = swap(done(rows_at(2, step(down), eighth)), "own")
    packet_here = done(
        kernel_call(packet_kernel, [like(rows, kv + size)], step(cotangent), token_adapter)[0]
    )
    packet = swap(packet_here, "own")
    x_got = [swap(done(columns_at(2, step(tokens))), "own")]
    down_piece = done(
        copy_call(
            lambda n, a, o: [
                (view(a[0], (at(n, 0), eighth), (0, size)), view(o[0], (0, eighth), (0, size))),
                (a[1], view(o[0], (0, eighth), (size, size))),
            ],
            [like(eighth, wide)],
            starts,
            down,
            step(down_got),
        )[0]
    )
    down_near = along(down_piece, NEIGHBOURS)
    packet, up_all = step(packet, up_all)
    dy_half, ids, dy_quarter = kernel_call(
        unpack_kernel,
        [like(both, kv), like(both, size), like(both, kvq)],
        packet_here,
        packet,
        scalars=flags,
    )
    compact = like(both, size, kind=f32)
    back_part = done(kernel_call(back_kernel, [compact], ids, dy_quarter, up_all)[0])
    back_tp = swap(back_part, "tp")
    weight_here = done(rows_at(0, step(frozen_value_weight), eighth))
    weight_near = along(weight_here, NEIGHBOURS)
    back_part = done(kernel_call(add_kernel, [compact], back_part, step(back_tp))[0])
    back_got = swap(back_part, "own")
    down_near, x_got[0] = step(down_near, x_got[0])
    crossing = done(side_by_side(down_piece, down_near))
    down_crossed = along(crossing, MIDDLE)
    down_other = swap(crossing, "rep")
    back_wide, back_sent = kernel_call(
        back_end_kernel,
        [like(both, number * size), like(both, wide)],
        ids,
        back_part,
        step(back_got),
        scalars=numbers,
    )
    back_in = along(done(back_sent), INWARD)
    crossing = done(side_by_side(weight_here, step(weight_near)))
    weight_crossed = along(crossing, MIDDLE)
    x_got.append(swap(done(columns_at(3, step(tokens))), "own"))
    back_in_wide = done(
        kernel_call(
            spread_in_kernel, [like(both, number * size)], step(back_in), scalars=numbers
        )[0]
    )
    x_mine = done(tokens_of(0, tokens, step(x_got[0])))
    x_in = [along(x_mine, INWARD)]
    weight_other = done(rows_at(1, step(frozen_value_weight), eighth))
    down_crossed = done(step(down_crossed))
    down_outer = along(down_crossed, OUTWARD)
    weight_near, down_other = step(weight_near, down_other)
    weight_near_other = swap(done(weight_near), "rep")
    x_other = done(tokens_of(1, tokens, step(x_got[1])))
    x_in.append(along(x_other, INWARD))
    x_both = [x_mine, x_other]

    def to_middle(half):
        x_in[half] = step(x_in[half])
        sums = kernel_call(
            to_middle_kernel,
            [like(eighth, 2 * wide)],
            x_both[half],
            back_wide,
            x_in[half],
            back_in_wide,
        )[0]
        return along(done(sums), MIDDLE)

    def to_end(half, crossed):
        sums = kernel_call(
            to_end_kernel, [like(eighth, wide)], x_both[half], back_wide, step(crossed)
        )[0]
        return along(done(sums), OUTWARD)

    def finish(half, crossed, outer, *others):
        outer, *_ = step(outer, x_mine, *others)
        here, there = kernel_call(
            finish_kernel,
            [like(eighth, size)] * 2,
            x_both[half],
            back_wide,
            x_in[half],
            back_in_wide,
            crossed,
            outer,
        )
        return done(here), there

    def far_of(crossed, outer):
        out = like(*crossed.shape)
        return kernel_call(far_kernel, [out], crossed, outer, scalars=flags)[0]

    middle = [to_middle(0)]
    weight_crossed = done(step(weight_crossed))
    weight_outer = along(weight_crossed, OUTWARD)
    down_outer, weight_near_other = step(down_outer, weight_near_other)
    down_far = done(far_of(down_crossed, down_outer))
    down_far_other = swap(down_far, "rep")
    middle.append(to_middle(1))
    outward = [to_end(0, middle[0])]
    dy_tp = swap(step(dy_half), "tp")
    dy_line = done(
        kernel_call(
            dy_line_kernel, [like(both, 2 * kv)], dy_half, step(dy_tp), scalars=places
        )[0]
    )
    weight_far = done(far_of(weight_crossed, step(weight_outer)))
    weight_far_other = swap(weight_far, "rep")
    half_grad = [like(rows, eighth)] * 2
    low_part = done(
        kernel_call(
            low_kernel,
            [compact],
            ids,
            x_mine,
            x_other,
            down_piece,
            down_near,
            down_far,
            down_other,
            step(down_far_other),
            scalars=numbers,
        )[0]
    )
    low_tp = swap(low_part, "tp")
    blocks = [like(2, both, cols, kind=f32)] * 2
    y_first = kernel_call(
        y_kernel, blocks, step(x_mine), weight_here, weight_near, weight_far, scalars=flags
    )
    done(y_first[0])
    low_part = done(kernel_call(add_kernel, [compact], low_part, step(low_tp))[0])
    low_got = swap(low_part, "own")
    dx_mine, dx_first_sent = kernel_call(
        dx_kernel,
        half_grad,
        step(dy_line),
        back_wide,
        weight_here,
        weight_near,
        weight_far,
        down_piece,
        down_near,
        down_far,
    )
    done(dx_mine)
    grad_here, grad_sent = finish(0, middle[0], outward[0])
    outward.append(to_end(1, middle[1]))
    low_got = step(low_got)
    dx_first_sent, grad_sent, _ = lax.optimization_barrier((dx_first_sent, grad_sent, low_got))
    grad_got = swap(grad_sent, "own")
    dx_mine_got = swap(dx_first_sent, "own")
    delta, *up_parts = kernel_call(
        low_end_kernel,
        [like(both, kvq)] + [like(wide, kvq)] * 4,
        ids,
        low_part,
        low_got,
        up_all,
        dy_quarter,
        scalars=numbers,
    )
    done(delta)
    up_got = [around(up_parts[k], k) for k in (1, 2, 3)]
    dx_other, dx_sent = kernel_call(
        dx_kernel,
        half_grad,
        dy_line,
        back_wide,
        weight_other,
        weight_near_other,
        step(weight_far_other),
        down_other,
        down_far_other,
    )
    dx_other_got = swap(done(dx_sent), "own")
    grad_last, grad_sent = finish(1, middle[1], outward[1], dx_mine_got)
    grad_last_got = swap(grad_sent, "own")
    *up_got, grad_got = step(*up_got, grad_got)
    up_mine, up_theirs = kernel_call(
        up_sum_kernel, [like(size, kvq)] * 2, up_parts[0], *up_got, scalars=numbers
    )
    up_theirs = swap(done(up_theirs), "own")
    x_other, dx_other_got = step(x_other, dx_other_got)
    y_keep, y_sent = kernel_call(
        y_kernel,
        blocks,
        x_other,
        weight_other,
        weight_near_other,
        weight_far_other,
        *y_first,
        scalars=flags,
    )
    y_got = swap(done(y_sent), "tp")
    y_got, grad_last_got = step(y_got, grad_last_got)
    y_here, y_sent = kernel_call(
        y_sum_kernel,
        [like(2, rows, cols, kind=f32), like(2, rows, cols)],
        y_keep,
        y_got,
        delta,
        scalars=flags,
    )
    y_got = swap(done(y_sent), "own")

    def in_place(axis, out, *pieces):
        def plan(n, a, o):
            spans = [[(0, length) for length in out.shape] for _ in range(4)]
            for i in range(4):
                spans[i][axis] = (at(n, i), eighth)
            return [(a[i], view(o[0], *spans[i])) for i in range(4)]

        return copy_call(plan, [out], starts, *pieces)[0]

    dx_other_got, _ = step(dx_other_got, dx_mine)
    input_grad = done(
        in_place(1, like(rows, width), dx_mine, dx_other, dx_mine_got, dx_other_got)
    )
    projected = done(kernel_call(y_end_kernel, [like(rows, kv)], y_here, step(y_got))[0])
    down_gradient = done(
        in_place(
            0, like(width, size), grad_here, grad_last, grad_got, step(grad_last_got)
        )[None]
    )
    up_gradient = kernel_call(
        up_place_kernel, [like(size, kv)], up_mine, step(up_theirs), scalars=flags
    )[0][None]
    return (projected, input_grad, down_gradient, up_gradient)


def body_routed(
    tokens,
    cotangent,
    frozen_value_weight,
    adapter_down_weight,
    adapter_up_weight,
    token_adapter,
    rank_step_count,
):
    rows, width_halved = tokens.shape
    half_kv = cotangent.shape[1]
    owning_adapters = lax.axis_size(("fsdp", "own"))
    greatest_rank = 3 * rows // (2 * owning_adapters)
    ids = token_adapter[:, 0]
    table = (ids[:, None] == jnp.arange(owning_adapters, dtype=jnp.int32)[None, :]).astype(
        f32
    )
    order = jnp.arange(rows, dtype=jnp.int32)
    earlier = (order[:, None] > order[None, :]).astype(f32)
    before = jnp.dot(earlier, table, precision=lax.Precision.HIGHEST)
    place = jnp.sum(before * table, axis=1).astype(jnp.int32)
    slot = ids * greatest_rank + place
    source_rows = jnp.full((owning_adapters * greatest_rank,), rows, jnp.int32).at[slot].set(order)
    padded_x = jnp.concatenate([tokens, jnp.zeros((1, width_halved), bf16)], axis=0)
    padded_dy = jnp.concatenate([cotangent, jnp.zeros((1, half_kv), bf16)], axis=0)
    send_x = jnp.take(padded_x, source_rows, axis=0)
    send_dy = jnp.take(padded_dy, source_rows, axis=0)
    recv_x, recv_dy = (
        lax.all_to_all(
            send_x.reshape(owning_adapters, greatest_rank, width_halved),
            ("fsdp", "own"),
            split_axis=0,
            concat_axis=0,
            tiled=True,
        ),
        lax.all_to_all(
            send_dy.reshape(owning_adapters, greatest_rank, half_kv),
            ("fsdp", "own"),
            split_axis=0,
            concat_axis=0,
            tiled=True,
        ),
    )
    flat_x = recv_x.reshape(owning_adapters * greatest_rank, width_halved)
    flat_dy = recv_dy.reshape(owning_adapters * greatest_rank, half_kv)
    dy_full = lax.all_gather(cotangent, "tp", axis=1, tiled=True)
    whole = lax.all_gather(frozen_value_weight, "fsdp", axis=1, tiled=True)
    partial_y = jnp.dot(tokens, whole, preferred_element_type=f32)
    base_dx = contract_final_axis(dy_full, whole)
    base_y = lax.psum_scatter(partial_y, "tp", scatter_dimension=1, tiled=True)
    down_matrix = adapter_down_weight[0]
    up_matrix = adapter_up_weight[0]
    part_low = jnp.dot(flat_x, down_matrix, preferred_element_type=f32)
    part_back = contract_final_axis(flat_dy, up_matrix)
    low_sum, back_sum = lax.psum((part_low, part_back), "tp")
    width_rank = down_matrix.shape[1]
    rank = width_rank // 8 * rank_step_count[lax.axis_index(("fsdp", "own"))]
    keep = jnp.arange(width_rank, dtype=jnp.int32)[None, :] < rank
    scale = 16.0 / rank.astype(f32)
    low = jnp.where(keep, low_sum, 0.0).astype(bf16)
    backward_pass = (scale * jnp.where(keep, back_sum, 0.0)).astype(bf16)
    delta = (scale * jnp.dot(low, up_matrix, preferred_element_type=f32)).astype(
        bf16
    )
    adapter_input_gradient = contract_final_axis(backward_pass, down_matrix).astype(bf16)
    down_gradient = contract_first(flat_x, backward_pass).astype(bf16)[None]
    up_gradient = (scale * contract_first(low, flat_dy)).astype(bf16)[None]
    home_delta, home_dx = (
        lax.all_to_all(
            delta.reshape(owning_adapters, greatest_rank, half_kv),
            ("fsdp", "own"),
            split_axis=0,
            concat_axis=0,
            tiled=True,
        ),
        lax.all_to_all(
            adapter_input_gradient.reshape(owning_adapters, greatest_rank, width_halved),
            ("fsdp", "own"),
            split_axis=0,
            concat_axis=0,
            tiled=True,
        ),
    )
    adapter_delta_rows = jnp.take(
        home_delta.reshape(owning_adapters * greatest_rank, half_kv), slot, axis=0
    )
    input_gradient_rows = jnp.take(
        home_dx.reshape(owning_adapters * greatest_rank, width_halved), slot, axis=0
    )
    projected = (base_y + adapter_delta_rows.astype(f32)).astype(bf16)
    input_grad = (base_dx + input_gradient_rows.astype(f32)).astype(bf16)
    return (projected, input_grad, down_gradient, up_gradient)


def solution(mesh):
    placed = (
        P(("rep", "fsdp", "own"), "tp"),
        P(("rep", "fsdp", "own"), "tp"),
        P("tp", "fsdp"),
        P(("fsdp", "own"), "tp", None),
        P(("fsdp", "own"), None, "tp"),
        P(("rep", "fsdp", "own"), None),
        P(),
    )
    line = mesh.shape["fsdp"] == 4 and mesh.shape["own"] == 2 and mesh.shape["rep"] == 2
    return jax.shard_map(
        body_line if line else body_routed,
        mesh=mesh,
        in_specs=placed,
        out_specs=(
            P(("rep", "fsdp", "own"), "tp"),
            P(("rep", "fsdp", "own"), "tp"),
            P(("rep", "fsdp", "own"), "tp", None),
            P(("rep", "fsdp", "own"), None, "tp"),
        ),
        check_vma=False,
    )
```

```python
import jax
import jax.numpy as jnp
from jax import lax
from jax.experimental import pallas as pl
from jax.experimental.pallas import tpu as pltpu
from jax.sharding import PartitionSpec as P

bf16 = jnp.bfloat16
f32 = jnp.float32


def contract_first(left, right):
    return lax.dot_general(
        left, right, (((0,), (0,)), ((), ())), preferred_element_type=f32
    )


def contract_final_axis(left, right):
    return lax.dot_general(
        left, right, (((1,), (1,)), ((), ())), preferred_element_type=f32
    )


def matmul(left, right):
    return jnp.dot(left, right, preferred_element_type=f32)


PAIR = [(0, 1), (1, 0)]
NEIGHBOURS = [(0, 1), (1, 0), (2, 3), (3, 2)]
MIDDLE = [(1, 2), (2, 1)]
OUTWARD = [(1, 0), (2, 3)]
INWARD = [(0, 1), (3, 2)]


def swap(value, axis):
    return lax.ppermute(value, axis, PAIR)


def along(value, pairs):
    return lax.ppermute(value, "fsdp", pairs)


def kernel_call(body, outs, *operands, scalars=None, scratch=(), space=pltpu.VMEM):
    specs = [pl.BlockSpec(memory_space=space)] * len(operands)
    if scalars is not None:
        operands = (scalars, *operands)
        specs = [pl.BlockSpec(memory_space=pltpu.SMEM), *specs]
    return pl.pallas_call(
        body,
        out_shape=list(outs),
        in_specs=specs,
        out_specs=[pl.BlockSpec(memory_space=pltpu.VMEM)] * len(outs),
        scratch_shapes=list(scratch),
        compiler_params=pltpu.CompilerParams(vmem_limit_bytes=28 * 2**20),
        cost_estimate=pl.CostEstimate(flops=0, bytes_accessed=0, transcendentals=0),
    )(*operands)


def copy_call(plan, outs, scalars, *operands):
    count = len(plan(None, [None] * len(operands), [None] * len(outs)))

    def body(numbers, *refs):
        sems = refs[-1]
        pairs = plan(numbers, refs[: len(operands)], refs[len(operands) : -1])
        copies = [pltpu.make_async_copy(a, b, sems.at[i]) for i, (a, b) in enumerate(pairs)]
        for copy in copies:
            copy.start()
        for copy in copies:
            copy.wait()

    return kernel_call(
        body,
        outs,
        *operands,
        scalars=scalars,
        scratch=[pltpu.SemaphoreType.DMA((count,))],
        space=pl.ANY,
    )


def view(ref, *spans):
    if ref is None:
        return None
    index = tuple(
        pl.ds(start if isinstance(start, int) else pl.multiple_of(start, 128), size)
        for start, size in spans
    )
    return ref.at[index]


def at(numbers, i):
    return None if numbers is None else numbers[i]


def ranks_of(ranks, ids):
    total = jnp.zeros(ids.shape, f32)
    for a in range(ranks.shape[0]):
        total = jnp.where(ids == a, ranks[a].astype(f32), total)
    return total


def kept(ids, ranks, value):
    rank = ranks_of(ranks, ids)
    column = lax.broadcasted_iota(jnp.int32, value.shape, 1).astype(f32)
    return jnp.where(column < rank, value, 0.0), 16.0 / rank


def roll_rows(value):
    half = value.shape[0] // 2
    return jnp.concatenate([value[half:], value[:half]], axis=0)


def back_kernel(ids, dy, up, out):
    size = out.shape[1]
    token = ids[...].astype(f32)
    for i in range(0, up.shape[0] // size, 2):
        both = contract_final_axis(dy[...], up[i * size : (i + 2) * size, :])
        for j in (0, 1):
            part = jnp.where(token == i + j, both[:, j * size : (j + 1) * size], 0.0)
            out[...] = part if i + j == 0 else out[...] + part


def spread_into(out, token, value, order):
    size = value.shape[1]
    for i in range(out.shape[1] // size):
        a = order[i].astype(f32)
        out[:, i * size : (i + 1) * size] = jnp.where(token == a, value, 0.0).astype(bf16)


def back_end_kernel(numbers, ids, part, got, wide, sent):
    token = ids[...].astype(f32)
    count = numbers.shape[0] // 3
    ranks, order = [numbers[i] for i in range(count)], [numbers[count + i] for i in range(count)]
    value, scale = kept(token, jnp.stack(ranks), part[...] + roll_rows(got[...]))
    value = (scale * value).astype(bf16)
    size = value.shape[1]
    sent[:, :size] = value
    sent[:, size:] = ids[...]
    spread_into(wide, token, value.astype(f32), order)


def spread_in_kernel(numbers, packet, wide):
    size = packet.shape[1] // 2
    count = numbers.shape[0] // 3
    order = [numbers[count + i] for i in range(count)]
    spread_into(wide, packet[:, size:].astype(f32), packet[:, :size].astype(f32), order)


def low_kernel(numbers, ids, x_mine, x_other, own, near, far, own_near_other, far_other, out):
    size = out.shape[1]
    wide = 2 * size
    token = ids[...].astype(f32)
    mine = [own[...], near[...], far[:, :wide], far[:, wide:]]
    other = [
        own_near_other[:, :wide],
        own_near_other[:, wide:],
        far_other[:, :wide],
        far_other[:, wide:],
    ]
    for i in range(4):
        both = matmul(x_mine[...], mine[i]) + matmul(x_other[...], other[i])
        for j in (0, 1):
            place = numbers[numbers.shape[0] // 3 + 2 * i + j].astype(f32)
            part = jnp.where(token == place, both[:, j * size : (j + 1) * size], 0.0)
            out[...] = part if i + j == 0 else out[...] + part


def low_end_kernel(numbers, ids, part, got, up, dy, delta, *grads):
    token = ids[...].astype(f32)
    count = numbers.shape[0] // 3
    size = part.shape[1]
    ranks = jnp.stack([numbers[i] for i in range(count)])
    value, scale = kept(token, ranks, part[...] + roll_rows(got[...]))
    value = value.astype(bf16).astype(f32)

    def pair(first, second):
        return jnp.concatenate(
            [jnp.where(token == a, value, 0.0) for a in (first, second)], axis=1
        ).astype(bf16)

    total = 0.0
    for i, out in enumerate(grads):
        places = [numbers[2 * count + 2 * i + j].astype(f32) for j in (0, 1)]
        out[...] = contract_first(pair(*places), dy[...]).astype(bf16)
        total += matmul(pair(2 * i, 2 * i + 1), up[2 * i * size : 2 * (i + 1) * size, :])
    delta[...] = (scale[:, :1] * total).astype(bf16)


def to_middle_kernel(x_here, back, x_in, back_in, out):
    half = back.shape[1] // 2
    sums = contract_first(x_here[...], back[:, half:])
    out[...] = (sums + contract_first(x_in[...], back_in[:, half:])).astype(bf16)


def to_end_kernel(x_here, back, crossed, out):
    wide = out.shape[1]
    sums = contract_first(x_here[...], back[:, wide : 2 * wide])
    out[...] = (sums + crossed[:, wide:].astype(f32)).astype(bf16)


def finish_kernel(x_here, back, x_in, back_in, crossed, outer, here, there):
    size = here.shape[1]
    wide = 2 * size
    sums = contract_first(x_here[...], back[:, :wide])
    sums += contract_first(x_in[...], back_in[:, :wide])
    sums += crossed[:, :wide].astype(f32) + outer[...].astype(f32)
    here[...] = sums[:, :size].astype(bf16)
    there[...] = sums[:, size:].astype(bf16)


def up_sent_kernel(up, out):
    cols = out.shape[2]
    for i in range(out.shape[0]):
        out[i] = up[:, (i % 2) * cols : (i % 2 + 1) * cols]


def packet_kernel(cotangent, adapters, out):
    rows, kv = cotangent.shape
    size = out.shape[1] - kv
    out[:, :kv] = cotangent[...]
    numbers = jnp.broadcast_to(adapters[...].astype(f32), (rows, size))
    out[:, kv:] = numbers.astype(bf16)


def unpack_kernel(flags, here, there, half, ids, quarter):
    rows = here.shape[0]
    kv = half.shape[1]
    cols = quarter.shape[1]
    span = pl.ds(pl.multiple_of(flags[3] * cols, 128), cols)
    for i, packet in enumerate((here, there)):
        place = slice(i * rows, (i + 1) * rows)
        half[place] = packet[:, :kv]
        ids[place] = packet[:, kv:]
        quarter[place] = packet[:, span]


def dy_line_kernel(places, here, got, out):
    cols = out.shape[1] // 4
    for i in range(4):
        place = places[i]
        span = pl.ds(pl.multiple_of((place % 2) * cols, 128), cols)
        own = place // 2 == places[4]

        @pl.when(own)
        def _():
            out[:, i * cols : (i + 1) * cols] = here[:, span]

        @pl.when(jnp.logical_not(own))
        def _():
            out[:, i * cols : (i + 1) * cols] = got[:, span]


def far_kernel(flags, crossed, outer, out):
    @pl.when(flags[4] == 1)
    def _():
        out[...] = crossed[...]

    @pl.when(flags[4] == 0)
    def _():
        out[...] = outer[...]


def up_sum_kernel(numbers, first, second, third, fourth, here, there):
    count = numbers.shape[0] // 3
    size = here.shape[0]
    for i, out in enumerate((here, there)):
        adapter = numbers[count + i]
        rank = jnp.float32(1.0)
        for a in range(count):
            rank = jnp.where(adapter == a, numbers[a].astype(f32), rank)
        span = slice(i * size, (i + 1) * size)
        part = sum(v[span, :].astype(f32) for v in (first, second, third, fourth))
        out[...] = (jnp.full(part.shape, 16.0, f32) / rank * part).astype(bf16)


def up_place_kernel(flags, here, there, out):
    cols = here.shape[1]
    out[:, pl.ds(pl.multiple_of(flags[3] * cols, 128), cols)] = here[...]
    out[:, pl.ds(pl.multiple_of((1 - flags[3]) * cols, 128), cols)] = there[...]


def add_kernel(left, right, out):
    out[...] = left[...] + right[...]


def dx_kernel(dy, back, own, near, far, *rest):
    *adapter, here, there = rest
    rows, width = here.shape
    cols = own.shape[1]
    tile = min(cols, width)
    for t in range(width // tile):
        span = slice(t * tile, (t + 1) * tile)
        base = contract_final_axis(dy[:, :cols], own[span, :])
        base += contract_final_axis(dy[:, cols : 2 * cols], near[span, :])
        base += contract_final_axis(dy[:, 2 * cols :], far[span, :])
        lora, start = 0.0, 0
        for piece in adapter:
            stop = start + piece.shape[1]
            lora += contract_final_axis(back[:, start:stop], piece[span, :])
            start = stop
        total = (base + lora.astype(bf16).astype(f32)).astype(bf16)
        here[:, span] = total[:rows]
        there[:, span] = total[rows:]


def y_kernel(flags, tokens, own, near, far, *rest):
    *before, keep, send = rest
    cols = own.shape[1]

    def store(pair, first, part):
        mine = flags[0] == (1 if pair else 0)
        for i in (0, 1):
            place = (first + i) % 2
            block = matmul(tokens[...], part(i))

            @pl.when(mine)
            def _():
                keep[place] = block + before[0][place] if before else block

            @pl.when(jnp.logical_not(mine))
            def _():
                send[place] = block + before[1][place] if before else block

    store(True, flags[1], lambda i: (own, near)[i][...])
    store(False, flags[2], lambda i: far[:, i * cols : (i + 1) * cols])


def y_sum_kernel(flags, keep, got, delta, here, there):
    rows = here.shape[1]
    for i in (0, 1):
        added = jnp.where(flags[3] == i, delta[...].astype(f32), 0.0)
        total = keep[i] + got[i] + added
        here[i] = total[:rows]
        there[i] = total[rows:].astype(bf16)


def y_end_kernel(here, got, out):
    cols = here.shape[2]
    for i in (0, 1):
        out[:, i * cols : (i + 1) * cols] = (here[i] + got[i].astype(f32)).astype(bf16)


def body_line(
    tokens,
    cotangent,
    frozen_value_weight,
    adapter_down_weight,
    adapter_up_weight,
    token_adapter,
    rank_step_count,
):
    rows, width = tokens.shape
    kv = cotangent.shape[1]
    cols = frozen_value_weight.shape[1]
    down = adapter_down_weight[0]
    up = adapter_up_weight[0]
    size = down.shape[1]
    wide = 2 * size
    quarter = width // 2
    eighth = quarter // 2
    kvq = kv // 2
    both = 2 * rows
    z, x = lax.axis_index("fsdp"), lax.axis_index("own")
    y, c = lax.axis_index("rep"), lax.axis_index("tp")
    first_pair = z < 2
    is_middle = (z == 1) | (z == 2)
    line = [z, z + 1 - 2 * (z % 2), jnp.where(first_pair, 2, 1), jnp.where(first_pair, 3, 0)]
    adapters = jnp.stack([2 * t + o for t in line for o in (x, 1 - x)]).astype(jnp.int32)
    number = adapters.shape[0]
    starts = jnp.stack(
        [side * quarter + half * eighth for side in (x, 1 - x) for half in (y, 1 - y)]
    ).astype(jnp.int32)
    ranks = size // 8 * rank_step_count
    ring = jnp.stack([2 * ((z + k) % 4) + o for k in range(4) for o in (x, 1 - x)])
    numbers = jnp.concatenate([ranks, adapters, ring.astype(jnp.int32)])
    flags = jnp.stack([(c == 0) == first_pair, z % 2 == 1, z >= 2, x == 1, is_middle])
    flags = flags.astype(jnp.int32)
    places = jnp.stack([*line, c]).astype(jnp.int32)

    latest = []

    def step(*values):
        if latest:
            values = lax.optimization_barrier((*values, latest[0]))[: len(values)]
        return values[0] if len(values) == 1 else values

    def done(value):
        latest[:] = [value]
        return value

    def like(*shape, kind=bf16):
        return jax.ShapeDtypeStruct(shape, kind)

    def around(value, shift):
        return along(value, [(i, (i + shift) % 4) for i in range(4)])

    def rows_at(i, value, length):
        out = like(length, value.shape[1])
        return copy_call(
            lambda n, a, o: [(view(a[0], (at(n, i), length), (0, value.shape[1])), o[0])],
            [out],
            starts,
            value,
        )[0]

    def columns_at(i, value):
        out = like(value.shape[0], eighth)
        return copy_call(
            lambda n, a, o: [(view(a[0], (0, value.shape[0]), (at(n, i), eighth)), o[0])],
            [out],
            starts,
            value,
        )[0]

    def side_by_side(*values):
        widths = [v.shape[1] for v in values]
        length = values[0].shape[0]
        return copy_call(
            lambda n, a, o: [
                (a[i], view(o[0], (0, length), (sum(widths[:i]), widths[i])))
                for i in range(len(values))
            ],
            [like(length, sum(widths))],
            starts,
            *values,
        )[0]

    def tokens_of(i, value, got):
        return copy_call(
            lambda n, a, o: [
                (view(a[0], (0, rows), (at(n, i), eighth)), view(o[0], (0, rows), (0, eighth))),
                (a[1], view(o[0], (rows, rows), (0, eighth))),
            ],
            [like(both, eighth)],
            starts,
            value,
            got,
        )[0]

    up_sent = kernel_call(up_sent_kernel, [like(number, size, kvq)], up)[0]
    up_all = lax.all_to_all(
        done(up_sent), ("fsdp", "own"), split_axis=0, concat_axis=0, tiled=True
    ).reshape(number * size, kvq)
    down_got = swap(done(rows_at(2, step(down), eighth)), "own")
    packet_here = done(
        kernel_call(packet_kernel, [like(rows, kv + size)], step(cotangent), token_adapter)[0]
    )
    packet = swap(packet_here, "own")
    x_got = [swap(done(columns_at(2, step(tokens))), "own")]
    down_piece = done(
        copy_call(
            lambda n, a, o: [
                (view(a[0], (at(n, 0), eighth), (0, size)), view(o[0], (0, eighth), (0, size))),
                (a[1], view(o[0], (0, eighth), (size, size))),
            ],
            [like(eighth, wide)],
            starts,
            down,
            step(down_got),
        )[0]
    )
    down_near = along(down_piece, NEIGHBOURS)
    packet, up_all = step(packet, up_all)
    dy_half, ids, dy_quarter = kernel_call(
        unpack_kernel,
        [like(both, kv), like(both, size), like(both, kvq)],
        packet_here,
        packet,
        scalars=flags,
    )
    compact = like(both, size, kind=f32)
    back_part = done(kernel_call(back_kernel, [compact], ids, dy_quarter, up_all)[0])
    back_tp = swap(back_part, "tp")
    weight_here = done(rows_at(0, step(frozen_value_weight), eighth))
    weight_near = along(weight_here, NEIGHBOURS)
    back_part = done(kernel_call(add_kernel, [compact], back_part, step(back_tp))[0])
    back_got = swap(back_part, "own")
    down_near, x_got[0] = step(down_near, x_got[0])
    crossing = done(side_by_side(down_piece, down_near))
    down_crossed = along(crossing, MIDDLE)
    down_other = swap(crossing, "rep")
    back_wide, back_sent = kernel_call(
        back_end_kernel,
        [like(both, number * size), like(both, wide)],
        ids,
        back_part,
        step(back_got),
        scalars=numbers,
    )
    back_in = along(done(back_sent), INWARD)
    crossing = done(side_by_side(weight_here, step(weight_near)))
    weight_crossed = along(crossing, MIDDLE)
    x_got.append(swap(done(columns_at(3, step(tokens))), "own"))
    back_in_wide = done(
        kernel_call(
            spread_in_kernel, [like(both, number * size)], step(back_in), scalars=numbers
        )[0]
    )
    x_mine = done(tokens_of(0, tokens, step(x_got[0])))
    x_in = [along(x_mine, INWARD)]
    weight_other = done(rows_at(1, step(frozen_value_weight), eighth))
    down_crossed = done(step(down_crossed))
    down_outer = along(down_crossed, OUTWARD)
    weight_near, down_other = step(weight_near, down_other)
    weight_near_other = swap(done(weight_near), "rep")
    x_other = done(tokens_of(1, tokens, step(x_got[1])))
    x_in.append(along(x_other, INWARD))
    x_both = [x_mine, x_other]

    def to_middle(half):
        x_in[half] = step(x_in[half])
        sums = kernel_call(
            to_middle_kernel,
            [like(eighth, 2 * wide)],
            x_both[half],
            back_wide,
            x_in[half],
            back_in_wide,
        )[0]
        return along(done(sums), MIDDLE)

    def to_end(half, crossed):
        sums = kernel_call(
            to_end_kernel, [like(eighth, wide)], x_both[half], back_wide, step(crossed)
        )[0]
        return along(done(sums), OUTWARD)

    def finish(half, crossed, outer, *others):
        outer, *_ = step(outer, x_mine, *others)
        here, there = kernel_call(
            finish_kernel,
            [like(eighth, size)] * 2,
            x_both[half],
            back_wide,
            x_in[half],
            back_in_wide,
            crossed,
            outer,
        )
        return done(here), there

    def far_of(crossed, outer):
        out = like(*crossed.shape)
        return kernel_call(far_kernel, [out], crossed, outer, scalars=flags)[0]

    middle = [to_middle(0)]
    weight_crossed = done(step(weight_crossed))
    weight_outer = along(weight_crossed, OUTWARD)
    dy_half, weight_near_other = step(dy_half, weight_near_other)
    dy_tp = swap(dy_half, "tp")
    dy_line = done(
        kernel_call(
            dy_line_kernel, [like(both, 2 * kv)], dy_half, step(dy_tp), scalars=places
        )[0]
    )
    down_far = done(far_of(down_crossed, step(down_outer)))
    down_far_other = swap(down_far, "rep")
    middle.append(to_middle(1))
    outward = [to_end(0, middle[0])]
    weight_far = done(far_of(weight_crossed, step(weight_outer)))
    weight_far_other = swap(weight_far, "rep")
    half_grad = [like(rows, eighth)] * 2
    dx_mine, dx_sent = kernel_call(
        dx_kernel,
        half_grad,
        step(dy_line),
        back_wide,
        weight_here,
        weight_near,
        weight_far,
        down_piece,
        down_near,
        down_far,
    )
    dx_mine_got = swap(done(dx_sent), "own")

    low_part = done(
        kernel_call(
            low_kernel,
            [compact],
            ids,
            x_mine,
            x_other,
            down_piece,
            down_near,
            down_far,
            down_other,
            step(down_far_other),
            scalars=numbers,
        )[0]
    )
    low_tp = swap(low_part, "tp")
    grad_here, grad_sent = finish(0, middle[0], outward[0])
    blocks = [like(2, both, cols, kind=f32)] * 2
    y_first = kernel_call(
        y_kernel, blocks, step(x_mine), weight_here, weight_near, weight_far, scalars=flags
    )
    done(y_first[0])
    low_tp, dx_mine_got = step(low_tp, dx_mine_got)
    low_part = done(kernel_call(add_kernel, [compact], low_part, low_tp)[0])
    low_got = swap(low_part, "own")
    outward.append(to_end(1, middle[1]))
    low_got = step(low_got)
    grad_got = swap(lax.optimization_barrier((grad_sent, low_got))[0], "own")
    delta, *up_parts = kernel_call(
        low_end_kernel,
        [like(both, kvq)] + [like(wide, kvq)] * 4,
        ids,
        low_part,
        low_got,
        up_all,
        dy_quarter,
        scalars=numbers,
    )
    done(delta)
    up_got = [around(up_parts[k], k) for k in (1, 2, 3)]
    dx_other, dx_sent = kernel_call(
        dx_kernel,
        half_grad,
        dy_line,
        back_wide,
        weight_other,
        weight_near_other,
        step(weight_far_other),
        down_other,
        down_far_other,
    )
    dx_other_got = swap(done(dx_sent), "own")
    grad_last, grad_sent = finish(1, middle[1], outward[1])
    grad_last_got = swap(grad_sent, "own")
    x_other, grad_got = step(x_other, grad_got)
    y_keep, y_sent = kernel_call(
        y_kernel,
        blocks,
        x_other,
        weight_other,
        weight_near_other,
        weight_far_other,
        *y_first,
        scalars=flags,
    )
    y_got = swap(done(y_sent), "tp")
    up_got = step(*up_got)
    up_mine, up_theirs = kernel_call(
        up_sum_kernel, [like(size, kvq)] * 2, up_parts[0], *up_got, scalars=numbers
    )
    up_theirs = swap(done(up_theirs), "own")
    y_got = step(y_got)
    y_here, y_sent = kernel_call(
        y_sum_kernel,
        [like(2, rows, cols, kind=f32), like(2, rows, cols)],
        y_keep,
        y_got,
        delta,
        scalars=flags,
    )
    y_got = swap(done(y_sent), "own")

    def in_place(axis, out, *pieces):
        def plan(n, a, o):
            spans = [[(0, length) for length in out.shape] for _ in range(4)]
            for i in range(4):
                spans[i][axis] = (at(n, i), eighth)
            return [(a[i], view(o[0], *spans[i])) for i in range(4)]

        return copy_call(plan, [out], starts, *pieces)[0]

    dx_other_got = step(dx_other_got)
    input_grad = done(
        in_place(1, like(rows, width), dx_mine, dx_other, dx_mine_got, dx_other_got)
    )
    projected = done(kernel_call(y_end_kernel, [like(rows, kv)], y_here, step(y_got))[0])
    down_gradient = done(
        in_place(
            0, like(width, size), grad_here, grad_last, grad_got, step(grad_last_got)
        )[None]
    )
    up_gradient = kernel_call(
        up_place_kernel, [like(size, kv)], up_mine, step(up_theirs), scalars=flags
    )[0][None]
    return (projected, input_grad, down_gradient, up_gradient)


def body_routed(
    tokens,
    cotangent,
    frozen_value_weight,
    adapter_down_weight,
    adapter_up_weight,
    token_adapter,
    rank_step_count,
):
    rows, width_halved = tokens.shape
    half_kv = cotangent.shape[1]
    owning_adapters = lax.axis_size(("fsdp", "own"))
    greatest_rank = 3 * rows // (2 * owning_adapters)
    ids = token_adapter[:, 0]
    table = (ids[:, None] == jnp.arange(owning_adapters, dtype=jnp.int32)[None, :]).astype(
        f32
    )
    order = jnp.arange(rows, dtype=jnp.int32)
    earlier = (order[:, None] > order[None, :]).astype(f32)
    before = jnp.dot(earlier, table, precision=lax.Precision.HIGHEST)
    place = jnp.sum(before * table, axis=1).astype(jnp.int32)
    slot = ids * greatest_rank + place
    source_rows = jnp.full((owning_adapters * greatest_rank,), rows, jnp.int32).at[slot].set(order)
    padded_x = jnp.concatenate([tokens, jnp.zeros((1, width_halved), bf16)], axis=0)
    padded_dy = jnp.concatenate([cotangent, jnp.zeros((1, half_kv), bf16)], axis=0)
    send_x = jnp.take(padded_x, source_rows, axis=0)
    send_dy = jnp.take(padded_dy, source_rows, axis=0)
    recv_x, recv_dy = (
        lax.all_to_all(
            send_x.reshape(owning_adapters, greatest_rank, width_halved),
            ("fsdp", "own"),
            split_axis=0,
            concat_axis=0,
            tiled=True,
        ),
        lax.all_to_all(
            send_dy.reshape(owning_adapters, greatest_rank, half_kv),
            ("fsdp", "own"),
            split_axis=0,
            concat_axis=0,
            tiled=True,
        ),
    )
    flat_x = recv_x.reshape(owning_adapters * greatest_rank, width_halved)
    flat_dy = recv_dy.reshape(owning_adapters * greatest_rank, half_kv)
    dy_full = lax.all_gather(cotangent, "tp", axis=1, tiled=True)
    whole = lax.all_gather(frozen_value_weight, "fsdp", axis=1, tiled=True)
    partial_y = jnp.dot(tokens, whole, preferred_element_type=f32)
    base_dx = contract_final_axis(dy_full, whole)
    base_y = lax.psum_scatter(partial_y, "tp", scatter_dimension=1, tiled=True)
    down_matrix = adapter_down_weight[0]
    up_matrix = adapter_up_weight[0]
    part_low = jnp.dot(flat_x, down_matrix, preferred_element_type=f32)
    part_back = contract_final_axis(flat_dy, up_matrix)
    low_sum, back_sum = lax.psum((part_low, part_back), "tp")
    width_rank = down_matrix.shape[1]
    rank = width_rank // 8 * rank_step_count[lax.axis_index(("fsdp", "own"))]
    keep = jnp.arange(width_rank, dtype=jnp.int32)[None, :] < rank
    scale = 16.0 / rank.astype(f32)
    low = jnp.where(keep, low_sum, 0.0).astype(bf16)
    backward_pass = (scale * jnp.where(keep, back_sum, 0.0)).astype(bf16)
    delta = (scale * jnp.dot(low, up_matrix, preferred_element_type=f32)).astype(
        bf16
    )
    adapter_input_gradient = contract_final_axis(backward_pass, down_matrix).astype(bf16)
    down_gradient = contract_first(flat_x, backward_pass).astype(bf16)[None]
    up_gradient = (scale * contract_first(low, flat_dy)).astype(bf16)[None]
    home_delta, home_dx = (
        lax.all_to_all(
            delta.reshape(owning_adapters, greatest_rank, half_kv),
            ("fsdp", "own"),
            split_axis=0,
            concat_axis=0,
            tiled=True,
        ),
        lax.all_to_all(
            adapter_input_gradient.reshape(owning_adapters, greatest_rank, width_halved),
            ("fsdp", "own"),
            split_axis=0,
            concat_axis=0,
            tiled=True,
        ),
    )
    adapter_delta_rows = jnp.take(
        home_delta.reshape(owning_adapters * greatest_rank, half_kv), slot, axis=0
    )
    input_gradient_rows = jnp.take(
        home_dx.reshape(owning_adapters * greatest_rank, width_halved), slot, axis=0
    )
    projected = (base_y + adapter_delta_rows.astype(f32)).astype(bf16)
    input_grad = (base_dx + input_gradient_rows.astype(f32)).astype(bf16)
    return (projected, input_grad, down_gradient, up_gradient)


def solution(mesh):
    placed = (
        P(("rep", "fsdp", "own"), "tp"),
        P(("rep", "fsdp", "own"), "tp"),
        P("tp", "fsdp"),
        P(("fsdp", "own"), "tp", None),
        P(("fsdp", "own"), None, "tp"),
        P(("rep", "fsdp", "own"), None),
        P(),
    )
    line = mesh.shape["fsdp"] == 4 and mesh.shape["own"] == 2 and mesh.shape["rep"] == 2
    return jax.shard_map(
        body_line if line else body_routed,
        mesh=mesh,
        in_specs=placed,
        out_specs=(
            P(("rep", "fsdp", "own"), "tp"),
            P(("rep", "fsdp", "own"), "tp"),
            P(("rep", "fsdp", "own"), "tp", None),
            P(("rep", "fsdp", "own"), None, "tp"),
        ),
        check_vma=False,
    )
```

```python
import jax
import jax.numpy as jnp
from jax import lax
from jax.experimental import pallas as pl
from jax.experimental.pallas import tpu as pltpu
from jax.sharding import PartitionSpec as P

bf16 = jnp.bfloat16
f32 = jnp.float32


def contract_first(left, right):
    return lax.dot_general(
        left, right, (((0,), (0,)), ((), ())), preferred_element_type=f32
    )


def contract_final_axis(left, right):
    return lax.dot_general(
        left, right, (((1,), (1,)), ((), ())), preferred_element_type=f32
    )


def matmul(left, right):
    return jnp.dot(left, right, preferred_element_type=f32)


PAIR = [(0, 1), (1, 0)]
NEIGHBOURS = [(0, 1), (1, 0), (2, 3), (3, 2)]
MIDDLE = [(1, 2), (2, 1)]
OUTWARD = [(1, 0), (2, 3)]
INWARD = [(0, 1), (3, 2)]


def swap(value, axis):
    return lax.ppermute(value, axis, PAIR)


def along(value, pairs):
    return lax.ppermute(value, "fsdp", pairs)


def kernel_call(body, outs, *operands, scalars=None, scratch=(), space=pltpu.VMEM):
    specs = [pl.BlockSpec(memory_space=space)] * len(operands)
    if scalars is not None:
        operands = (scalars, *operands)
        specs = [pl.BlockSpec(memory_space=pltpu.SMEM), *specs]
    return pl.pallas_call(
        body,
        out_shape=list(outs),
        in_specs=specs,
        out_specs=[pl.BlockSpec(memory_space=pltpu.VMEM)] * len(outs),
        scratch_shapes=list(scratch),
        compiler_params=pltpu.CompilerParams(vmem_limit_bytes=28 * 2**20),
        cost_estimate=pl.CostEstimate(flops=0, bytes_accessed=0, transcendentals=0),
    )(*operands)


def copy_call(plan, outs, scalars, *operands):
    count = len(plan(None, [None] * len(operands), [None] * len(outs)))

    def body(numbers, *refs):
        sems = refs[-1]
        pairs = plan(numbers, refs[: len(operands)], refs[len(operands) : -1])
        copies = [pltpu.make_async_copy(a, b, sems.at[i]) for i, (a, b) in enumerate(pairs)]
        for copy in copies:
            copy.start()
        for copy in copies:
            copy.wait()

    return kernel_call(
        body,
        outs,
        *operands,
        scalars=scalars,
        scratch=[pltpu.SemaphoreType.DMA((count,))],
        space=pl.ANY,
    )


def view(ref, *spans):
    if ref is None:
        return None
    index = tuple(
        pl.ds(start if isinstance(start, int) else pl.multiple_of(start, 128), size)
        for start, size in spans
    )
    return ref.at[index]


def at(numbers, i):
    return None if numbers is None else numbers[i]


def ranks_of(ranks, ids):
    total = jnp.zeros(ids.shape, f32)
    for a in range(ranks.shape[0]):
        total = jnp.where(ids == a, ranks[a].astype(f32), total)
    return total


def kept(ids, ranks, value):
    rank = ranks_of(ranks, ids)
    column = lax.broadcasted_iota(jnp.int32, value.shape, 1).astype(f32)
    return jnp.where(column < rank, value, 0.0), 16.0 / rank


def roll_rows(value):
    half = value.shape[0] // 2
    return jnp.concatenate([value[half:], value[:half]], axis=0)


def back_kernel(ids, dy, up, out):
    size = out.shape[1]
    token = ids[...].astype(f32)
    for i in range(0, up.shape[0] // size, 2):
        both = contract_final_axis(dy[...], up[i * size : (i + 2) * size, :])
        for j in (0, 1):
            part = jnp.where(token == i + j, both[:, j * size : (j + 1) * size], 0.0)
            out[...] = part if i + j == 0 else out[...] + part


def spread_into(out, token, value, order):
    size = value.shape[1]
    for i in range(out.shape[1] // size):
        a = order[i].astype(f32)
        out[:, i * size : (i + 1) * size] = jnp.where(token == a, value, 0.0).astype(bf16)


def back_end_kernel(numbers, ids, part, got, wide, sent):
    token = ids[...].astype(f32)
    count = numbers.shape[0] // 3
    ranks, order = [numbers[i] for i in range(count)], [numbers[count + i] for i in range(count)]
    value, scale = kept(token, jnp.stack(ranks), part[...] + roll_rows(got[...]))
    value = (scale * value).astype(bf16)
    size = value.shape[1]
    sent[:, :size] = value
    sent[:, size:] = ids[...]
    spread_into(wide, token, value.astype(f32), order)


def spread_in_kernel(numbers, packet, wide):
    size = packet.shape[1] // 2
    count = numbers.shape[0] // 3
    order = [numbers[count + i] for i in range(count)]
    spread_into(wide, packet[:, size:].astype(f32), packet[:, :size].astype(f32), order)


def low_kernel(numbers, ids, x_mine, x_other, own, near, far, own_near_other, far_other, out):
    size = out.shape[1]
    wide = 2 * size
    token = ids[...].astype(f32)
    mine = [own[...], near[...], far[:, :wide], far[:, wide:]]
    other = [
        own_near_other[:, :wide],
        own_near_other[:, wide:],
        far_other[:, :wide],
        far_other[:, wide:],
    ]
    for i in range(4):
        both = matmul(x_mine[...], mine[i]) + matmul(x_other[...], other[i])
        for j in (0, 1):
            place = numbers[numbers.shape[0] // 3 + 2 * i + j].astype(f32)
            part = jnp.where(token == place, both[:, j * size : (j + 1) * size], 0.0)
            out[...] = part if i + j == 0 else out[...] + part


def low_end_kernel(numbers, ids, part, got, up, dy, delta, *grads):
    token = ids[...].astype(f32)
    count = numbers.shape[0] // 3
    size = part.shape[1]
    ranks = jnp.stack([numbers[i] for i in range(count)])
    value, scale = kept(token, ranks, part[...] + roll_rows(got[...]))
    value = value.astype(bf16).astype(f32)

    def pair(first, second):
        return jnp.concatenate(
            [jnp.where(token == a, value, 0.0) for a in (first, second)], axis=1
        ).astype(bf16)

    total = 0.0
    for i, out in enumerate(grads):
        places = [numbers[2 * count + 2 * i + j].astype(f32) for j in (0, 1)]
        out[...] = contract_first(pair(*places), dy[...]).astype(bf16)
        total += matmul(pair(2 * i, 2 * i + 1), up[2 * i * size : 2 * (i + 1) * size, :])
    delta[...] = (scale[:, :1] * total).astype(bf16)


def to_middle_kernel(x_here, back, x_in, back_in, out):
    half = back.shape[1] // 2
    sums = contract_first(x_here[...], back[:, half:])
    out[...] = (sums + contract_first(x_in[...], back_in[:, half:])).astype(bf16)


def to_end_kernel(x_here, back, crossed, out):
    wide = out.shape[1]
    sums = contract_first(x_here[...], back[:, wide : 2 * wide])
    out[...] = (sums + crossed[:, wide:].astype(f32)).astype(bf16)


def finish_kernel(x_here, back, x_in, back_in, crossed, outer, here, there):
    size = here.shape[1]
    wide = 2 * size
    sums = contract_first(x_here[...], back[:, :wide])
    sums += contract_first(x_in[...], back_in[:, :wide])
    sums += crossed[:, :wide].astype(f32) + outer[...].astype(f32)
    here[...] = sums[:, :size].astype(bf16)
    there[...] = sums[:, size:].astype(bf16)


def up_sent_kernel(up, out):
    cols = out.shape[2]
    for i in range(out.shape[0]):
        out[i] = up[:, (i % 2) * cols : (i % 2 + 1) * cols]


def packet_kernel(cotangent, adapters, out):
    rows, kv = cotangent.shape
    size = out.shape[1] - kv
    out[:, :kv] = cotangent[...]
    numbers = jnp.broadcast_to(adapters[...].astype(f32), (rows, size))
    out[:, kv:] = numbers.astype(bf16)


def unpack_kernel(flags, here, there, half, ids, quarter):
    rows = here.shape[0]
    kv = half.shape[1]
    cols = quarter.shape[1]
    span = pl.ds(pl.multiple_of(flags[3] * cols, 128), cols)
    for i, packet in enumerate((here, there)):
        place = slice(i * rows, (i + 1) * rows)
        half[place] = packet[:, :kv]
        ids[place] = packet[:, kv:]
        quarter[place] = packet[:, span]


def dy_line_kernel(places, here, got, out):
    cols = out.shape[1] // 4
    for i in range(4):
        place = places[i]
        span = pl.ds(pl.multiple_of((place % 2) * cols, 128), cols)
        own = place // 2 == places[4]

        @pl.when(own)
        def _():
            out[:, i * cols : (i + 1) * cols] = here[:, span]

        @pl.when(jnp.logical_not(own))
        def _():
            out[:, i * cols : (i + 1) * cols] = got[:, span]


def far_kernel(flags, crossed, outer, out):
    @pl.when(flags[4] == 1)
    def _():
        out[...] = crossed[...]

    @pl.when(flags[4] == 0)
    def _():
        out[...] = outer[...]


def up_sum_kernel(numbers, first, second, third, fourth, here, there):
    count = numbers.shape[0] // 3
    size = here.shape[0]
    for i, out in enumerate((here, there)):
        adapter = numbers[count + i]
        rank = jnp.float32(1.0)
        for a in range(count):
            rank = jnp.where(adapter == a, numbers[a].astype(f32), rank)
        span = slice(i * size, (i + 1) * size)
        part = sum(v[span, :].astype(f32) for v in (first, second, third, fourth))
        out[...] = (jnp.full(part.shape, 16.0, f32) / rank * part).astype(bf16)


def up_place_kernel(flags, here, there, out):
    cols = here.shape[1]
    out[:, pl.ds(pl.multiple_of(flags[3] * cols, 128), cols)] = here[...]
    out[:, pl.ds(pl.multiple_of((1 - flags[3]) * cols, 128), cols)] = there[...]


def add_kernel(left, right, out):
    out[...] = left[...] + right[...]


def dx_kernel(dy, back, own, near, far, *rest):
    *adapter, here, there = rest
    rows, width = here.shape
    cols = own.shape[1]
    tile = min(cols, width)
    for t in range(width // tile):
        span = slice(t * tile, (t + 1) * tile)
        base = contract_final_axis(dy[:, :cols], own[span, :])
        base += contract_final_axis(dy[:, cols : 2 * cols], near[span, :])
        base += contract_final_axis(dy[:, 2 * cols :], far[span, :])
        lora, start = 0.0, 0
        for piece in adapter:
            stop = start + piece.shape[1]
            lora += contract_final_axis(back[:, start:stop], piece[span, :])
            start = stop
        total = (base + lora.astype(bf16).astype(f32)).astype(bf16)
        here[:, span] = total[:rows]
        there[:, span] = total[rows:]


def y_kernel(flags, tokens, own, near, far, *rest):
    *before, keep, send = rest
    cols = own.shape[1]

    def store(pair, first, part):
        mine = flags[0] == (1 if pair else 0)
        for i in (0, 1):
            place = (first + i) % 2
            block = matmul(tokens[...], part(i))

            @pl.when(mine)
            def _():
                keep[place] = block + before[0][place] if before else block

            @pl.when(jnp.logical_not(mine))
            def _():
                send[place] = block + before[1][place] if before else block

    store(True, flags[1], lambda i: (own, near)[i][...])
    store(False, flags[2], lambda i: far[:, i * cols : (i + 1) * cols])


def y_sum_kernel(flags, keep, got, delta, here, there):
    rows = here.shape[1]
    for i in (0, 1):
        added = jnp.where(flags[3] == i, delta[...].astype(f32), 0.0)
        total = keep[i] + got[i] + added
        here[i] = total[:rows]
        there[i] = total[rows:].astype(bf16)


def y_end_kernel(here, got, out):
    cols = here.shape[2]
    for i in (0, 1):
        out[:, i * cols : (i + 1) * cols] = (here[i] + got[i].astype(f32)).astype(bf16)


def body_line(
    tokens,
    cotangent,
    frozen_value_weight,
    adapter_down_weight,
    adapter_up_weight,
    token_adapter,
    rank_step_count,
):
    rows, width = tokens.shape
    kv = cotangent.shape[1]
    cols = frozen_value_weight.shape[1]
    down = adapter_down_weight[0]
    up = adapter_up_weight[0]
    size = down.shape[1]
    wide = 2 * size
    quarter = width // 2
    eighth = quarter // 2
    kvq = kv // 2
    both = 2 * rows
    z, x = lax.axis_index("fsdp"), lax.axis_index("own")
    y, c = lax.axis_index("rep"), lax.axis_index("tp")
    first_pair = z < 2
    is_middle = (z == 1) | (z == 2)
    line = [z, z + 1 - 2 * (z % 2), jnp.where(first_pair, 2, 1), jnp.where(first_pair, 3, 0)]
    adapters = jnp.stack([2 * t + o for t in line for o in (x, 1 - x)]).astype(jnp.int32)
    number = adapters.shape[0]
    starts = jnp.stack(
        [side * quarter + half * eighth for side in (x, 1 - x) for half in (y, 1 - y)]
    ).astype(jnp.int32)
    ranks = size // 8 * rank_step_count
    ring = jnp.stack([2 * ((z + k) % 4) + o for k in range(4) for o in (x, 1 - x)])
    numbers = jnp.concatenate([ranks, adapters, ring.astype(jnp.int32)])
    flags = jnp.stack([(c == 0) == first_pair, z % 2 == 1, z >= 2, x == 1, is_middle])
    flags = flags.astype(jnp.int32)
    places = jnp.stack([*line, c]).astype(jnp.int32)

    latest = []

    def step(*values):
        if latest:
            values = lax.optimization_barrier((*values, latest[0]))[: len(values)]
        return values[0] if len(values) == 1 else values

    def done(value):
        latest[:] = [value]
        return value

    def like(*shape, kind=bf16):
        return jax.ShapeDtypeStruct(shape, kind)

    def around(value, shift):
        return along(value, [(i, (i + shift) % 4) for i in range(4)])

    def rows_at(i, value, length):
        out = like(length, value.shape[1])
        return copy_call(
            lambda n, a, o: [(view(a[0], (at(n, i), length), (0, value.shape[1])), o[0])],
            [out],
            starts,
            value,
        )[0]

    def columns_at(i, value):
        out = like(value.shape[0], eighth)
        return copy_call(
            lambda n, a, o: [(view(a[0], (0, value.shape[0]), (at(n, i), eighth)), o[0])],
            [out],
            starts,
            value,
        )[0]

    def side_by_side(*values):
        widths = [v.shape[1] for v in values]
        length = values[0].shape[0]
        return copy_call(
            lambda n, a, o: [
                (a[i], view(o[0], (0, length), (sum(widths[:i]), widths[i])))
                for i in range(len(values))
            ],
            [like(length, sum(widths))],
            starts,
            *values,
        )[0]

    def tokens_of(i, value, got):
        return copy_call(
            lambda n, a, o: [
                (view(a[0], (0, rows), (at(n, i), eighth)), view(o[0], (0, rows), (0, eighth))),
                (a[1], view(o[0], (rows, rows), (0, eighth))),
            ],
            [like(both, eighth)],
            starts,
            value,
            got,
        )[0]

    up_sent = kernel_call(up_sent_kernel, [like(number, size, kvq)], up)[0]
    up_all = lax.all_to_all(
        done(up_sent), ("fsdp", "own"), split_axis=0, concat_axis=0, tiled=True
    ).reshape(number * size, kvq)
    down_got = swap(done(rows_at(2, step(down), eighth)), "own")
    packet_here = done(
        kernel_call(packet_kernel, [like(rows, kv + size)], step(cotangent), token_adapter)[0]
    )
    packet = swap(packet_here, "own")
    x_got = [swap(done(columns_at(2, step(tokens))), "own")]
    down_piece = done(
        copy_call(
            lambda n, a, o: [
                (view(a[0], (at(n, 0), eighth), (0, size)), view(o[0], (0, eighth), (0, size))),
                (a[1], view(o[0], (0, eighth), (size, size))),
            ],
            [like(eighth, wide)],
            starts,
            down,
            step(down_got),
        )[0]
    )
    down_near = along(down_piece, NEIGHBOURS)
    packet, up_all = step(packet, up_all)
    dy_half, ids, dy_quarter = kernel_call(
        unpack_kernel,
        [like(both, kv), like(both, size), like(both, kvq)],
        packet_here,
        packet,
        scalars=flags,
    )
    compact = like(both, size, kind=f32)
    back_part = done(kernel_call(back_kernel, [compact], ids, dy_quarter, up_all)[0])
    back_tp = swap(back_part, "tp")
    weight_here = done(rows_at(0, step(frozen_value_weight), eighth))
    weight_near = along(weight_here, NEIGHBOURS)
    back_part = done(kernel_call(add_kernel, [compact], back_part, step(back_tp))[0])
    back_got = swap(back_part, "own")
    down_near, x_got[0] = step(down_near, x_got[0])
    crossing = done(side_by_side(down_piece, down_near))
    down_crossed = along(crossing, MIDDLE)
    down_other = swap(crossing, "rep")
    back_wide, back_sent = kernel_call(
        back_end_kernel,
        [like(both, number * size), like(both, wide)],
        ids,
        back_part,
        step(back_got),
        scalars=numbers,
    )
    back_in = along(done(back_sent), INWARD)
    crossing = done(side_by_side(weight_here, step(weight_near)))
    weight_crossed = along(crossing, MIDDLE)
    x_got.append(swap(done(columns_at(3, step(tokens))), "own"))
    back_in_wide = done(
        kernel_call(
            spread_in_kernel, [like(both, number * size)], step(back_in), scalars=numbers
        )[0]
    )
    x_mine = done(tokens_of(0, tokens, step(x_got[0])))
    x_in = [along(x_mine, INWARD)]
    weight_other = done(rows_at(1, step(frozen_value_weight), eighth))
    down_crossed = done(step(down_crossed))
    down_outer = along(down_crossed, OUTWARD)
    weight_near, down_other = step(weight_near, down_other)
    weight_near_other = swap(done(weight_near), "rep")
    x_other = done(tokens_of(1, tokens, step(x_got[1])))
    x_in.append(along(x_other, INWARD))
    x_both = [x_mine, x_other]

    def to_middle(half):
        x_in[half] = step(x_in[half])
        sums = kernel_call(
            to_middle_kernel,
            [like(eighth, 2 * wide)],
            x_both[half],
            back_wide,
            x_in[half],
            back_in_wide,
        )[0]
        return along(done(sums), MIDDLE)

    def to_end(half, crossed):
        sums = kernel_call(
            to_end_kernel, [like(eighth, wide)], x_both[half], back_wide, step(crossed)
        )[0]
        return along(done(sums), OUTWARD)

    def finish(half, crossed, outer, *others):
        outer, *_ = step(outer, x_mine, *others)
        here, there = kernel_call(
            finish_kernel,
            [like(eighth, size)] * 2,
            x_both[half],
            back_wide,
            x_in[half],
            back_in_wide,
            crossed,
            outer,
        )
        return done(here), there

    def far_of(crossed, outer):
        out = like(*crossed.shape)
        return kernel_call(far_kernel, [out], crossed, outer, scalars=flags)[0]

    middle = [to_middle(0)]
    weight_crossed = done(step(weight_crossed))
    weight_outer = along(weight_crossed, OUTWARD)
    dy_half, weight_near_other = step(dy_half, weight_near_other)
    dy_tp = swap(dy_half, "tp")
    dy_line = done(
        kernel_call(
            dy_line_kernel, [like(both, 2 * kv)], dy_half, step(dy_tp), scalars=places
        )[0]
    )
    down_far = done(far_of(down_crossed, step(down_outer)))
    down_far_other = swap(down_far, "rep")
    middle.append(to_middle(1))
    outward = [to_end(0, middle[0])]
    weight_far = done(far_of(weight_crossed, step(weight_outer)))
    weight_far_other = swap(weight_far, "rep")
    half_grad = [like(rows, eighth)] * 2
    dx_mine, dx_sent = kernel_call(
        dx_kernel,
        half_grad,
        step(dy_line),
        back_wide,
        weight_here,
        weight_near,
        weight_far,
        down_piece,
        down_near,
        down_far,
    )
    dx_mine_got = swap(done(dx_sent), "own")

    low_part = done(
        kernel_call(
            low_kernel,
            [compact],
            ids,
            x_mine,
            x_other,
            down_piece,
            down_near,
            down_far,
            down_other,
            step(down_far_other),
            scalars=numbers,
        )[0]
    )
    low_tp = swap(low_part, "tp")
    grad_here, grad_sent = finish(0, middle[0], outward[0])
    blocks = [like(2, both, cols, kind=f32)] * 2
    y_first = kernel_call(
        y_kernel, blocks, step(x_mine), weight_here, weight_near, weight_far, scalars=flags
    )
    done(y_first[0])
    low_tp, dx_mine_got = step(low_tp, dx_mine_got)
    low_part = done(kernel_call(add_kernel, [compact], low_part, low_tp)[0])
    low_got = swap(low_part, "own")
    outward.append(to_end(1, middle[1]))
    low_got = step(low_got)
    grad_got = swap(lax.optimization_barrier((grad_sent, low_got))[0], "own")
    delta, *up_parts = kernel_call(
        low_end_kernel,
        [like(both, kvq)] + [like(wide, kvq)] * 4,
        ids,
        low_part,
        low_got,
        up_all,
        dy_quarter,
        scalars=numbers,
    )
    done(delta)
    up_got = [around(up_parts[k], k) for k in (1, 2, 3)]
    dx_other, dx_sent = kernel_call(
        dx_kernel,
        half_grad,
        dy_line,
        back_wide,
        weight_other,
        weight_near_other,
        step(weight_far_other),
        down_other,
        down_far_other,
    )
    dx_other_got = swap(done(dx_sent), "own")
    grad_last, grad_sent = finish(1, middle[1], outward[1])
    grad_last_got = swap(grad_sent, "own")
    *up_got, grad_got = step(*up_got, grad_got)
    up_mine, up_theirs = kernel_call(
        up_sum_kernel, [like(size, kvq)] * 2, up_parts[0], *up_got, scalars=numbers
    )
    up_theirs = swap(done(up_theirs), "own")
    x_other, dx_other_got = step(x_other, dx_other_got)
    y_keep, y_sent = kernel_call(
        y_kernel,
        blocks,
        x_other,
        weight_other,
        weight_near_other,
        weight_far_other,
        *y_first,
        scalars=flags,
    )
    y_got = swap(done(y_sent), "tp")
    y_got = step(y_got)
    y_here, y_sent = kernel_call(
        y_sum_kernel,
        [like(2, rows, cols, kind=f32), like(2, rows, cols)],
        y_keep,
        y_got,
        delta,
        scalars=flags,
    )
    y_got = swap(done(y_sent), "own")

    def in_place(axis, out, *pieces):
        def plan(n, a, o):
            spans = [[(0, length) for length in out.shape] for _ in range(4)]
            for i in range(4):
                spans[i][axis] = (at(n, i), eighth)
            return [(a[i], view(o[0], *spans[i])) for i in range(4)]

        return copy_call(plan, [out], starts, *pieces)[0]

    dx_other_got = step(dx_other_got)
    input_grad = done(
        in_place(1, like(rows, width), dx_mine, dx_other, dx_mine_got, dx_other_got)
    )
    projected = done(kernel_call(y_end_kernel, [like(rows, kv)], y_here, step(y_got))[0])
    down_gradient = done(
        in_place(
            0, like(width, size), grad_here, grad_last, grad_got, step(grad_last_got)
        )[None]
    )
    up_gradient = kernel_call(
        up_place_kernel, [like(size, kv)], up_mine, step(up_theirs), scalars=flags
    )[0][None]
    return (projected, input_grad, down_gradient, up_gradient)


def body_routed(
    tokens,
    cotangent,
    frozen_value_weight,
    adapter_down_weight,
    adapter_up_weight,
    token_adapter,
    rank_step_count,
):
    rows, width_halved = tokens.shape
    half_kv = cotangent.shape[1]
    owning_adapters = lax.axis_size(("fsdp", "own"))
    greatest_rank = 3 * rows // (2 * owning_adapters)
    ids = token_adapter[:, 0]
    table = (ids[:, None] == jnp.arange(owning_adapters, dtype=jnp.int32)[None, :]).astype(
        f32
    )
    order = jnp.arange(rows, dtype=jnp.int32)
    earlier = (order[:, None] > order[None, :]).astype(f32)
    before = jnp.dot(earlier, table, precision=lax.Precision.HIGHEST)
    place = jnp.sum(before * table, axis=1).astype(jnp.int32)
    slot = ids * greatest_rank + place
    source_rows = jnp.full((owning_adapters * greatest_rank,), rows, jnp.int32).at[slot].set(order)
    padded_x = jnp.concatenate([tokens, jnp.zeros((1, width_halved), bf16)], axis=0)
    padded_dy = jnp.concatenate([cotangent, jnp.zeros((1, half_kv), bf16)], axis=0)
    send_x = jnp.take(padded_x, source_rows, axis=0)
    send_dy = jnp.take(padded_dy, source_rows, axis=0)
    recv_x, recv_dy = (
        lax.all_to_all(
            send_x.reshape(owning_adapters, greatest_rank, width_halved),
            ("fsdp", "own"),
            split_axis=0,
            concat_axis=0,
            tiled=True,
        ),
        lax.all_to_all(
            send_dy.reshape(owning_adapters, greatest_rank, half_kv),
            ("fsdp", "own"),
            split_axis=0,
            concat_axis=0,
            tiled=True,
        ),
    )
    flat_x = recv_x.reshape(owning_adapters * greatest_rank, width_halved)
    flat_dy = recv_dy.reshape(owning_adapters * greatest_rank, half_kv)
    dy_full = lax.all_gather(cotangent, "tp", axis=1, tiled=True)
    whole = lax.all_gather(frozen_value_weight, "fsdp", axis=1, tiled=True)
    partial_y = jnp.dot(tokens, whole, preferred_element_type=f32)
    base_dx = contract_final_axis(dy_full, whole)
    base_y = lax.psum_scatter(partial_y, "tp", scatter_dimension=1, tiled=True)
    down_matrix = adapter_down_weight[0]
    up_matrix = adapter_up_weight[0]
    part_low = jnp.dot(flat_x, down_matrix, preferred_element_type=f32)
    part_back = contract_final_axis(flat_dy, up_matrix)
    low_sum, back_sum = lax.psum((part_low, part_back), "tp")
    width_rank = down_matrix.shape[1]
    rank = width_rank // 8 * rank_step_count[lax.axis_index(("fsdp", "own"))]
    keep = jnp.arange(width_rank, dtype=jnp.int32)[None, :] < rank
    scale = 16.0 / rank.astype(f32)
    low = jnp.where(keep, low_sum, 0.0).astype(bf16)
    backward_pass = (scale * jnp.where(keep, back_sum, 0.0)).astype(bf16)
    delta = (scale * jnp.dot(low, up_matrix, preferred_element_type=f32)).astype(
        bf16
    )
    adapter_input_gradient = contract_final_axis(backward_pass, down_matrix).astype(bf16)
    down_gradient = contract_first(flat_x, backward_pass).astype(bf16)[None]
    up_gradient = (scale * contract_first(low, flat_dy)).astype(bf16)[None]
    home_delta, home_dx = (
        lax.all_to_all(
            delta.reshape(owning_adapters, greatest_rank, half_kv),
            ("fsdp", "own"),
            split_axis=0,
            concat_axis=0,
            tiled=True,
        ),
        lax.all_to_all(
            adapter_input_gradient.reshape(owning_adapters, greatest_rank, width_halved),
            ("fsdp", "own"),
            split_axis=0,
            concat_axis=0,
            tiled=True,
        ),
    )
    adapter_delta_rows = jnp.take(
        home_delta.reshape(owning_adapters * greatest_rank, half_kv), slot, axis=0
    )
    input_gradient_rows = jnp.take(
        home_dx.reshape(owning_adapters * greatest_rank, width_halved), slot, axis=0
    )
    projected = (base_y + adapter_delta_rows.astype(f32)).astype(bf16)
    input_grad = (base_dx + input_gradient_rows.astype(f32)).astype(bf16)
    return (projected, input_grad, down_gradient, up_gradient)


def solution(mesh):
    placed = (
        P(("rep", "fsdp", "own"), "tp"),
        P(("rep", "fsdp", "own"), "tp"),
        P("tp", "fsdp"),
        P(("fsdp", "own"), "tp", None),
        P(("fsdp", "own"), None, "tp"),
        P(("rep", "fsdp", "own"), None),
        P(),
    )
    line = mesh.shape["fsdp"] == 4 and mesh.shape["own"] == 2 and mesh.shape["rep"] == 2
    return jax.shard_map(
        body_line if line else body_routed,
        mesh=mesh,
        in_specs=placed,
        out_specs=(
            P(("rep", "fsdp", "own"), "tp"),
            P(("rep", "fsdp", "own"), "tp"),
            P(("rep", "fsdp", "own"), "tp", None),
            P(("rep", "fsdp", "own"), None, "tp"),
        ),
        check_vma=False,
    )
```

```python
import jax
import jax.numpy as jnp
from jax import lax
from jax.experimental import pallas as pl
from jax.experimental.pallas import tpu as pltpu
from jax.sharding import PartitionSpec as P

bf16 = jnp.bfloat16
f32 = jnp.float32


def contract_first(left, right):
    return lax.dot_general(
        left, right, (((0,), (0,)), ((), ())), preferred_element_type=f32
    )


def contract_final_axis(left, right):
    return lax.dot_general(
        left, right, (((1,), (1,)), ((), ())), preferred_element_type=f32
    )


def matmul(left, right):
    return jnp.dot(left, right, preferred_element_type=f32)


PAIR = [(0, 1), (1, 0)]
NEIGHBOURS = [(0, 1), (1, 0), (2, 3), (3, 2)]
MIDDLE = [(1, 2), (2, 1)]
OUTWARD = [(1, 0), (2, 3)]
INWARD = [(0, 1), (3, 2)]


def swap(value, axis):
    return lax.ppermute(value, axis, PAIR)


def along(value, pairs):
    return lax.ppermute(value, "fsdp", pairs)


def kernel_call(body, outs, *operands, scalars=None, scratch=(), space=pltpu.VMEM):
    specs = [pl.BlockSpec(memory_space=space)] * len(operands)
    if scalars is not None:
        operands = (scalars, *operands)
        specs = [pl.BlockSpec(memory_space=pltpu.SMEM), *specs]
    return pl.pallas_call(
        body,
        out_shape=list(outs),
        in_specs=specs,
        out_specs=[pl.BlockSpec(memory_space=pltpu.VMEM)] * len(outs),
        scratch_shapes=list(scratch),
        compiler_params=pltpu.CompilerParams(vmem_limit_bytes=28 * 2**20),
        cost_estimate=pl.CostEstimate(flops=0, bytes_accessed=0, transcendentals=0),
    )(*operands)


def copy_call(plan, outs, scalars, *operands):
    count = len(plan(None, [None] * len(operands), [None] * len(outs)))

    def body(numbers, *refs):
        sems = refs[-1]
        pairs = plan(numbers, refs[: len(operands)], refs[len(operands) : -1])
        copies = [pltpu.make_async_copy(a, b, sems.at[i]) for i, (a, b) in enumerate(pairs)]
        for copy in copies:
            copy.start()
        for copy in copies:
            copy.wait()

    return kernel_call(
        body,
        outs,
        *operands,
        scalars=scalars,
        scratch=[pltpu.SemaphoreType.DMA((count,))],
        space=pl.ANY,
    )


def view(ref, *spans):
    if ref is None:
        return None
    index = tuple(
        pl.ds(start if isinstance(start, int) else pl.multiple_of(start, 128), size)
        for start, size in spans
    )
    return ref.at[index]


def at(numbers, i):
    return None if numbers is None else numbers[i]


def ranks_of(ranks, ids):
    total = jnp.zeros(ids.shape, f32)
    for a in range(ranks.shape[0]):
        total = jnp.where(ids == a, ranks[a].astype(f32), total)
    return total


def kept(ids, ranks, value):
    rank = ranks_of(ranks, ids)
    column = lax.broadcasted_iota(jnp.int32, value.shape, 1).astype(f32)
    return jnp.where(column < rank, value, 0.0), 16.0 / rank


def roll_rows(value):
    half = value.shape[0] // 2
    return jnp.concatenate([value[half:], value[:half]], axis=0)


def back_kernel(ids, dy, up, out):
    size = out.shape[1]
    token = ids[...].astype(f32)
    for i in range(0, up.shape[0] // size, 2):
        both = contract_final_axis(dy[...], up[i * size : (i + 2) * size, :])
        for j in (0, 1):
            part = jnp.where(token == i + j, both[:, j * size : (j + 1) * size], 0.0)
            out[...] = part if i + j == 0 else out[...] + part


def spread_into(out, token, value, order):
    size = value.shape[1]
    for i in range(out.shape[1] // size):
        a = order[i].astype(f32)
        out[:, i * size : (i + 1) * size] = jnp.where(token == a, value, 0.0).astype(bf16)


def back_end_kernel(numbers, ids, part, got, wide, sent):
    token = ids[...].astype(f32)
    count = numbers.shape[0] // 3
    ranks, order = [numbers[i] for i in range(count)], [numbers[count + i] for i in range(count)]
    value, scale = kept(token, jnp.stack(ranks), part[...] + roll_rows(got[...]))
    value = (scale * value).astype(bf16)
    size = value.shape[1]
    sent[:, :size] = value
    sent[:, size:] = ids[...]
    spread_into(wide, token, value.astype(f32), order)


def spread_in_kernel(numbers, packet, wide):
    size = packet.shape[1] // 2
    count = numbers.shape[0] // 3
    order = [numbers[count + i] for i in range(count)]
    spread_into(wide, packet[:, size:].astype(f32), packet[:, :size].astype(f32), order)


def low_kernel(numbers, ids, x_mine, x_other, own, near, far, own_near_other, far_other, out):
    size = out.shape[1]
    wide = 2 * size
    token = ids[...].astype(f32)
    mine = [own[...], near[...], far[:, :wide], far[:, wide:]]
    other = [
        own_near_other[:, :wide],
        own_near_other[:, wide:],
        far_other[:, :wide],
        far_other[:, wide:],
    ]
    for i in range(4):
        both = matmul(x_mine[...], mine[i]) + matmul(x_other[...], other[i])
        for j in (0, 1):
            place = numbers[numbers.shape[0] // 3 + 2 * i + j].astype(f32)
            part = jnp.where(token == place, both[:, j * size : (j + 1) * size], 0.0)
            out[...] = part if i + j == 0 else out[...] + part


def low_end_kernel(numbers, ids, part, got, up, dy, delta, *grads):
    token = ids[...].astype(f32)
    count = numbers.shape[0] // 3
    size = part.shape[1]
    ranks = jnp.stack([numbers[i] for i in range(count)])
    value, scale = kept(token, ranks, part[...] + roll_rows(got[...]))
    value = value.astype(bf16).astype(f32)

    def pair(first, second):
        return jnp.concatenate(
            [jnp.where(token == a, value, 0.0) for a in (first, second)], axis=1
        ).astype(bf16)

    total = 0.0
    for i, out in enumerate(grads):
        places = [numbers[2 * count + 2 * i + j].astype(f32) for j in (0, 1)]
        out[...] = contract_first(pair(*places), dy[...]).astype(bf16)
        total += matmul(pair(2 * i, 2 * i + 1), up[2 * i * size : 2 * (i + 1) * size, :])
    delta[...] = (scale[:, :1] * total).astype(bf16)


def to_middle_kernel(x_here, back, x_in, back_in, out):
    half = back.shape[1] // 2
    sums = contract_first(x_here[...], back[:, half:])
    out[...] = (sums + contract_first(x_in[...], back_in[:, half:])).astype(bf16)


def to_end_kernel(x_here, back, crossed, out):
    wide = out.shape[1]
    sums = contract_first(x_here[...], back[:, wide : 2 * wide])
    out[...] = (sums + crossed[:, wide:].astype(f32)).astype(bf16)


def finish_kernel(x_here, back, x_in, back_in, crossed, outer, here, there):
    size = here.shape[1]
    wide = 2 * size
    sums = contract_first(x_here[...], back[:, :wide])
    sums += contract_first(x_in[...], back_in[:, :wide])
    sums += crossed[:, :wide].astype(f32) + outer[...].astype(f32)
    here[...] = sums[:, :size].astype(bf16)
    there[...] = sums[:, size:].astype(bf16)


def up_sent_kernel(up, out):
    cols = out.shape[2]
    for i in range(out.shape[0]):
        out[i] = up[:, (i % 2) * cols : (i % 2 + 1) * cols]


def packet_kernel(cotangent, adapters, out):
    rows, kv = cotangent.shape
    size = out.shape[1] - kv
    out[:, :kv] = cotangent[...]
    numbers = jnp.broadcast_to(adapters[...].astype(f32), (rows, size))
    out[:, kv:] = numbers.astype(bf16)


def unpack_kernel(flags, here, there, half, ids, quarter):
    rows = here.shape[0]
    kv = half.shape[1]
    cols = quarter.shape[1]
    span = pl.ds(pl.multiple_of(flags[3] * cols, 128), cols)
    for i, packet in enumerate((here, there)):
        place = slice(i * rows, (i + 1) * rows)
        half[place] = packet[:, :kv]
        ids[place] = packet[:, kv:]
        quarter[place] = packet[:, span]


def dy_line_kernel(places, here, got, out):
    cols = out.shape[1] // 4
    for i in range(4):
        place = places[i]
        span = pl.ds(pl.multiple_of((place % 2) * cols, 128), cols)
        own = place // 2 == places[4]

        @pl.when(own)
        def _():
            out[:, i * cols : (i + 1) * cols] = here[:, span]

        @pl.when(jnp.logical_not(own))
        def _():
            out[:, i * cols : (i + 1) * cols] = got[:, span]


def far_kernel(flags, crossed, outer, out):
    @pl.when(flags[4] == 1)
    def _():
        out[...] = crossed[...]

    @pl.when(flags[4] == 0)
    def _():
        out[...] = outer[...]


def up_sum_kernel(numbers, first, second, third, fourth, here, there):
    count = numbers.shape[0] // 3
    size = here.shape[0]
    for i, out in enumerate((here, there)):
        adapter = numbers[count + i]
        rank = jnp.float32(1.0)
        for a in range(count):
            rank = jnp.where(adapter == a, numbers[a].astype(f32), rank)
        span = slice(i * size, (i + 1) * size)
        part = sum(v[span, :].astype(f32) for v in (first, second, third, fourth))
        out[...] = (jnp.full(part.shape, 16.0, f32) / rank * part).astype(bf16)


def up_place_kernel(flags, here, there, out):
    cols = here.shape[1]
    out[:, pl.ds(pl.multiple_of(flags[3] * cols, 128), cols)] = here[...]
    out[:, pl.ds(pl.multiple_of((1 - flags[3]) * cols, 128), cols)] = there[...]


def add_kernel(left, right, out):
    out[...] = left[...] + right[...]


def dx_kernel(dy, back, own, near, far, *rest):
    *adapter, here, there = rest
    rows, width = here.shape
    cols = own.shape[1]
    tile = min(cols, width)
    for t in range(width // tile):
        span = slice(t * tile, (t + 1) * tile)
        base = contract_final_axis(dy[:, :cols], own[span, :])
        base += contract_final_axis(dy[:, cols : 2 * cols], near[span, :])
        base += contract_final_axis(dy[:, 2 * cols :], far[span, :])
        lora, start = 0.0, 0
        for piece in adapter:
            stop = start + piece.shape[1]
            lora += contract_final_axis(back[:, start:stop], piece[span, :])
            start = stop
        total = (base + lora.astype(bf16).astype(f32)).astype(bf16)
        here[:, span] = total[:rows]
        there[:, span] = total[rows:]


def y_kernel(flags, tokens, own, near, far, *rest):
    *before, keep, send = rest
    cols = own.shape[1]

    def store(pair, first, part):
        mine = flags[0] == (1 if pair else 0)
        for i in (0, 1):
            place = (first + i) % 2
            block = matmul(tokens[...], part(i))

            @pl.when(mine)
            def _():
                keep[place] = block + before[0][place] if before else block

            @pl.when(jnp.logical_not(mine))
            def _():
                send[place] = block + before[1][place] if before else block

    store(True, flags[1], lambda i: (own, near)[i][...])
    store(False, flags[2], lambda i: far[:, i * cols : (i + 1) * cols])


def y_sum_kernel(flags, keep, got, delta, here, there):
    rows = here.shape[1]
    for i in (0, 1):
        added = jnp.where(flags[3] == i, delta[...].astype(f32), 0.0)
        total = keep[i] + got[i] + added
        here[i] = total[:rows]
        there[i] = total[rows:].astype(bf16)


def y_end_kernel(here, got, out):
    cols = here.shape[2]
    for i in (0, 1):
        out[:, i * cols : (i + 1) * cols] = (here[i] + got[i].astype(f32)).astype(bf16)


def body_line(
    tokens,
    cotangent,
    frozen_value_weight,
    adapter_down_weight,
    adapter_up_weight,
    token_adapter,
    rank_step_count,
):
    rows, width = tokens.shape
    kv = cotangent.shape[1]
    cols = frozen_value_weight.shape[1]
    down = adapter_down_weight[0]
    up = adapter_up_weight[0]
    size = down.shape[1]
    wide = 2 * size
    quarter = width // 2
    eighth = quarter // 2
    kvq = kv // 2
    both = 2 * rows
    z, x = lax.axis_index("fsdp"), lax.axis_index("own")
    y, c = lax.axis_index("rep"), lax.axis_index("tp")
    first_pair = z < 2
    is_middle = (z == 1) | (z == 2)
    line = [z, z + 1 - 2 * (z % 2), jnp.where(first_pair, 2, 1), jnp.where(first_pair, 3, 0)]
    adapters = jnp.stack([2 * t + o for t in line for o in (x, 1 - x)]).astype(jnp.int32)
    number = adapters.shape[0]
    starts = jnp.stack(
        [side * quarter + half * eighth for side in (x, 1 - x) for half in (y, 1 - y)]
    ).astype(jnp.int32)
    ranks = size // 8 * rank_step_count
    ring = jnp.stack([2 * ((z + k) % 4) + o for k in range(4) for o in (x, 1 - x)])
    numbers = jnp.concatenate([ranks, adapters, ring.astype(jnp.int32)])
    flags = jnp.stack([(c == 0) == first_pair, z % 2 == 1, z >= 2, x == 1, is_middle])
    flags = flags.astype(jnp.int32)
    places = jnp.stack([*line, c]).astype(jnp.int32)

    latest = []

    def step(*values):
        if latest:
            values = lax.optimization_barrier((*values, latest[0]))[: len(values)]
        return values[0] if len(values) == 1 else values

    def done(value):
        latest[:] = [value]
        return value

    def like(*shape, kind=bf16):
        return jax.ShapeDtypeStruct(shape, kind)

    def around(value, shift):
        return along(value, [(i, (i + shift) % 4) for i in range(4)])

    def rows_at(i, value, length):
        out = like(length, value.shape[1])
        return copy_call(
            lambda n, a, o: [(view(a[0], (at(n, i), length), (0, value.shape[1])), o[0])],
            [out],
            starts,
            value,
        )[0]

    def columns_at(i, value):
        out = like(value.shape[0], eighth)
        return copy_call(
            lambda n, a, o: [(view(a[0], (0, value.shape[0]), (at(n, i), eighth)), o[0])],
            [out],
            starts,
            value,
        )[0]

    def side_by_side(*values):
        widths = [v.shape[1] for v in values]
        length = values[0].shape[0]
        return copy_call(
            lambda n, a, o: [
                (a[i], view(o[0], (0, length), (sum(widths[:i]), widths[i])))
                for i in range(len(values))
            ],
            [like(length, sum(widths))],
            starts,
            *values,
        )[0]

    def tokens_of(i, value, got):
        return copy_call(
            lambda n, a, o: [
                (view(a[0], (0, rows), (at(n, i), eighth)), view(o[0], (0, rows), (0, eighth))),
                (a[1], view(o[0], (rows, rows), (0, eighth))),
            ],
            [like(both, eighth)],
            starts,
            value,
            got,
        )[0]

    up_sent = kernel_call(up_sent_kernel, [like(number, size, kvq)], up)[0]
    up_all = lax.all_to_all(
        done(up_sent), ("fsdp", "own"), split_axis=0, concat_axis=0, tiled=True
    ).reshape(number * size, kvq)
    down_got = swap(done(rows_at(2, step(down), eighth)), "own")
    packet_here = done(
        kernel_call(packet_kernel, [like(rows, kv + size)], step(cotangent), token_adapter)[0]
    )
    packet = swap(packet_here, "own")
    x_got = [swap(done(columns_at(2, step(tokens))), "own")]
    down_piece = done(
        copy_call(
            lambda n, a, o: [
                (view(a[0], (at(n, 0), eighth), (0, size)), view(o[0], (0, eighth), (0, size))),
                (a[1], view(o[0], (0, eighth), (size, size))),
            ],
            [like(eighth, wide)],
            starts,
            down,
            step(down_got),
        )[0]
    )
    down_near = along(down_piece, NEIGHBOURS)
    packet, up_all = step(packet, up_all)
    dy_half, ids, dy_quarter = kernel_call(
        unpack_kernel,
        [like(both, kv), like(both, size), like(both, kvq)],
        packet_here,
        packet,
        scalars=flags,
    )
    compact = like(both, size, kind=f32)
    back_part = done(kernel_call(back_kernel, [compact], ids, dy_quarter, up_all)[0])
    back_tp = swap(back_part, "tp")
    weight_here = done(rows_at(0, step(frozen_value_weight), eighth))
    weight_near = along(weight_here, NEIGHBOURS)
    back_part = done(kernel_call(add_kernel, [compact], back_part, step(back_tp))[0])
    back_got = swap(back_part, "own")
    down_near, x_got[0] = step(down_near, x_got[0])
    crossing = done(side_by_side(down_piece, down_near))
    down_crossed = along(crossing, MIDDLE)
    down_other = swap(crossing, "rep")
    back_wide, back_sent = kernel_call(
        back_end_kernel,
        [like(both, number * size), like(both, wide)],
        ids,
        back_part,
        step(back_got),
        scalars=numbers,
    )
    back_in = along(done(back_sent), INWARD)
    crossing = done(side_by_side(weight_here, step(weight_near)))
    weight_crossed = along(crossing, MIDDLE)
    x_got.append(swap(done(columns_at(3, step(tokens))), "own"))
    back_in_wide = done(
        kernel_call(
            spread_in_kernel, [like(both, number * size)], step(back_in), scalars=numbers
        )[0]
    )
    x_mine = done(tokens_of(0, tokens, step(x_got[0])))
    x_in = [along(x_mine, INWARD)]
    weight_other = done(rows_at(1, step(frozen_value_weight), eighth))
    down_crossed = done(step(down_crossed))
    down_outer = along(down_crossed, OUTWARD)
    weight_near, down_other = step(weight_near, down_other)
    weight_near_other = swap(done(weight_near), "rep")
    x_other = done(tokens_of(1, tokens, step(x_got[1])))
    x_in.append(along(x_other, INWARD))
    x_both = [x_mine, x_other]

    def to_middle(half):
        x_in[half] = step(x_in[half])
        sums = kernel_call(
            to_middle_kernel,
            [like(eighth, 2 * wide)],
            x_both[half],
            back_wide,
            x_in[half],
            back_in_wide,
        )[0]
        return along(done(sums), MIDDLE)

    def to_end(half, crossed):
        sums = kernel_call(
            to_end_kernel, [like(eighth, wide)], x_both[half], back_wide, step(crossed)
        )[0]
        return along(done(sums), OUTWARD)

    def finish(half, crossed, outer, *others):
        outer, *_ = step(outer, x_mine, *others)
        here, there = kernel_call(
            finish_kernel,
            [like(eighth, size)] * 2,
            x_both[half],
            back_wide,
            x_in[half],
            back_in_wide,
            crossed,
            outer,
        )
        return done(here), there

    def far_of(crossed, outer):
        out = like(*crossed.shape)
        return kernel_call(far_kernel, [out], crossed, outer, scalars=flags)[0]

    middle = [to_middle(0)]
    weight_crossed = done(step(weight_crossed))
    weight_outer = along(weight_crossed, OUTWARD)
    dy_half, weight_near_other = step(dy_half, weight_near_other)
    dy_tp = swap(dy_half, "tp")
    dy_line = done(
        kernel_call(
            dy_line_kernel, [like(both, 2 * kv)], dy_half, step(dy_tp), scalars=places
        )[0]
    )
    down_far = done(far_of(down_crossed, step(down_outer)))
    down_far_other = swap(down_far, "rep")
    middle.append(to_middle(1))
    outward = [to_end(0, middle[0])]
    weight_far = done(far_of(weight_crossed, step(weight_outer)))
    weight_far_other = swap(weight_far, "rep")
    half_grad = [like(rows, eighth)] * 2
    dx_mine, dx_sent = kernel_call(
        dx_kernel,
        half_grad,
        step(dy_line),
        back_wide,
        weight_here,
        weight_near,
        weight_far,
        down_piece,
        down_near,
        down_far,
    )
    dx_mine_got = swap(done(dx_sent), "own")

    low_part = done(
        kernel_call(
            low_kernel,
            [compact],
            ids,
            x_mine,
            x_other,
            down_piece,
            down_near,
            down_far,
            down_other,
            step(down_far_other),
            scalars=numbers,
        )[0]
    )
    low_tp = swap(low_part, "tp")
    grad_here, grad_sent = finish(0, middle[0], outward[0])
    blocks = [like(2, both, cols, kind=f32)] * 2
    y_first = kernel_call(
        y_kernel, blocks, step(x_mine), weight_here, weight_near, weight_far, scalars=flags
    )
    done(y_first[0])
    low_tp, dx_mine_got = step(low_tp, dx_mine_got)
    low_part = done(kernel_call(add_kernel, [compact], low_part, low_tp)[0])
    low_got = swap(low_part, "own")
    outward.append(to_end(1, middle[1]))
    low_got = step(low_got)
    grad_got = swap(lax.optimization_barrier((grad_sent, low_got))[0], "own")
    delta, *up_parts = kernel_call(
        low_end_kernel,
        [like(both, kvq)] + [like(wide, kvq)] * 4,
        ids,
        low_part,
        low_got,
        up_all,
        dy_quarter,
        scalars=numbers,
    )
    done(delta)
    up_got = [around(up_parts[k], k) for k in (1, 2, 3)]
    dx_other, dx_sent = kernel_call(
        dx_kernel,
        half_grad,
        dy_line,
        back_wide,
        weight_other,
        weight_near_other,
        step(weight_far_other),
        down_other,
        down_far_other,
    )
    dx_other_got = swap(done(dx_sent), "own")
    grad_last, grad_sent = finish(1, middle[1], outward[1], grad_got)
    grad_last_got = swap(grad_sent, "own")
    up_got = step(*up_got)
    up_mine, up_theirs = kernel_call(
        up_sum_kernel, [like(size, kvq)] * 2, up_parts[0], *up_got, scalars=numbers
    )
    up_theirs = swap(done(up_theirs), "own")
    x_other, dx_other_got, grad_last_got = step(x_other, dx_other_got, grad_last_got)
    y_keep, y_sent = kernel_call(
        y_kernel,
        blocks,
        x_other,
        weight_other,
        weight_near_other,
        weight_far_other,
        *y_first,
        scalars=flags,
    )
    y_got = swap(done(y_sent), "tp")
    y_got = step(y_got)
    y_here, y_sent = kernel_call(
        y_sum_kernel,
        [like(2, rows, cols, kind=f32), like(2, rows, cols)],
        y_keep,
        y_got,
        delta,
        scalars=flags,
    )
    y_got = swap(done(y_sent), "own")

    def in_place(axis, out, *pieces):
        def plan(n, a, o):
            spans = [[(0, length) for length in out.shape] for _ in range(4)]
            for i in range(4):
                spans[i][axis] = (at(n, i), eighth)
            return [(a[i], view(o[0], *spans[i])) for i in range(4)]

        return copy_call(plan, [out], starts, *pieces)[0]

    dx_other_got = step(dx_other_got)
    input_grad = done(
        in_place(1, like(rows, width), dx_mine, dx_other, dx_mine_got, dx_other_got)
    )
    projected = done(kernel_call(y_end_kernel, [like(rows, kv)], y_here, step(y_got))[0])
    down_gradient = done(
        in_place(
            0, like(width, size), grad_here, grad_last, grad_got, step(grad_last_got)
        )[None]
    )
    up_gradient = kernel_call(
        up_place_kernel, [like(size, kv)], up_mine, step(up_theirs), scalars=flags
    )[0][None]
    return (projected, input_grad, down_gradient, up_gradient)


def body_routed(
    tokens,
    cotangent,
    frozen_value_weight,
    adapter_down_weight,
    adapter_up_weight,
    token_adapter,
    rank_step_count,
):
    rows, width_halved = tokens.shape
    half_kv = cotangent.shape[1]
    owning_adapters = lax.axis_size(("fsdp", "own"))
    greatest_rank = 3 * rows // (2 * owning_adapters)
    ids = token_adapter[:, 0]
    table = (ids[:, None] == jnp.arange(owning_adapters, dtype=jnp.int32)[None, :]).astype(
        f32
    )
    order = jnp.arange(rows, dtype=jnp.int32)
    earlier = (order[:, None] > order[None, :]).astype(f32)
    before = jnp.dot(earlier, table, precision=lax.Precision.HIGHEST)
    place = jnp.sum(before * table, axis=1).astype(jnp.int32)
    slot = ids * greatest_rank + place
    source_rows = jnp.full((owning_adapters * greatest_rank,), rows, jnp.int32).at[slot].set(order)
    padded_x = jnp.concatenate([tokens, jnp.zeros((1, width_halved), bf16)], axis=0)
    padded_dy = jnp.concatenate([cotangent, jnp.zeros((1, half_kv), bf16)], axis=0)
    send_x = jnp.take(padded_x, source_rows, axis=0)
    send_dy = jnp.take(padded_dy, source_rows, axis=0)
    recv_x, recv_dy = (
        lax.all_to_all(
            send_x.reshape(owning_adapters, greatest_rank, width_halved),
            ("fsdp", "own"),
            split_axis=0,
            concat_axis=0,
            tiled=True,
        ),
        lax.all_to_all(
            send_dy.reshape(owning_adapters, greatest_rank, half_kv),
            ("fsdp", "own"),
            split_axis=0,
            concat_axis=0,
            tiled=True,
        ),
    )
    flat_x = recv_x.reshape(owning_adapters * greatest_rank, width_halved)
    flat_dy = recv_dy.reshape(owning_adapters * greatest_rank, half_kv)
    dy_full = lax.all_gather(cotangent, "tp", axis=1, tiled=True)
    whole = lax.all_gather(frozen_value_weight, "fsdp", axis=1, tiled=True)
    partial_y = jnp.dot(tokens, whole, preferred_element_type=f32)
    base_dx = contract_final_axis(dy_full, whole)
    base_y = lax.psum_scatter(partial_y, "tp", scatter_dimension=1, tiled=True)
    down_matrix = adapter_down_weight[0]
    up_matrix = adapter_up_weight[0]
    part_low = jnp.dot(flat_x, down_matrix, preferred_element_type=f32)
    part_back = contract_final_axis(flat_dy, up_matrix)
    low_sum, back_sum = lax.psum((part_low, part_back), "tp")
    width_rank = down_matrix.shape[1]
    rank = width_rank // 8 * rank_step_count[lax.axis_index(("fsdp", "own"))]
    keep = jnp.arange(width_rank, dtype=jnp.int32)[None, :] < rank
    scale = 16.0 / rank.astype(f32)
    low = jnp.where(keep, low_sum, 0.0).astype(bf16)
    backward_pass = (scale * jnp.where(keep, back_sum, 0.0)).astype(bf16)
    delta = (scale * jnp.dot(low, up_matrix, preferred_element_type=f32)).astype(
        bf16
    )
    adapter_input_gradient = contract_final_axis(backward_pass, down_matrix).astype(bf16)
    down_gradient = contract_first(flat_x, backward_pass).astype(bf16)[None]
    up_gradient = (scale * contract_first(low, flat_dy)).astype(bf16)[None]
    home_delta, home_dx = (
        lax.all_to_all(
            delta.reshape(owning_adapters, greatest_rank, half_kv),
            ("fsdp", "own"),
            split_axis=0,
            concat_axis=0,
            tiled=True,
        ),
        lax.all_to_all(
            adapter_input_gradient.reshape(owning_adapters, greatest_rank, width_halved),
            ("fsdp", "own"),
            split_axis=0,
            concat_axis=0,
            tiled=True,
        ),
    )
    adapter_delta_rows = jnp.take(
        home_delta.reshape(owning_adapters * greatest_rank, half_kv), slot, axis=0
    )
    input_gradient_rows = jnp.take(
        home_dx.reshape(owning_adapters * greatest_rank, width_halved), slot, axis=0
    )
    projected = (base_y + adapter_delta_rows.astype(f32)).astype(bf16)
    input_grad = (base_dx + input_gradient_rows.astype(f32)).astype(bf16)
    return (projected, input_grad, down_gradient, up_gradient)


def solution(mesh):
    placed = (
        P(("rep", "fsdp", "own"), "tp"),
        P(("rep", "fsdp", "own"), "tp"),
        P("tp", "fsdp"),
        P(("fsdp", "own"), "tp", None),
        P(("fsdp", "own"), None, "tp"),
        P(("rep", "fsdp", "own"), None),
        P(),
    )
    line = mesh.shape["fsdp"] == 4 and mesh.shape["own"] == 2 and mesh.shape["rep"] == 2
    return jax.shard_map(
        body_line if line else body_routed,
        mesh=mesh,
        in_specs=placed,
        out_specs=(
            P(("rep", "fsdp", "own"), "tp"),
            P(("rep", "fsdp", "own"), "tp"),
            P(("rep", "fsdp", "own"), "tp", None),
            P(("rep", "fsdp", "own"), None, "tp"),
        ),
        check_vma=False,
    )
```

```python
import jax
import jax.numpy as jnp
from jax import lax
from jax.experimental import pallas as pl
from jax.experimental.pallas import tpu as pltpu
from jax.sharding import PartitionSpec as P

bf16 = jnp.bfloat16
f32 = jnp.float32


def contract_first(left, right):
    return lax.dot_general(
        left, right, (((0,), (0,)), ((), ())), preferred_element_type=f32
    )


def contract_final_axis(left, right):
    return lax.dot_general(
        left, right, (((1,), (1,)), ((), ())), preferred_element_type=f32
    )


def matmul(left, right):
    return jnp.dot(left, right, preferred_element_type=f32)


PAIR = [(0, 1), (1, 0)]
NEIGHBOURS = [(0, 1), (1, 0), (2, 3), (3, 2)]
MIDDLE = [(1, 2), (2, 1)]
OUTWARD = [(1, 0), (2, 3)]
INWARD = [(0, 1), (3, 2)]


def swap(value, axis):
    return lax.ppermute(value, axis, PAIR)


def along(value, pairs):
    return lax.ppermute(value, "fsdp", pairs)


def kernel_call(body, outs, *operands, scalars=None, scratch=(), space=pltpu.VMEM):
    specs = [pl.BlockSpec(memory_space=space)] * len(operands)
    if scalars is not None:
        operands = (scalars, *operands)
        specs = [pl.BlockSpec(memory_space=pltpu.SMEM), *specs]
    return pl.pallas_call(
        body,
        out_shape=list(outs),
        in_specs=specs,
        out_specs=[pl.BlockSpec(memory_space=pltpu.VMEM)] * len(outs),
        scratch_shapes=list(scratch),
        compiler_params=pltpu.CompilerParams(vmem_limit_bytes=28 * 2**20),
        cost_estimate=pl.CostEstimate(flops=0, bytes_accessed=0, transcendentals=0),
    )(*operands)


def copy_call(plan, outs, scalars, *operands):
    count = len(plan(None, [None] * len(operands), [None] * len(outs)))

    def body(numbers, *refs):
        sems = refs[-1]
        pairs = plan(numbers, refs[: len(operands)], refs[len(operands) : -1])
        copies = [pltpu.make_async_copy(a, b, sems.at[i]) for i, (a, b) in enumerate(pairs)]
        for copy in copies:
            copy.start()
        for copy in copies:
            copy.wait()

    return kernel_call(
        body,
        outs,
        *operands,
        scalars=scalars,
        scratch=[pltpu.SemaphoreType.DMA((count,))],
        space=pl.ANY,
    )


def view(ref, *spans):
    if ref is None:
        return None
    index = tuple(
        pl.ds(start if isinstance(start, int) else pl.multiple_of(start, 128), size)
        for start, size in spans
    )
    return ref.at[index]


def at(numbers, i):
    return None if numbers is None else numbers[i]


def ranks_of(ranks, ids):
    total = jnp.zeros(ids.shape, f32)
    for a in range(ranks.shape[0]):
        total = jnp.where(ids == a, ranks[a].astype(f32), total)
    return total


def kept(ids, ranks, value):
    rank = ranks_of(ranks, ids)
    column = lax.broadcasted_iota(jnp.int32, value.shape, 1).astype(f32)
    return jnp.where(column < rank, value, 0.0), 16.0 / rank


def roll_rows(value):
    half = value.shape[0] // 2
    return jnp.concatenate([value[half:], value[:half]], axis=0)


def back_kernel(ids, dy, up, out):
    size = out.shape[1]
    token = ids[...].astype(f32)
    for i in range(0, up.shape[0] // size, 2):
        both = contract_final_axis(dy[...], up[i * size : (i + 2) * size, :])
        for j in (0, 1):
            part = jnp.where(token == i + j, both[:, j * size : (j + 1) * size], 0.0)
            out[...] = part if i + j == 0 else out[...] + part


def spread_into(out, token, value, order):
    size = value.shape[1]
    for i in range(out.shape[1] // size):
        a = order[i].astype(f32)
        out[:, i * size : (i + 1) * size] = jnp.where(token == a, value, 0.0).astype(bf16)


def back_end_kernel(numbers, ids, part, got, wide, sent):
    token = ids[...].astype(f32)
    count = numbers.shape[0] // 3
    ranks, order = [numbers[i] for i in range(count)], [numbers[count + i] for i in range(count)]
    value, scale = kept(token, jnp.stack(ranks), part[...] + roll_rows(got[...]))
    value = (scale * value).astype(bf16)
    size = value.shape[1]
    sent[:, :size] = value
    sent[:, size:] = ids[...]
    spread_into(wide, token, value.astype(f32), order)


def spread_in_kernel(numbers, packet, wide):
    size = packet.shape[1] // 2
    count = numbers.shape[0] // 3
    order = [numbers[count + i] for i in range(count)]
    spread_into(wide, packet[:, size:].astype(f32), packet[:, :size].astype(f32), order)


def low_kernel(numbers, ids, x_mine, x_other, own, near, far, own_near_other, far_other, out):
    size = out.shape[1]
    wide = 2 * size
    token = ids[...].astype(f32)
    mine = [own[...], near[...], far[:, :wide], far[:, wide:]]
    other = [
        own_near_other[:, :wide],
        own_near_other[:, wide:],
        far_other[:, :wide],
        far_other[:, wide:],
    ]
    for i in range(4):
        both = matmul(x_mine[...], mine[i]) + matmul(x_other[...], other[i])
        for j in (0, 1):
            place = numbers[numbers.shape[0] // 3 + 2 * i + j].astype(f32)
            part = jnp.where(token == place, both[:, j * size : (j + 1) * size], 0.0)
            out[...] = part if i + j == 0 else out[...] + part


def low_end_kernel(numbers, ids, part, got, up, dy, delta, *grads):
    token = ids[...].astype(f32)
    count = numbers.shape[0] // 3
    size = part.shape[1]
    ranks = jnp.stack([numbers[i] for i in range(count)])
    value, scale = kept(token, ranks, part[...] + roll_rows(got[...]))
    value = value.astype(bf16).astype(f32)

    def pair(first, second):
        return jnp.concatenate(
            [jnp.where(token == a, value, 0.0) for a in (first, second)], axis=1
        ).astype(bf16)

    total = 0.0
    for i, out in enumerate(grads):
        places = [numbers[2 * count + 2 * i + j].astype(f32) for j in (0, 1)]
        out[...] = contract_first(pair(*places), dy[...]).astype(bf16)
        total += matmul(pair(2 * i, 2 * i + 1), up[2 * i * size : 2 * (i + 1) * size, :])
    delta[...] = (scale[:, :1] * total).astype(bf16)


def to_middle_kernel(x_here, back, x_in, back_in, out):
    half = back.shape[1] // 2
    sums = contract_first(x_here[...], back[:, half:])
    out[...] = (sums + contract_first(x_in[...], back_in[:, half:])).astype(bf16)


def to_end_kernel(x_here, back, crossed, out):
    wide = out.shape[1]
    sums = contract_first(x_here[...], back[:, wide : 2 * wide])
    out[...] = (sums + crossed[:, wide:].astype(f32)).astype(bf16)


def finish_kernel(x_here, back, x_in, back_in, crossed, outer, here, there):
    size = here.shape[1]
    wide = 2 * size
    sums = contract_first(x_here[...], back[:, :wide])
    sums += contract_first(x_in[...], back_in[:, :wide])
    sums += crossed[:, :wide].astype(f32) + outer[...].astype(f32)
    here[...] = sums[:, :size].astype(bf16)
    there[...] = sums[:, size:].astype(bf16)


def up_sent_kernel(up, out):
    cols = out.shape[2]
    for i in range(out.shape[0]):
        out[i] = up[:, (i % 2) * cols : (i % 2 + 1) * cols]


def packet_kernel(cotangent, adapters, out):
    rows, kv = cotangent.shape
    size = out.shape[1] - kv
    out[:, :kv] = cotangent[...]
    numbers = jnp.broadcast_to(adapters[...].astype(f32), (rows, size))
    out[:, kv:] = numbers.astype(bf16)


def unpack_kernel(flags, here, there, half, ids, quarter):
    rows = here.shape[0]
    kv = half.shape[1]
    cols = quarter.shape[1]
    span = pl.ds(pl.multiple_of(flags[3] * cols, 128), cols)
    for i, packet in enumerate((here, there)):
        place = slice(i * rows, (i + 1) * rows)
        half[place] = packet[:, :kv]
        ids[place] = packet[:, kv:]
        quarter[place] = packet[:, span]


def dy_line_kernel(places, here, got, out):
    cols = out.shape[1] // 4
    for i in range(4):
        place = places[i]
        span = pl.ds(pl.multiple_of((place % 2) * cols, 128), cols)
        own = place // 2 == places[4]

        @pl.when(own)
        def _():
            out[:, i * cols : (i + 1) * cols] = here[:, span]

        @pl.when(jnp.logical_not(own))
        def _():
            out[:, i * cols : (i + 1) * cols] = got[:, span]


def far_kernel(flags, crossed, outer, out):
    @pl.when(flags[4] == 1)
    def _():
        out[...] = crossed[...]

    @pl.when(flags[4] == 0)
    def _():
        out[...] = outer[...]


def up_sum_kernel(numbers, first, second, third, fourth, here, there):
    count = numbers.shape[0] // 3
    size = here.shape[0]
    for i, out in enumerate((here, there)):
        adapter = numbers[count + i]
        rank = jnp.float32(1.0)
        for a in range(count):
            rank = jnp.where(adapter == a, numbers[a].astype(f32), rank)
        span = slice(i * size, (i + 1) * size)
        part = sum(v[span, :].astype(f32) for v in (first, second, third, fourth))
        out[...] = (jnp.full(part.shape, 16.0, f32) / rank * part).astype(bf16)


def up_place_kernel(flags, here, there, out):
    cols = here.shape[1]
    out[:, pl.ds(pl.multiple_of(flags[3] * cols, 128), cols)] = here[...]
    out[:, pl.ds(pl.multiple_of((1 - flags[3]) * cols, 128), cols)] = there[...]


def add_kernel(left, right, out):
    out[...] = left[...] + right[...]


def dx_kernel(dy, back, own, near, far, *rest):
    *adapter, here, there = rest
    rows, width = here.shape
    cols = own.shape[1]
    tile = min(cols, width)
    for t in range(width // tile):
        span = slice(t * tile, (t + 1) * tile)
        base = contract_final_axis(dy[:, :cols], own[span, :])
        base += contract_final_axis(dy[:, cols : 2 * cols], near[span, :])
        base += contract_final_axis(dy[:, 2 * cols :], far[span, :])
        lora, start = 0.0, 0
        for piece in adapter:
            stop = start + piece.shape[1]
            lora += contract_final_axis(back[:, start:stop], piece[span, :])
            start = stop
        total = (base + lora.astype(bf16).astype(f32)).astype(bf16)
        here[:, span] = total[:rows]
        there[:, span] = total[rows:]


def y_kernel(flags, tokens, own, near, far, *rest):
    *before, keep, send = rest
    cols = own.shape[1]

    def store(pair, first, part):
        mine = flags[0] == (1 if pair else 0)
        for i in (0, 1):
            place = (first + i) % 2
            block = matmul(tokens[...], part(i))

            @pl.when(mine)
            def _():
                keep[place] = block + before[0][place] if before else block

            @pl.when(jnp.logical_not(mine))
            def _():
                send[place] = block + before[1][place] if before else block

    store(True, flags[1], lambda i: (own, near)[i][...])
    store(False, flags[2], lambda i: far[:, i * cols : (i + 1) * cols])


def y_sum_kernel(flags, keep, got, delta, here, there):
    rows = here.shape[1]
    for i in (0, 1):
        added = jnp.where(flags[3] == i, delta[...].astype(f32), 0.0)
        total = keep[i] + got[i] + added
        here[i] = total[:rows]
        there[i] = total[rows:].astype(bf16)


def y_end_kernel(here, got, out):
    cols = here.shape[2]
    for i in (0, 1):
        out[:, i * cols : (i + 1) * cols] = (here[i] + got[i].astype(f32)).astype(bf16)


def body_line(
    tokens,
    cotangent,
    frozen_value_weight,
    adapter_down_weight,
    adapter_up_weight,
    token_adapter,
    rank_step_count,
):
    rows, width = tokens.shape
    kv = cotangent.shape[1]
    cols = frozen_value_weight.shape[1]
    down = adapter_down_weight[0]
    up = adapter_up_weight[0]
    size = down.shape[1]
    wide = 2 * size
    quarter = width // 2
    eighth = quarter // 2
    kvq = kv // 2
    both = 2 * rows
    z, x = lax.axis_index("fsdp"), lax.axis_index("own")
    y, c = lax.axis_index("rep"), lax.axis_index("tp")
    first_pair = z < 2
    is_middle = (z == 1) | (z == 2)
    line = [z, z + 1 - 2 * (z % 2), jnp.where(first_pair, 2, 1), jnp.where(first_pair, 3, 0)]
    adapters = jnp.stack([2 * t + o for t in line for o in (x, 1 - x)]).astype(jnp.int32)
    number = adapters.shape[0]
    starts = jnp.stack(
        [side * quarter + half * eighth for side in (x, 1 - x) for half in (y, 1 - y)]
    ).astype(jnp.int32)
    ranks = size // 8 * rank_step_count
    ring = jnp.stack([2 * ((z + k) % 4) + o for k in range(4) for o in (x, 1 - x)])
    numbers = jnp.concatenate([ranks, adapters, ring.astype(jnp.int32)])
    flags = jnp.stack([(c == 0) == first_pair, z % 2 == 1, z >= 2, x == 1, is_middle])
    flags = flags.astype(jnp.int32)
    places = jnp.stack([*line, c]).astype(jnp.int32)

    latest = []

    def step(*values):
        if latest:
            values = lax.optimization_barrier((*values, latest[0]))[: len(values)]
        return values[0] if len(values) == 1 else values

    def done(value):
        latest[:] = [value]
        return value

    def like(*shape, kind=bf16):
        return jax.ShapeDtypeStruct(shape, kind)

    def around(value, shift):
        return along(value, [(i, (i + shift) % 4) for i in range(4)])

    def rows_at(i, value, length):
        out = like(length, value.shape[1])
        return copy_call(
            lambda n, a, o: [(view(a[0], (at(n, i), length), (0, value.shape[1])), o[0])],
            [out],
            starts,
            value,
        )[0]

    def columns_at(i, value):
        out = like(value.shape[0], eighth)
        return copy_call(
            lambda n, a, o: [(view(a[0], (0, value.shape[0]), (at(n, i), eighth)), o[0])],
            [out],
            starts,
            value,
        )[0]

    def side_by_side(*values):
        widths = [v.shape[1] for v in values]
        length = values[0].shape[0]
        return copy_call(
            lambda n, a, o: [
                (a[i], view(o[0], (0, length), (sum(widths[:i]), widths[i])))
                for i in range(len(values))
            ],
            [like(length, sum(widths))],
            starts,
            *values,
        )[0]

    def tokens_of(i, value, got):
        return copy_call(
            lambda n, a, o: [
                (view(a[0], (0, rows), (at(n, i), eighth)), view(o[0], (0, rows), (0, eighth))),
                (a[1], view(o[0], (rows, rows), (0, eighth))),
            ],
            [like(both, eighth)],
            starts,
            value,
            got,
        )[0]

    up_sent = kernel_call(up_sent_kernel, [like(number, size, kvq)], up)[0]
    up_all = lax.all_to_all(
        done(up_sent), ("fsdp", "own"), split_axis=0, concat_axis=0, tiled=True
    ).reshape(number * size, kvq)
    down_got = swap(done(rows_at(2, step(down), eighth)), "own")
    packet_here = done(
        kernel_call(packet_kernel, [like(rows, kv + size)], step(cotangent), token_adapter)[0]
    )
    packet = swap(packet_here, "own")
    x_got = [swap(done(columns_at(2, step(tokens))), "own")]
    down_piece = done(
        copy_call(
            lambda n, a, o: [
                (view(a[0], (at(n, 0), eighth), (0, size)), view(o[0], (0, eighth), (0, size))),
                (a[1], view(o[0], (0, eighth), (size, size))),
            ],
            [like(eighth, wide)],
            starts,
            down,
            step(down_got),
        )[0]
    )
    down_near = along(down_piece, NEIGHBOURS)
    packet, up_all = step(packet, up_all)
    dy_half, ids, dy_quarter = kernel_call(
        unpack_kernel,
        [like(both, kv), like(both, size), like(both, kvq)],
        packet_here,
        packet,
        scalars=flags,
    )
    compact = like(both, size, kind=f32)
    back_part = done(kernel_call(back_kernel, [compact], ids, dy_quarter, up_all)[0])
    back_tp = swap(back_part, "tp")
    weight_here = done(rows_at(0, step(frozen_value_weight), eighth))
    weight_near = along(weight_here, NEIGHBOURS)
    back_part = done(kernel_call(add_kernel, [compact], back_part, step(back_tp))[0])
    back_got = swap(back_part, "own")
    down_near, x_got[0] = step(down_near, x_got[0])
    crossing = done(side_by_side(down_piece, down_near))
    down_crossed = along(crossing, MIDDLE)
    down_other = swap(crossing, "rep")
    back_wide, back_sent = kernel_call(
        back_end_kernel,
        [like(both, number * size), like(both, wide)],
        ids,
        back_part,
        step(back_got),
        scalars=numbers,
    )
    back_in = along(done(back_sent), INWARD)
    crossing = done(side_by_side(weight_here, step(weight_near)))
    weight_crossed = along(crossing, MIDDLE)
    x_got.append(swap(done(columns_at(3, step(tokens))), "own"))
    back_in_wide = done(
        kernel_call(
            spread_in_kernel, [like(both, number * size)], step(back_in), scalars=numbers
        )[0]
    )
    x_mine = done(tokens_of(0, tokens, step(x_got[0])))
    x_in = [along(x_mine, INWARD)]
    weight_other = done(rows_at(1, step(frozen_value_weight), eighth))
    down_crossed = done(step(down_crossed))
    down_outer = along(down_crossed, OUTWARD)
    weight_near, down_other = step(weight_near, down_other)
    weight_near_other = swap(done(weight_near), "rep")
    x_other = done(tokens_of(1, tokens, step(x_got[1])))
    x_in.append(along(x_other, INWARD))
    x_both = [x_mine, x_other]

    def to_middle(half):
        x_in[half] = step(x_in[half])
        sums = kernel_call(
            to_middle_kernel,
            [like(eighth, 2 * wide)],
            x_both[half],
            back_wide,
            x_in[half],
            back_in_wide,
        )[0]
        return along(done(sums), MIDDLE)

    def to_end(half, crossed):
        sums = kernel_call(
            to_end_kernel, [like(eighth, wide)], x_both[half], back_wide, step(crossed)
        )[0]
        return along(done(sums), OUTWARD)

    def finish(half, crossed, outer, *others):
        outer, *_ = step(outer, x_mine, *others)
        here, there = kernel_call(
            finish_kernel,
            [like(eighth, size)] * 2,
            x_both[half],
            back_wide,
            x_in[half],
            back_in_wide,
            crossed,
            outer,
        )
        return done(here), there

    def far_of(crossed, outer):
        out = like(*crossed.shape)
        return kernel_call(far_kernel, [out], crossed, outer, scalars=flags)[0]

    middle = [to_middle(0)]
    weight_crossed = done(step(weight_crossed))
    weight_outer = along(weight_crossed, OUTWARD)
    dy_half, weight_near_other = step(dy_half, weight_near_other)
    dy_tp = swap(dy_half, "tp")
    dy_line = done(
        kernel_call(
            dy_line_kernel, [like(both, 2 * kv)], dy_half, step(dy_tp), scalars=places
        )[0]
    )
    down_far = done(far_of(down_crossed, step(down_outer)))
    down_far_other = swap(down_far, "rep")
    middle.append(to_middle(1))
    outward = [to_end(0, middle[0])]
    weight_far = done(far_of(weight_crossed, step(weight_outer)))
    weight_far_other = swap(weight_far, "rep")
    half_grad = [like(rows, eighth)] * 2
    dx_mine, dx_sent = kernel_call(
        dx_kernel,
        half_grad,
        step(dy_line),
        back_wide,
        weight_here,
        weight_near,
        weight_far,
        down_piece,
        down_near,
        down_far,
    )
    dx_mine_got = swap(done(dx_sent), "own")

    low_part = done(
        kernel_call(
            low_kernel,
            [compact],
            ids,
            x_mine,
            x_other,
            down_piece,
            down_near,
            down_far,
            down_other,
            step(down_far_other),
            scalars=numbers,
        )[0]
    )
    low_tp = swap(low_part, "tp")
    grad_here, grad_sent = finish(0, middle[0], outward[0])
    blocks = [like(2, both, cols, kind=f32)] * 2
    y_first = kernel_call(
        y_kernel, blocks, step(x_mine), weight_here, weight_near, weight_far, scalars=flags
    )
    done(y_first[0])
    low_tp, dx_mine_got = step(low_tp, dx_mine_got)
    low_part = done(kernel_call(add_kernel, [compact], low_part, low_tp)[0])
    low_got = swap(low_part, "own")
    outward.append(to_end(1, middle[1]))
    low_got = step(low_got)
    grad_got = swap(lax.optimization_barrier((grad_sent, low_got))[0], "own")
    delta, *up_parts = kernel_call(
        low_end_kernel,
        [like(both, kvq)] + [like(wide, kvq)] * 4,
        ids,
        low_part,
        low_got,
        up_all,
        dy_quarter,
        scalars=numbers,
    )
    done(delta)
    up_got = [around(up_parts[k], k) for k in (1, 2, 3)]
    dx_other, dx_sent = kernel_call(
        dx_kernel,
        half_grad,
        dy_line,
        back_wide,
        weight_other,
        weight_near_other,
        step(weight_far_other),
        down_other,
        down_far_other,
    )
    dx_other_got = swap(done(dx_sent), "own")
    grad_last, grad_sent = finish(1, middle[1], outward[1])
    grad_last_got = swap(grad_sent, "own")
    x_other, grad_got = step(x_other, grad_got)
    y_keep, y_sent = kernel_call(
        y_kernel,
        blocks,
        x_other,
        weight_other,
        weight_near_other,
        weight_far_other,
        *y_first,
        scalars=flags,
    )
    y_got = swap(done(y_sent), "tp")
    y_got = step(y_got)
    y_here, y_sent = kernel_call(
        y_sum_kernel,
        [like(2, rows, cols, kind=f32), like(2, rows, cols)],
        y_keep,
        y_got,
        delta,
        scalars=flags,
    )
    y_got = swap(done(y_sent), "own")
    up_got = step(*up_got)
    up_mine, up_theirs = kernel_call(
        up_sum_kernel, [like(size, kvq)] * 2, up_parts[0], *up_got, scalars=numbers
    )
    up_theirs = swap(done(up_theirs), "own")

    def in_place(axis, out, *pieces):
        def plan(n, a, o):
            spans = [[(0, length) for length in out.shape] for _ in range(4)]
            for i in range(4):
                spans[i][axis] = (at(n, i), eighth)
            return [(a[i], view(o[0], *spans[i])) for i in range(4)]

        return copy_call(plan, [out], starts, *pieces)[0]

    dx_other_got = step(dx_other_got)
    input_grad = done(
        in_place(1, like(rows, width), dx_mine, dx_other, dx_mine_got, dx_other_got)
    )
    projected = done(kernel_call(y_end_kernel, [like(rows, kv)], y_here, step(y_got))[0])
    down_gradient = done(
        in_place(
            0, like(width, size), grad_here, grad_last, grad_got, step(grad_last_got)
        )[None]
    )
    up_gradient = kernel_call(
        up_place_kernel, [like(size, kv)], up_mine, step(up_theirs), scalars=flags
    )[0][None]
    return (projected, input_grad, down_gradient, up_gradient)


def body_routed(
    tokens,
    cotangent,
    frozen_value_weight,
    adapter_down_weight,
    adapter_up_weight,
    token_adapter,
    rank_step_count,
):
    rows, width_halved = tokens.shape
    half_kv = cotangent.shape[1]
    owning_adapters = lax.axis_size(("fsdp", "own"))
    greatest_rank = 3 * rows // (2 * owning_adapters)
    ids = token_adapter[:, 0]
    table = (ids[:, None] == jnp.arange(owning_adapters, dtype=jnp.int32)[None, :]).astype(
        f32
    )
    order = jnp.arange(rows, dtype=jnp.int32)
    earlier = (order[:, None] > order[None, :]).astype(f32)
    before = jnp.dot(earlier, table, precision=lax.Precision.HIGHEST)
    place = jnp.sum(before * table, axis=1).astype(jnp.int32)
    slot = ids * greatest_rank + place
    source_rows = jnp.full((owning_adapters * greatest_rank,), rows, jnp.int32).at[slot].set(order)
    padded_x = jnp.concatenate([tokens, jnp.zeros((1, width_halved), bf16)], axis=0)
    padded_dy = jnp.concatenate([cotangent, jnp.zeros((1, half_kv), bf16)], axis=0)
    send_x = jnp.take(padded_x, source_rows, axis=0)
    send_dy = jnp.take(padded_dy, source_rows, axis=0)
    recv_x, recv_dy = (
        lax.all_to_all(
            send_x.reshape(owning_adapters, greatest_rank, width_halved),
            ("fsdp", "own"),
            split_axis=0,
            concat_axis=0,
            tiled=True,
        ),
        lax.all_to_all(
            send_dy.reshape(owning_adapters, greatest_rank, half_kv),
            ("fsdp", "own"),
            split_axis=0,
            concat_axis=0,
            tiled=True,
        ),
    )
    flat_x = recv_x.reshape(owning_adapters * greatest_rank, width_halved)
    flat_dy = recv_dy.reshape(owning_adapters * greatest_rank, half_kv)
    dy_full = lax.all_gather(cotangent, "tp", axis=1, tiled=True)
    whole = lax.all_gather(frozen_value_weight, "fsdp", axis=1, tiled=True)
    partial_y = jnp.dot(tokens, whole, preferred_element_type=f32)
    base_dx = contract_final_axis(dy_full, whole)
    base_y = lax.psum_scatter(partial_y, "tp", scatter_dimension=1, tiled=True)
    down_matrix = adapter_down_weight[0]
    up_matrix = adapter_up_weight[0]
    part_low = jnp.dot(flat_x, down_matrix, preferred_element_type=f32)
    part_back = contract_final_axis(flat_dy, up_matrix)
    low_sum, back_sum = lax.psum((part_low, part_back), "tp")
    width_rank = down_matrix.shape[1]
    rank = width_rank // 8 * rank_step_count[lax.axis_index(("fsdp", "own"))]
    keep = jnp.arange(width_rank, dtype=jnp.int32)[None, :] < rank
    scale = 16.0 / rank.astype(f32)
    low = jnp.where(keep, low_sum, 0.0).astype(bf16)
    backward_pass = (scale * jnp.where(keep, back_sum, 0.0)).astype(bf16)
    delta = (scale * jnp.dot(low, up_matrix, preferred_element_type=f32)).astype(
        bf16
    )
    adapter_input_gradient = contract_final_axis(backward_pass, down_matrix).astype(bf16)
    down_gradient = contract_first(flat_x, backward_pass).astype(bf16)[None]
    up_gradient = (scale * contract_first(low, flat_dy)).astype(bf16)[None]
    home_delta, home_dx = (
        lax.all_to_all(
            delta.reshape(owning_adapters, greatest_rank, half_kv),
            ("fsdp", "own"),
            split_axis=0,
            concat_axis=0,
            tiled=True,
        ),
        lax.all_to_all(
            adapter_input_gradient.reshape(owning_adapters, greatest_rank, width_halved),
            ("fsdp", "own"),
            split_axis=0,
            concat_axis=0,
            tiled=True,
        ),
    )
    adapter_delta_rows = jnp.take(
        home_delta.reshape(owning_adapters * greatest_rank, half_kv), slot, axis=0
    )
    input_gradient_rows = jnp.take(
        home_dx.reshape(owning_adapters * greatest_rank, width_halved), slot, axis=0
    )
    projected = (base_y + adapter_delta_rows.astype(f32)).astype(bf16)
    input_grad = (base_dx + input_gradient_rows.astype(f32)).astype(bf16)
    return (projected, input_grad, down_gradient, up_gradient)


def solution(mesh):
    placed = (
        P(("rep", "fsdp", "own"), "tp"),
        P(("rep", "fsdp", "own"), "tp"),
        P("tp", "fsdp"),
        P(("fsdp", "own"), "tp", None),
        P(("fsdp", "own"), None, "tp"),
        P(("rep", "fsdp", "own"), None),
        P(),
    )
    line = mesh.shape["fsdp"] == 4 and mesh.shape["own"] == 2 and mesh.shape["rep"] == 2
    return jax.shard_map(
        body_line if line else body_routed,
        mesh=mesh,
        in_specs=placed,
        out_specs=(
            P(("rep", "fsdp", "own"), "tp"),
            P(("rep", "fsdp", "own"), "tp"),
            P(("rep", "fsdp", "own"), "tp", None),
            P(("rep", "fsdp", "own"), None, "tp"),
        ),
        check_vma=False,
    )
```
